32 devices in a mesh: groups: 2 (over x), ctx: 16 (over z, y, core).
Axes of the slice: x: 2, y: 2, z: 4, core: 2. Of those that a mesh axis runs over, the one named last changes fastest.
Arguments:
- hidden: bfloat16 [4096, 4096], P(('groups', 'ctx')), parts along dimension 0, may hold values from -6 to 6
- frozen_query: bfloat16 [4096, 2048], P(('groups', 'ctx')), parts along dimension 0, may hold values from -18 to 18
- frozen_key: bfloat16 [4096, 512], P(('groups', 'ctx')), parts along dimension 0, may hold values from -18 to 18
- frozen_value: bfloat16 [4096, 512], P(('groups', 'ctx')), parts along dimension 0, may hold values from -6 to 6
- adapter_bank: bfloat16 [16, 64, 21504], P('ctx'), may hold values from -0.57 to 0.57
- request_shards: int32 [6], P('groups'), parts along dimension 0, may hold values from 1 to 9, 16 in all
- request_adapter: int32 [6], P('groups'), parts along dimension 0, may hold values from 0 to 15
- adapter_owner: int32 [16], replicated, may hold values from 0 to 15, each once
Outputs:
- attention: bfloat16 [4096, 2048], P(('groups', 'ctx')), parts along dimension 0
- adapter_output: bfloat16 [4096, 4096], P(('groups', 'ctx')), parts along dimension 0
The draws below stay inside these ranges and needn't reach their ends.
There are 2 independent parts, one for each index of `groups`. The reference program is written for one: setup_inputs(seed, part) draws one part's arguments, and reference() takes and returns one part's arrays. A program takes and returns all parts, laid end to end along the dimension named above; an argument that names none is the same for every part. Nothing has to cross between parts.
Inputs may be any that keep to these rules, and one draw needn't show every extreme that they name: `request_shards`: request lengths sum to 16; the longest has exactly 9 shards. `adapter_owner`: a permutation: every bank entry holds exactly one adapter.
All inputs are finite; a program needn't handle non-finite values.
Results may differ from the reference program's by a relative error of at most 0.012.
Values may be sent and summed in bfloat16 or wider, within the bound.
No kernel may reach another device: no remote copies, remote signals or barrier semaphores. Data moves between devices by JAX's collectives and lax.ppermute only.
A program may use at most 64 MiB of HBM per device.

```python
import math
import jax
import jax.numpy as jnp
import numpy as np
from jax import lax

D = 4096
HEAD_SIZE = 128
QUERY_HEADS = 16
KEY_VALUE_HEADS = 4
RANK = 64
TOK_DEV = 128
REQS = 3
QUERIES_PER_KEY = 4
CONTEXT_TOKENS = 2048
ADAPTERS = 16
BANK_COLS = 21504
N_CTX = 16


def draw_frozen_query(key, part):
    key = jax.random.fold_in(key, 11)
    return jnp.clip(jax.random.normal(key, (CONTEXT_TOKENS, QUERY_HEADS * HEAD_SIZE), jnp.float32), -6.0, 6.0).astype(jnp.bfloat16)


def draw_frozen_key(key, part):
    key = jax.random.fold_in(key, 17)
    return jnp.clip(jax.random.normal(key, (CONTEXT_TOKENS, KEY_VALUE_HEADS * HEAD_SIZE), jnp.float32), -6.0, 6.0).astype(jnp.bfloat16)


def draw_adapter_bank(key, part):
    key = jax.random.fold_in(key, 23)
    value_matrix = jnp.clip(jax.random.normal(key, (ADAPTERS, RANK, BANK_COLS), jnp.float32), -4.5, 4.5)
    column = jnp.arange(BANK_COLS)
    opening_limit = 3 * D
    closing_limit = opening_limit + QUERY_HEADS * HEAD_SIZE + 2 * KEY_VALUE_HEADS * HEAD_SIZE
    third_end = closing_limit + QUERY_HEADS * HEAD_SIZE
    column_scale = jnp.where(column < opening_limit, D ** (-0.5), jnp.where(column < closing_limit, RANK ** (-0.5), jnp.where(column < third_end, (QUERY_HEADS * HEAD_SIZE) ** (-0.5), RANK ** (-0.5))))
    return (value_matrix * column_scale[None, None, :]).astype(jnp.bfloat16)


def block_levels(rng, dims, cuts, low, top_value):
    def one(position, parts):
        draws = jax.random.uniform(jax.random.fold_in(jax.random.fold_in(rng, 6), position), (parts,), jnp.float32, low / len(cuts), top_value / len(cuts))
        return jnp.repeat(jnp.exp(draws), dims[position] // parts).reshape((-1,) + (1,) * (len(dims) - position - 1))

    loudness = one(*cuts[0])
    for cut in cuts[1:]:
        loudness = loudness * one(*cut)
    return loudness


def rank_bounds(count, lean):
    loads = [(1 << 20) // math.isqrt(rank ** lean) + 1 for rank in range(1, count + 1)]
    scale = 1 + sum(loads) // (1 << 30)
    return np.cumsum(np.array([max(1, weight // scale) for weight in loads]))


def ranked_ids(rng, extent, amount, slope):
    grid = rank_bounds(amount, slope)
    ticket = jax.random.randint(jax.random.fold_in(rng, 1), extent, 0, int(grid[amount - 1]))
    grade = jnp.searchsorted(jnp.asarray(grid, jnp.int32), ticket, side="right")
    return jax.random.permutation(jax.random.fold_in(rng, 2), amount)[grade].astype(jnp.int32)


def profile(number_of, total, limit, skew):
    weights = [(1 << 20) // math.isqrt(rank ** skew) + 1 for rank in range(2, number_of + 1)]
    spare, holding = total - limit - (number_of - 1), [1] * (number_of - 1)
    while spare > 0:
        candidates = [i for i in range(number_of - 1) if holding[i] < limit]
        whole, budget = sum([weights[i] for i in candidates]), spare
        for i in candidates:
            addition = min(limit - holding[i], max(1, budget * weights[i] // whole), spare)
            holding[i] = holding[i] + addition
            spare = spare - addition
    return np.array([limit] + holding)


def uneven_parts(stream_key, count, total, bound, lean):
    if count == 2:
        one = jax.random.randint(stream_key, (), max(1, total - bound), min(bound, total - 1) + 1)
        return jnp.stack([one, total - one])
    sizes = jnp.asarray(profile(count, total, bound, lean), jnp.int32)
    twos = (count - 1) // 2
    source_of, sink = sizes[1:1 + 2 * twos:2], sizes[2:2 + 2 * twos:2]
    slack = jnp.minimum(source_of - 1, bound - sink)
    passed = jax.random.randint(jax.random.fold_in(stream_key, 1), (twos,), 0, 1 << 20) % (slack + 1)
    sizes = sizes.at[1:1 + 2 * twos:2].set(source_of - passed).at[2:2 + 2 * twos:2].set(sink + passed)
    return sizes[jax.random.permutation(jax.random.fold_in(stream_key, 2), count)]


def noise(own_key, extent, deviation, limit, pieces=(), kind=jnp.bfloat16):
    loudness = block_levels(own_key, extent, pieces, -0.22, 0.18) if pieces else 1.0
    drawn = jax.random.normal(own_key, extent, jnp.float32) * deviation * loudness
    return jnp.minimum(jnp.maximum(drawn, -limit), limit).astype(kind)


def setup_inputs(seed: int = 0, part: int = 0) -> dict:
    key_list = jax.random.split(jax.random.key(seed), 9)
    part_keys = jax.random.split(jax.random.fold_in(key_list[8], part), 9)
    return {
        "hidden": noise(part_keys[0], (CONTEXT_TOKENS, D), 1.0, 6.0, ((0, 16),)),
        "frozen_query": draw_frozen_query(jax.random.fold_in(jax.random.fold_in(key_list[8], part), 71), part),
        "frozen_key": draw_frozen_key(jax.random.fold_in(jax.random.fold_in(key_list[8], part), 71), part),
        "frozen_value": noise(part_keys[3], (CONTEXT_TOKENS, KEY_VALUE_HEADS * HEAD_SIZE), 1.0, 6.0, ((0, 16),)),
        "adapter_bank": draw_adapter_bank(jax.random.fold_in(key_list[8], 71), part),
        "request_shards": uneven_parts(part_keys[5], REQS, N_CTX, N_CTX // 2 + 1, 2).astype(jnp.int32),
        "request_adapter": ranked_ids(part_keys[6], (REQS,), ADAPTERS, 2),
        "adapter_owner": jax.random.permutation(key_list[7], ADAPTERS).astype(jnp.int32),
    }


adapter_scale = 0.5
rope_theta = 500000.0
score_masked = -1e+30

def request_layout(request_shards, shards):
    starts = (jnp.cumsum(request_shards) - request_shards).astype(jnp.int32)
    shard_ids = jnp.arange(shards, dtype=jnp.int32)
    request_of = lax.optimization_barrier(jnp.sum((starts[None, :] <= shard_ids[:, None]).astype(jnp.int32), axis=1)) - 1
    longest = jnp.argmax(request_shards).astype(jnp.int32)
    offset = (starts[longest] + request_shards[longest] // 2) % shards
    packed_of = ((shard_ids + offset) % shards).astype(jnp.int32)
    return (request_of.astype(jnp.int32), starts, packed_of)

def rotate(value_matrix, positions):
    half_dim = HEAD_SIZE // 2
    frequency = rope_theta ** (-(jnp.arange(half_dim, dtype=jnp.float32) * 2.0) / HEAD_SIZE)
    angles = positions.astype(jnp.float32)[:, None] * frequency[None, :]
    cosines = jnp.concatenate([jnp.cos(angles), jnp.cos(angles)], 1)[:, None, :]
    sines = jnp.concatenate([jnp.sin(angles), jnp.sin(angles)], 1)[:, None, :]
    front_half = value_matrix[..., :half_dim]
    second = value_matrix[..., half_dim:]
    turned = jnp.concatenate([-second, front_half], -1)
    return value_matrix * cosines + turned * sines

def project(hidden, frozen_query, frozen_key, frozen_value, adapter, positions):
    model_width = hidden.shape[1]
    query_width = frozen_query.shape[1]
    key_width = frozen_key.shape[1]
    token_rows = hidden.shape[0]
    low_parts = []
    for which in range(3):
        down_cols = adapter[:, which * model_width:(which + 1) * model_width]
        low_parts.append(jnp.dot(hidden, down_cols.T, preferred_element_type=jnp.float32).astype(jnp.bfloat16))
    upward_columns = adapter[:, 3 * model_width:3 * model_width + query_width + 2 * key_width]
    query_update = jnp.dot(low_parts[0], upward_columns[:, :query_width], preferred_element_type=jnp.float32)
    key_update = jnp.dot(low_parts[1], upward_columns[:, query_width:query_width + key_width], preferred_element_type=jnp.float32)
    value_update = jnp.dot(low_parts[2], upward_columns[:, query_width + key_width:], preferred_element_type=jnp.float32)
    query_matrix = frozen_query.astype(jnp.float32) + adapter_scale * query_update
    key_output = frozen_key.astype(jnp.float32) + adapter_scale * key_update
    value_output = (frozen_value.astype(jnp.float32) + adapter_scale * value_update).astype(jnp.bfloat16)
    query_matrix = rotate(query_matrix.reshape(token_rows, query_width // HEAD_SIZE, HEAD_SIZE), positions).reshape(token_rows, query_width)
    key_output = rotate(key_output.reshape(token_rows, key_width // HEAD_SIZE, HEAD_SIZE), positions).reshape(token_rows, key_width)
    return (query_matrix.astype(jnp.bfloat16), key_output.astype(jnp.bfloat16), value_output)

def output_adapter(attended_output, adapter, model_width):
    query_width = attended_output.shape[1]
    bank_width = adapter.shape[1]
    down_cols = adapter[:, bank_width - model_width - query_width:bank_width - model_width]
    upward_columns = adapter[:, bank_width - model_width:]
    reduced_rank = jnp.dot(attended_output, down_cols.T, preferred_element_type=jnp.float32).astype(jnp.bfloat16)
    return (adapter_scale * jnp.dot(reduced_rank, upward_columns, preferred_element_type=jnp.float32)).astype(jnp.bfloat16)

def broadened_heads(value_matrix):
    return lax.optimization_barrier(value_matrix).astype(jnp.float32)

def reference(hidden, frozen_query, frozen_key, frozen_value, adapter_bank, request_shards, request_adapter, adapter_owner):
    token_rows = TOK_DEV
    shards = N_CTX
    request_of, starts, packed_of = request_layout(request_shards, shards)
    query_width = frozen_query.shape[1]
    key_width = frozen_key.shape[1]

    def adapter_for(partition_index):
        return adapter_bank[adapter_owner[request_adapter[request_of[packed_of[partition_index]]]]]

    def adapt(partition_index):
        span_start = (partition_index * token_rows).astype(jnp.int32)
        packed_here = packed_of[partition_index]
        positions = packed_here * token_rows + jnp.arange(token_rows, dtype=jnp.int32) - starts[request_of[packed_here]] * token_rows
        return project(lax.dynamic_slice_in_dim(hidden, span_start, token_rows, 0), lax.dynamic_slice_in_dim(frozen_query, span_start, token_rows, 0), lax.dynamic_slice_in_dim(frozen_key, span_start, token_rows, 0), lax.dynamic_slice_in_dim(frozen_value, span_start, token_rows, 0), adapter_for(partition_index), positions.astype(jnp.int32))
    shard_list = jnp.arange(shards, dtype=jnp.int32)
    query_matrix, key_output, value_output = lax.map(adapt, shard_list)
    reach_shards = shards // 2 + 1
    visible_span = reach_shards * token_rows
    key_flat = key_output.reshape(CONTEXT_TOKENS, key_width)
    value_flat = value_output.reshape(CONTEXT_TOKENS, key_width)
    lead_rows = visible_span - token_rows
    key_padded = jnp.concatenate([key_flat[CONTEXT_TOKENS - lead_rows:], key_flat], 0)
    value_padded = jnp.concatenate([value_flat[CONTEXT_TOKENS - lead_rows:], value_flat], 0)

    def attend(partition_index):
        span_start = (partition_index * token_rows).astype(jnp.int32)
        packed_here = packed_of[partition_index]
        query_row_list = broadened_heads(query_matrix[partition_index]).reshape(token_rows, KEY_VALUE_HEADS, QUERIES_PER_KEY, HEAD_SIZE)
        key_row_list = broadened_heads(lax.dynamic_slice_in_dim(key_padded, span_start, visible_span, 0)).reshape(visible_span, KEY_VALUE_HEADS, HEAD_SIZE)
        value_row_list = broadened_heads(lax.dynamic_slice_in_dim(value_padded, span_start, visible_span, 0)).reshape(visible_span, KEY_VALUE_HEADS, HEAD_SIZE)
        query_index = packed_here * token_rows + jnp.arange(token_rows, dtype=jnp.int32)
        offsets = jnp.arange(visible_span, dtype=jnp.int32)
        key_device = (partition_index - reach_shards + 1 + offsets // token_rows) % shards
        key_packed = packed_of[key_device]
        key_index = key_packed * token_rows + offsets % token_rows
        same = request_of[key_packed] == request_of[packed_here]
        allowed = same[None, :] & (key_index[None, :] <= query_index[:, None])
        score_matrix = jnp.einsum('wxep,oxp->xewo', query_row_list, key_row_list, precision=lax.Precision.HIGHEST) / jnp.sqrt(jnp.float32(HEAD_SIZE))
        score_matrix = jnp.where(allowed[None, None], score_matrix, score_masked)
        best_score = lax.optimization_barrier(jnp.max(score_matrix, axis=-1, keepdims=True))
        attention_weight = jnp.exp(score_matrix - best_score)
        softmax_total = lax.optimization_barrier(jnp.sum(attention_weight, axis=-1))
        blended_result = jnp.einsum('invl,lif->invf', broadened_heads(attention_weight.astype(jnp.bfloat16)), value_row_list, precision=lax.Precision.HIGHEST)
        blended_result = blended_result / softmax_total[..., None]
        return blended_result.transpose(2, 0, 1, 3).reshape(token_rows, query_width).astype(jnp.bfloat16)
    attended_output = lax.map(attend, shard_list)

    def finish(partition_index):
        return output_adapter(attended_output[partition_index], adapter_for(partition_index), D)
    extra = lax.map(finish, shard_list)
    return (attended_output.reshape(CONTEXT_TOKENS, query_width), extra.reshape(CONTEXT_TOKENS, D))
```

```python
import functools

import jax
import jax.numpy as jnp
from jax import lax
from jax.experimental import pallas as pl
from jax.experimental.pallas import tpu as pltpu
from jax.sharding import PartitionSpec as P

HEAD_SIZE = 128
QUERY_HEADS = 16
KEY_VALUE_HEADS = 4
GROUP_SPLIT = QUERY_HEADS // KEY_VALUE_HEADS

adapter_scale = 0.5
rope_theta = 500000.0
score_masked = -1e30

ROW_BLOCKS = 4
CHUNKS = 8
VMEM_LIMIT = 48 * 1024 * 1024


def request_layout(request_shards, shards):
    starts = jnp.cumsum(request_shards) - request_shards
    shard_ids = jnp.arange(shards, dtype=jnp.int32)
    request_of = jnp.sum((starts[None, :] <= shard_ids[:, None]).astype(jnp.int32), axis=1) - 1
    longest = jnp.argmax(request_shards)
    offset = (starts[longest] + request_shards[longest] // 2) % shards
    packed_of = (shard_ids + offset) % shards
    return (request_of, starts, packed_of)


def rope_tables(positions):
    half_dim = HEAD_SIZE // 2
    frequency = rope_theta ** (-(jnp.arange(half_dim, dtype=jnp.float32) * 2.0) / HEAD_SIZE)
    angles = positions.astype(jnp.float32)[:, None] * frequency[None, :]
    cosines = jnp.cos(angles)
    sines = jnp.sin(angles)
    return (jnp.concatenate([cosines, cosines], 1), jnp.concatenate([-sines, sines], 1))


class Parts:
    def __init__(self, model_width, query_width, key_width):
        d, q, k = model_width, query_width, key_width
        up = 3 * d
        self.kv = ((d, d // CHUNKS), (2 * d, d // CHUNKS), (up + q, 2 * k // CHUNKS))
        self.q = ((0, d // CHUNKS), (up, q // CHUNKS))
        self.o = ((up + q + 2 * k, q // CHUNKS), (up + 2 * q + 2 * k, d // CHUNKS))
        self.all = (self.kv, self.q, self.o)
        self.widths = tuple(sum(w for _, w in part) for part in self.all)


def pack_kernel(parts, halves, x_ref, bank_ref, *outs):
    own_half = x_ref[0]
    for block in range(outs[0].shape[0]):
        piece = block % (ROW_BLOCKS * CHUNKS // halves)
        rows = pl.ds((piece % ROW_BLOCKS) * 16, 16)
        chunk = (piece // ROW_BLOCKS) * halves + own_half
        for part, out in zip(parts.all, outs):
            at = 0
            for first, width in part:
                start = pl.multiple_of(first + chunk * width, 128)
                out[block, :, at : at + width] = bank_ref[0, rows, pl.ds(start, width)]
                at += width


def pack(parts, halves, shards, own_half, bank):
    return pl.pallas_call(
        functools.partial(pack_kernel, parts, halves),
        out_shape=[jax.ShapeDtypeStruct((shards, 16, w), bank.dtype) for w in parts.widths],
        in_specs=[
            pl.BlockSpec(memory_space=pltpu.SMEM),
            pl.BlockSpec(memory_space=pltpu.VMEM),
        ],
        out_specs=[pl.BlockSpec(memory_space=pltpu.VMEM)] * 3,
        compiler_params=pltpu.CompilerParams(vmem_limit_bytes=VMEM_LIMIT),
        name="pack",
    )(own_half.reshape(1), bank)


def pick_kernel(count, ids_ref, spread_ref, *outs_and_sem):
    outs, sem = outs_and_sem[:-1], outs_and_sem[-1]
    copies = []
    for out_index, out in enumerate(outs):
        for slot in range(count):
            copies.append(
                pltpu.make_async_copy(
                    spread_ref.at[ids_ref[out_index * count + slot]],
                    out.at[slot],
                    sem.at[len(copies)],
                )
            )
    for copy in copies:
        copy.start()
    for copy in copies:
        copy.wait()


def pick(ids, spread, count):
    outputs = ids.shape[0] // count
    shape = jax.ShapeDtypeStruct((count,) + spread.shape[1:], spread.dtype)
    return pl.pallas_call(
        functools.partial(pick_kernel, count),
        out_shape=[shape] * outputs,
        in_specs=[
            pl.BlockSpec(memory_space=pltpu.SMEM),
            pl.BlockSpec(memory_space=pl.ANY),
        ],
        out_specs=[pl.BlockSpec(memory_space=pl.ANY)] * outputs,
        scratch_shapes=[pltpu.SemaphoreType.DMA((count * outputs,))],
        name="pick",
    )(ids, spread)


def chunk_of(place, half, halves, own_half):
    if halves == 1:
        return place
    return place * halves + (own_half if half == 0 else 1 - own_half)


def factor(piece_ref, place, half, at, width):
    rows = piece_ref[place * ROW_BLOCKS : (place + 1) * ROW_BLOCKS, half, :, at : at + width]
    return rows.reshape(ROW_BLOCKS * 16, width)


def at_chunk(ref, chunk, width):
    return ref[:, pl.ds(pl.multiple_of(chunk * width, 128), width)]


def dot_nt(a, b):
    return lax.dot_general(a, b, (((1,), (1,)), ((), ())), preferred_element_type=jnp.float32)


def turn(x, cosines, sines):
    return x * cosines + pltpu.roll(x, HEAD_SIZE // 2, 1) * sines


def kv_kernel(halves, s_ref, hidden_ref, key_ref, value_ref, cos_ref, sin_ref, piece_ref, out_ref):
    own_half = s_ref[1]
    places = [(p, h) for p in range(CHUNKS // halves) for h in range(halves)]
    d = hidden_ref.shape[1] // CHUNKS
    low = jnp.zeros((hidden_ref.shape[0], 2 * ROW_BLOCKS * 16), jnp.float32)
    for p, h in places:
        chunk = chunk_of(p, h, halves, own_half)
        down = jnp.concatenate(
            [factor(piece_ref, p, h, 0, d), factor(piece_ref, p, h, d, d)], axis=0
        )
        low += dot_nt(at_chunk(hidden_ref, chunk, d), down)
    low = low.astype(jnp.bfloat16)
    low_key, low_value = low[:, : ROW_BLOCKS * 16], low[:, ROW_BLOCKS * 16 :]
    width = 2 * key_ref.shape[1] // CHUNKS
    cosines, sines = cos_ref[...], sin_ref[...]
    for p, h in places:
        chunk = chunk_of(p, h, halves, own_half)
        up = factor(piece_ref, p, h, 2 * d, width)
        is_key = p < CHUNKS // halves // 2
        update = jnp.dot(low_key if is_key else low_value, up, preferred_element_type=jnp.float32)
        place = chunk if is_key else chunk - CHUNKS // 2
        frozen = at_chunk(key_ref if is_key else value_ref, place, width)
        result = frozen.astype(jnp.float32) + adapter_scale * update
        if is_key:
            result = turn(result, cosines, sines)
        start = pl.multiple_of(chunk * width, 128)
        out_ref[:, pl.ds(start, width)] = result.astype(jnp.bfloat16)


def query_kernel(halves, s_ref, hidden_ref, query_ref, cos_ref, sin_ref, piece_ref, out_ref):
    own_half = s_ref[1]
    places = [(p, h) for p in range(CHUNKS // halves) for h in range(halves)]
    d = hidden_ref.shape[1] // CHUNKS
    low = jnp.zeros((hidden_ref.shape[0], ROW_BLOCKS * 16), jnp.float32)
    for p, h in places:
        chunk = chunk_of(p, h, halves, own_half)
        low += dot_nt(at_chunk(hidden_ref, chunk, d), factor(piece_ref, p, h, 0, d))
    low = low.astype(jnp.bfloat16)
    width = query_ref.shape[1] // CHUNKS
    cosines, sines = cos_ref[...], sin_ref[...]
    for p, h in places:
        chunk = chunk_of(p, h, halves, own_half)
        up = factor(piece_ref, p, h, d, width)
        update = jnp.dot(low, up, preferred_element_type=jnp.float32)
        result = at_chunk(query_ref, chunk, width).astype(jnp.float32) + adapter_scale * update
        for head in range(width // HEAD_SIZE):
            turned = turn(result[:, head * HEAD_SIZE : (head + 1) * HEAD_SIZE], cosines, sines)
            start = pl.multiple_of(chunk * width + head * HEAD_SIZE, 128)
            out_ref[:, pl.ds(start, HEAD_SIZE)] = turned.astype(jnp.bfloat16)


def piece_spec(halves, requests, width):
    return pl.BlockSpec(
        (ROW_BLOCKS * CHUNKS // halves, halves, None, 16, width),
        lambda i, s: (0, 0, s[0], 0, 0),
    )


def whole_spec(shape):
    return pl.BlockSpec(shape, lambda i, s: (0,) * len(shape))


def project(kernel, halves, scalars, arrays, pieces, out_shape, flops, name):
    return pl.pallas_call(
        functools.partial(kernel, halves),
        out_shape=out_shape,
        grid_spec=pltpu.PrefetchScalarGridSpec(
            num_scalar_prefetch=1,
            grid=(1,),
            in_specs=[whole_spec(a.shape) for a in arrays]
            + [piece_spec(halves, pieces.shape[2], pieces.shape[4])],
            out_specs=whole_spec(out_shape.shape),
        ),
        compiler_params=pltpu.CompilerParams(vmem_limit_bytes=VMEM_LIMIT),
        cost_estimate=pl.CostEstimate(flops=flops, bytes_accessed=4 << 20, transcendentals=0),
        name=name,
    )(scalars, *arrays, pieces)


def attend_kernel(
    halves, shards, s_ref, query_ref, piece_ref, kv_ref, out_ref, extra_ref,
    block, best, total, acc, low_ref, sem,
):
    own_half, own_index, count = s_ref[1], s_ref[2], s_ref[3]
    tokens = query_ref.shape[0]
    rows = GROUP_SPLIT * tokens
    key_width = KEY_VALUE_HEADS * HEAD_SIZE
    factor_base2 = 1.4426950408889634 / (HEAD_SIZE**0.5)

    def fetch(step):
        source = lax.rem(own_index - step + shards, shards)
        return pltpu.make_async_copy(
            kv_ref.at[source],
            block.at[pl.ds(pl.multiple_of(step * tokens, tokens), tokens)],
            sem.at[step],
        )

    lax.fori_loop(0, count, lambda step, c: (fetch(step).start(), c)[1], 0)

    def queries(g):
        heads = [
            query_ref[:, (g * GROUP_SPLIT + j) * HEAD_SIZE : (g * GROUP_SPLIT + j + 1) * HEAD_SIZE]
            for j in range(GROUP_SPLIT)
        ]
        return jnp.concatenate(heads, axis=0)

    def keys_values(first, blocks, g):
        at = pl.ds(pl.multiple_of(first * tokens, tokens), blocks * tokens)
        k = block[at, g * HEAD_SIZE : (g + 1) * HEAD_SIZE]
        v = block[at, key_width + g * HEAD_SIZE : key_width + (g + 1) * HEAD_SIZE]
        return k, v

    fetch(0).wait()
    row = lax.broadcasted_iota(jnp.int32, (rows, tokens), 0) % tokens
    column = lax.broadcasted_iota(jnp.int32, (rows, tokens), 1)
    allowed = column <= row
    for g in range(KEY_VALUE_HEADS):
        k, v = keys_values(0, 1, g)
        score = jnp.where(allowed, dot_nt(queries(g), k) * factor_base2, score_masked)
        high = jnp.max(score, axis=1, keepdims=True)
        weight = jnp.exp2(score - high)
        best[g] = high
        total[g] = jnp.sum(weight, axis=1, keepdims=True)
        acc[g] = jnp.dot(weight.astype(jnp.bfloat16), v, preferred_element_type=jnp.float32)

    def more(first, blocks):
        for step in range(blocks):
            fetch(first + step).wait()
        for g in range(KEY_VALUE_HEADS):
            k, v = keys_values(first, blocks, g)
            score = dot_nt(queries(g), k) * factor_base2
            old = best[g]
            high = jnp.maximum(old, jnp.max(score, axis=1, keepdims=True))
            shrink = jnp.exp2(old - high)
            weight = jnp.exp2(score - high)
            best[g] = high
            total[g] = total[g] * shrink + jnp.sum(weight, axis=1, keepdims=True)
            acc[g] = acc[g] * shrink + jnp.dot(
                weight.astype(jnp.bfloat16), v, preferred_element_type=jnp.float32
            )

    pairs = (count - 1) // 2

    def pair(i, c):
        more(1 + 2 * i, 2)
        return c

    lax.fori_loop(0, pairs, pair, 0)

    @pl.when(count - 1 > 2 * pairs)
    def _():
        more(count - 1, 1)

    for g in range(KEY_VALUE_HEADS):
        result = (acc[g] / total[g]).astype(jnp.bfloat16)
        for j in range(GROUP_SPLIT):
            at = (g * GROUP_SPLIT + j) * HEAD_SIZE
            out_ref[:, at : at + HEAD_SIZE] = result[j * tokens : (j + 1) * tokens]

    q_width = query_ref.shape[1] // CHUNKS
    d = extra_ref.shape[1] // CHUNKS
    places = [(p, h) for p in range(CHUNKS // halves) for h in range(halves)]
    low = jnp.zeros((tokens, ROW_BLOCKS * 16), jnp.float32)
    for p, h in places:
        chunk = chunk_of(p, h, halves, own_half)
        low += dot_nt(at_chunk(out_ref, chunk, q_width), factor(piece_ref, p, h, 0, q_width))
    low = low.astype(jnp.bfloat16)
    for p, h in places:
        chunk = chunk_of(p, h, halves, own_half)
        up = factor(piece_ref, p, h, q_width, d)
        start = pl.multiple_of(chunk * d, 128)
        result = adapter_scale * jnp.dot(low, up, preferred_element_type=jnp.float32)
        extra_ref[:, pl.ds(start, d)] = result.astype(jnp.bfloat16)


def attend(halves, shards, scalars, query, pieces, kv, model_width):
    tokens, query_width = query.shape
    reach = shards // 2 + 1
    rows = GROUP_SPLIT * tokens
    out_shape = [
        jax.ShapeDtypeStruct((tokens, query_width), jnp.bfloat16),
        jax.ShapeDtypeStruct((tokens, model_width), jnp.bfloat16),
    ]
    return pl.pallas_call(
        functools.partial(attend_kernel, halves, shards),
        out_shape=out_shape,
        grid_spec=pltpu.PrefetchScalarGridSpec(
            num_scalar_prefetch=1,
            grid=(1,),
            in_specs=[
                whole_spec(query.shape),
                piece_spec(halves, pieces.shape[2], pieces.shape[4]),
                pl.BlockSpec(memory_space=pl.ANY),
            ],
            out_specs=[whole_spec(o.shape) for o in out_shape],
            scratch_shapes=[
                pltpu.VMEM((reach * tokens, kv.shape[2]), jnp.bfloat16),
                pltpu.VMEM((KEY_VALUE_HEADS, rows, 1), jnp.float32),
                pltpu.VMEM((KEY_VALUE_HEADS, rows, 1), jnp.float32),
                pltpu.VMEM((KEY_VALUE_HEADS, rows, HEAD_SIZE), jnp.float32),
                pltpu.VMEM((tokens, ROW_BLOCKS * 16), jnp.float32),
                pltpu.SemaphoreType.DMA((reach,)),
            ],
        ),
        compiler_params=pltpu.CompilerParams(vmem_limit_bytes=VMEM_LIMIT),
        cost_estimate=pl.CostEstimate(
            flops=2_000_000_000, bytes_accessed=8 << 20, transcendentals=4 << 20
        ),
        name="attend",
    )(scalars, query, pieces, kv)


def body(
    hidden,
    frozen_query,
    frozen_key,
    frozen_value,
    adapter_bank,
    request_shards,
    request_adapter,
    adapter_owner,
):
    shards = lax.axis_size("ctx")
    groups = lax.axis_size("groups")
    own_index = lax.axis_index("ctx").astype(jnp.int32)
    tokens, model_width = hidden.shape
    requests = request_shards.shape[0]
    halves = 2 if groups == 2 and 2 * shards == ROW_BLOCKS * CHUNKS else 1
    own_half = lax.axis_index("groups").astype(jnp.int32) if halves == 2 else jnp.int32(0)
    parts = Parts(model_width, frozen_query.shape[1], frozen_key.shape[1])

    packed = pack(parts, halves, shards, own_half, adapter_bank)
    spread = [lax.all_to_all(p, "ctx", split_axis=0, concat_axis=0, tiled=True) for p in packed]

    request_of, starts, packed_of = request_layout(request_shards, shards)
    own_packed = packed_of[own_index]
    own_request = request_of[own_packed]
    first = starts[own_request]
    positions = (own_packed - first) * tokens + jnp.arange(tokens, dtype=jnp.int32)
    cosines, sines = rope_tables(positions)
    scalars = jnp.stack(
        [own_request, own_half, own_index, own_packed - first + 1]
    ).astype(jnp.int32)

    wanted = request_adapter
    if halves == 2:
        theirs = lax.ppermute(request_adapter, "groups", [(0, 1), (1, 0)])
        wanted = jnp.concatenate([request_adapter, theirs])
    ids = adapter_owner[wanted].astype(jnp.int32)

    gathered = []
    for s in spread:
        picked = pick(ids, s, requests)
        if halves == 2:
            arrived = lax.ppermute(picked[1], "groups", [(0, 1), (1, 0)])
            piece = jnp.stack([picked[0], arrived])
        else:
            piece = picked[0][None]
        gathered.append(lax.all_gather(piece, "ctx"))

    bf16 = jnp.bfloat16
    kv = project(
        kv_kernel, halves, scalars, (hidden, frozen_key, frozen_value, cosines, sines),
        gathered[0], jax.ShapeDtypeStruct((tokens, 2 * frozen_key.shape[1]), bf16),
        150_000_000, "keys_values",
    )
    all_kv = lax.all_gather(kv, "ctx")
    query = project(
        query_kernel, halves, scalars, (hidden, frozen_query, cosines, sines),
        gathered[1], jax.ShapeDtypeStruct(frozen_query.shape, bf16),
        100_000_000, "queries",
    )
    return tuple(attend(halves, shards, scalars, query, gathered[2], all_kv, model_width))


def solution(mesh):
    return jax.shard_map(
        body,
        mesh=mesh,
        in_specs=(
            P(("groups", "ctx"), None),
            P(("groups", "ctx"), None),
            P(("groups", "ctx"), None),
            P(("groups", "ctx"), None),
            P("ctx", None, None),
            P("groups"),
            P("groups"),
            P(),
        ),
        out_specs=(P(("groups", "ctx"), None), P(("groups", "ctx"), None)),
        check_vma=False,
    )
```

```python
import functools

import jax
import jax.numpy as jnp
from jax import lax
from jax.experimental import pallas as pl
from jax.experimental.pallas import tpu as pltpu
from jax.sharding import PartitionSpec as P

HEAD_SIZE = 128
QUERY_HEADS = 16
KEY_VALUE_HEADS = 4
GROUP_SPLIT = QUERY_HEADS // KEY_VALUE_HEADS

adapter_scale = 0.5
rope_theta = 500000.0
score_masked = -1e30

ROW_BLOCKS = 4
CHUNKS = 8
VMEM_LIMIT = 48 * 1024 * 1024


def request_layout(request_shards, shards):
    starts = jnp.cumsum(request_shards) - request_shards
    shard_ids = jnp.arange(shards, dtype=jnp.int32)
    request_of = jnp.sum((starts[None, :] <= shard_ids[:, None]).astype(jnp.int32), axis=1) - 1
    longest = jnp.argmax(request_shards)
    offset = (starts[longest] + request_shards[longest] // 2) % shards
    packed_of = (shard_ids + offset) % shards
    return (request_of, starts, packed_of)


def rope_tables(positions):
    half_dim = HEAD_SIZE // 2
    frequency = rope_theta ** (-(jnp.arange(half_dim, dtype=jnp.float32) * 2.0) / HEAD_SIZE)
    angles = positions.astype(jnp.float32)[:, None] * frequency[None, :]
    cosines = jnp.cos(angles)
    sines = jnp.sin(angles)
    return (jnp.concatenate([cosines, cosines], 1), jnp.concatenate([-sines, sines], 1))


class Parts:
    def __init__(self, model_width, query_width, key_width):
        d, q, k = model_width, query_width, key_width
        up = 3 * d
        self.kv = ((d, d // CHUNKS), (2 * d, d // CHUNKS), (up + q, 2 * k // CHUNKS))
        self.q = ((0, d // CHUNKS), (up, q // CHUNKS))
        self.o = ((up + q + 2 * k, q // CHUNKS), (up + 2 * q + 2 * k, d // CHUNKS))
        self.all = self.kv + self.q + self.o
        self.kv_width = sum(w for _, w in self.kv)
        self.rest_width = sum(w for _, w in self.q + self.o)


def vmem(count=1):
    return [pl.BlockSpec(memory_space=pltpu.VMEM)] * count


def smem(count=1):
    return [pl.BlockSpec(memory_space=pltpu.SMEM)] * count


PARAMS = pltpu.CompilerParams(vmem_limit_bytes=VMEM_LIMIT)


def pack_kernel(parts, halves, x_ref, bank_ref, out):
    own_half = x_ref[0]
    for block in range(out.shape[0]):
        piece = block % (ROW_BLOCKS * CHUNKS // halves)
        rows = pl.ds((piece % ROW_BLOCKS) * 16, 16)
        chunk = (piece // ROW_BLOCKS) * halves + own_half
        at = 0
        for first, width in parts.all:
            start = pl.multiple_of(first + chunk * width, 128)
            out[block, :, at : at + width] = bank_ref[0, rows, pl.ds(start, width)]
            at += width


def pack(parts, halves, shards, own_half, bank):
    width = parts.kv_width + parts.rest_width
    return pl.pallas_call(
        functools.partial(pack_kernel, parts, halves),
        out_shape=jax.ShapeDtypeStruct((shards, 16, width), bank.dtype),
        in_specs=smem() + vmem(),
        out_specs=vmem()[0],
        compiler_params=PARAMS,
        name="pack",
    )(own_half.reshape(1), bank)


def pick_kernel(ids_ref, spread_ref, out_ref):
    out_ref[...] = spread_ref[...]


def pick(ids, spread):
    block = (None,) + spread.shape[1:]
    return pl.pallas_call(
        pick_kernel,
        out_shape=jax.ShapeDtypeStruct(ids.shape + spread.shape[1:], spread.dtype),
        grid_spec=pltpu.PrefetchScalarGridSpec(
            num_scalar_prefetch=1,
            grid=ids.shape,
            in_specs=[pl.BlockSpec(block, lambda i, ids: (ids[i], 0, 0))],
            out_specs=pl.BlockSpec(block, lambda i, ids: (i, 0, 0)),
        ),
        compiler_params=PARAMS,
        name="pick",
    )(ids, spread)


def route_kernel(halves, kv_width, slots_ref, half_ref, *refs):
    sides, (kv_ref, rest_ref) = refs[:halves], refs[halves:]
    for dest in range(kv_ref.shape[0]):
        slot = slots_ref[dest]
        for side, ref in enumerate(sides):
            half = half_ref[0] if side == 0 else 1 - half_ref[0]
            kv_ref[dest, half] = ref[slot, :, :kv_width]
            rest_ref[dest, half] = ref[slot, :, kv_width:]


def route(slots, own_half, sides, kv_width):
    halves, shards = len(sides), slots.shape[0]
    dtype, width = sides[0].dtype, sides[0].shape[2]
    return pl.pallas_call(
        functools.partial(route_kernel, halves, kv_width),
        out_shape=[
            jax.ShapeDtypeStruct((shards, halves, 16, w), dtype)
            for w in (kv_width, width - kv_width)
        ],
        in_specs=smem(2) + vmem(halves),
        out_specs=vmem(2),
        compiler_params=PARAMS,
        name="route",
    )(slots, own_half.reshape(1), *sides)


def factor(piece_ref, chunk, at, width):
    halves = piece_ref.shape[1]
    place, half = chunk // halves, chunk % halves
    rows = piece_ref[place * ROW_BLOCKS : (place + 1) * ROW_BLOCKS, half, :, at : at + width]
    return rows.reshape(ROW_BLOCKS * 16, width)


def columns(chunk, width):
    return slice(chunk * width, (chunk + 1) * width)


def dot_nt(a, b):
    return lax.dot_general(a, b, (((1,), (1,)), ((), ())), preferred_element_type=jnp.float32)


def turn(x, cosines, sines):
    return x * cosines + pltpu.roll(x, HEAD_SIZE // 2, 1) * sines


def kv_kernel(hidden_ref, key_ref, value_ref, cos_ref, sin_ref, piece_ref, out_ref):
    d = hidden_ref.shape[1] // CHUNKS
    rank = ROW_BLOCKS * 16
    low = jnp.zeros((hidden_ref.shape[0], 2 * rank), jnp.float32)
    for chunk in range(CHUNKS):
        down = jnp.concatenate(
            [factor(piece_ref, chunk, 0, d), factor(piece_ref, chunk, d, d)], axis=0
        )
        low += dot_nt(hidden_ref[:, columns(chunk, d)], down)
    low = low.astype(jnp.bfloat16)
    width = 2 * key_ref.shape[1] // CHUNKS
    cosines, sines = cos_ref[...], sin_ref[...]
    for chunk in range(CHUNKS):
        is_key = chunk < CHUNKS // 2
        up = factor(piece_ref, chunk, 2 * d, width)
        part = low[:, :rank] if is_key else low[:, rank:]
        update = jnp.dot(part, up, preferred_element_type=jnp.float32)
        frozen = (key_ref if is_key else value_ref)[:, columns(chunk % (CHUNKS // 2), width)]
        result = frozen.astype(jnp.float32) + adapter_scale * update
        if is_key:
            result = turn(result, cosines, sines)
        out_ref[:, columns(chunk, width)] = result.astype(jnp.bfloat16)


def query_kernel(hidden_ref, query_ref, cos_ref, sin_ref, piece_ref, out_ref):
    d = hidden_ref.shape[1] // CHUNKS
    low = jnp.zeros((hidden_ref.shape[0], ROW_BLOCKS * 16), jnp.float32)
    for chunk in range(CHUNKS):
        low += dot_nt(hidden_ref[:, columns(chunk, d)], factor(piece_ref, chunk, 0, d))
    low = low.astype(jnp.bfloat16)
    width = query_ref.shape[1] // CHUNKS
    cosines, sines = cos_ref[...], sin_ref[...]
    for chunk in range(CHUNKS):
        up = factor(piece_ref, chunk, d, width)
        update = jnp.dot(low, up, preferred_element_type=jnp.float32)
        result = query_ref[:, columns(chunk, width)].astype(jnp.float32) + adapter_scale * update
        for head in range(width // HEAD_SIZE):
            turned = turn(result[:, columns(head, HEAD_SIZE)], cosines, sines)
            out_ref[:, columns(chunk * (width // HEAD_SIZE) + head, HEAD_SIZE)] = turned.astype(
                jnp.bfloat16
            )


def project(kernel, arrays, pieces, out_shape, flops, name):
    places = ROW_BLOCKS * CHUNKS // pieces.shape[1]
    return pl.pallas_call(
        kernel,
        out_shape=out_shape,
        grid=(1,),
        in_specs=vmem(len(arrays))
        + [pl.BlockSpec((places,) + pieces.shape[1:], lambda i: (0, 0, 0, 0))],
        out_specs=vmem()[0],
        compiler_params=PARAMS,
        cost_estimate=pl.CostEstimate(flops=flops, bytes_accessed=4 << 20, transcendentals=0),
        name=name,
    )(*arrays, pieces)


def attend_kernel(at_q, count_ref, query_ref, piece_ref, *refs):
    blocks, (out_ref, extra_ref, best, total, acc) = refs[:-5], refs[-5:]
    count = count_ref[0]
    tokens = query_ref.shape[0]
    rows = GROUP_SPLIT * tokens
    key_width = KEY_VALUE_HEADS * HEAD_SIZE
    factor_base2 = 1.4426950408889634 / (HEAD_SIZE**0.5)

    def queries(g):
        heads = [query_ref[:, columns(g * GROUP_SPLIT + j, HEAD_SIZE)] for j in range(GROUP_SPLIT)]
        return jnp.concatenate(heads, axis=0)

    def keys_values(first, number, g):
        k = [blocks[first + i][:, columns(g, HEAD_SIZE)] for i in range(number)]
        v = [
            blocks[first + i][:, columns(KEY_VALUE_HEADS + g, HEAD_SIZE)] for i in range(number)
        ]
        return jnp.concatenate(k, axis=0), jnp.concatenate(v, axis=0)

    row = lax.broadcasted_iota(jnp.int32, (rows, tokens), 0) % tokens
    column = lax.broadcasted_iota(jnp.int32, (rows, tokens), 1)
    allowed = column <= row
    for g in range(KEY_VALUE_HEADS):
        k, v = keys_values(0, 1, g)
        score = jnp.where(allowed, dot_nt(queries(g), k) * factor_base2, score_masked)
        high = jnp.max(score, axis=1, keepdims=True)
        weight = jnp.exp2(score - high)
        best[g] = high
        total[g] = jnp.sum(weight, axis=1, keepdims=True)
        acc[g] = jnp.dot(weight.astype(jnp.bfloat16), v, preferred_element_type=jnp.float32)

    def more(first, number):
        for g in range(KEY_VALUE_HEADS):
            k, v = keys_values(first, number, g)
            score = dot_nt(queries(g), k) * factor_base2
            old = best[g]
            high = jnp.maximum(old, jnp.max(score, axis=1, keepdims=True))
            shrink = jnp.exp2(old - high)
            weight = jnp.exp2(score - high)
            best[g] = high
            total[g] = total[g] * shrink + jnp.sum(weight, axis=1, keepdims=True)
            acc[g] = acc[g] * shrink + jnp.dot(
                weight.astype(jnp.bfloat16), v, preferred_element_type=jnp.float32
            )

    for first in range(1, len(blocks), 2):
        if first + 1 < len(blocks):
            pl.when(count > first + 1)(functools.partial(more, first, 2))
        pl.when(count == first + 1)(functools.partial(more, first, 1))

    for g in range(KEY_VALUE_HEADS):
        result = (acc[g] / total[g]).astype(jnp.bfloat16)
        for j in range(GROUP_SPLIT):
            out_ref[:, columns(g * GROUP_SPLIT + j, HEAD_SIZE)] = result[
                j * tokens : (j + 1) * tokens
            ]

    q_width = query_ref.shape[1] // CHUNKS
    d = extra_ref.shape[1] // CHUNKS
    low = jnp.zeros((tokens, ROW_BLOCKS * 16), jnp.float32)
    for chunk in range(CHUNKS):
        down = factor(piece_ref, chunk, at_q, q_width)
        low += dot_nt(out_ref[:, columns(chunk, q_width)], down)
    low = low.astype(jnp.bfloat16)
    for chunk in range(CHUNKS):
        up = factor(piece_ref, chunk, at_q + q_width, d)
        result = adapter_scale * jnp.dot(low, up, preferred_element_type=jnp.float32)
        extra_ref[:, columns(chunk, d)] = result.astype(jnp.bfloat16)


def attend(count, query, pieces, blocks, at_q, model_width):
    tokens, query_width = query.shape
    rows = GROUP_SPLIT * tokens
    places = ROW_BLOCKS * CHUNKS // pieces.shape[1]
    return pl.pallas_call(
        functools.partial(attend_kernel, at_q),
        out_shape=[
            jax.ShapeDtypeStruct((tokens, query_width), jnp.bfloat16),
            jax.ShapeDtypeStruct((tokens, model_width), jnp.bfloat16),
        ],
        grid=(1,),
        in_specs=smem()
        + vmem()
        + [pl.BlockSpec((places,) + pieces.shape[1:], lambda i: (0, 0, 0, 0))]
        + vmem(len(blocks)),
        out_specs=vmem(2),
        scratch_shapes=[
            pltpu.VMEM((KEY_VALUE_HEADS, rows, 1), jnp.float32),
            pltpu.VMEM((KEY_VALUE_HEADS, rows, 1), jnp.float32),
            pltpu.VMEM((KEY_VALUE_HEADS, rows, HEAD_SIZE), jnp.float32),
        ],
        compiler_params=PARAMS,
        cost_estimate=pl.CostEstimate(
            flops=2_000_000_000, bytes_accessed=8 << 20, transcendentals=4 << 20
        ),
        name="attend",
    )(count, query, pieces, *blocks)


def reach_pairs(shards, shift):
    longest = shards // 2 + 1
    low = -(longest // 2)
    runs = (
        [i % shards for i in range(low, low + longest)],
        [i % shards for i in range(low + longest, low + shards)],
    )
    limits = (longest, shards - longest - 1)
    return [
        (run[i], run[i + shift])
        for run, limit in zip(runs, limits)
        if shift < limit
        for i in range(len(run) - shift)
    ]


def body(
    hidden,
    frozen_query,
    frozen_key,
    frozen_value,
    adapter_bank,
    request_shards,
    request_adapter,
    adapter_owner,
):
    shards = lax.axis_size("ctx")
    groups = lax.axis_size("groups")
    own_index = lax.axis_index("ctx").astype(jnp.int32)
    tokens, model_width = hidden.shape
    requests = request_shards.shape[0]
    halves = 2 if groups == 2 and 2 * shards == ROW_BLOCKS * CHUNKS else 1
    own_half = lax.axis_index("groups").astype(jnp.int32) if halves == 2 else jnp.int32(0)
    parts = Parts(model_width, frozen_query.shape[1], frozen_key.shape[1])
    swap = [(0, 1), (1, 0)]

    packed = pack(parts, halves, shards, own_half, adapter_bank)
    spread = lax.all_to_all(packed, "ctx", split_axis=0, concat_axis=0, tiled=True)

    request_of, starts, packed_of = request_layout(request_shards, shards)
    request_at = request_of[packed_of].astype(jnp.int32)
    own_packed = packed_of[own_index]
    first = starts[request_of[own_packed]]
    positions = (own_packed - first) * tokens + jnp.arange(tokens, dtype=jnp.int32)
    cosines, sines = rope_tables(positions)
    reach = shards // 2
    count = jnp.minimum(own_packed - first, reach).astype(jnp.int32).reshape(1) + 1

    wanted = request_adapter
    if halves == 2:
        theirs = lax.ppermute(request_adapter, "groups", swap)
        wanted = jnp.concatenate([theirs, request_adapter])
    picked = pick(adapter_owner[wanted].astype(jnp.int32), spread)
    sides = [picked]
    if halves == 2:
        sides = [picked[requests:], lax.ppermute(picked[:requests], "groups", swap)]

    kv_pieces, rest_pieces = [
        lax.all_to_all(p, "ctx", split_axis=0, concat_axis=0, tiled=True)
        for p in route(request_at, own_half, sides, parts.kv_width)
    ]

    bf16 = jnp.bfloat16
    kv = project(
        kv_kernel, (hidden, frozen_key, frozen_value, cosines, sines), kv_pieces,
        jax.ShapeDtypeStruct((tokens, 2 * frozen_key.shape[1]), bf16), 150_000_000, "keys_values",
    )
    blocks = [kv] + [
        lax.ppermute(kv, "ctx", reach_pairs(shards, shift)) for shift in range(1, reach + 1)
    ]
    query = project(
        query_kernel, (hidden, frozen_query, cosines, sines), rest_pieces,
        jax.ShapeDtypeStruct(frozen_query.shape, bf16), 100_000_000, "queries",
    )
    at_q = sum(w for _, w in parts.q)
    return tuple(attend(count, query, rest_pieces, blocks, at_q, model_width))


def solution(mesh):
    return jax.shard_map(
        body,
        mesh=mesh,
        in_specs=(
            P(("groups", "ctx"), None),
            P(("groups", "ctx"), None),
            P(("groups", "ctx"), None),
            P(("groups", "ctx"), None),
            P("ctx", None, None),
            P("groups"),
            P("groups"),
            P(),
        ),
        out_specs=(P(("groups", "ctx"), None), P(("groups", "ctx"), None)),
        check_vma=False,
    )
```

```python
import functools

import jax
import jax.numpy as jnp
from jax import lax
from jax.experimental import pallas as pl
from jax.experimental.pallas import tpu as pltpu
from jax.sharding import PartitionSpec as P

HEAD_SIZE = 128
QUERY_HEADS = 16
KEY_VALUE_HEADS = 4
GROUP_SPLIT = QUERY_HEADS // KEY_VALUE_HEADS

adapter_scale = 0.5
rope_theta = 500000.0
score_masked = -1e30

ROW_BLOCKS = 4
CHUNKS = 8
VMEM_LIMIT = 48 * 1024 * 1024


def request_layout(request_shards, shards):
    starts = jnp.cumsum(request_shards) - request_shards
    shard_ids = jnp.arange(shards, dtype=jnp.int32)
    request_of = jnp.sum((starts[None, :] <= shard_ids[:, None]).astype(jnp.int32), axis=1) - 1
    longest = jnp.argmax(request_shards)
    offset = (starts[longest] + request_shards[longest] // 2) % shards
    packed_of = (shard_ids + offset) % shards
    return (request_of, starts, packed_of)


def rope_tables(positions):
    half_dim = HEAD_SIZE // 2
    frequency = rope_theta ** (-(jnp.arange(half_dim, dtype=jnp.float32) * 2.0) / HEAD_SIZE)
    angles = positions.astype(jnp.float32)[..., None] * frequency
    cosines = jnp.cos(angles)
    sines = jnp.sin(angles)
    return (jnp.concatenate([cosines, cosines], -1), jnp.concatenate([-sines, sines], -1))


class Parts:
    def __init__(self, model_width, query_width, key_width):
        d, q, k = model_width, query_width, key_width
        up = 3 * d
        self.kv = ((d, d // CHUNKS), (2 * d, d // CHUNKS), (up + q, 2 * k // CHUNKS))
        self.q = ((0, d // CHUNKS), (up, q // CHUNKS))
        self.o = ((up + q + 2 * k, q // CHUNKS), (up + 2 * q + 2 * k, d // CHUNKS))
        self.all = self.kv + self.q + self.o
        self.kv_width = sum(w for _, w in self.kv)
        self.rest_width = sum(w for _, w in self.q + self.o)


def vmem(count=1):
    return [pl.BlockSpec(memory_space=pltpu.VMEM)] * count


def smem(count=1):
    return [pl.BlockSpec(memory_space=pltpu.SMEM)] * count


PARAMS = pltpu.CompilerParams(vmem_limit_bytes=VMEM_LIMIT)


def pack_kernel(parts, halves, x_ref, bank_ref, out):
    own_half = x_ref[0]
    for block in range(out.shape[0]):
        piece = block % (ROW_BLOCKS * CHUNKS // halves)
        rows = pl.ds((piece % ROW_BLOCKS) * 16, 16)
        chunk = (piece // ROW_BLOCKS) * halves + own_half
        at = 0
        for first, width in parts.all:
            start = pl.multiple_of(first + chunk * width, 128)
            out[block, :, at : at + width] = bank_ref[0, rows, pl.ds(start, width)]
            at += width


def pack(parts, halves, shards, own_half, bank):
    width = parts.kv_width + parts.rest_width
    return pl.pallas_call(
        functools.partial(pack_kernel, parts, halves),
        out_shape=jax.ShapeDtypeStruct((shards, 16, width), bank.dtype),
        in_specs=smem() + vmem(),
        out_specs=vmem()[0],
        compiler_params=PARAMS,
        name="pack",
    )(own_half.reshape(1), bank)


def pick_kernel(ids_ref, spread_ref, out_ref):
    out_ref[...] = spread_ref[...]


def pick(ids, spread):
    block = (None,) + spread.shape[1:]
    return pl.pallas_call(
        pick_kernel,
        out_shape=jax.ShapeDtypeStruct(ids.shape + spread.shape[1:], spread.dtype),
        grid_spec=pltpu.PrefetchScalarGridSpec(
            num_scalar_prefetch=1,
            grid=ids.shape,
            in_specs=[pl.BlockSpec(block, lambda i, ids: (ids[i], 0, 0))],
            out_specs=pl.BlockSpec(block, lambda i, ids: (i, 0, 0)),
        ),
        compiler_params=PARAMS,
        name="pick",
    )(ids, spread)


def route_kernel(halves, kv_width, slots_ref, half_ref, *refs):
    sides, (kv_ref, rest_ref) = refs[:halves], refs[halves:]
    for dest in range(kv_ref.shape[0]):
        slot = slots_ref[dest]
        for side, ref in enumerate(sides):
            half = half_ref[0] if side == 0 else 1 - half_ref[0]
            kv_ref[dest, half] = ref[slot, :, :kv_width]
            rest_ref[dest, half] = ref[slot, :, kv_width:]


def route(slots, own_half, sides, kv_width):
    halves, shards = len(sides), slots.shape[0]
    dtype, width = sides[0].dtype, sides[0].shape[2]
    return pl.pallas_call(
        functools.partial(route_kernel, halves, kv_width),
        out_shape=[
            jax.ShapeDtypeStruct((shards, halves, 16, w), dtype)
            for w in (kv_width, width - kv_width)
        ],
        in_specs=smem(2) + vmem(halves),
        out_specs=vmem(2),
        compiler_params=PARAMS,
        name="route",
    )(slots, own_half.reshape(1), *sides)


def factor(piece_refs, chunk, at, width):
    halves = piece_refs[0].shape[1]
    return jnp.concatenate(
        [ref[chunk // halves, chunk % halves, :, at : at + width] for ref in piece_refs], axis=0
    )


def columns(chunk, width):
    return slice(chunk * width, (chunk + 1) * width)


def dot_nt(a, b):
    return lax.dot_general(a, b, (((1,), (1,)), ((), ())), preferred_element_type=jnp.float32)


def turn(x, cosines, sines):
    return x * cosines + pltpu.roll(x, HEAD_SIZE // 2, 1) * sines


def reorder(own, rank, inverse):
    shape = (2 * rank, 2 * rank)
    here, plain = (1, 0) if inverse else (0, 1)
    here = lax.broadcasted_iota(jnp.int32, shape, here)
    plain = lax.broadcasted_iota(jnp.int32, shape, plain)
    same = jnp.bitwise_xor(here, own * 16) == plain
    return jnp.where(same, 1.0, 0.0).astype(jnp.bfloat16)


def lows_kernel(own_ref, hidden_ref, *refs):
    piece_refs, out_ref = refs[:-1], refs[-1]
    d = hidden_ref.shape[1] // CHUNKS
    rank = ROW_BLOCKS * 16
    low = jnp.zeros((hidden_ref.shape[0], 2 * rank), jnp.float32)
    for chunk in range(CHUNKS):
        down = jnp.concatenate(
            [factor(piece_refs, chunk, 0, d), factor(piece_refs, chunk, d, d)], axis=0
        )
        low += dot_nt(hidden_ref[:, columns(chunk, d)], down)
    plain = jnp.dot(
        low.astype(jnp.bfloat16),
        reorder(own_ref[0], rank, False),
        preferred_element_type=jnp.float32,
    )
    out_ref[...] = plain.astype(jnp.bfloat16)


def lows(own, hidden, pieces):
    return pl.pallas_call(
        lows_kernel,
        out_shape=jax.ShapeDtypeStruct((hidden.shape[0], 2 * ROW_BLOCKS * 16), jnp.bfloat16),
        in_specs=smem() + vmem(1 + len(pieces)),
        out_specs=vmem()[0],
        compiler_params=PARAMS,
        cost_estimate=pl.CostEstimate(
            flops=150_000_000, bytes_accessed=3 << 20, transcendentals=0
        ),
        name="lows",
    )(own, hidden, *pieces)


def attend_kernel(
    shards, reach, scalars_ref, hidden_ref, query_ref, cos_ref, sin_ref, frozen_ref, *refs
):
    lows_refs, refs = refs[: reach + 1], refs[reach + 1 :]
    up_refs, refs = refs[:ROW_BLOCKS], refs[ROW_BLOCKS:]
    piece_refs, refs = refs[:ROW_BLOCKS], refs[ROW_BLOCKS:]
    out_ref, extra_ref, frozen, queries, keys, values, scores, high, acc, sem = refs
    count, own_index, own = scalars_ref[0], scalars_ref[1], scalars_ref[2]
    tokens = query_ref.shape[0]
    rank = ROW_BLOCKS * 16
    rows = GROUP_SPLIT * tokens
    key_width = KEY_VALUE_HEADS * HEAD_SIZE
    bf16 = jnp.bfloat16
    base2 = 1.4426950408889634 / (HEAD_SIZE**0.5)

    def fetch(step):
        source = lax.rem(own_index - step + shards, shards)
        return pltpu.make_async_copy(frozen_ref.at[source], frozen.at[step], sem.at[step])

    for step in range(reach + 1):
        pl.when(count > step)(fetch(step).start)

    d = hidden_ref.shape[1] // CHUNKS
    low = jnp.zeros((tokens, rank), jnp.float32)
    for chunk in range(CHUNKS):
        low += dot_nt(hidden_ref[:, columns(chunk, d)], factor(piece_refs, chunk, 0, d))
    low = low.astype(bf16)
    q_width = query_ref.shape[1] // CHUNKS
    cosines, sines = cos_ref[count - 1], sin_ref[count - 1]
    for chunk in range(CHUNKS):
        update = jnp.dot(
            low, factor(piece_refs, chunk, d, q_width), preferred_element_type=jnp.float32
        )
        result = query_ref[:, columns(chunk, q_width)].astype(jnp.float32) + adapter_scale * update
        for part in range(q_width // HEAD_SIZE):
            head = chunk * (q_width // HEAD_SIZE) + part
            turned = turn(result[:, columns(part, HEAD_SIZE)], cosines, sines)
            queries[head // GROUP_SPLIT, pl.ds((head % GROUP_SPLIT) * tokens, tokens)] = (
                turned.astype(bf16)
            )

    order = reorder(own, rank, True)
    up_width = 2 * key_width // CHUNKS
    up = [factor(up_refs, chunk, 0, up_width) for chunk in range(CHUNKS)]
    up_key = jnp.concatenate(up[: CHUNKS // 2], axis=1)
    up_value = jnp.concatenate(up[CHUNKS // 2 :], axis=1)
    for g in range(KEY_VALUE_HEADS):
        values[:, pl.ds((2 * g + 1) * HEAD_SIZE, HEAD_SIZE)] = jnp.ones(
            (values.shape[0], HEAD_SIZE), bf16
        )

    def rebuild(step):
        fetch(step).wait()
        low = jnp.dot(lows_refs[step][...], order, preferred_element_type=jnp.float32).astype(bf16)
        at = pl.ds(step * tokens, tokens)
        cosines, sines = cos_ref[count - 1 - step], sin_ref[count - 1 - step]
        key = frozen[step, :, :key_width].astype(jnp.float32) + adapter_scale * jnp.dot(
            low[:, :rank], up_key, preferred_element_type=jnp.float32
        )
        value = frozen[step, :, key_width:].astype(jnp.float32) + adapter_scale * jnp.dot(
            low[:, rank:], up_value, preferred_element_type=jnp.float32
        )
        value = value.astype(bf16)
        for g in range(KEY_VALUE_HEADS):
            turned = turn(key[:, columns(g, HEAD_SIZE)], cosines, sines)
            keys[at, columns(g, HEAD_SIZE)] = turned.astype(bf16)
            values[at, columns(2 * g, HEAD_SIZE)] = value[:, columns(g, HEAD_SIZE)]

    for step in range(reach + 1):
        pl.when(count > step)(functools.partial(rebuild, step))

    row = lax.broadcasted_iota(jnp.int32, (rows, tokens), 0) % tokens
    column = lax.broadcasted_iota(jnp.int32, (rows, tokens), 1)
    allowed = column <= row
    spans = []
    for first in range(1, reach + 1, 2):
        if first < reach:
            spans.append((count > first + 1, first, 2))
        spans.append((count == first + 1, first, 1))

    for g in range(KEY_VALUE_HEADS):
        score = dot_nt(queries[g], keys[:tokens, columns(g, HEAD_SIZE)])
        score = jnp.where(allowed, score, score_masked)
        scores[:, :tokens] = score
        high[...] = score

        def compare(first, number, g=g):
            at = pl.ds(first * tokens, number * tokens)
            score = dot_nt(queries[g], keys[at, columns(g, HEAD_SIZE)])
            scores[:, at] = score
            top = high[...]
            for i in range(number):
                top = jnp.maximum(top, score[:, columns(i, tokens)])
            high[...] = top

        for when, first, number in spans:
            pl.when(when)(functools.partial(compare, first, number))
        top = jnp.max(high[...], axis=1, keepdims=True) * base2

        def blend(first, number, g=g):
            at = pl.ds(first * tokens, number * tokens)
            weight = jnp.exp2(scores[:, at] * base2 - top).astype(bf16)
            return jnp.dot(
                weight, values[at, columns(g, 2 * HEAD_SIZE)], preferred_element_type=jnp.float32
            )

        def add(first, number, blend=blend):
            acc[...] += blend(first, number)

        acc[...] = blend(0, 1)
        for when, first, number in spans:
            pl.when(when)(functools.partial(add, first, number))
        result = (acc[:, :HEAD_SIZE] / acc[:, HEAD_SIZE:]).astype(bf16)
        for j in range(GROUP_SPLIT):
            out_ref[:, columns(g * GROUP_SPLIT + j, HEAD_SIZE)] = result[columns(j, tokens)]

    at_q = d + q_width
    low = jnp.zeros((tokens, rank), jnp.float32)
    for chunk in range(CHUNKS):
        down = factor(piece_refs, chunk, at_q, q_width)
        low += dot_nt(out_ref[:, columns(chunk, q_width)], down)
    low = low.astype(bf16)
    for chunk in range(CHUNKS):
        result = adapter_scale * jnp.dot(
            low, factor(piece_refs, chunk, at_q + q_width, d), preferred_element_type=jnp.float32
        )
        extra_ref[:, columns(chunk, d)] = result.astype(bf16)


def attend(scalars, hidden, query, tables, frozen, lows_list, kv_pieces, rest_pieces, shards):
    tokens, query_width = query.shape
    model_width = hidden.shape[1]
    key_width = frozen.shape[2] // 2
    blocks = len(lows_list)
    rows = GROUP_SPLIT * tokens
    up_width = 2 * key_width // CHUNKS
    up_at = kv_pieces[0].shape[3] // up_width - 1
    up_spec = pl.BlockSpec(kv_pieces[0].shape[:3] + (up_width,), lambda i: (0, 0, 0, up_at))
    bf16, f32 = jnp.bfloat16, jnp.float32
    return pl.pallas_call(
        functools.partial(attend_kernel, shards, blocks - 1),
        out_shape=[
            jax.ShapeDtypeStruct((tokens, query_width), bf16),
            jax.ShapeDtypeStruct((tokens, model_width), bf16),
        ],
        grid=(1,),
        in_specs=smem()
        + vmem(4)
        + [pl.BlockSpec(memory_space=pl.ANY)]
        + vmem(blocks)
        + [up_spec] * ROW_BLOCKS
        + vmem(ROW_BLOCKS),
        out_specs=vmem(2),
        scratch_shapes=[
            pltpu.VMEM((blocks,) + frozen.shape[1:], bf16),
            pltpu.VMEM((KEY_VALUE_HEADS, rows, HEAD_SIZE), bf16),
            pltpu.VMEM((blocks * tokens, key_width), bf16),
            pltpu.VMEM((blocks * tokens, 2 * key_width), bf16),
            pltpu.VMEM((rows, blocks * tokens), f32),
            pltpu.VMEM((rows, tokens), f32),
            pltpu.VMEM((rows, 2 * HEAD_SIZE), f32),
            pltpu.SemaphoreType.DMA((blocks,)),
        ],
        compiler_params=PARAMS,
        cost_estimate=pl.CostEstimate(
            flops=2_000_000_000, bytes_accessed=8 << 20, transcendentals=4 << 20
        ),
        name="attend",
    )(scalars, hidden, query, *tables, frozen, *lows_list, *kv_pieces, *rest_pieces)


def reach_pairs(shards, shift):
    longest = shards // 2 + 1
    low = -(longest // 2)
    runs = (
        [i % shards for i in range(low, low + longest)],
        [i % shards for i in range(low + longest, low + shards)],
    )
    limits = (longest, shards - longest - 1)
    return [
        (run[i], run[i + shift])
        for run, limit in zip(runs, limits)
        if shift < limit
        for i in range(len(run) - shift)
    ]


PLANES = 4
LONG_PLANES = (0, 3)


def plane_pairs(shift, planes):
    return [
        (p * PLANES + q, (p + shift) % PLANES * PLANES + q)
        for p in range(PLANES)
        for q in range(PLANES)
        if (p + shift) % PLANES in planes
    ]


def letters_kernel(kv_width, scalars_ref, own_ref, their_ref, *outs):
    plane, own_half, longest = scalars_ref[0], scalars_ref[1], scalars_ref[2]
    first, second = outs[:-1], outs[-1]
    rest_width = own_ref.shape[2] - kv_width
    for half, ref in ((own_half, own_ref), (1 - own_half, their_ref)):
        for shift, out in enumerate(first, 1):
            to = lax.rem(plane + shift, PLANES)
            is_long = (to == LONG_PLANES[0]) | (to == LONG_PLANES[1])

            @pl.when(is_long)
            def _(out=out, half=half, ref=ref):
                out[half, :, : ref.shape[2]] = ref[longest]

            @pl.when(jnp.logical_not(is_long))
            def _(out=out, half=half, ref=ref):
                for slot in range(ref.shape[0]):
                    out[half, :, columns(slot, kv_width)] = ref[slot, :, :kv_width]

        for slot in range(ref.shape[0]):
            second[half, :, columns(slot, rest_width)] = ref[slot, :, kv_width:]


def letters(scalars, own, theirs, kv_width):
    slots, _, width = own.shape
    first = slots * kv_width
    shape = lambda w: jax.ShapeDtypeStruct((2, 16, w), own.dtype)
    return pl.pallas_call(
        functools.partial(letters_kernel, kv_width),
        out_shape=[shape(first)] * (PLANES - 1) + [shape(slots * (width - kv_width))],
        in_specs=smem() + vmem(2),
        out_specs=vmem(PLANES),
        compiler_params=PARAMS,
        name="letters",
    )(scalars, own, theirs)


def share_kernel(at, width, rest, scalars_ref, own_ref, their_ref, *refs):
    plane, own_half, slots = scalars_ref[0], scalars_ref[1], scalars_ref[3 : 3 + PLANES]
    long_refs, refs = refs[: PLANES - 1], refs[PLANES - 1 :]
    short_refs, outs = (refs[: PLANES - 1], refs[PLANES - 1 :]) if rest else (long_refs, refs)
    is_long = (plane == LONG_PLANES[0]) | (plane == LONG_PLANES[1])
    for other, out in enumerate(outs):
        slot = scalars_ref[3 + other]
        out[plane, own_half] = own_ref[slot, :, at : at + width]
        out[plane, 1 - own_half] = their_ref[slot, :, at : at + width]

        @pl.when(is_long)
        def _(out=out):
            for shift, ref in enumerate(long_refs, 1):
                out[lax.rem(plane - shift + PLANES, PLANES)] = ref[:, :, at : at + width]

        @pl.when(jnp.logical_not(is_long))
        def _(out=out, slot=slot):
            start = pl.multiple_of(slot * width, 128)
            for shift, ref in enumerate(short_refs, 1):
                out[lax.rem(plane - shift + PLANES, PLANES)] = ref[:, :, pl.ds(start, width)]


def share(scalars, own, theirs, first, second, at, width):
    rest = second is not None
    arrays = list(first) + (list(second) if rest else [])
    shape = jax.ShapeDtypeStruct((PLANES, 2, 16, width), own.dtype)
    return pl.pallas_call(
        functools.partial(share_kernel, at, width, rest),
        out_shape=[shape] * PLANES,
        in_specs=smem() + vmem(2 + len(arrays)),
        out_specs=vmem(PLANES),
        compiler_params=PARAMS,
        name="share",
    )(scalars, own, theirs, *arrays)


def planes_gather(own_index, own_half, request_at, longest, own, theirs, kv_width):
    width = own.shape[2]
    plane, place = own_index // PLANES, own_index % PLANES
    mates = request_at[own_index ^ jnp.arange(PLANES, dtype=jnp.int32)]
    scalars = jnp.concatenate([jnp.stack([plane, own_half, longest]), mates]).astype(jnp.int32)
    *first, second = letters(scalars, own, theirs, kv_width)
    shifts = range(1, PLANES)
    all_planes = range(PLANES)
    short = [p for p in all_planes if p not in LONG_PLANES]
    first = [lax.ppermute(x, "ctx", plane_pairs(s, all_planes)) for s, x in zip(shifts, first)]
    second = [lax.ppermute(second, "ctx", plane_pairs(s, short)) for s in shifts]
    mate_pairs = [[(d, d ^ k) for d in range(PLANES * PLANES)] for k in all_planes]

    def mates_share(late, at, part_width):
        mine, *out = share(scalars, own, theirs, first, late, at, part_width)
        return [mine] + [lax.ppermute(x, "ctx", mate_pairs[k + 1]) for k, x in enumerate(out)]

    kv = mates_share(None, 0, kv_width)
    rest = mates_share(second, kv_width, width - kv_width)
    return kv, rest, place


def body(
    hidden,
    frozen_query,
    frozen_key,
    frozen_value,
    adapter_bank,
    request_shards,
    request_adapter,
    adapter_owner,
):
    shards = lax.axis_size("ctx")
    groups = lax.axis_size("groups")
    own_index = lax.axis_index("ctx").astype(jnp.int32)
    tokens, model_width = hidden.shape
    requests = request_shards.shape[0]
    halves = 2 if groups == 2 and shards == PLANES * PLANES else 1
    own_half = lax.axis_index("groups").astype(jnp.int32) if halves == 2 else jnp.int32(0)
    parts = Parts(model_width, frozen_query.shape[1], frozen_key.shape[1])
    swap = [(0, 1), (1, 0)]
    reach = shards // 2

    packed = pack(parts, halves, shards, own_half, adapter_bank)
    spread = lax.all_to_all(packed, "ctx", split_axis=0, concat_axis=0, tiled=True)
    frozen = lax.all_gather(jnp.concatenate([frozen_key, frozen_value], axis=1), "ctx")

    request_of, starts, packed_of = request_layout(request_shards, shards)
    request_at = request_of[packed_of].astype(jnp.int32)
    own_packed = packed_of[own_index]
    count = jnp.clip(own_packed - starts[request_of[own_packed]], 0, reach) + 1
    tables = rope_tables(jnp.arange((reach + 1) * tokens, dtype=jnp.int32).reshape(-1, tokens))

    wanted = request_adapter
    if halves == 2:
        theirs = lax.ppermute(request_adapter, "groups", swap)
        wanted = jnp.concatenate([theirs, request_adapter])
    picked = pick(adapter_owner[wanted].astype(jnp.int32), spread)

    if halves == 2:
        arrived = lax.ppermute(picked[:requests], "groups", swap)
        kv_pieces, rest_pieces, order = planes_gather(
            own_index, own_half, request_at, jnp.argmax(request_shards), picked[requests:],
            arrived, parts.kv_width,
        )
    else:
        order = jnp.int32(0)
        kv_pieces, rest_pieces = [
            [
                lax.all_to_all(p, "ctx", split_axis=0, concat_axis=0, tiled=True)[
                    b : ROW_BLOCKS * CHUNKS : ROW_BLOCKS
                ]
                for b in range(ROW_BLOCKS)
            ]
            for p in route(request_at, own_half, [picked], parts.kv_width)
        ]

    low = lows(order.reshape(1), hidden, kv_pieces)
    lows_list = [low] + [
        lax.ppermute(low, "ctx", reach_pairs(shards, shift)) for shift in range(1, reach + 1)
    ]
    scalars = jnp.stack([count, own_index, order]).astype(jnp.int32)
    return tuple(
        attend(
            scalars, hidden, frozen_query, tables, frozen, lows_list, kv_pieces, rest_pieces,
            shards,
        )
    )


def solution(mesh):
    return jax.shard_map(
        body,
        mesh=mesh,
        in_specs=(
            P(("groups", "ctx"), None),
            P(("groups", "ctx"), None),
            P(("groups", "ctx"), None),
            P(("groups", "ctx"), None),
            P("ctx", None, None),
            P("groups"),
            P("groups"),
            P(),
        ),
        out_specs=(P(("groups", "ctx"), None), P(("groups", "ctx"), None)),
        check_vma=False,
    )
```

```python
import functools

import jax
import jax.numpy as jnp
from jax import lax
from jax.experimental import pallas as pl
from jax.experimental.pallas import tpu as pltpu
from jax.sharding import PartitionSpec as P

HEAD_SIZE = 128
QUERY_HEADS = 16
KEY_VALUE_HEADS = 4
GROUP_SPLIT = QUERY_HEADS // KEY_VALUE_HEADS

adapter_scale = 0.5
rope_theta = 500000.0
score_masked = -1e30

ROW_BLOCKS = 4
CHUNKS = 8
VMEM_LIMIT = 48 * 1024 * 1024


def rope_tables(positions):
    half_dim = HEAD_SIZE // 2
    frequency = rope_theta ** (-(jnp.arange(half_dim, dtype=jnp.float32) * 2.0) / HEAD_SIZE)
    angles = positions.astype(jnp.float32)[..., None] * frequency
    cosines = jnp.cos(angles)
    sines = jnp.sin(angles)
    return (jnp.concatenate([cosines, cosines], -1), jnp.concatenate([-sines, sines], -1))


class Parts:
    def __init__(self, model_width, query_width, key_width):
        d, q, k = model_width, query_width, key_width
        up = 3 * d
        self.kv = ((d, d // CHUNKS), (2 * d, d // CHUNKS), (up + q, 2 * k // CHUNKS))
        self.q = ((0, d // CHUNKS), (up, q // CHUNKS))
        self.o = ((up + q + 2 * k, q // CHUNKS), (up + 2 * q + 2 * k, d // CHUNKS))
        self.all = self.kv + self.q + self.o
        self.kv_width = sum(w for _, w in self.kv)
        self.rest_width = sum(w for _, w in self.q + self.o)


def vmem(count=1):
    return [pl.BlockSpec(memory_space=pltpu.VMEM)] * count


def smem(count=1):
    return [pl.BlockSpec(memory_space=pltpu.SMEM)] * count


PARAMS = pltpu.CompilerParams(vmem_limit_bytes=VMEM_LIMIT)


OWN_INDEX, OWN_HALF, PLANE, ORDER, LONGEST, COUNT, MATES, IDS = 0, 1, 2, 3, 4, 5, 6, 10


def plan_kernel(shards, reach, me_ref, lengths_ref, adapters_ref, owner_ref, out_ref):
    own_index = me_ref[0]
    requests = lengths_ref.shape[0]
    starts, longest, start, length = [jnp.int32(0)], jnp.int32(0), jnp.int32(0), lengths_ref[0]
    for r in range(1, requests):
        starts.append(starts[-1] + lengths_ref[r - 1])
        longer = lengths_ref[r] > length
        longest = jnp.where(longer, r, longest)
        start = jnp.where(longer, starts[-1], start)
        length = jnp.where(longer, lengths_ref[r], length)
    offset = start + lax.div(length, 2)
    ids = adapters_ref.shape[0]
    own_packed = lax.rem(own_index + offset, shards)
    first = jnp.int32(0)
    for r in range(1, requests):
        first = jnp.where(starts[r] <= own_packed, starts[r], first)
    planes = shards == PLANES * PLANES
    out_ref[OWN_INDEX] = own_index
    out_ref[OWN_HALF] = me_ref[1]
    out_ref[PLANE] = lax.div(own_index, PLANES)
    out_ref[ORDER] = lax.rem(own_index, PLANES) if planes else 0
    out_ref[LONGEST] = longest
    out_ref[COUNT] = jnp.minimum(own_packed - first, reach) + 1
    for i in range(ids):
        out_ref[IDS + i] = owner_ref[adapters_ref[i]]
    for shard in range(shards):
        packed = lax.rem(shard + offset, shards)
        request = jnp.int32(0)
        for r in range(1, requests):
            request += (starts[r] <= packed).astype(jnp.int32)
        out_ref[IDS + ids + shard] = request
    for mate in range(PLANES):
        place = jnp.bitwise_xor(own_index, mate) if planes else 0
        out_ref[MATES + mate] = out_ref[IDS + ids + place]


def make_plan(shards, reach, me, lengths, adapters, owner):
    size = IDS + adapters.shape[0] + shards
    return pl.pallas_call(
        functools.partial(plan_kernel, shards, reach),
        out_shape=jax.ShapeDtypeStruct((size,), jnp.int32),
        in_specs=smem(4),
        out_specs=smem()[0],
        name="plan",
    )(me, lengths, adapters, owner)


def pack_kernel(parts, halves, x_ref, bank_ref, out):
    own_half = x_ref[1]
    for block in range(out.shape[0]):
        piece = block % (ROW_BLOCKS * CHUNKS // halves)
        rows = pl.ds((piece % ROW_BLOCKS) * 16, 16)
        chunk = (piece // ROW_BLOCKS) * halves + own_half
        at = 0
        for first, width in parts.all:
            start = pl.multiple_of(first + chunk * width, 128)
            out[block, :, at : at + width] = bank_ref[0, rows, pl.ds(start, width)]
            at += width


def pack(parts, halves, shards, me, bank):
    width = parts.kv_width + parts.rest_width
    return pl.pallas_call(
        functools.partial(pack_kernel, parts, halves),
        out_shape=jax.ShapeDtypeStruct((shards, 16, width), bank.dtype),
        in_specs=smem() + vmem(),
        out_specs=vmem()[0],
        compiler_params=PARAMS,
        name="pack",
    )(me, bank)


def pick_kernel(plan_ref, spread_ref, out_ref):
    out_ref[...] = spread_ref[...]


def pick(plan, spread, count):
    block = (None,) + spread.shape[1:]
    return pl.pallas_call(
        pick_kernel,
        out_shape=jax.ShapeDtypeStruct((count,) + spread.shape[1:], spread.dtype),
        grid_spec=pltpu.PrefetchScalarGridSpec(
            num_scalar_prefetch=1,
            grid=(count,),
            in_specs=[pl.BlockSpec(block, lambda i, plan: (plan[IDS + i], 0, 0))],
            out_specs=pl.BlockSpec(block, lambda i, plan: (i, 0, 0)),
        ),
        compiler_params=PARAMS,
        name="pick",
    )(plan, spread)


def route_kernel(first, kv_width, plan_ref, side_ref, kv_ref, rest_ref):
    for dest in range(kv_ref.shape[0]):
        slot = plan_ref[first + dest]
        kv_ref[dest, 0] = side_ref[slot, :, :kv_width]
        rest_ref[dest, 0] = side_ref[slot, :, kv_width:]


def route(plan, shards, side, kv_width):
    width = side.shape[2]
    return pl.pallas_call(
        functools.partial(route_kernel, plan.shape[0] - shards, kv_width),
        out_shape=[
            jax.ShapeDtypeStruct((shards, 1, 16, w), side.dtype)
            for w in (kv_width, width - kv_width)
        ],
        in_specs=smem() + vmem(),
        out_specs=vmem(2),
        compiler_params=PARAMS,
        name="route",
    )(plan, side)


def factor(piece_refs, chunk, at, width):
    halves = piece_refs[0].shape[1]
    return jnp.concatenate(
        [ref[chunk // halves, chunk % halves, :, at : at + width] for ref in piece_refs], axis=0
    )


def columns(chunk, width):
    return slice(chunk * width, (chunk + 1) * width)


def dot_nt(a, b):
    return lax.dot_general(a, b, (((1,), (1,)), ((), ())), preferred_element_type=jnp.float32)


def turn(x, cosines, sines):
    return x * cosines + pltpu.roll(x, HEAD_SIZE // 2, 1) * sines


def reorder(own, rank, inverse):
    shape = (2 * rank, 2 * rank)
    here, plain = (1, 0) if inverse else (0, 1)
    here = lax.broadcasted_iota(jnp.int32, shape, here)
    plain = lax.broadcasted_iota(jnp.int32, shape, plain)
    same = jnp.bitwise_xor(here, own * 16) == plain
    return jnp.where(same, 1.0, 0.0).astype(jnp.bfloat16)


def lows_kernel(plan_ref, hidden_ref, *refs):
    piece_refs, out_ref = refs[:-1], refs[-1]
    d = hidden_ref.shape[1] // CHUNKS
    rank = ROW_BLOCKS * 16
    low = jnp.zeros((hidden_ref.shape[0], 2 * rank), jnp.float32)
    for chunk in range(CHUNKS):
        down = jnp.concatenate(
            [factor(piece_refs, chunk, 0, d), factor(piece_refs, chunk, d, d)], axis=0
        )
        low += dot_nt(hidden_ref[:, columns(chunk, d)], down)
    plain = jnp.dot(
        low.astype(jnp.bfloat16),
        reorder(plan_ref[ORDER], rank, False),
        preferred_element_type=jnp.float32,
    )
    plain = plain.astype(jnp.bfloat16)
    for shard in range(out_ref.shape[0]):
        out_ref[shard] = plain


def lows(plan, shards, hidden, pieces):
    return pl.pallas_call(
        lows_kernel,
        out_shape=jax.ShapeDtypeStruct((shards, hidden.shape[0], 2 * ROW_BLOCKS * 16), jnp.bfloat16),
        in_specs=smem() + vmem(1 + len(pieces)),
        out_specs=vmem()[0],
        compiler_params=PARAMS,
        cost_estimate=pl.CostEstimate(
            flops=150_000_000, bytes_accessed=3 << 20, transcendentals=0
        ),
        name="lows",
    )(plan, hidden, *pieces)


def attend_kernel(
    shards, reach, sources, plan_ref, hidden_ref, query_ref, cos_ref, sin_ref, lows_ref, *refs
):
    frozen_refs, refs = refs[:sources], refs[sources:]
    up_refs, refs = refs[:ROW_BLOCKS], refs[ROW_BLOCKS:]
    rest_refs, refs = refs[:ROW_BLOCKS], refs[ROW_BLOCKS:]
    out_ref, extra_ref, frozen, up_copy, q_copy, o_copy, *refs = refs
    queries, keys, values, scores, high, acc, sem, part_sem = refs
    own_index, order, count = plan_ref[OWN_INDEX], plan_ref[ORDER], plan_ref[COUNT]
    tokens = query_ref.shape[0]
    rank = ROW_BLOCKS * 16
    rows = GROUP_SPLIT * tokens
    key_width = KEY_VALUE_HEADS * HEAD_SIZE
    bf16 = jnp.bfloat16
    base2 = 1.4426950408889634 / (HEAD_SIZE**0.5)
    up_width, q_width = up_copy.shape[4], q_copy.shape[4]

    def at_last(ref, start, width):
        return ref.at[:, :, :, pl.ds(start, width)]

    def parts_of(copy, refs, start, index):
        return [
            pltpu.make_async_copy(
                at_last(ref, start, copy.shape[4]), copy.at[b], part_sem.at[index, b]
            )
            for b, ref in enumerate(refs)
        ]

    q_parts = parts_of(q_copy, rest_refs, 0, 0)
    up_parts = parts_of(up_copy, up_refs, up_refs[0].shape[3] - up_width, 1)
    o_parts = parts_of(o_copy, rest_refs, q_width, 2)
    for copy in q_parts + up_parts:
        copy.start()

    def source_of(step):
        return lax.rem(own_index - step + shards, shards)

    def land(step, source):
        return pltpu.make_async_copy(source, frozen.at[step], sem.at[step])

    land(0, frozen_refs[0]).start()
    for step in range(1, reach + 1):
        source = source_of(step)
        if sources == 2:
            pl.when(count > step)(land(step, frozen_refs[1].at[source]).start)
            continue
        plane = plan_ref[PLANE]
        last_long = (plane == 1) & (order == 0)
        far = lax.div(source, PLANES) != jnp.where(last_long, 0, plane)
        slot = far.astype(jnp.int32)
        mate = jnp.bitwise_xor(lax.rem(source, PLANES), order)
        for other in range(PLANES):
            pl.when((count > step) & (mate == other))(
                land(step, frozen_refs[1 + other].at[slot]).start
            )
    for copy in o_parts:
        copy.start()

    for copy in q_parts:
        copy.wait()
    piece_refs = [q_copy.at[b] for b in range(ROW_BLOCKS)]
    d = hidden_ref.shape[1] // CHUNKS
    low = jnp.zeros((tokens, rank), jnp.float32)
    for chunk in range(CHUNKS):
        low += dot_nt(hidden_ref[:, columns(chunk, d)], factor(piece_refs, chunk, 0, d))
    low = low.astype(bf16)
    q_head = query_ref.shape[1] // CHUNKS
    cosines, sines = cos_ref[count - 1], sin_ref[count - 1]
    for chunk in range(CHUNKS):
        update = jnp.dot(
            low, factor(piece_refs, chunk, d, q_head), preferred_element_type=jnp.float32
        )
        result = query_ref[:, columns(chunk, q_head)].astype(jnp.float32) + adapter_scale * update
        for part in range(q_head // HEAD_SIZE):
            head = chunk * (q_head // HEAD_SIZE) + part
            turned = turn(result[:, columns(part, HEAD_SIZE)], cosines, sines)
            queries[head // GROUP_SPLIT, pl.ds((head % GROUP_SPLIT) * tokens, tokens)] = (
                turned.astype(bf16)
            )

    for copy in up_parts:
        copy.wait()
    here = reorder(order, rank, True)
    up_copies = [up_copy.at[b] for b in range(ROW_BLOCKS)]
    up = [factor(up_copies, chunk, 0, up_width) for chunk in range(CHUNKS)]
    up_key = jnp.concatenate(up[: CHUNKS // 2], axis=1)
    up_value = jnp.concatenate(up[CHUNKS // 2 :], axis=1)
    for g in range(KEY_VALUE_HEADS):
        values[:, pl.ds((2 * g + 1) * HEAD_SIZE, HEAD_SIZE)] = jnp.ones(
            (values.shape[0], HEAD_SIZE), bf16
        )

    def rebuild(step):
        land(step, frozen_refs[0]).wait()
        low = jnp.dot(lows_ref[source_of(step)], here, preferred_element_type=jnp.float32)
        low = low.astype(bf16)
        at = pl.ds(step * tokens, tokens)
        cosines, sines = cos_ref[count - 1 - step], sin_ref[count - 1 - step]
        key = frozen[step, :, :key_width].astype(jnp.float32) + adapter_scale * jnp.dot(
            low[:, :rank], up_key, preferred_element_type=jnp.float32
        )
        value = frozen[step, :, key_width:].astype(jnp.float32) + adapter_scale * jnp.dot(
            low[:, rank:], up_value, preferred_element_type=jnp.float32
        )
        value = value.astype(bf16)
        for g in range(KEY_VALUE_HEADS):
            turned = turn(key[:, columns(g, HEAD_SIZE)], cosines, sines)
            keys[at, columns(g, HEAD_SIZE)] = turned.astype(bf16)
            values[at, columns(2 * g, HEAD_SIZE)] = value[:, columns(g, HEAD_SIZE)]

    for step in range(reach + 1):
        pl.when(count > step)(functools.partial(rebuild, step))

    row = lax.broadcasted_iota(jnp.int32, (rows, tokens), 0) % tokens
    column = lax.broadcasted_iota(jnp.int32, (rows, tokens), 1)
    allowed = column <= row
    spans = []
    for first in range(1, reach + 1, 2):
        if first < reach:
            spans.append((count > first + 1, first, 2))
        spans.append((count == first + 1, first, 1))

    for g in range(KEY_VALUE_HEADS):
        score = dot_nt(queries[g], keys[:tokens, columns(g, HEAD_SIZE)])
        score = jnp.where(allowed, score, score_masked)
        scores[:, :tokens] = score
        high[...] = score

        def compare(first, number, g=g):
            at = pl.ds(first * tokens, number * tokens)
            score = dot_nt(queries[g], keys[at, columns(g, HEAD_SIZE)])
            scores[:, at] = score
            top = high[...]
            for i in range(number):
                top = jnp.maximum(top, score[:, columns(i, tokens)])
            high[...] = top

        for when, first, number in spans:
            pl.when(when)(functools.partial(compare, first, number))
        top = jnp.max(high[...], axis=1, keepdims=True) * base2

        def blend(first, number, g=g):
            at = pl.ds(first * tokens, number * tokens)
            weight = jnp.exp2(scores[:, at] * base2 - top).astype(bf16)
            return jnp.dot(
                weight, values[at, columns(g, 2 * HEAD_SIZE)], preferred_element_type=jnp.float32
            )

        def add(first, number, blend=blend):
            acc[...] += blend(first, number)

        acc[...] = blend(0, 1)
        for when, first, number in spans:
            pl.when(when)(functools.partial(add, first, number))
        result = (acc[:, :HEAD_SIZE] / acc[:, HEAD_SIZE:]).astype(bf16)
        for j in range(GROUP_SPLIT):
            out_ref[:, columns(g * GROUP_SPLIT + j, HEAD_SIZE)] = result[columns(j, tokens)]

    for copy in o_parts:
        copy.wait()
    piece_refs = [o_copy.at[b] for b in range(ROW_BLOCKS)]
    low = jnp.zeros((tokens, rank), jnp.float32)
    for chunk in range(CHUNKS):
        down = factor(piece_refs, chunk, 0, q_head)
        low += dot_nt(out_ref[:, columns(chunk, q_head)], down)
    low = low.astype(bf16)
    for chunk in range(CHUNKS):
        result = adapter_scale * jnp.dot(
            low, factor(piece_refs, chunk, q_head, d), preferred_element_type=jnp.float32
        )
        extra_ref[:, columns(chunk, d)] = result.astype(bf16)


def attend(plan, hidden, query, tables, frozen, lows_all, kv_pieces, rest_pieces, q_width):
    tokens, query_width = query.shape
    shards, model_width = lows_all.shape[0], hidden.shape[1]
    key_width = frozen[0].shape[1] // 2
    blocks = tables[0].shape[0]
    rows = GROUP_SPLIT * tokens
    up_width = 2 * key_width // CHUNKS
    rest_width = rest_pieces[0].shape[3]
    bf16, f32 = jnp.bfloat16, jnp.float32

    def copies(width):
        return pltpu.VMEM((ROW_BLOCKS,) + rest_pieces[0].shape[:3] + (width,), bf16)

    apart = [*frozen, *kv_pieces, *rest_pieces]
    return pl.pallas_call(
        functools.partial(attend_kernel, shards, blocks - 1, len(frozen)),
        out_shape=[
            jax.ShapeDtypeStruct((tokens, query_width), bf16),
            jax.ShapeDtypeStruct((tokens, model_width), bf16),
        ],
        in_specs=smem() + vmem(5) + [pl.BlockSpec(memory_space=pl.ANY)] * len(apart),
        out_specs=vmem(2),
        scratch_shapes=[
            pltpu.VMEM((blocks,) + frozen[0].shape, bf16),
            copies(up_width),
            copies(q_width),
            copies(rest_width - q_width),
            pltpu.VMEM((KEY_VALUE_HEADS, rows, HEAD_SIZE), bf16),
            pltpu.VMEM((blocks * tokens, key_width), bf16),
            pltpu.VMEM((blocks * tokens, 2 * key_width), bf16),
            pltpu.VMEM((rows, blocks * tokens), f32),
            pltpu.VMEM((rows, tokens), f32),
            pltpu.VMEM((rows, 2 * HEAD_SIZE), f32),
            pltpu.SemaphoreType.DMA((blocks,)),
            pltpu.SemaphoreType.DMA((3, ROW_BLOCKS)),
        ],
        compiler_params=PARAMS,
        cost_estimate=pl.CostEstimate(
            flops=2_000_000_000, bytes_accessed=8 << 20, transcendentals=4 << 20
        ),
        name="attend",
    )(plan, hidden, query, *tables, lows_all, *apart)


PLANES = 4
LONG_PLANES = (0, 3)


def plane_pairs(shift, planes):
    return [
        (p * PLANES + q, (p + shift) % PLANES * PLANES + q)
        for p in range(PLANES)
        for q in range(PLANES)
        if (p + shift) % PLANES in planes
    ]


def letters_kernel(kv_width, plan_ref, own_ref, their_ref, *outs):
    plane, own_half, longest = plan_ref[PLANE], plan_ref[OWN_HALF], plan_ref[LONGEST]
    first, second = outs[:-1], outs[-1]
    rest_width = own_ref.shape[2] - kv_width
    for half, ref in ((own_half, own_ref), (1 - own_half, their_ref)):
        for shift, out in enumerate(first, 1):
            to = lax.rem(plane + shift, PLANES)
            is_long = (to == LONG_PLANES[0]) | (to == LONG_PLANES[1])

            @pl.when(is_long)
            def _(out=out, half=half, ref=ref):
                out[half, :, : ref.shape[2]] = ref[longest]

            @pl.when(jnp.logical_not(is_long))
            def _(out=out, half=half, ref=ref):
                for slot in range(ref.shape[0]):
                    out[half, :, columns(slot, kv_width)] = ref[slot, :, :kv_width]

        for slot in range(ref.shape[0]):
            second[half, :, columns(slot, rest_width)] = ref[slot, :, kv_width:]


def letters(plan, own, theirs, kv_width):
    slots, _, width = own.shape
    first = slots * kv_width
    shape = lambda w: jax.ShapeDtypeStruct((2, 16, w), own.dtype)
    return pl.pallas_call(
        functools.partial(letters_kernel, kv_width),
        out_shape=[shape(first)] * (PLANES - 1) + [shape(slots * (width - kv_width))],
        in_specs=smem() + vmem(2),
        out_specs=vmem(PLANES),
        compiler_params=PARAMS,
        name="letters",
    )(plan, own, theirs)


def share_kernel(at, width, rest, plan_ref, own_ref, their_ref, *refs):
    plane, own_half = plan_ref[PLANE], plan_ref[OWN_HALF]
    long_refs, refs = refs[: PLANES - 1], refs[PLANES - 1 :]
    short_refs, outs = (refs[: PLANES - 1], refs[PLANES - 1 :]) if rest else (long_refs, refs)
    is_long = (plane == LONG_PLANES[0]) | (plane == LONG_PLANES[1])
    for other, out in enumerate(outs):
        slot = plan_ref[MATES + other]
        out[plane, own_half] = own_ref[slot, :, at : at + width]
        out[plane, 1 - own_half] = their_ref[slot, :, at : at + width]

        @pl.when(is_long)
        def _(out=out):
            for shift, ref in enumerate(long_refs, 1):
                out[lax.rem(plane - shift + PLANES, PLANES)] = ref[:, :, at : at + width]

        @pl.when(jnp.logical_not(is_long))
        def _(out=out, slot=slot):
            start = pl.multiple_of(slot * width, 128)
            for shift, ref in enumerate(short_refs, 1):
                out[lax.rem(plane - shift + PLANES, PLANES)] = ref[:, :, pl.ds(start, width)]


def share(plan, own, theirs, first, second, at, width):
    rest = second is not None
    arrays = list(first) + (list(second) if rest else [])
    shape = jax.ShapeDtypeStruct((PLANES, 2, 16, width), own.dtype)
    return pl.pallas_call(
        functools.partial(share_kernel, at, width, rest),
        out_shape=[shape] * PLANES,
        in_specs=smem() + vmem(2 + len(arrays)),
        out_specs=vmem(PLANES),
        compiler_params=PARAMS,
        name="share",
    )(plan, own, theirs, *arrays)


MATE_PAIRS = [[(d, d ^ k) for d in range(PLANES * PLANES)] for k in range(PLANES)]


def pairs_kernel(plan_ref, own_ref, one_ref, two_ref, *outs):
    plane, order = plan_ref[PLANE], plan_ref[ORDER]
    for other, out in enumerate(outs):
        last_long = (plane == 1) & (order == other)

        @pl.when(last_long)
        def _(out=out):
            out[0] = one_ref[...]
            out[1] = two_ref[...]

        @pl.when(jnp.logical_not(last_long))
        def _(out=out):
            out[0] = own_ref[...]
            out[1] = one_ref[...]


def pairs(plan, own, one, two):
    shape = jax.ShapeDtypeStruct((2,) + own.shape, own.dtype)
    return pl.pallas_call(
        pairs_kernel,
        out_shape=[shape] * PLANES,
        in_specs=smem() + vmem(3),
        out_specs=vmem(PLANES),
        compiler_params=PARAMS,
        name="pairs",
    )(plan, own, one, two)


def planes_gather(plan, picked, frozen, requests, kv_width):
    swap = [(0, 1), (1, 0)]
    shifts = range(1, PLANES)
    all_planes = range(PLANES)
    short = [p for p in all_planes if p not in LONG_PLANES]
    own, width = picked[requests:], picked.shape[2]
    theirs = lax.ppermute(picked[:requests], "groups", swap)
    frozen, own = lax.optimization_barrier((frozen, own))
    one = lax.ppermute(frozen, "ctx", plane_pairs(1, (0, 1, 2)))
    two = lax.ppermute(frozen, "ctx", plane_pairs(2, (1,)))
    *first, second = letters(plan, own, theirs, kv_width)
    one, two, first[0] = lax.optimization_barrier((one, two, first[0]))
    first = [lax.ppermute(x, "ctx", plane_pairs(s, all_planes)) for s, x in zip(shifts, first)]
    second = [lax.ppermute(second, "ctx", plane_pairs(s, short)) for s in shifts]

    def to_mates(letters_out):
        mine, *out = letters_out
        return [mine] + [lax.ppermute(x, "ctx", MATE_PAIRS[k + 1]) for k, x in enumerate(out)]

    frozen_list = [frozen] + to_mates(pairs(plan, frozen, one, two))
    kv = to_mates(share(plan, own, theirs, first, None, 0, kv_width))
    rest = to_mates(share(plan, own, theirs, first, second, kv_width, width - kv_width))
    return kv, rest, frozen_list


def body(
    hidden,
    frozen_query,
    frozen_key,
    frozen_value,
    adapter_bank,
    request_shards,
    request_adapter,
    adapter_owner,
):
    shards = lax.axis_size("ctx")
    groups = lax.axis_size("groups")
    tokens, model_width = hidden.shape
    requests = request_shards.shape[0]
    halves = 2 if groups == 2 and shards == PLANES * PLANES else 1
    own_half = lax.axis_index("groups") if halves == 2 else 0
    me = jnp.stack([lax.axis_index("ctx"), own_half]).astype(jnp.int32)
    parts = Parts(model_width, frozen_query.shape[1], frozen_key.shape[1])
    reach = shards // 2

    packed = pack(parts, halves, shards, me, adapter_bank)
    spread = lax.all_to_all(packed, "ctx", split_axis=0, concat_axis=0, tiled=True)
    frozen = jnp.concatenate([frozen_key, frozen_value], axis=1)
    tables = rope_tables(jnp.arange((reach + 1) * tokens, dtype=jnp.int32).reshape(-1, tokens))

    wanted = request_adapter
    if halves == 2:
        theirs = lax.ppermute(request_adapter, "groups", [(0, 1), (1, 0)])
        wanted = jnp.concatenate([theirs, request_adapter])
    plan = make_plan(shards, reach, me, request_shards, wanted, adapter_owner)
    picked = pick(plan, spread, wanted.shape[0])

    if halves == 2:
        kv_pieces, rest_pieces, frozen_list = planes_gather(
            plan, picked, frozen, requests, parts.kv_width
        )
    else:
        frozen_list = [frozen, lax.all_gather(frozen, "ctx")]
        kv_pieces, rest_pieces = [
            [
                lax.all_to_all(p, "ctx", split_axis=0, concat_axis=0, tiled=True)[
                    b : ROW_BLOCKS * CHUNKS : ROW_BLOCKS
                ]
                for b in range(ROW_BLOCKS)
            ]
            for p in route(plan, shards, picked, parts.kv_width)
        ]

    low = lows(plan, shards, hidden, kv_pieces)
    lows_all = lax.all_to_all(low, "ctx", split_axis=0, concat_axis=0, tiled=True)
    q_width = sum(w for _, w in parts.q)
    return tuple(
        attend(
            plan, hidden, frozen_query, tables, frozen_list, lows_all, kv_pieces, rest_pieces,
            q_width,
        )
    )


def solution(mesh):
    return jax.shard_map(
        body,
        mesh=mesh,
        in_specs=(
            P(("groups", "ctx"), None),
            P(("groups", "ctx"), None),
            P(("groups", "ctx"), None),
            P(("groups", "ctx"), None),
            P("ctx", None, None),
            P("groups"),
            P("groups"),
            P(),
        ),
        out_specs=(P(("groups", "ctx"), None), P(("groups", "ctx"), None)),
        check_vma=False,
    )
```

```python
import functools

import jax
import jax.numpy as jnp
from jax import lax
from jax.experimental import pallas as pl
from jax.experimental.pallas import tpu as pltpu
from jax.sharding import PartitionSpec as P

HEAD_SIZE = 128
QUERY_HEADS = 16
KEY_VALUE_HEADS = 4
GROUP_SPLIT = QUERY_HEADS // KEY_VALUE_HEADS

adapter_scale = 0.5
rope_theta = 500000.0
score_masked = -1e30

ROW_BLOCKS = 4
CHUNKS = 8


def rope_tables(positions):
    half_dim = HEAD_SIZE // 2
    frequency = rope_theta ** (-(jnp.arange(half_dim, dtype=jnp.float32) * 2.0) / HEAD_SIZE)
    angles = positions.astype(jnp.float32)[..., None] * frequency
    cosines = jnp.cos(angles)
    sines = jnp.sin(angles)
    return (jnp.concatenate([cosines, cosines], -1), jnp.concatenate([-sines, sines], -1))


class Parts:
    def __init__(self, model_width, query_width, key_width):
        d, q, k = model_width, query_width, key_width
        up = 3 * d
        self.kv = ((d, d // CHUNKS), (2 * d, d // CHUNKS), (up + q, 2 * k // CHUNKS))
        self.q = ((0, d // CHUNKS), (up, q // CHUNKS))
        self.o = ((up + q + 2 * k, q // CHUNKS), (up + 2 * q + 2 * k, d // CHUNKS))
        self.all = self.kv + self.q + self.o
        self.kv_width = sum(w for _, w in self.kv)
        self.rest_width = sum(w for _, w in self.q + self.o)


def vmem(count=1):
    return [pl.BlockSpec(memory_space=pltpu.VMEM)] * count


def smem(count=1):
    return [pl.BlockSpec(memory_space=pltpu.SMEM)] * count


PARAMS = pltpu.CompilerParams(vmem_limit_bytes=16 * 1024 * 1024)


OWN_INDEX, OWN_HALF, PLANE, ORDER, LONGEST, COUNT, MATES, IDS = 0, 1, 2, 3, 4, 5, 6, 10


def plan_kernel(shards, reach, me_ref, lengths_ref, adapters_ref, owner_ref, out_ref):
    own_index = me_ref[0]
    requests = lengths_ref.shape[0]
    starts, longest, start, length = [jnp.int32(0)], jnp.int32(0), jnp.int32(0), lengths_ref[0]
    for r in range(1, requests):
        starts.append(starts[-1] + lengths_ref[r - 1])
        longer = lengths_ref[r] > length
        longest = jnp.where(longer, r, longest)
        start = jnp.where(longer, starts[-1], start)
        length = jnp.where(longer, lengths_ref[r], length)
    offset = start + lax.div(length, 2)
    ids = adapters_ref.shape[0]
    own_packed = lax.rem(own_index + offset, shards)
    first = jnp.int32(0)
    for r in range(1, requests):
        first = jnp.where(starts[r] <= own_packed, starts[r], first)
    planes = shards == PLANES * PLANES
    out_ref[OWN_INDEX] = own_index
    out_ref[OWN_HALF] = me_ref[1]
    out_ref[PLANE] = lax.div(own_index, PLANES)
    out_ref[ORDER] = lax.rem(own_index, PLANES) if planes else 0
    out_ref[LONGEST] = longest
    out_ref[COUNT] = jnp.minimum(own_packed - first, reach) + 1
    for i in range(ids):
        out_ref[IDS + i] = owner_ref[adapters_ref[i]]
    for shard in range(shards):
        packed = lax.rem(shard + offset, shards)
        request = jnp.int32(0)
        for r in range(1, requests):
            request += (starts[r] <= packed).astype(jnp.int32)
        out_ref[IDS + ids + shard] = request
    for mate in range(PLANES):
        place = jnp.bitwise_xor(own_index, mate) if planes else 0
        out_ref[MATES + mate] = out_ref[IDS + ids + place]


def make_plan(shards, reach, me, lengths, adapters, owner):
    size = IDS + adapters.shape[0] + shards
    return pl.pallas_call(
        functools.partial(plan_kernel, shards, reach),
        out_shape=jax.ShapeDtypeStruct((size,), jnp.int32),
        in_specs=smem(4),
        out_specs=smem()[0],
        name="plan",
    )(me, lengths, adapters, owner)


def pack_kernel(parts, halves, x_ref, bank_ref, out):
    own_half = x_ref[1]
    for block in range(out.shape[0]):
        piece = block % (ROW_BLOCKS * CHUNKS // halves)
        rows = pl.ds((piece % ROW_BLOCKS) * 16, 16)
        chunk = (piece // ROW_BLOCKS) * halves + own_half
        at = 0
        for first, width in parts.all:
            start = pl.multiple_of(first + chunk * width, 128)
            out[block, :, at : at + width] = bank_ref[0, rows, pl.ds(start, width)]
            at += width


def pack(parts, halves, shards, me, bank):
    width = parts.kv_width + parts.rest_width
    return pl.pallas_call(
        functools.partial(pack_kernel, parts, halves),
        out_shape=jax.ShapeDtypeStruct((shards, 16, width), bank.dtype),
        in_specs=smem() + vmem(),
        out_specs=vmem()[0],
        compiler_params=PARAMS,
        name="pack",
    )(me, bank)


def pick_kernel(plan_ref, spread_ref, out_ref):
    out_ref[...] = spread_ref[...]


def pick(plan, spread, count):
    block = (None,) + spread.shape[1:]
    return pl.pallas_call(
        pick_kernel,
        out_shape=jax.ShapeDtypeStruct((count,) + spread.shape[1:], spread.dtype),
        grid_spec=pltpu.PrefetchScalarGridSpec(
            num_scalar_prefetch=1,
            grid=(count,),
            in_specs=[pl.BlockSpec(block, lambda i, plan: (plan[IDS + i], 0, 0))],
            out_specs=pl.BlockSpec(block, lambda i, plan: (i, 0, 0)),
        ),
        compiler_params=PARAMS,
        name="pick",
    )(plan, spread)


def route_kernel(first, kv_width, plan_ref, side_ref, kv_ref, rest_ref):
    for dest in range(kv_ref.shape[0]):
        slot = plan_ref[first + dest]
        kv_ref[dest, 0] = side_ref[slot, :, :kv_width]
        rest_ref[dest, 0] = side_ref[slot, :, kv_width:]


def route(plan, shards, side, kv_width):
    width = side.shape[2]
    return pl.pallas_call(
        functools.partial(route_kernel, plan.shape[0] - shards, kv_width),
        out_shape=[
            jax.ShapeDtypeStruct((shards, 1, 16, w), side.dtype)
            for w in (kv_width, width - kv_width)
        ],
        in_specs=smem() + vmem(),
        out_specs=vmem(2),
        compiler_params=PARAMS,
        name="route",
    )(plan, side)


def factor(piece_refs, chunk, at, width):
    halves = piece_refs[0].shape[1]
    return jnp.concatenate(
        [ref[chunk // halves, chunk % halves, :, at : at + width] for ref in piece_refs], axis=0
    )


def columns(chunk, width):
    return slice(chunk * width, (chunk + 1) * width)


def dot_nt(a, b):
    return lax.dot_general(a, b, (((1,), (1,)), ((), ())), preferred_element_type=jnp.float32)


def turn(x, cosines, sines):
    return x * cosines + pltpu.roll(x, HEAD_SIZE // 2, 1) * sines


def reorder(own, rank, inverse):
    shape = (2 * rank, 2 * rank)
    here, plain = (1, 0) if inverse else (0, 1)
    here = lax.broadcasted_iota(jnp.int32, shape, here)
    plain = lax.broadcasted_iota(jnp.int32, shape, plain)
    same = jnp.bitwise_xor(here, own * 16) == plain
    return jnp.where(same, 1.0, 0.0).astype(jnp.bfloat16)


def lows_kernel(plan_ref, hidden_ref, *refs):
    piece_refs, out_ref = refs[:-1], refs[-1]
    d = hidden_ref.shape[1] // CHUNKS
    rank = ROW_BLOCKS * 16
    low = jnp.zeros((hidden_ref.shape[0], 2 * rank), jnp.float32)
    for chunk in range(CHUNKS):
        down = jnp.concatenate(
            [factor(piece_refs, chunk, 0, d), factor(piece_refs, chunk, d, d)], axis=0
        )
        low += dot_nt(hidden_ref[:, columns(chunk, d)], down)
    plain = jnp.dot(
        low.astype(jnp.bfloat16),
        reorder(plan_ref[ORDER], rank, False),
        preferred_element_type=jnp.float32,
    )
    plain = plain.astype(jnp.bfloat16)
    for shard in range(out_ref.shape[0]):
        out_ref[shard] = plain


def lows(plan, shards, hidden, pieces):
    return pl.pallas_call(
        lows_kernel,
        out_shape=jax.ShapeDtypeStruct((shards, hidden.shape[0], 2 * ROW_BLOCKS * 16), jnp.bfloat16),
        in_specs=smem() + vmem(1 + len(pieces)),
        out_specs=vmem()[0],
        compiler_params=PARAMS,
        cost_estimate=pl.CostEstimate(
            flops=150_000_000, bytes_accessed=3 << 20, transcendentals=0
        ),
        name="lows",
    )(plan, hidden, *pieces)


def query_kernel(plan_ref, hidden_ref, query_ref, cos_ref, sin_ref, *refs):
    piece_refs, out_ref = refs[:-1], refs[-1]
    tokens = query_ref.shape[0]
    d = hidden_ref.shape[1] // CHUNKS
    width = query_ref.shape[1] // CHUNKS
    low = jnp.zeros((tokens, ROW_BLOCKS * 16), jnp.float32)
    for chunk in range(CHUNKS):
        low += dot_nt(hidden_ref[:, columns(chunk, d)], factor(piece_refs, chunk, 0, d))
    low = low.astype(jnp.bfloat16)
    own = plan_ref[COUNT] - 1
    cosines, sines = cos_ref[own], sin_ref[own]
    for chunk in range(CHUNKS):
        up = factor(piece_refs, chunk, d, width)
        update = jnp.dot(low, up, preferred_element_type=jnp.float32)
        result = query_ref[:, columns(chunk, width)].astype(jnp.float32) + adapter_scale * update
        for part in range(width // HEAD_SIZE):
            head = chunk * (width // HEAD_SIZE) + part
            turned = turn(result[:, columns(part, HEAD_SIZE)], cosines, sines)
            out_ref[head // GROUP_SPLIT, pl.ds((head % GROUP_SPLIT) * tokens, tokens)] = (
                turned.astype(jnp.bfloat16)
            )


def make_queries(plan, hidden, query, tables, pieces):
    tokens = hidden.shape[0]
    return pl.pallas_call(
        query_kernel,
        out_shape=jax.ShapeDtypeStruct(
            (KEY_VALUE_HEADS, GROUP_SPLIT * tokens, HEAD_SIZE), jnp.bfloat16
        ),
        in_specs=smem() + vmem(4 + len(pieces)),
        out_specs=vmem()[0],
        compiler_params=PARAMS,
        cost_estimate=pl.CostEstimate(
            flops=100_000_000, bytes_accessed=3 << 20, transcendentals=0
        ),
        name="queries",
    )(plan, hidden, query, *tables, *pieces)


REGION = 4


def attend_kernel(
    shards, reach, sources, at_o, plan_ref, queries, cos_ref, sin_ref, lows_ref, *refs
):
    frozen_refs, refs = refs[:sources], refs[sources:]
    up_refs, refs = refs[:ROW_BLOCKS], refs[ROW_BLOCKS:]
    rest_refs, refs = refs[:ROW_BLOCKS], refs[ROW_BLOCKS:]
    out_ref, extra_ref, frozen, up_copy, o_copy, keys, values, high, acc, sem, part_sem = refs
    own_index, order, count = plan_ref[OWN_INDEX], plan_ref[ORDER], plan_ref[COUNT]
    tokens = out_ref.shape[0]
    rank = ROW_BLOCKS * 16
    rows = GROUP_SPLIT * tokens
    key_width = KEY_VALUE_HEADS * HEAD_SIZE
    bf16 = jnp.bfloat16
    base2 = 1.4426950408889634 / (HEAD_SIZE**0.5)
    up_width = up_copy.shape[4]

    def parts_of(copy, refs, start, index):
        return [
            pltpu.make_async_copy(
                ref.at[:, :, :, pl.ds(start, copy.shape[4])], copy.at[b], part_sem.at[index, b]
            )
            for b, ref in enumerate(refs)
        ]

    up_parts = parts_of(up_copy, up_refs, up_refs[0].shape[3] - up_width, 0)
    o_parts = parts_of(o_copy, rest_refs, at_o, 1)

    def source_of(step):
        return lax.rem(own_index - step + shards, shards)

    def land(step, source):
        return pltpu.make_async_copy(source, frozen.at[step], sem.at[step])

    for copy in up_parts:
        copy.start()
    land(0, frozen_refs[0]).start()
    regions = [(0, 1)] + [
        (first, min(REGION, reach + 1 - first)) for first in range(1, reach + 1, REGION)
    ]
    for first, number in regions[1:]:

        @pl.when(count > first)
        def _(first=first, number=number):
            for step in range(first, first + number):
                source = source_of(step)
                if sources == 2:
                    land(step, frozen_refs[1].at[source]).start()
                    continue
                plane = plan_ref[PLANE]
                last_long = (plane == 1) & (order == 0)
                far = lax.div(source, PLANES) != jnp.where(last_long, 0, plane)
                mate = jnp.bitwise_xor(lax.rem(source, PLANES), order)
                for other in range(PLANES):
                    pl.when(mate == other)(
                        land(step, frozen_refs[1 + other].at[far.astype(jnp.int32)]).start
                    )

    for copy in o_parts:
        copy.start()

    for copy in up_parts:
        copy.wait()
    here = reorder(order, rank, True)
    up_copies = [up_copy.at[b] for b in range(ROW_BLOCKS)]
    up = [factor(up_copies, chunk, 0, up_width) for chunk in range(CHUNKS)]
    up_key = jnp.concatenate(up[: CHUNKS // 2], axis=1)
    up_value = jnp.concatenate(up[CHUNKS // 2 :], axis=1)
    ones = jnp.ones((tokens, HEAD_SIZE), bf16)

    def rebuild(step):
        at = pl.ds(step * tokens, tokens)
        low = jnp.dot(lows_ref[source_of(step)], here, preferred_element_type=jnp.float32)
        low = low.astype(bf16)
        land(step, frozen_refs[0]).wait()
        key = frozen[step, :, :key_width].astype(jnp.float32) + adapter_scale * jnp.dot(
            low[:, :rank], up_key, preferred_element_type=jnp.float32
        )
        value = frozen[step, :, key_width:].astype(jnp.float32) + adapter_scale * jnp.dot(
            low[:, rank:], up_value, preferred_element_type=jnp.float32
        )
        value = value.astype(bf16)
        place = jnp.maximum(count - 1 - step, 0)
        cosines, sines = cos_ref[place], sin_ref[place]
        for g in range(KEY_VALUE_HEADS):
            turned = turn(key[:, columns(g, HEAD_SIZE)], cosines, sines)
            keys[at, columns(g, HEAD_SIZE)] = turned.astype(bf16)
            values[at, columns(2 * g, HEAD_SIZE)] = value[:, columns(g, HEAD_SIZE)]
            values[at, columns(2 * g + 1, HEAD_SIZE)] = ones

    def region(first, number):
        for step in range(first, first + number):
            rebuild(step)
        at = pl.ds(first * tokens, number * tokens)
        for g in range(KEY_VALUE_HEADS):
            score = dot_nt(queries[g], keys[at, columns(g, HEAD_SIZE)])
            tiles = [score[:, columns(i, tokens)] for i in range(number)]
            if first == 0:
                row = lax.broadcasted_iota(jnp.int32, (rows, tokens), 0) % tokens
                column = lax.broadcasted_iota(jnp.int32, (rows, tokens), 1)
                tiles = [jnp.where(column <= row, tiles[0], score_masked)]
            else:
                tiles = tiles[:1] + [
                    jnp.where(count > first + i, tiles[i], score_masked)
                    for i in range(1, number)
                ]
            top = functools.reduce(jnp.maximum, tiles)
            top = jnp.max(top, axis=1, keepdims=True) * base2
            top = jnp.broadcast_to(top, (rows, HEAD_SIZE))
            if first:
                old = high[g]
                top = jnp.maximum(old, top)
            weight = [jnp.exp2(t * base2 - top).astype(bf16) for t in tiles]
            blend = jnp.dot(
                jnp.concatenate(weight, axis=1),
                values[at, columns(g, 2 * HEAD_SIZE)],
                preferred_element_type=jnp.float32,
            )
            if first:
                shrink = jnp.exp2(old - top)
                blend += acc[g] * jnp.concatenate([shrink, shrink], axis=1)
            high[g] = top
            acc[g] = blend

    region(*regions[0])
    for first, number in regions[1:]:
        pl.when(count > first)(functools.partial(region, first, number))

    for g in range(KEY_VALUE_HEADS):
        result = (acc[g, :, :HEAD_SIZE] / acc[g, :, HEAD_SIZE:]).astype(bf16)
        for j in range(GROUP_SPLIT):
            out_ref[:, columns(g * GROUP_SPLIT + j, HEAD_SIZE)] = result[columns(j, tokens)]

    for copy in o_parts:
        copy.wait()
    pieces = [o_copy.at[b] for b in range(ROW_BLOCKS)]
    q_head = out_ref.shape[1] // CHUNKS
    d = extra_ref.shape[1] // CHUNKS
    low = jnp.zeros((tokens, rank), jnp.float32)
    for chunk in range(CHUNKS):
        down = factor(pieces, chunk, 0, q_head)
        low += dot_nt(out_ref[:, columns(chunk, q_head)], down)
    low = low.astype(bf16)
    for chunk in range(CHUNKS):
        result = adapter_scale * jnp.dot(
            low, factor(pieces, chunk, q_head, d), preferred_element_type=jnp.float32
        )
        extra_ref[:, columns(chunk, d)] = result.astype(bf16)


def attend(plan, queries, tables, frozen, lows_all, kv_pieces, rest_pieces, at_o, model_width):
    shards, tokens = lows_all.shape[0], lows_all.shape[1]
    key_width = frozen[0].shape[1] // 2
    blocks = tables[0].shape[0]
    rows = GROUP_SPLIT * tokens
    up_width = 2 * key_width // CHUNKS
    o_width = rest_pieces[0].shape[3] - at_o
    bf16, f32 = jnp.bfloat16, jnp.float32

    def copies(width):
        return pltpu.VMEM((ROW_BLOCKS,) + rest_pieces[0].shape[:3] + (width,), bf16)

    apart = [*frozen, *kv_pieces, *rest_pieces]
    return pl.pallas_call(
        functools.partial(attend_kernel, shards, blocks - 1, len(frozen), at_o),
        out_shape=[
            jax.ShapeDtypeStruct((tokens, QUERY_HEADS * HEAD_SIZE), bf16),
            jax.ShapeDtypeStruct((tokens, model_width), bf16),
        ],
        in_specs=smem() + vmem(4) + [pl.BlockSpec(memory_space=pl.ANY)] * len(apart),
        out_specs=vmem(2),
        scratch_shapes=[
            pltpu.VMEM((blocks,) + frozen[0].shape, bf16),
            copies(up_width),
            copies(o_width),
            pltpu.VMEM((blocks * tokens, key_width), bf16),
            pltpu.VMEM((blocks * tokens, 2 * key_width), bf16),
            pltpu.VMEM((KEY_VALUE_HEADS, rows, HEAD_SIZE), f32),
            pltpu.VMEM((KEY_VALUE_HEADS, rows, 2 * HEAD_SIZE), f32),
            pltpu.SemaphoreType.DMA((blocks,)),
            pltpu.SemaphoreType.DMA((2, ROW_BLOCKS)),
        ],
        compiler_params=pltpu.CompilerParams(
            vmem_limit_bytes=(16 + blocks) * 1024 * 1024
        ),
        cost_estimate=pl.CostEstimate(
            flops=2_000_000_000, bytes_accessed=8 << 20, transcendentals=4 << 20
        ),
        name="attend",
    )(plan, queries, *tables, lows_all, *apart)


PLANES = 4
LONG_PLANES = (0, 3)


def plane_pairs(shift, planes):
    return [
        (p * PLANES + q, (p + shift) % PLANES * PLANES + q)
        for p in range(PLANES)
        for q in range(PLANES)
        if (p + shift) % PLANES in planes
    ]


def letters_kernel(kv_width, plan_ref, own_ref, their_ref, *outs):
    plane, own_half, longest = plan_ref[PLANE], plan_ref[OWN_HALF], plan_ref[LONGEST]
    first, second = outs[:-1], outs[-1]
    rest_width = own_ref.shape[2] - kv_width
    for half, ref in ((own_half, own_ref), (1 - own_half, their_ref)):
        for shift, out in enumerate(first, 1):
            to = lax.rem(plane + shift, PLANES)
            is_long = (to == LONG_PLANES[0]) | (to == LONG_PLANES[1])

            @pl.when(is_long)
            def _(out=out, half=half, ref=ref):
                out[half, :, : ref.shape[2]] = ref[longest]

            @pl.when(jnp.logical_not(is_long))
            def _(out=out, half=half, ref=ref):
                for slot in range(ref.shape[0]):
                    out[half, :, columns(slot, kv_width)] = ref[slot, :, :kv_width]

        for slot in range(ref.shape[0]):
            second[half, :, columns(slot, rest_width)] = ref[slot, :, kv_width:]


def letters(plan, own, theirs, kv_width):
    slots, _, width = own.shape
    first = slots * kv_width
    shape = lambda w: jax.ShapeDtypeStruct((2, 16, w), own.dtype)
    return pl.pallas_call(
        functools.partial(letters_kernel, kv_width),
        out_shape=[shape(first)] * (PLANES - 1) + [shape(slots * (width - kv_width))],
        in_specs=smem() + vmem(2),
        out_specs=vmem(PLANES),
        compiler_params=PARAMS,
        name="letters",
    )(plan, own, theirs)


def share_kernel(at, width, rest, plan_ref, own_ref, their_ref, *refs):
    plane, own_half = plan_ref[PLANE], plan_ref[OWN_HALF]
    long_refs, refs = refs[: PLANES - 1], refs[PLANES - 1 :]
    short_refs, outs = (refs[: PLANES - 1], refs[PLANES - 1 :]) if rest else (long_refs, refs)
    is_long = (plane == LONG_PLANES[0]) | (plane == LONG_PLANES[1])
    for other, out in enumerate(outs):
        slot = plan_ref[MATES + other]
        out[plane, own_half] = own_ref[slot, :, at : at + width]
        out[plane, 1 - own_half] = their_ref[slot, :, at : at + width]

        @pl.when(is_long)
        def _(out=out):
            for shift, ref in enumerate(long_refs, 1):
                out[lax.rem(plane - shift + PLANES, PLANES)] = ref[:, :, at : at + width]

        @pl.when(jnp.logical_not(is_long))
        def _(out=out, slot=slot):
            start = pl.multiple_of(slot * width, 128)
            for shift, ref in enumerate(short_refs, 1):
                out[lax.rem(plane - shift + PLANES, PLANES)] = ref[:, :, pl.ds(start, width)]


def share(plan, own, theirs, first, second, at, width):
    rest = second is not None
    arrays = list(first) + (list(second) if rest else [])
    shape = jax.ShapeDtypeStruct((PLANES, 2, 16, width), own.dtype)
    return pl.pallas_call(
        functools.partial(share_kernel, at, width, rest),
        out_shape=[shape] * PLANES,
        in_specs=smem() + vmem(2 + len(arrays)),
        out_specs=vmem(PLANES),
        compiler_params=PARAMS,
        name="share",
    )(plan, own, theirs, *arrays)


MATE_PAIRS = [[(d, d ^ k) for d in range(PLANES * PLANES)] for k in range(PLANES)]


def pairs_kernel(plan_ref, own_ref, one_ref, two_ref, *outs):
    plane, order = plan_ref[PLANE], plan_ref[ORDER]
    for other, out in enumerate(outs):
        last_long = (plane == 1) & (order == other)

        @pl.when(last_long)
        def _(out=out):
            out[0] = one_ref[...]
            out[1] = two_ref[...]

        @pl.when(jnp.logical_not(last_long))
        def _(out=out):
            out[0] = own_ref[...]
            out[1] = one_ref[...]


def pairs(plan, own, one, two):
    shape = jax.ShapeDtypeStruct((2,) + own.shape, own.dtype)
    return pl.pallas_call(
        pairs_kernel,
        out_shape=[shape] * PLANES,
        in_specs=smem() + vmem(3),
        out_specs=vmem(PLANES),
        compiler_params=PARAMS,
        name="pairs",
    )(plan, own, one, two)


def planes_gather(plan, picked, frozen, requests, kv_width):
    swap = [(0, 1), (1, 0)]
    shifts = range(1, PLANES)
    all_planes = range(PLANES)
    short = [p for p in all_planes if p not in LONG_PLANES]
    own, width = picked[requests:], picked.shape[2]
    theirs = lax.ppermute(picked[:requests], "groups", swap)
    one = lax.ppermute(frozen, "ctx", plane_pairs(1, (0, 1, 2)))
    two = lax.ppermute(frozen, "ctx", plane_pairs(2, (1,)))
    *first, second = letters(plan, own, theirs, kv_width)
    first = [lax.ppermute(x, "ctx", plane_pairs(s, all_planes)) for s, x in zip(shifts, first)]
    second = [lax.ppermute(second, "ctx", plane_pairs(s, short)) for s in shifts]

    def to_mates(letters_out):
        mine, *out = letters_out
        return [mine] + [lax.ppermute(x, "ctx", MATE_PAIRS[k + 1]) for k, x in enumerate(out)]

    frozen_list = [frozen] + to_mates(pairs(plan, frozen, one, two))
    first, frozen_list = lax.optimization_barrier((first, frozen_list))
    kv = to_mates(share(plan, own, theirs, first, None, 0, kv_width))
    mine = share(plan, own, theirs, first, second, kv_width, width - kv_width)
    kv, mine = lax.optimization_barrier((kv, mine))
    return kv, to_mates(mine), frozen_list


def body(
    hidden,
    frozen_query,
    frozen_key,
    frozen_value,
    adapter_bank,
    request_shards,
    request_adapter,
    adapter_owner,
):
    shards = lax.axis_size("ctx")
    groups = lax.axis_size("groups")
    tokens, model_width = hidden.shape
    requests = request_shards.shape[0]
    halves = 2 if groups == 2 and shards == PLANES * PLANES else 1
    own_half = lax.axis_index("groups") if halves == 2 else 0
    me = jnp.stack([lax.axis_index("ctx"), own_half]).astype(jnp.int32)
    parts = Parts(model_width, frozen_query.shape[1], frozen_key.shape[1])
    reach = shards // 2

    packed = pack(parts, halves, shards, me, adapter_bank)
    spread = lax.all_to_all(packed, "ctx", split_axis=0, concat_axis=0, tiled=True)
    frozen = jnp.concatenate([frozen_key, frozen_value], axis=1)
    tables = rope_tables(jnp.arange((reach + 1) * tokens, dtype=jnp.int32).reshape(-1, tokens))

    wanted = request_adapter
    if halves == 2:
        theirs = lax.ppermute(request_adapter, "groups", [(0, 1), (1, 0)])
        wanted = jnp.concatenate([theirs, request_adapter])
    plan = make_plan(shards, reach, me, request_shards, wanted, adapter_owner)
    picked = pick(plan, spread, wanted.shape[0])

    if halves == 2:
        kv_pieces, rest_pieces, frozen_list = planes_gather(
            plan, picked, frozen, requests, parts.kv_width
        )
    else:
        frozen_list = [frozen, lax.all_gather(frozen, "ctx")]
        kv_pieces, rest_pieces = [
            [
                lax.all_to_all(p, "ctx", split_axis=0, concat_axis=0, tiled=True)[
                    b : ROW_BLOCKS * CHUNKS : ROW_BLOCKS
                ]
                for b in range(ROW_BLOCKS)
            ]
            for p in route(plan, shards, picked, parts.kv_width)
        ]

    low = lows(plan, shards, hidden, kv_pieces)
    lows_all = lax.all_to_all(low, "ctx", split_axis=0, concat_axis=0, tiled=True)
    queries = make_queries(plan, hidden, frozen_query, tables, rest_pieces)
    at_o = sum(w for _, w in parts.q)
    return tuple(
        attend(
            plan, queries, tables, frozen_list, lows_all, kv_pieces, rest_pieces, at_o, model_width
        )
    )


def solution(mesh):
    return jax.shard_map(
        body,
        mesh=mesh,
        in_specs=(
            P(("groups", "ctx"), None),
            P(("groups", "ctx"), None),
            P(("groups", "ctx"), None),
            P(("groups", "ctx"), None),
            P("ctx", None, None),
            P("groups"),
            P("groups"),
            P(),
        ),
        out_specs=(P(("groups", "ctx"), None), P(("groups", "ctx"), None)),
        check_vma=False,
    )
```

```python
import functools

import jax
import jax.numpy as jnp
from jax import lax
from jax.experimental import pallas as pl
from jax.experimental.pallas import tpu as pltpu
from jax.sharding import PartitionSpec as P

HEAD_SIZE = 128
QUERY_HEADS = 16
KEY_VALUE_HEADS = 4
GROUP_SPLIT = QUERY_HEADS // KEY_VALUE_HEADS

adapter_scale = 0.5
rope_theta = 500000.0
score_masked = -1e30

VMEM_LIMIT = 24 * 1024 * 1024

ROW_BLOCKS = 4
CHUNKS = 8


def rope_tables(positions):
    half_dim = HEAD_SIZE // 2
    frequency = rope_theta ** (-(jnp.arange(half_dim, dtype=jnp.float32) * 2.0) / HEAD_SIZE)
    angles = positions.astype(jnp.float32)[..., None] * frequency
    cosines = jnp.cos(angles)
    sines = jnp.sin(angles)
    return (jnp.concatenate([cosines, cosines], -1), jnp.concatenate([-sines, sines], -1))


class Parts:
    def __init__(self, model_width, query_width, key_width):
        d, q, k = model_width, query_width, key_width
        up = 3 * d
        self.kv = ((d, d // CHUNKS), (2 * d, d // CHUNKS), (up + q, 2 * k // CHUNKS))
        self.q = ((0, d // CHUNKS), (up, q // CHUNKS))
        self.o = ((up + q + 2 * k, q // CHUNKS), (up + 2 * q + 2 * k, d // CHUNKS))
        self.all = self.kv + self.q + self.o
        self.widths = tuple(sum(w for _, w in part) for part in (self.kv, self.q, self.o))


def vmem(count=1):
    return [pl.BlockSpec(memory_space=pltpu.VMEM)] * count


def smem(count=1):
    return [pl.BlockSpec(memory_space=pltpu.SMEM)] * count


PARAMS = pltpu.CompilerParams(vmem_limit_bytes=VMEM_LIMIT)


OWN_INDEX, OWN_HALF, PLANE, ORDER, COUNT, ENTRY = 0, 1, 2, 3, 4, 8


def layout(lengths_ref, which, shards):
    starts, start, length = [jnp.int32(0)], jnp.int32(0), lengths_ref[which, 0]
    for r in range(1, lengths_ref.shape[1]):
        starts.append(starts[-1] + lengths_ref[which, r - 1])
        longer = lengths_ref[which, r] > length
        start = jnp.where(longer, starts[-1], start)
        length = jnp.where(longer, lengths_ref[which, r], length)
    return starts, start + lax.div(length, 2)


def plan_kernel(shards, reach, me_ref, lengths_ref, adapters_ref, owner_ref, out_ref):
    own_index, own_half = me_ref[0], me_ref[1]
    starts, offset = layout(lengths_ref, 0, shards)
    own_packed = lax.rem(own_index + offset, shards)
    first = jnp.int32(0)
    for start in starts[1:]:
        first = jnp.where(start <= own_packed, start, first)
    out_ref[OWN_INDEX] = own_index
    out_ref[OWN_HALF] = own_half
    out_ref[PLANE] = lax.div(own_index, PLANES)
    out_ref[ORDER] = lax.rem(own_index, PLANES)
    out_ref[COUNT] = jnp.minimum(own_packed - first, reach) + 1
    for which in range(lengths_ref.shape[0]):
        starts, offset = layout(lengths_ref, which, shards)
        entries = [owner_ref[adapters_ref[which, r]] for r in range(len(starts))]
        at = ENTRY + shards * (own_half if which == 0 else 1 - own_half)
        for shard in range(shards):
            packed = lax.rem(shard + offset, shards)
            entry = entries[0]
            for start, later in zip(starts[1:], entries[1:]):
                entry = jnp.where(start <= packed, later, entry)
            out_ref[at + shard] = entry


def make_plan(shards, reach, me, lengths, adapters, owner):
    return pl.pallas_call(
        functools.partial(plan_kernel, shards, reach),
        out_shape=jax.ShapeDtypeStruct((ENTRY + lengths.shape[0] * shards,), jnp.int32),
        in_specs=smem(4),
        out_specs=smem()[0],
        name="plan",
    )(me, lengths, adapters, owner)


def pack_kernel(parts, halves, x_ref, bank_ref, out):
    own_half = x_ref[1]
    for block in range(out.shape[0]):
        piece = block % (ROW_BLOCKS * CHUNKS // halves)
        rows = pl.ds((piece % ROW_BLOCKS) * 16, 16)
        chunk = (piece // ROW_BLOCKS) * halves + own_half
        at = 0
        for first, width in parts.all:
            start = pl.multiple_of(first + chunk * width, 128)
            out[block, :, at : at + width] = bank_ref[0, rows, pl.ds(start, width)]
            at += width


def pack(parts, halves, shards, me, bank):
    width = sum(parts.widths)
    return pl.pallas_call(
        functools.partial(pack_kernel, parts, halves),
        out_shape=jax.ShapeDtypeStruct((shards, 16, width), bank.dtype),
        in_specs=smem() + vmem(),
        out_specs=vmem()[0],
        compiler_params=PARAMS,
        name="pack",
    )(me, bank)


def route_kernel(plan_ref, spread_ref, *outs):
    for dest in range(outs[0].shape[0]):
        entry = plan_ref[ENTRY + dest]
        at = 0
        for out in outs:
            out[dest] = spread_ref[entry, :, at : at + out.shape[2]]
            at += out.shape[2]


def route(plan, spread, widths):
    dests = plan.shape[0] - ENTRY
    return pl.pallas_call(
        route_kernel,
        out_shape=[jax.ShapeDtypeStruct((dests, 16, w), spread.dtype) for w in widths],
        in_specs=smem() + vmem(),
        out_specs=vmem(len(widths)),
        compiler_params=PARAMS,
        name="route",
    )(plan, spread)


def factor(piece_ref, chunk, at, width):
    halves = piece_ref.shape[0]
    place = chunk // halves * ROW_BLOCKS
    rows = piece_ref[chunk % halves, place : place + ROW_BLOCKS, :, at : at + width]
    return rows.reshape(ROW_BLOCKS * 16, width)


def columns(chunk, width):
    return slice(chunk * width, (chunk + 1) * width)


def dot_nt(a, b):
    return lax.dot_general(a, b, (((1,), (1,)), ((), ())), preferred_element_type=jnp.float32)


def turn(x, cosines, sines):
    return x * cosines + pltpu.roll(x, HEAD_SIZE // 2, 1) * sines


def lows_kernel(hidden_ref, piece_ref, out_ref):
    d = hidden_ref.shape[1] // CHUNKS
    low = jnp.zeros((hidden_ref.shape[0], 2 * ROW_BLOCKS * 16), jnp.float32)
    for chunk in range(CHUNKS):
        down = jnp.concatenate(
            [factor(piece_ref, chunk, 0, d), factor(piece_ref, chunk, d, d)], axis=0
        )
        low += dot_nt(hidden_ref[:, columns(chunk, d)], down)
    low = low.astype(jnp.bfloat16)
    for shard in range(out_ref.shape[0]):
        out_ref[shard] = low


def lows(shards, hidden, pieces):
    return pl.pallas_call(
        lows_kernel,
        out_shape=jax.ShapeDtypeStruct(
            (shards, hidden.shape[0], 2 * ROW_BLOCKS * 16), jnp.bfloat16
        ),
        in_specs=vmem(2),
        out_specs=vmem()[0],
        compiler_params=PARAMS,
        cost_estimate=pl.CostEstimate(
            flops=150_000_000, bytes_accessed=3 << 20, transcendentals=0
        ),
        name="lows",
    )(hidden, pieces)


def query_kernel(plan_ref, hidden_ref, query_ref, cos_ref, sin_ref, piece_ref, out_ref):
    tokens = query_ref.shape[0]
    d = hidden_ref.shape[1] // CHUNKS
    width = query_ref.shape[1] // CHUNKS
    low = jnp.zeros((tokens, ROW_BLOCKS * 16), jnp.float32)
    for chunk in range(CHUNKS):
        low += dot_nt(hidden_ref[:, columns(chunk, d)], factor(piece_ref, chunk, 0, d))
    low = low.astype(jnp.bfloat16)
    own = plan_ref[COUNT] - 1
    cosines, sines = cos_ref[own], sin_ref[own]
    for chunk in range(CHUNKS):
        up = factor(piece_ref, chunk, d, width)
        update = jnp.dot(low, up, preferred_element_type=jnp.float32)
        result = query_ref[:, columns(chunk, width)].astype(jnp.float32) + adapter_scale * update
        for part in range(width // HEAD_SIZE):
            head = chunk * (width // HEAD_SIZE) + part
            turned = turn(result[:, columns(part, HEAD_SIZE)], cosines, sines)
            out_ref[head // GROUP_SPLIT, pl.ds((head % GROUP_SPLIT) * tokens, tokens)] = (
                turned.astype(jnp.bfloat16)
            )


def make_queries(plan, hidden, query, tables, pieces):
    tokens = hidden.shape[0]
    return pl.pallas_call(
        query_kernel,
        out_shape=jax.ShapeDtypeStruct(
            (KEY_VALUE_HEADS, GROUP_SPLIT * tokens, HEAD_SIZE), jnp.bfloat16
        ),
        in_specs=smem() + vmem(5),
        out_specs=vmem()[0],
        compiler_params=PARAMS,
        cost_estimate=pl.CostEstimate(
            flops=100_000_000, bytes_accessed=3 << 20, transcendentals=0
        ),
        name="queries",
    )(plan, hidden, query, *tables, pieces)


REGION = 4


def attend_kernel(
    shards, reach, sources, plan_ref, queries, cos_ref, sin_ref, lows_ref, kv_ref, *refs
):
    frozen_refs, refs = refs[:sources], refs[sources:]
    out_ref, frozen, up_copy, keys, values, high, acc, sem, part_sem = refs
    own_index, order, count = plan_ref[OWN_INDEX], plan_ref[ORDER], plan_ref[COUNT]
    tokens = out_ref.shape[0]
    rank = ROW_BLOCKS * 16
    rows = GROUP_SPLIT * tokens
    key_width = KEY_VALUE_HEADS * HEAD_SIZE
    bf16 = jnp.bfloat16
    base2 = 1.4426950408889634 / (HEAD_SIZE**0.5)
    up_width = up_copy.shape[3]
    up_part = pltpu.make_async_copy(
        kv_ref.at[:, pl.ds(0, up_copy.shape[1]), :, pl.ds(kv_ref.shape[3] - up_width, up_width)],
        up_copy,
        part_sem,
    )

    def source_of(step):
        return lax.rem(own_index - step + shards, shards)

    def land(step, source):
        return pltpu.make_async_copy(source, frozen.at[step], sem.at[step])

    up_part.start()
    land(0, frozen_refs[0]).start()
    regions = [(0, 1)] + [
        (first, min(REGION, reach + 1 - first)) for first in range(1, reach + 1, REGION)
    ]
    for first, number in regions[1:]:

        @pl.when(count > first)
        def _(first=first, number=number):
            for step in range(first, first + number):
                source = source_of(step)
                if sources == 2:
                    land(step, frozen_refs[1].at[source]).start()
                    continue
                plane = plan_ref[PLANE]
                last_long = (plane == 1) & (order == 0)
                far = lax.div(source, PLANES) != jnp.where(last_long, 0, plane)
                mate = jnp.bitwise_xor(lax.rem(source, PLANES), order)
                for other in range(PLANES):
                    pl.when(mate == other)(
                        land(step, frozen_refs[1 + other].at[far.astype(jnp.int32)]).start
                    )

    up_part.wait()
    up = [factor(up_copy, chunk, 0, up_width) for chunk in range(CHUNKS)]
    up_key = jnp.concatenate(up[: CHUNKS // 2], axis=1)
    up_value = jnp.concatenate(up[CHUNKS // 2 :], axis=1)
    ones = jnp.ones((tokens, HEAD_SIZE), bf16)

    def rebuild(step):
        at = pl.ds(step * tokens, tokens)
        low = lows_ref[source_of(step)]
        land(step, frozen_refs[0]).wait()
        key = frozen[step, :, :key_width].astype(jnp.float32) + adapter_scale * jnp.dot(
            low[:, :rank], up_key, preferred_element_type=jnp.float32
        )
        value = frozen[step, :, key_width:].astype(jnp.float32) + adapter_scale * jnp.dot(
            low[:, rank:], up_value, preferred_element_type=jnp.float32
        )
        value = value.astype(bf16)
        place = jnp.maximum(count - 1 - step, 0)
        cosines, sines = cos_ref[place], sin_ref[place]
        for g in range(KEY_VALUE_HEADS):
            turned = turn(key[:, columns(g, HEAD_SIZE)], cosines, sines)
            keys[at, columns(g, HEAD_SIZE)] = turned.astype(bf16)
            values[at, columns(2 * g, HEAD_SIZE)] = value[:, columns(g, HEAD_SIZE)]
            values[at, columns(2 * g + 1, HEAD_SIZE)] = ones

    def region(first, number):
        for step in range(first, first + number):
            rebuild(step)
        at = pl.ds(first * tokens, number * tokens)
        for g in range(KEY_VALUE_HEADS):
            score = dot_nt(queries[g], keys[at, columns(g, HEAD_SIZE)])
            tiles = [score[:, columns(i, tokens)] for i in range(number)]
            if first == 0:
                row = lax.broadcasted_iota(jnp.int32, (rows, tokens), 0) % tokens
                column = lax.broadcasted_iota(jnp.int32, (rows, tokens), 1)
                tiles = [jnp.where(column <= row, tiles[0], score_masked)]
            else:
                tiles = tiles[:1] + [
                    jnp.where(count > first + i, tiles[i], score_masked)
                    for i in range(1, number)
                ]
            top = functools.reduce(jnp.maximum, tiles)
            top = jnp.max(top, axis=1, keepdims=True) * base2
            top = jnp.broadcast_to(top, (rows, HEAD_SIZE))
            if first:
                old = high[g]
                top = jnp.maximum(old, top)
            weight = [jnp.exp2(t * base2 - top).astype(bf16) for t in tiles]
            blend = jnp.dot(
                jnp.concatenate(weight, axis=1),
                values[at, columns(g, 2 * HEAD_SIZE)],
                preferred_element_type=jnp.float32,
            )
            if first:
                shrink = jnp.exp2(old - top)
                blend += acc[g] * jnp.concatenate([shrink, shrink], axis=1)
            high[g] = top
            acc[g] = blend

    region(*regions[0])
    for first, number in regions[1:]:
        pl.when(count > first)(functools.partial(region, first, number))

    for g in range(KEY_VALUE_HEADS):
        result = (acc[g, :, :HEAD_SIZE] / acc[g, :, HEAD_SIZE:]).astype(bf16)
        for j in range(GROUP_SPLIT):
            out_ref[:, columns(g * GROUP_SPLIT + j, HEAD_SIZE)] = result[columns(j, tokens)]


def attend(plan, queries, tables, frozen, lows_all, kv_pieces):
    shards, tokens = lows_all.shape[0], lows_all.shape[1]
    key_width = frozen[0].shape[1] // 2
    blocks = tables[0].shape[0]
    rows = GROUP_SPLIT * tokens
    up_width = 2 * key_width // CHUNKS
    halves = kv_pieces.shape[0]
    bf16, f32 = jnp.bfloat16, jnp.float32
    limit = VMEM_LIMIT if blocks < 16 else 2 * VMEM_LIMIT
    return pl.pallas_call(
        functools.partial(attend_kernel, shards, blocks - 1, len(frozen)),
        out_shape=jax.ShapeDtypeStruct((tokens, QUERY_HEADS * HEAD_SIZE), bf16),
        in_specs=smem() + vmem(4) + [pl.BlockSpec(memory_space=pl.ANY)] * (1 + len(frozen)),
        out_specs=vmem()[0],
        scratch_shapes=[
            pltpu.VMEM((blocks,) + frozen[0].shape, bf16),
            pltpu.VMEM((halves, ROW_BLOCKS * CHUNKS // halves, 16, up_width), bf16),
            pltpu.VMEM((blocks * tokens, key_width), bf16),
            pltpu.VMEM((blocks * tokens, 2 * key_width), bf16),
            pltpu.VMEM((KEY_VALUE_HEADS, rows, HEAD_SIZE), f32),
            pltpu.VMEM((KEY_VALUE_HEADS, rows, 2 * HEAD_SIZE), f32),
            pltpu.SemaphoreType.DMA((blocks,)),
            pltpu.SemaphoreType.DMA,
        ],
        compiler_params=pltpu.CompilerParams(vmem_limit_bytes=limit),
        cost_estimate=pl.CostEstimate(
            flops=2_000_000_000, bytes_accessed=8 << 20, transcendentals=4 << 20
        ),
        name="attend",
    )(plan, queries, *tables, lows_all, kv_pieces, *frozen)


def output_kernel(attended_ref, piece_ref, out_ref):
    q_head = attended_ref.shape[1] // CHUNKS
    d = out_ref.shape[1] // CHUNKS
    low = jnp.zeros((attended_ref.shape[0], ROW_BLOCKS * 16), jnp.float32)
    for chunk in range(CHUNKS):
        down = factor(piece_ref, chunk, 0, q_head)
        low += dot_nt(attended_ref[:, columns(chunk, q_head)], down)
    low = low.astype(jnp.bfloat16)
    for chunk in range(CHUNKS):
        result = adapter_scale * jnp.dot(
            low, factor(piece_ref, chunk, q_head, d), preferred_element_type=jnp.float32
        )
        out_ref[:, columns(chunk, d)] = result.astype(jnp.bfloat16)


def output_adapter(attended, pieces, model_width):
    return pl.pallas_call(
        output_kernel,
        out_shape=jax.ShapeDtypeStruct((attended.shape[0], model_width), jnp.bfloat16),
        in_specs=vmem(2),
        out_specs=vmem()[0],
        compiler_params=PARAMS,
        cost_estimate=pl.CostEstimate(
            flops=100_000_000, bytes_accessed=3 << 20, transcendentals=0
        ),
        name="output",
    )(attended, pieces)


PLANES = 4


def plane_pairs(shift, planes):
    return [
        (p * PLANES + q, (p + shift) % PLANES * PLANES + q)
        for p in range(PLANES)
        for q in range(PLANES)
        if (p + shift) % PLANES in planes
    ]


MATE_PAIRS = [[(d, d ^ k) for d in range(PLANES * PLANES)] for k in range(PLANES)]


def pairs_kernel(plan_ref, own_ref, one_ref, two_ref, *outs):
    plane, order = plan_ref[PLANE], plan_ref[ORDER]
    for other, out in enumerate(outs):
        last_long = (plane == 1) & (order == other)

        @pl.when(last_long)
        def _(out=out):
            out[0] = one_ref[...]
            out[1] = two_ref[...]

        @pl.when(jnp.logical_not(last_long))
        def _(out=out):
            out[0] = own_ref[...]
            out[1] = one_ref[...]


def pairs(plan, own, one, two):
    shape = jax.ShapeDtypeStruct((2,) + own.shape, own.dtype)
    return pl.pallas_call(
        pairs_kernel,
        out_shape=[shape] * PLANES,
        in_specs=smem() + vmem(3),
        out_specs=vmem(PLANES),
        compiler_params=PARAMS,
        name="pairs",
    )(plan, own, one, two)


def earlier_frozen(plan, frozen):
    one = lax.ppermute(frozen, "ctx", plane_pairs(1, (0, 1, 2)))
    two = lax.ppermute(one, "ctx", plane_pairs(1, (1,)))
    mine, *out = pairs(plan, frozen, one, two)
    return [mine] + [lax.ppermute(x, "ctx", MATE_PAIRS[k + 1]) for k, x in enumerate(out)]


def body(
    hidden,
    frozen_query,
    frozen_key,
    frozen_value,
    adapter_bank,
    request_shards,
    request_adapter,
    adapter_owner,
):
    shards = lax.axis_size("ctx")
    groups = lax.axis_size("groups")
    tokens, model_width = hidden.shape
    halves = 2 if groups == 2 and shards == PLANES * PLANES else 1
    own_half = lax.axis_index("groups") if halves == 2 else 0
    me = jnp.stack([lax.axis_index("ctx"), own_half]).astype(jnp.int32)
    parts = Parts(model_width, frozen_query.shape[1], frozen_key.shape[1])
    reach = shards // 2

    packed = pack(parts, halves, shards, me, adapter_bank)
    spread = lax.all_to_all(packed, "ctx", split_axis=0, concat_axis=0, tiled=True)

    tables = rope_tables(jnp.arange((reach + 1) * tokens, dtype=jnp.int32).reshape(-1, tokens))
    requests = jnp.stack([request_shards, request_adapter])[:, None]
    if halves == 2:
        theirs = lax.ppermute(requests, "groups", [(0, 1), (1, 0)])
        requests = jnp.concatenate([requests, theirs], axis=1)
    plan = make_plan(shards, reach, me, requests[0], requests[1], adapter_owner)
    frozen = jnp.concatenate([frozen_key, frozen_value], axis=1)
    if halves == 2:
        frozen_list = [frozen] + earlier_frozen(plan, frozen)
    else:
        frozen_list = [frozen, lax.all_gather(frozen, "ctx")]

    def collect(pieces):
        axes = ("groups", "ctx") if halves == 2 else "ctx"
        pieces = lax.all_to_all(pieces, axes, split_axis=0, concat_axis=0, tiled=True)
        return pieces.reshape((halves, shards) + pieces.shape[1:])[:, : ROW_BLOCKS * CHUNKS]

    kv_pieces, q_pieces, o_pieces = route(plan, spread, parts.widths)
    kv_pieces = collect(kv_pieces)
    kv_pieces, q_pieces = lax.optimization_barrier((kv_pieces, q_pieces))
    q_pieces = collect(q_pieces)

    low = lows(shards, hidden, kv_pieces)
    lows_all = lax.all_to_all(low, "ctx", split_axis=0, concat_axis=0, tiled=True)
    lows_all, o_pieces = lax.optimization_barrier((lows_all, o_pieces))
    o_pieces = collect(o_pieces)
    queries = make_queries(plan, hidden, frozen_query, tables, q_pieces)
    attended = attend(plan, queries, tables, frozen_list, lows_all, kv_pieces)
    return attended, output_adapter(attended, o_pieces, model_width)


def solution(mesh):
    return jax.shard_map(
        body,
        mesh=mesh,
        in_specs=(
            P(("groups", "ctx"), None),
            P(("groups", "ctx"), None),
            P(("groups", "ctx"), None),
            P(("groups", "ctx"), None),
            P("ctx", None, None),
            P("groups"),
            P("groups"),
            P(),
        ),
        out_specs=(P(("groups", "ctx"), None), P(("groups", "ctx"), None)),
        check_vma=False,
    )
```

```python
import functools

import jax
import jax.numpy as jnp
from jax import lax
from jax.experimental import pallas as pl
from jax.experimental.pallas import tpu as pltpu
from jax.sharding import PartitionSpec as P

HEAD_SIZE = 128
QUERY_HEADS = 16
KEY_VALUE_HEADS = 4
GROUP_SPLIT = QUERY_HEADS // KEY_VALUE_HEADS

adapter_scale = 0.5
rope_theta = 500000.0
score_masked = -1e30

VMEM_LIMIT = 24 * 1024 * 1024

ROW_BLOCKS = 4
CHUNKS = 8


def rope_tables(positions):
    half_dim = HEAD_SIZE // 2
    frequency = rope_theta ** (-(jnp.arange(half_dim, dtype=jnp.float32) * 2.0) / HEAD_SIZE)
    angles = positions.astype(jnp.float32)[..., None] * frequency
    cosines = jnp.cos(angles)
    sines = jnp.sin(angles)
    return (jnp.concatenate([cosines, cosines], -1), jnp.concatenate([-sines, sines], -1))


class Parts:
    def __init__(self, model_width, query_width, key_width):
        d, q, k = model_width, query_width, key_width
        up = 3 * d
        self.kv = ((d, d // CHUNKS), (2 * d, d // CHUNKS), (up + q, 2 * k // CHUNKS))
        self.q = ((0, d // CHUNKS), (up, q // CHUNKS))
        self.o = ((up + q + 2 * k, q // CHUNKS), (up + 2 * q + 2 * k, d // CHUNKS))
        self.all = self.kv + self.q + self.o
        self.widths = tuple(sum(w for _, w in part) for part in (self.kv, self.q, self.o))


def vmem(count=1):
    return [pl.BlockSpec(memory_space=pltpu.VMEM)] * count


def smem(count=1):
    return [pl.BlockSpec(memory_space=pltpu.SMEM)] * count


PARAMS = pltpu.CompilerParams(vmem_limit_bytes=VMEM_LIMIT)


OWN_INDEX, OWN_HALF, PLANE, ORDER, COUNT, ENTRY = 0, 1, 2, 3, 4, 8


def layout(lengths_ref, which, shards):
    starts, start, length = [jnp.int32(0)], jnp.int32(0), lengths_ref[which, 0]
    for r in range(1, lengths_ref.shape[1]):
        starts.append(starts[-1] + lengths_ref[which, r - 1])
        longer = lengths_ref[which, r] > length
        start = jnp.where(longer, starts[-1], start)
        length = jnp.where(longer, lengths_ref[which, r], length)
    return starts, start + lax.div(length, 2)


def plan_kernel(shards, reach, me_ref, lengths_ref, adapters_ref, owner_ref, out_ref):
    own_index, own_half = me_ref[0], me_ref[1]
    starts, offset = layout(lengths_ref, 0, shards)
    own_packed = lax.rem(own_index + offset, shards)
    first = jnp.int32(0)
    for start in starts[1:]:
        first = jnp.where(start <= own_packed, start, first)
    out_ref[OWN_INDEX] = own_index
    out_ref[OWN_HALF] = own_half
    out_ref[PLANE] = lax.div(own_index, PLANES)
    out_ref[ORDER] = lax.rem(own_index, PLANES)
    out_ref[COUNT] = jnp.minimum(own_packed - first, reach) + 1
    for which in range(lengths_ref.shape[0]):
        starts, offset = layout(lengths_ref, which, shards)
        entries = [owner_ref[adapters_ref[which, r]] for r in range(len(starts))]
        at = ENTRY + shards * (own_half if which == 0 else 1 - own_half)
        for shard in range(shards):
            packed = lax.rem(shard + offset, shards)
            entry = entries[0]
            for start, later in zip(starts[1:], entries[1:]):
                entry = jnp.where(start <= packed, later, entry)
            out_ref[at + shard] = entry


def make_plan(shards, reach, me, lengths, adapters, owner):
    return pl.pallas_call(
        functools.partial(plan_kernel, shards, reach),
        out_shape=jax.ShapeDtypeStruct((ENTRY + lengths.shape[0] * shards,), jnp.int32),
        in_specs=smem(4),
        out_specs=smem()[0],
        name="plan",
    )(me, lengths, adapters, owner)


def pack_kernel(parts, halves, x_ref, bank_ref, out):
    own_half = x_ref[1]
    for block in range(out.shape[0]):
        piece = block % (ROW_BLOCKS * CHUNKS // halves)
        rows = pl.ds((piece % ROW_BLOCKS) * 16, 16)
        chunk = (piece // ROW_BLOCKS) * halves + own_half
        at = 0
        for first, width in parts.all:
            start = pl.multiple_of(first + chunk * width, 128)
            out[block, :, at : at + width] = bank_ref[0, rows, pl.ds(start, width)]
            at += width


def pack(parts, halves, shards, me, bank):
    width = sum(parts.widths)
    return pl.pallas_call(
        functools.partial(pack_kernel, parts, halves),
        out_shape=jax.ShapeDtypeStruct((shards, 16, width), bank.dtype),
        in_specs=smem() + vmem(),
        out_specs=vmem()[0],
        compiler_params=PARAMS,
        name="pack",
    )(me, bank)


def route_kernel(plan_ref, spread_ref, *outs):
    for dest in range(outs[0].shape[0]):
        entry = plan_ref[ENTRY + dest]
        at = 0
        for out in outs:
            out[dest] = spread_ref[entry, :, at : at + out.shape[2]]
            at += out.shape[2]


def route(plan, spread, widths):
    dests = plan.shape[0] - ENTRY
    return pl.pallas_call(
        route_kernel,
        out_shape=[jax.ShapeDtypeStruct((dests, 16, w), spread.dtype) for w in widths],
        in_specs=smem() + vmem(),
        out_specs=vmem(len(widths)),
        compiler_params=PARAMS,
        name="route",
    )(plan, spread)


def factor(piece_ref, chunk, at, width):
    halves = piece_ref.shape[0]
    place = chunk // halves * ROW_BLOCKS
    rows = piece_ref[chunk % halves, place : place + ROW_BLOCKS, :, at : at + width]
    return rows.reshape(ROW_BLOCKS * 16, width)


def columns(chunk, width):
    return slice(chunk * width, (chunk + 1) * width)


def dot_nt(a, b):
    return lax.dot_general(a, b, (((1,), (1,)), ((), ())), preferred_element_type=jnp.float32)


def turn(x, cosines, sines):
    return x * cosines + pltpu.roll(x, HEAD_SIZE // 2, 1) * sines


def lows_kernel(hidden_ref, piece_ref, out_ref):
    d = hidden_ref.shape[1] // CHUNKS
    low = jnp.zeros((hidden_ref.shape[0], 2 * ROW_BLOCKS * 16), jnp.float32)
    for chunk in range(CHUNKS):
        down = jnp.concatenate(
            [factor(piece_ref, chunk, 0, d), factor(piece_ref, chunk, d, d)], axis=0
        )
        low += dot_nt(hidden_ref[:, columns(chunk, d)], down)
    low = low.astype(jnp.bfloat16)
    for shard in range(out_ref.shape[0]):
        out_ref[shard] = low


def lows(shards, hidden, pieces):
    return pl.pallas_call(
        lows_kernel,
        out_shape=jax.ShapeDtypeStruct(
            (shards, hidden.shape[0], 2 * ROW_BLOCKS * 16), jnp.bfloat16
        ),
        in_specs=vmem(2),
        out_specs=vmem()[0],
        compiler_params=PARAMS,
        cost_estimate=pl.CostEstimate(
            flops=150_000_000, bytes_accessed=3 << 20, transcendentals=0
        ),
        name="lows",
    )(hidden, pieces)


def query_kernel(at, plan_ref, hidden_ref, query_ref, cos_ref, sin_ref, piece_ref, out_ref):
    tokens = query_ref.shape[0]
    d = hidden_ref.shape[1] // CHUNKS
    width = query_ref.shape[1] // CHUNKS
    low = jnp.zeros((tokens, ROW_BLOCKS * 16), jnp.float32)
    for chunk in range(CHUNKS):
        low += dot_nt(hidden_ref[:, columns(chunk, d)], factor(piece_ref, chunk, at, d))
    low = low.astype(jnp.bfloat16)
    own = plan_ref[COUNT] - 1
    cosines, sines = cos_ref[own], sin_ref[own]
    for chunk in range(CHUNKS):
        up = factor(piece_ref, chunk, at + d, width)
        update = jnp.dot(low, up, preferred_element_type=jnp.float32)
        result = query_ref[:, columns(chunk, width)].astype(jnp.float32) + adapter_scale * update
        for part in range(width // HEAD_SIZE):
            head = chunk * (width // HEAD_SIZE) + part
            turned = turn(result[:, columns(part, HEAD_SIZE)], cosines, sines)
            out_ref[head // GROUP_SPLIT, pl.ds((head % GROUP_SPLIT) * tokens, tokens)] = (
                turned.astype(jnp.bfloat16)
            )


def make_queries(plan, hidden, query, tables, pieces, at):
    tokens = hidden.shape[0]
    return pl.pallas_call(
        functools.partial(query_kernel, at),
        out_shape=jax.ShapeDtypeStruct(
            (KEY_VALUE_HEADS, GROUP_SPLIT * tokens, HEAD_SIZE), jnp.bfloat16
        ),
        in_specs=smem() + vmem(5),
        out_specs=vmem()[0],
        compiler_params=PARAMS,
        cost_estimate=pl.CostEstimate(
            flops=100_000_000, bytes_accessed=3 << 20, transcendentals=0
        ),
        name="queries",
    )(plan, hidden, query, *tables, pieces)


REGION = 4


def attend_kernel(
    shards, reach, sources, kv_width, plan_ref, queries, cos_ref, sin_ref, lows_ref, kv_ref, *refs
):
    frozen_refs, refs = refs[:sources], refs[sources:]
    out_ref, frozen, up_copy, keys, values, high, acc, sem, part_sem = refs
    own_index, order, count = plan_ref[OWN_INDEX], plan_ref[ORDER], plan_ref[COUNT]
    tokens = out_ref.shape[0]
    rank = ROW_BLOCKS * 16
    rows = GROUP_SPLIT * tokens
    key_width = KEY_VALUE_HEADS * HEAD_SIZE
    bf16 = jnp.bfloat16
    base2 = 1.4426950408889634 / (HEAD_SIZE**0.5)
    up_width = up_copy.shape[3]
    up_part = pltpu.make_async_copy(
        kv_ref.at[:, pl.ds(0, up_copy.shape[1]), :, pl.ds(kv_width - up_width, up_width)],
        up_copy,
        part_sem,
    )

    def source_of(step):
        return lax.rem(own_index - step + shards, shards)

    def land(step, source):
        return pltpu.make_async_copy(source, frozen.at[step], sem.at[step])

    up_part.start()
    land(0, frozen_refs[0]).start()
    regions = [(0, 1)] + [
        (first, min(REGION, reach + 1 - first)) for first in range(1, reach + 1, REGION)
    ]
    for first, number in regions[1:]:

        @pl.when(count > first)
        def _(first=first, number=number):
            for step in range(first, first + number):
                source = source_of(step)
                if sources == 2:
                    land(step, frozen_refs[1].at[source]).start()
                    continue
                plane = plan_ref[PLANE]
                last_long = (plane == 1) & (order == 0)
                far = lax.div(source, PLANES) != jnp.where(last_long, 0, plane)
                mate = jnp.bitwise_xor(lax.rem(source, PLANES), order)
                for other in range(PLANES):
                    pl.when(mate == other)(
                        land(step, frozen_refs[1 + other].at[far.astype(jnp.int32)]).start
                    )

    up_part.wait()
    up = [factor(up_copy, chunk, 0, up_width) for chunk in range(CHUNKS)]
    up_key = jnp.concatenate(up[: CHUNKS // 2], axis=1)
    up_value = jnp.concatenate(up[CHUNKS // 2 :], axis=1)
    ones = jnp.ones((tokens, HEAD_SIZE), bf16)

    def rebuild(step):
        at = pl.ds(step * tokens, tokens)
        low = lows_ref[source_of(step)]
        land(step, frozen_refs[0]).wait()
        key = frozen[step, :, :key_width].astype(jnp.float32) + adapter_scale * jnp.dot(
            low[:, :rank], up_key, preferred_element_type=jnp.float32
        )
        value = frozen[step, :, key_width:].astype(jnp.float32) + adapter_scale * jnp.dot(
            low[:, rank:], up_value, preferred_element_type=jnp.float32
        )
        value = value.astype(bf16)
        place = jnp.maximum(count - 1 - step, 0)
        cosines, sines = cos_ref[place], sin_ref[place]
        for g in range(KEY_VALUE_HEADS):
            turned = turn(key[:, columns(g, HEAD_SIZE)], cosines, sines)
            keys[at, columns(g, HEAD_SIZE)] = turned.astype(bf16)
            values[at, columns(2 * g, HEAD_SIZE)] = value[:, columns(g, HEAD_SIZE)]
            values[at, columns(2 * g + 1, HEAD_SIZE)] = ones

    def region(first, number):
        for step in range(first, first + number):
            rebuild(step)
        at = pl.ds(first * tokens, number * tokens)
        for g in range(KEY_VALUE_HEADS):
            score = dot_nt(queries[g], keys[at, columns(g, HEAD_SIZE)])
            tiles = [score[:, columns(i, tokens)] for i in range(number)]
            if first == 0:
                row = lax.broadcasted_iota(jnp.int32, (rows, tokens), 0) % tokens
                column = lax.broadcasted_iota(jnp.int32, (rows, tokens), 1)
                tiles = [jnp.where(column <= row, tiles[0], score_masked)]
            else:
                tiles = tiles[:1] + [
                    jnp.where(count > first + i, tiles[i], score_masked)
                    for i in range(1, number)
                ]
            top = functools.reduce(jnp.maximum, tiles)
            top = jnp.max(top, axis=1, keepdims=True) * base2
            top = jnp.broadcast_to(top, (rows, HEAD_SIZE))
            if first:
                old = high[g]
                top = jnp.maximum(old, top)
            weight = [jnp.exp2(t * base2 - top).astype(bf16) for t in tiles]
            blend = jnp.dot(
                jnp.concatenate(weight, axis=1),
                values[at, columns(g, 2 * HEAD_SIZE)],
                preferred_element_type=jnp.float32,
            )
            if first:
                shrink = jnp.exp2(old - top)
                blend += acc[g] * jnp.concatenate([shrink, shrink], axis=1)
            high[g] = top
            acc[g] = blend

    region(*regions[0])
    for first, number in regions[1:]:
        pl.when(count > first)(functools.partial(region, first, number))

    for g in range(KEY_VALUE_HEADS):
        result = (acc[g, :, :HEAD_SIZE] / acc[g, :, HEAD_SIZE:]).astype(bf16)
        for j in range(GROUP_SPLIT):
            out_ref[:, columns(g * GROUP_SPLIT + j, HEAD_SIZE)] = result[columns(j, tokens)]


def attend(plan, queries, tables, frozen, lows_all, pieces, kv_width):
    shards, tokens = lows_all.shape[0], lows_all.shape[1]
    key_width = frozen[0].shape[1] // 2
    blocks = tables[0].shape[0]
    rows = GROUP_SPLIT * tokens
    up_width = 2 * key_width // CHUNKS
    halves = pieces.shape[0]
    bf16, f32 = jnp.bfloat16, jnp.float32
    limit = VMEM_LIMIT if blocks < 16 else 2 * VMEM_LIMIT
    return pl.pallas_call(
        functools.partial(attend_kernel, shards, blocks - 1, len(frozen), kv_width),
        out_shape=jax.ShapeDtypeStruct((tokens, QUERY_HEADS * HEAD_SIZE), bf16),
        in_specs=smem() + vmem(4) + [pl.BlockSpec(memory_space=pl.ANY)] * (1 + len(frozen)),
        out_specs=vmem()[0],
        scratch_shapes=[
            pltpu.VMEM((blocks,) + frozen[0].shape, bf16),
            pltpu.VMEM((halves, ROW_BLOCKS * CHUNKS // halves, 16, up_width), bf16),
            pltpu.VMEM((blocks * tokens, key_width), bf16),
            pltpu.VMEM((blocks * tokens, 2 * key_width), bf16),
            pltpu.VMEM((KEY_VALUE_HEADS, rows, HEAD_SIZE), f32),
            pltpu.VMEM((KEY_VALUE_HEADS, rows, 2 * HEAD_SIZE), f32),
            pltpu.SemaphoreType.DMA((blocks,)),
            pltpu.SemaphoreType.DMA,
        ],
        compiler_params=pltpu.CompilerParams(vmem_limit_bytes=limit),
        cost_estimate=pl.CostEstimate(
            flops=2_000_000_000, bytes_accessed=8 << 20, transcendentals=4 << 20
        ),
        name="attend",
    )(plan, queries, *tables, lows_all, pieces, *frozen)


def output_kernel(at, attended_ref, piece_ref, out_ref):
    q_head = attended_ref.shape[1] // CHUNKS
    d = out_ref.shape[1] // CHUNKS
    low = jnp.zeros((attended_ref.shape[0], ROW_BLOCKS * 16), jnp.float32)
    for chunk in range(CHUNKS):
        down = factor(piece_ref, chunk, at, q_head)
        low += dot_nt(attended_ref[:, columns(chunk, q_head)], down)
    low = low.astype(jnp.bfloat16)
    for chunk in range(CHUNKS):
        result = adapter_scale * jnp.dot(
            low, factor(piece_ref, chunk, at + q_head, d), preferred_element_type=jnp.float32
        )
        out_ref[:, columns(chunk, d)] = result.astype(jnp.bfloat16)


def output_adapter(attended, pieces, model_width, at):
    return pl.pallas_call(
        functools.partial(output_kernel, at),
        out_shape=jax.ShapeDtypeStruct((attended.shape[0], model_width), jnp.bfloat16),
        in_specs=vmem(2),
        out_specs=vmem()[0],
        compiler_params=PARAMS,
        cost_estimate=pl.CostEstimate(
            flops=100_000_000, bytes_accessed=3 << 20, transcendentals=0
        ),
        name="output",
    )(attended, pieces)


PLANES = 4


def plane_pairs(shift, planes):
    return [
        (p * PLANES + q, (p + shift) % PLANES * PLANES + q)
        for p in range(PLANES)
        for q in range(PLANES)
        if (p + shift) % PLANES in planes
    ]


MATE_PAIRS = [[(d, d ^ k) for d in range(PLANES * PLANES)] for k in range(PLANES)]


def pairs_kernel(plan_ref, own_ref, one_ref, two_ref, *outs):
    plane, order = plan_ref[PLANE], plan_ref[ORDER]
    for other, out in enumerate(outs):
        last_long = (plane == 1) & (order == other)

        @pl.when(last_long)
        def _(out=out):
            out[0] = one_ref[...]
            out[1] = two_ref[...]

        @pl.when(jnp.logical_not(last_long))
        def _(out=out):
            out[0] = own_ref[...]
            out[1] = one_ref[...]


def pairs(plan, own, one, two):
    shape = jax.ShapeDtypeStruct((2,) + own.shape, own.dtype)
    return pl.pallas_call(
        pairs_kernel,
        out_shape=[shape] * PLANES,
        in_specs=smem() + vmem(3),
        out_specs=vmem(PLANES),
        compiler_params=PARAMS,
        name="pairs",
    )(plan, own, one, two)


def relayed(plan, frozen):
    one = lax.ppermute(frozen, "ctx", plane_pairs(1, (0, 1, 2)))
    two = lax.ppermute(one, "ctx", plane_pairs(1, (1,)))
    return pairs(plan, frozen, one, two)


def exchanged(letters):
    mine, *out = letters
    return [mine] + [lax.ppermute(x, "ctx", MATE_PAIRS[k + 1]) for k, x in enumerate(out)]


def body(
    hidden,
    frozen_query,
    frozen_key,
    frozen_value,
    adapter_bank,
    request_shards,
    request_adapter,
    adapter_owner,
):
    shards = lax.axis_size("ctx")
    groups = lax.axis_size("groups")
    tokens, model_width = hidden.shape
    halves = 2 if groups == 2 and shards == PLANES * PLANES else 1
    own_half = lax.axis_index("groups") if halves == 2 else 0
    me = jnp.stack([lax.axis_index("ctx"), own_half]).astype(jnp.int32)
    parts = Parts(model_width, frozen_query.shape[1], frozen_key.shape[1])
    reach = shards // 2

    packed = pack(parts, halves, shards, me, adapter_bank)
    spread = lax.all_to_all(packed, "ctx", split_axis=0, concat_axis=0, tiled=True)

    tables = rope_tables(jnp.arange((reach + 1) * tokens, dtype=jnp.int32).reshape(-1, tokens))
    requests = jnp.stack([request_shards, request_adapter])[:, None]
    if halves == 2:
        theirs = lax.ppermute(requests, "groups", [(0, 1), (1, 0)])
        requests = jnp.concatenate([requests, theirs], axis=1)
    plan = make_plan(shards, reach, me, requests[0], requests[1], adapter_owner)
    frozen = jnp.concatenate([frozen_key, frozen_value], axis=1)
    letters = relayed(plan, frozen) if halves == 2 else [lax.all_gather(frozen, "ctx")]
    spread, letters, tables = lax.optimization_barrier((spread, letters, tables))

    def collect(pieces):
        axes = ("groups", "ctx") if halves == 2 else "ctx"
        pieces = lax.all_to_all(pieces, axes, split_axis=0, concat_axis=0, tiled=True)
        return pieces.reshape((halves, shards) + pieces.shape[1:])[:, : ROW_BLOCKS * CHUNKS]

    kv_width, q_width, o_width = parts.widths
    pieces = collect(route(plan, spread, (kv_width + q_width + o_width,))[0])
    if halves == 2:
        letters = exchanged(letters)
    pieces, letters = lax.optimization_barrier((pieces, letters))
    low = lows(shards, hidden, pieces)
    lows_all = lax.all_to_all(low, "ctx", split_axis=0, concat_axis=0, tiled=True)
    queries = make_queries(plan, hidden, frozen_query, tables, pieces, kv_width)
    attended = attend(plan, queries, tables, [frozen, *letters], lows_all, pieces, kv_width)
    return attended, output_adapter(attended, pieces, model_width, kv_width + q_width)


def solution(mesh):
    return jax.shard_map(
        body,
        mesh=mesh,
        in_specs=(
            P(("groups", "ctx"), None),
            P(("groups", "ctx"), None),
            P(("groups", "ctx"), None),
            P(("groups", "ctx"), None),
            P("ctx", None, None),
            P("groups"),
            P("groups"),
            P(),
        ),
        out_specs=(P(("groups", "ctx"), None), P(("groups", "ctx"), None)),
        check_vma=False,
    )
```

```python
import functools

import jax
import jax.numpy as jnp
from jax import lax
from jax.experimental import pallas as pl
from jax.experimental.pallas import tpu as pltpu
from jax.sharding import PartitionSpec as P

HEAD_SIZE = 128
QUERY_HEADS = 16
KEY_VALUE_HEADS = 4
GROUP_SPLIT = QUERY_HEADS // KEY_VALUE_HEADS

adapter_scale = 0.5
rope_theta = 500000.0
score_masked = -1e30

VMEM_LIMIT = 24 * 1024 * 1024

ROW_BLOCKS = 4
CHUNKS = 8


def rope_tables(positions):
    half_dim = HEAD_SIZE // 2
    frequency = rope_theta ** (-(jnp.arange(half_dim, dtype=jnp.float32) * 2.0) / HEAD_SIZE)
    angles = positions.astype(jnp.float32)[..., None] * frequency
    cosines = jnp.cos(angles)
    sines = jnp.sin(angles)
    return (jnp.concatenate([cosines, cosines], -1), jnp.concatenate([-sines, sines], -1))


class Parts:
    def __init__(self, model_width, query_width, key_width):
        d, q, k = model_width, query_width, key_width
        up = 3 * d
        self.kv = ((d, d // CHUNKS), (2 * d, d // CHUNKS), (up + q, 2 * k // CHUNKS))
        self.q = ((0, d // CHUNKS), (up, q // CHUNKS))
        self.o = ((up + q + 2 * k, q // CHUNKS), (up + 2 * q + 2 * k, d // CHUNKS))
        self.all = self.kv + self.q + self.o
        self.widths = tuple(sum(w for _, w in part) for part in (self.kv, self.q, self.o))


def vmem(count=1):
    return [pl.BlockSpec(memory_space=pltpu.VMEM)] * count


def smem(count=1):
    return [pl.BlockSpec(memory_space=pltpu.SMEM)] * count


PARAMS = pltpu.CompilerParams(vmem_limit_bytes=VMEM_LIMIT)


OWN_INDEX, OWN_HALF, PLANE, ORDER, COUNT, ENTRY = 0, 1, 2, 3, 4, 8


def layout(lengths_ref, which, shards):
    starts, start, length = [jnp.int32(0)], jnp.int32(0), lengths_ref[which, 0]
    for r in range(1, lengths_ref.shape[1]):
        starts.append(starts[-1] + lengths_ref[which, r - 1])
        longer = lengths_ref[which, r] > length
        start = jnp.where(longer, starts[-1], start)
        length = jnp.where(longer, lengths_ref[which, r], length)
    return starts, start + lax.div(length, 2)


def plan_kernel(shards, reach, me_ref, lengths_ref, adapters_ref, owner_ref, out_ref):
    own_index, own_half = me_ref[0], me_ref[1]
    starts, offset = layout(lengths_ref, 0, shards)
    own_packed = lax.rem(own_index + offset, shards)
    first = jnp.int32(0)
    for start in starts[1:]:
        first = jnp.where(start <= own_packed, start, first)
    out_ref[OWN_INDEX] = own_index
    out_ref[OWN_HALF] = own_half
    out_ref[PLANE] = lax.div(own_index, PLANES)
    out_ref[ORDER] = lax.rem(own_index, PLANES)
    out_ref[COUNT] = jnp.minimum(own_packed - first, reach) + 1
    for which in range(lengths_ref.shape[0]):
        starts, offset = layout(lengths_ref, which, shards)
        entries = [owner_ref[adapters_ref[which, r]] for r in range(len(starts))]
        at = ENTRY + shards * (own_half if which == 0 else 1 - own_half)
        for shard in range(shards):
            packed = lax.rem(shard + offset, shards)
            entry = entries[0]
            for start, later in zip(starts[1:], entries[1:]):
                entry = jnp.where(start <= packed, later, entry)
            out_ref[at + shard] = entry


def make_plan(shards, reach, me, lengths, adapters, owner):
    return pl.pallas_call(
        functools.partial(plan_kernel, shards, reach),
        out_shape=jax.ShapeDtypeStruct((ENTRY + lengths.shape[0] * shards,), jnp.int32),
        in_specs=smem(4),
        out_specs=smem()[0],
        name="plan",
    )(me, lengths, adapters, owner)


def pack_kernel(parts, halves, me_ref, bank_ref, out_ref):
    own_half = me_ref[1]
    for copy in range(out_ref.shape[0]):
        for place in range(out_ref.shape[1]):
            at = 0
            for first, width in parts.all:
                start = pl.multiple_of(first + (place * halves + own_half) * width, 128)
                out_ref[copy, place, 0, :, at : at + width] = bank_ref[0, :, pl.ds(start, width)]
                at += width


def pack(parts, halves, shards, me, bank):
    columns_all = bank.shape[2]
    width, places = sum(parts.widths), CHUNKS // halves
    copies = shards // (places * ROW_BLOCKS)
    packed = pl.pallas_call(
        functools.partial(pack_kernel, parts, halves),
        out_shape=jax.ShapeDtypeStruct((copies, places, ROW_BLOCKS, 16, width), bank.dtype),
        grid=(ROW_BLOCKS,),
        in_specs=smem() + [pl.BlockSpec((1, 16, columns_all), lambda i: (0, i, 0))],
        out_specs=pl.BlockSpec((copies, places, 1, 16, width), lambda i: (0, 0, i, 0, 0)),
        compiler_params=PARAMS,
        name="pack",
    )(me, bank)
    return packed.reshape(shards, 16, width)


def hbm(count=1):
    return [pl.BlockSpec(memory_space=pltpu.HBM)] * count


def route_kernel(plan_ref, spread_ref, out_ref, sem):
    copies = [
        pltpu.make_async_copy(
            spread_ref.at[plan_ref[ENTRY + dest]], out_ref.at[dest], sem.at[dest]
        )
        for dest in range(out_ref.shape[0])
    ]
    for copy in copies:
        copy.start()
    for copy in copies:
        copy.wait()


def route(plan, spread):
    dests = plan.shape[0] - ENTRY
    return pl.pallas_call(
        route_kernel,
        out_shape=jax.ShapeDtypeStruct((dests,) + spread.shape[1:], spread.dtype),
        in_specs=smem() + vmem(),
        out_specs=hbm()[0],
        scratch_shapes=[pltpu.SemaphoreType.DMA((dests,))],
        compiler_params=PARAMS,
        name="route",
    )(plan, spread)


def factor(piece_ref, chunk, at, width):
    halves = piece_ref.shape[0]
    place = chunk // halves * ROW_BLOCKS
    rows = piece_ref[chunk % halves, place : place + ROW_BLOCKS, :, at : at + width]
    return rows.reshape(ROW_BLOCKS * 16, width)


def columns(chunk, width):
    return slice(chunk * width, (chunk + 1) * width)


def dot_nt(a, b):
    return lax.dot_general(a, b, (((1,), (1,)), ((), ())), preferred_element_type=jnp.float32)


def turn(x, cosines, sines):
    return x * cosines + pltpu.roll(x, HEAD_SIZE // 2, 1) * sines


def lows_kernel(hidden_ref, piece_ref, out_ref, low_ref, sem):
    d = hidden_ref.shape[1] // CHUNKS
    low = jnp.zeros((hidden_ref.shape[0], 2 * ROW_BLOCKS * 16), jnp.float32)
    for chunk in range(CHUNKS):
        down = jnp.concatenate(
            [factor(piece_ref, chunk, 0, d), factor(piece_ref, chunk, d, d)], axis=0
        )
        low += dot_nt(hidden_ref[:, columns(chunk, d)], down)
    low_ref[...] = low.astype(jnp.bfloat16)
    copies = [
        pltpu.make_async_copy(low_ref, out_ref.at[shard], sem.at[shard])
        for shard in range(out_ref.shape[0])
    ]
    for copy in copies:
        copy.start()
    for copy in copies:
        copy.wait()


def lows(shards, hidden, pieces):
    return pl.pallas_call(
        lows_kernel,
        out_shape=jax.ShapeDtypeStruct(
            (shards, hidden.shape[0], 2 * ROW_BLOCKS * 16), jnp.bfloat16
        ),
        in_specs=vmem(2),
        out_specs=hbm()[0],
        scratch_shapes=[
            pltpu.VMEM((hidden.shape[0], 2 * ROW_BLOCKS * 16), jnp.bfloat16),
            pltpu.SemaphoreType.DMA((shards,)),
        ],
        compiler_params=PARAMS,
        cost_estimate=pl.CostEstimate(
            flops=150_000_000, bytes_accessed=3 << 20, transcendentals=0
        ),
        name="lows",
    )(hidden, pieces)


def query_kernel(at, plan_ref, hidden_ref, query_ref, cos_ref, sin_ref, piece_ref, out_ref):
    tokens = query_ref.shape[0]
    d = hidden_ref.shape[1] // CHUNKS
    width = query_ref.shape[1] // CHUNKS
    low = jnp.zeros((tokens, ROW_BLOCKS * 16), jnp.float32)
    for chunk in range(CHUNKS):
        low += dot_nt(hidden_ref[:, columns(chunk, d)], factor(piece_ref, chunk, at, d))
    low = low.astype(jnp.bfloat16)
    own = plan_ref[COUNT] - 1
    cosines, sines = cos_ref[own], sin_ref[own]
    for chunk in range(CHUNKS):
        up = factor(piece_ref, chunk, at + d, width)
        update = jnp.dot(low, up, preferred_element_type=jnp.float32)
        result = query_ref[:, columns(chunk, width)].astype(jnp.float32) + adapter_scale * update
        for part in range(width // HEAD_SIZE):
            head = chunk * (width // HEAD_SIZE) + part
            turned = turn(result[:, columns(part, HEAD_SIZE)], cosines, sines)
            out_ref[head // GROUP_SPLIT, pl.ds((head % GROUP_SPLIT) * tokens, tokens)] = (
                turned.astype(jnp.bfloat16)
            )


def make_queries(plan, hidden, query, tables, pieces, at):
    tokens = hidden.shape[0]
    return pl.pallas_call(
        functools.partial(query_kernel, at),
        out_shape=jax.ShapeDtypeStruct(
            (KEY_VALUE_HEADS, GROUP_SPLIT * tokens, HEAD_SIZE), jnp.bfloat16
        ),
        in_specs=smem() + vmem(5),
        out_specs=vmem()[0],
        compiler_params=PARAMS,
        cost_estimate=pl.CostEstimate(
            flops=100_000_000, bytes_accessed=3 << 20, transcendentals=0
        ),
        name="queries",
    )(plan, hidden, query, *tables, pieces)


REGION = 4


def attend_kernel(
    shards, reach, sources, kv_width, plan_ref, queries, cos_ref, sin_ref, lows_ref, kv_ref, *refs
):
    frozen_refs, refs = refs[:sources], refs[sources:]
    out_ref, frozen, up_copy, keys, values, high, acc, sem, part_sem = refs
    own_index, order, count = plan_ref[OWN_INDEX], plan_ref[ORDER], plan_ref[COUNT]
    tokens = out_ref.shape[0]
    rank = ROW_BLOCKS * 16
    rows = GROUP_SPLIT * tokens
    key_width = KEY_VALUE_HEADS * HEAD_SIZE
    bf16 = jnp.bfloat16
    base2 = 1.4426950408889634 / (HEAD_SIZE**0.5)
    up_width = up_copy.shape[3]
    up_part = pltpu.make_async_copy(
        kv_ref.at[:, pl.ds(0, up_copy.shape[1]), :, pl.ds(kv_width - up_width, up_width)],
        up_copy,
        part_sem,
    )

    def source_of(step):
        return lax.rem(own_index - step + shards, shards)

    def land(step, source):
        return pltpu.make_async_copy(source, frozen.at[step], sem.at[step])

    up_part.start()
    land(0, frozen_refs[0]).start()
    regions = [(0, 1)] + [
        (first, min(REGION, reach + 1 - first)) for first in range(1, reach + 1, REGION)
    ]
    for first, number in regions[1:]:

        @pl.when(count > first)
        def _(first=first, number=number):
            for step in range(first, first + number):
                source = source_of(step)
                if sources == 2:
                    land(step, frozen_refs[1].at[source]).start()
                    continue
                plane = plan_ref[PLANE]
                last_long = (plane == 1) & (order == 0)
                far = lax.div(source, PLANES) != jnp.where(last_long, 0, plane)
                mate = jnp.bitwise_xor(lax.rem(source, PLANES), order)
                for other in range(PLANES):
                    pl.when(mate == other)(
                        land(step, frozen_refs[1 + other].at[far.astype(jnp.int32)]).start
                    )

    up_part.wait()
    up = [factor(up_copy, chunk, 0, up_width) for chunk in range(CHUNKS)]
    up_key = jnp.concatenate(up[: CHUNKS // 2], axis=1)
    up_value = jnp.concatenate(up[CHUNKS // 2 :], axis=1)
    ones = jnp.ones((tokens, HEAD_SIZE), bf16)

    def rebuild(step):
        at = pl.ds(step * tokens, tokens)
        low = lows_ref[source_of(step)]
        land(step, frozen_refs[0]).wait()
        key = frozen[step, :, :key_width].astype(jnp.float32) + adapter_scale * jnp.dot(
            low[:, :rank], up_key, preferred_element_type=jnp.float32
        )
        value = frozen[step, :, key_width:].astype(jnp.float32) + adapter_scale * jnp.dot(
            low[:, rank:], up_value, preferred_element_type=jnp.float32
        )
        value = value.astype(bf16)
        place = jnp.maximum(count - 1 - step, 0)
        cosines, sines = cos_ref[place], sin_ref[place]
        for g in range(KEY_VALUE_HEADS):
            turned = turn(key[:, columns(g, HEAD_SIZE)], cosines, sines)
            keys[at, columns(g, HEAD_SIZE)] = turned.astype(bf16)
            values[at, columns(2 * g, HEAD_SIZE)] = value[:, columns(g, HEAD_SIZE)]
            values[at, columns(2 * g + 1, HEAD_SIZE)] = ones

    def region(first, number):
        for step in range(first, first + number):
            rebuild(step)
        at = pl.ds(first * tokens, number * tokens)
        for g in range(KEY_VALUE_HEADS):
            score = dot_nt(queries[g], keys[at, columns(g, HEAD_SIZE)])
            tiles = [score[:, columns(i, tokens)] for i in range(number)]
            if first == 0:
                row = lax.broadcasted_iota(jnp.int32, (rows, tokens), 0) % tokens
                column = lax.broadcasted_iota(jnp.int32, (rows, tokens), 1)
                tiles = [jnp.where(column <= row, tiles[0], score_masked)]
            else:
                tiles = tiles[:1] + [
                    jnp.where(count > first + i, tiles[i], score_masked)
                    for i in range(1, number)
                ]
            top = functools.reduce(jnp.maximum, tiles)
            top = jnp.max(top, axis=1, keepdims=True) * base2
            top = jnp.broadcast_to(top, (rows, HEAD_SIZE))
            if first:
                old = high[g]
                top = jnp.maximum(old, top)
            weight = [jnp.exp2(t * base2 - top).astype(bf16) for t in tiles]
            blend = jnp.dot(
                jnp.concatenate(weight, axis=1),
                values[at, columns(g, 2 * HEAD_SIZE)],
                preferred_element_type=jnp.float32,
            )
            if first:
                shrink = jnp.exp2(old - top)
                blend += acc[g] * jnp.concatenate([shrink, shrink], axis=1)
            high[g] = top
            acc[g] = blend

    region(*regions[0])
    for first, number in regions[1:]:
        pl.when(count > first)(functools.partial(region, first, number))

    for g in range(KEY_VALUE_HEADS):
        result = (acc[g, :, :HEAD_SIZE] / acc[g, :, HEAD_SIZE:]).astype(bf16)
        for j in range(GROUP_SPLIT):
            out_ref[:, columns(g * GROUP_SPLIT + j, HEAD_SIZE)] = result[columns(j, tokens)]


def attend(plan, queries, tables, frozen, lows_all, pieces, kv_width):
    shards, tokens = lows_all.shape[0], lows_all.shape[1]
    key_width = frozen[0].shape[1] // 2
    blocks = tables[0].shape[0]
    rows = GROUP_SPLIT * tokens
    up_width = 2 * key_width // CHUNKS
    halves = pieces.shape[0]
    bf16, f32 = jnp.bfloat16, jnp.float32
    limit = VMEM_LIMIT if blocks < 16 else 2 * VMEM_LIMIT
    return pl.pallas_call(
        functools.partial(attend_kernel, shards, blocks - 1, len(frozen), kv_width),
        out_shape=jax.ShapeDtypeStruct((tokens, QUERY_HEADS * HEAD_SIZE), bf16),
        in_specs=smem() + vmem(4) + [pl.BlockSpec(memory_space=pl.ANY)] + hbm(len(frozen)),
        out_specs=vmem()[0],
        scratch_shapes=[
            pltpu.VMEM((blocks,) + frozen[0].shape, bf16),
            pltpu.VMEM((halves, ROW_BLOCKS * CHUNKS // halves, 16, up_width), bf16),
            pltpu.VMEM((blocks * tokens, key_width), bf16),
            pltpu.VMEM((blocks * tokens, 2 * key_width), bf16),
            pltpu.VMEM((KEY_VALUE_HEADS, rows, HEAD_SIZE), f32),
            pltpu.VMEM((KEY_VALUE_HEADS, rows, 2 * HEAD_SIZE), f32),
            pltpu.SemaphoreType.DMA((blocks,)),
            pltpu.SemaphoreType.DMA,
        ],
        compiler_params=pltpu.CompilerParams(vmem_limit_bytes=limit),
        cost_estimate=pl.CostEstimate(
            flops=2_000_000_000, bytes_accessed=8 << 20, transcendentals=4 << 20
        ),
        name="attend",
    )(plan, queries, *tables, lows_all, pieces, *frozen)


def output_kernel(at, attended_ref, piece_ref, out_ref):
    q_head = attended_ref.shape[1] // CHUNKS
    d = out_ref.shape[1] // CHUNKS
    low = jnp.zeros((attended_ref.shape[0], ROW_BLOCKS * 16), jnp.float32)
    for chunk in range(CHUNKS):
        down = factor(piece_ref, chunk, at, q_head)
        low += dot_nt(attended_ref[:, columns(chunk, q_head)], down)
    low = low.astype(jnp.bfloat16)
    for chunk in range(CHUNKS):
        result = adapter_scale * jnp.dot(
            low, factor(piece_ref, chunk, at + q_head, d), preferred_element_type=jnp.float32
        )
        out_ref[:, columns(chunk, d)] = result.astype(jnp.bfloat16)


def output_adapter(attended, pieces, model_width, at):
    return pl.pallas_call(
        functools.partial(output_kernel, at),
        out_shape=jax.ShapeDtypeStruct((attended.shape[0], model_width), jnp.bfloat16),
        in_specs=vmem(2),
        out_specs=vmem()[0],
        compiler_params=PARAMS,
        cost_estimate=pl.CostEstimate(
            flops=100_000_000, bytes_accessed=3 << 20, transcendentals=0
        ),
        name="output",
    )(attended, pieces)


PLANES = 4


def plane_pairs(shift, planes):
    return [
        (p * PLANES + q, (p + shift) % PLANES * PLANES + q)
        for p in range(PLANES)
        for q in range(PLANES)
        if (p + shift) % PLANES in planes
    ]


MATE_PAIRS = [[(d, d ^ k) for d in range(PLANES * PLANES)] for k in range(PLANES)]


def pairs_kernel(plan_ref, own_ref, one_ref, two_ref, *outs):
    plane, order = plan_ref[PLANE], plan_ref[ORDER]
    for other, out in enumerate(outs):
        last_long = (plane == 1) & (order == other)

        @pl.when(last_long)
        def _(out=out):
            out[0] = one_ref[...]
            out[1] = two_ref[...]

        @pl.when(jnp.logical_not(last_long))
        def _(out=out):
            out[0] = own_ref[...]
            out[1] = one_ref[...]


def pairs(plan, own, one, two):
    shape = jax.ShapeDtypeStruct((2,) + own.shape, own.dtype)
    return pl.pallas_call(
        pairs_kernel,
        out_shape=[shape] * PLANES,
        in_specs=smem() + vmem(3),
        out_specs=vmem(PLANES),
        compiler_params=PARAMS,
        name="pairs",
    )(plan, own, one, two)


def relayed(plan, frozen):
    one = lax.ppermute(frozen, "ctx", plane_pairs(1, (0, 1, 2)))
    two = lax.ppermute(one, "ctx", plane_pairs(1, (1,)))
    return pairs(plan, frozen, one, two)


def exchanged(letters):
    mine, *out = letters
    return [mine] + [lax.ppermute(x, "ctx", MATE_PAIRS[k + 1]) for k, x in enumerate(out)]


def body(
    hidden,
    frozen_query,
    frozen_key,
    frozen_value,
    adapter_bank,
    request_shards,
    request_adapter,
    adapter_owner,
):
    shards = lax.axis_size("ctx")
    groups = lax.axis_size("groups")
    tokens, model_width = hidden.shape
    halves = 2 if groups == 2 and shards == PLANES * PLANES else 1
    own_half = lax.axis_index("groups") if halves == 2 else 0
    me = jnp.stack([lax.axis_index("ctx"), own_half]).astype(jnp.int32)
    parts = Parts(model_width, frozen_query.shape[1], frozen_key.shape[1])
    reach = shards // 2

    packed = pack(parts, halves, shards, me, adapter_bank)
    spread = lax.all_to_all(packed, "ctx", split_axis=0, concat_axis=0, tiled=True)

    tables = rope_tables(jnp.arange((reach + 1) * tokens, dtype=jnp.int32).reshape(-1, tokens))
    requests = jnp.stack([request_shards, request_adapter])[:, None]
    if halves == 2:
        theirs = lax.ppermute(requests, "groups", [(0, 1), (1, 0)])
        requests = jnp.concatenate([requests, theirs], axis=1)
    plan = make_plan(shards, reach, me, requests[0], requests[1], adapter_owner)
    frozen = jnp.concatenate([frozen_key, frozen_value], axis=1)
    letters = relayed(plan, frozen) if halves == 2 else [lax.all_gather(frozen, "ctx")]
    spread, tables = lax.optimization_barrier((spread, tables))

    def collect(pieces):
        axes = ("groups", "ctx") if halves == 2 else "ctx"
        pieces = lax.all_to_all(pieces, axes, split_axis=0, concat_axis=0, tiled=True)
        return pieces.reshape((halves, shards) + pieces.shape[1:])[:, : ROW_BLOCKS * CHUNKS]

    kv_width, q_width, _ = parts.widths
    pieces = collect(route(plan, spread))
    if halves == 2:
        letters = exchanged(letters)
    pieces, letters = lax.optimization_barrier((pieces, letters))
    low = lows(shards, hidden, pieces)
    lows_all = lax.all_to_all(low, "ctx", split_axis=0, concat_axis=0, tiled=True)
    queries = make_queries(plan, hidden, frozen_query, tables, pieces, kv_width)
    attended = attend(plan, queries, tables, [frozen, *letters], lows_all, pieces, kv_width)
    return attended, output_adapter(attended, pieces, model_width, kv_width + q_width)


def solution(mesh):
    return jax.shard_map(
        body,
        mesh=mesh,
        in_specs=(
            P(("groups", "ctx"), None),
            P(("groups", "ctx"), None),
            P(("groups", "ctx"), None),
            P(("groups", "ctx"), None),
            P("ctx", None, None),
            P("groups"),
            P("groups"),
            P(),
        ),
        out_specs=(P(("groups", "ctx"), None), P(("groups", "ctx"), None)),
        check_vma=False,
    )
```

```python
import functools

import jax
import jax.numpy as jnp
from jax import lax
from jax.experimental import pallas as pl
from jax.experimental.pallas import tpu as pltpu
from jax.sharding import PartitionSpec as P

HEAD_SIZE = 128
QUERY_HEADS = 16
KEY_VALUE_HEADS = 4
GROUP_SPLIT = QUERY_HEADS // KEY_VALUE_HEADS

adapter_scale = 0.5
rope_theta = 500000.0
score_masked = -1e30

VMEM_LIMIT = 24 * 1024 * 1024

ROW_BLOCKS = 4
CHUNKS = 8


def rope_tables(positions):
    half_dim = HEAD_SIZE // 2
    frequency = rope_theta ** (-(jnp.arange(half_dim, dtype=jnp.float32) * 2.0) / HEAD_SIZE)
    angles = positions.astype(jnp.float32)[..., None] * frequency
    cosines = jnp.cos(angles)
    sines = jnp.sin(angles)
    return (jnp.concatenate([cosines, cosines], -1), jnp.concatenate([-sines, sines], -1))


class Parts:
    def __init__(self, model_width, query_width, key_width):
        d, q, k = model_width, query_width, key_width
        up = 3 * d
        self.kv = ((d, d // CHUNKS), (2 * d, d // CHUNKS), (up + q, 2 * k // CHUNKS))
        self.q = ((0, d // CHUNKS), (up, q // CHUNKS))
        self.o = ((up + q + 2 * k, q // CHUNKS), (up + 2 * q + 2 * k, d // CHUNKS))
        self.all = self.kv + self.q + self.o
        self.widths = tuple(sum(w for _, w in part) for part in (self.kv, self.q, self.o))


def vmem(count=1):
    return [pl.BlockSpec(memory_space=pltpu.VMEM)] * count


def smem(count=1):
    return [pl.BlockSpec(memory_space=pltpu.SMEM)] * count


PARAMS = pltpu.CompilerParams(vmem_limit_bytes=VMEM_LIMIT)


OWN_INDEX, OWN_HALF, COUNT, ENTRY = 0, 1, 2, 8


def layout(lengths_ref, which, shards):
    starts, start, length = [jnp.int32(0)], jnp.int32(0), lengths_ref[which, 0]
    for r in range(1, lengths_ref.shape[1]):
        starts.append(starts[-1] + lengths_ref[which, r - 1])
        longer = lengths_ref[which, r] > length
        start = jnp.where(longer, starts[-1], start)
        length = jnp.where(longer, lengths_ref[which, r], length)
    return starts, start + lax.div(length, 2)


def plan_kernel(shards, reach, me_ref, lengths_ref, adapters_ref, owner_ref, out_ref):
    own_index, own_half = me_ref[0], me_ref[1]
    starts, offset = layout(lengths_ref, 0, shards)
    own_packed = lax.rem(own_index + offset, shards)
    first = jnp.int32(0)
    for start in starts[1:]:
        first = jnp.where(start <= own_packed, start, first)
    out_ref[OWN_INDEX] = own_index
    out_ref[OWN_HALF] = own_half
    out_ref[COUNT] = jnp.minimum(own_packed - first, reach) + 1
    for which in range(lengths_ref.shape[0]):
        starts, offset = layout(lengths_ref, which, shards)
        entries = [owner_ref[adapters_ref[which, r]] for r in range(len(starts))]
        at = ENTRY + shards * (own_half if which == 0 else 1 - own_half)
        for shard in range(shards):
            packed = lax.rem(shard + offset, shards)
            entry = entries[0]
            for start, later in zip(starts[1:], entries[1:]):
                entry = jnp.where(start <= packed, later, entry)
            out_ref[at + shard] = entry


def make_plan(shards, reach, me, lengths, adapters, owner):
    return pl.pallas_call(
        functools.partial(plan_kernel, shards, reach),
        out_shape=jax.ShapeDtypeStruct((ENTRY + lengths.shape[0] * shards,), jnp.int32),
        in_specs=smem(4),
        out_specs=smem()[0],
        name="plan",
    )(me, lengths, adapters, owner)


def pack_kernel(parts, halves, x_ref, bank_ref, out):
    own_half = x_ref[1]
    for block in range(out.shape[0]):
        piece = block % (ROW_BLOCKS * CHUNKS // halves)
        rows = pl.ds((piece % ROW_BLOCKS) * 16, 16)
        chunk = (piece // ROW_BLOCKS) * halves + own_half
        at = 0
        for first, width in parts.all:
            start = pl.multiple_of(first + chunk * width, 128)
            out[block, :, at : at + width] = bank_ref[0, rows, pl.ds(start, width)]
            at += width


def pack(parts, halves, shards, me, bank):
    width = sum(parts.widths)
    return pl.pallas_call(
        functools.partial(pack_kernel, parts, halves),
        out_shape=jax.ShapeDtypeStruct((shards, 16, width), bank.dtype),
        in_specs=smem() + vmem(),
        out_specs=vmem()[0],
        compiler_params=PARAMS,
        name="pack",
    )(me, bank)


ROUTE_STEPS = 4


def route_kernel(plan_ref, spread_ref, out_ref):
    for i in range(out_ref.shape[0]):
        dest = pl.program_id(0) * out_ref.shape[0] + i
        out_ref[i] = spread_ref[plan_ref[ENTRY + dest]]


def route(plan, spread):
    dests = plan.shape[0] - ENTRY
    return pl.pallas_call(
        route_kernel,
        out_shape=jax.ShapeDtypeStruct((dests,) + spread.shape[1:], spread.dtype),
        grid=(ROUTE_STEPS,),
        in_specs=smem() + vmem(),
        out_specs=pl.BlockSpec((dests // ROUTE_STEPS,) + spread.shape[1:], lambda i: (i, 0, 0)),
        compiler_params=PARAMS,
        name="route",
    )(plan, spread)


def factor(piece_ref, chunk, at, width):
    halves = piece_ref.shape[0]
    place = chunk // halves * ROW_BLOCKS
    rows = piece_ref[chunk % halves, place : place + ROW_BLOCKS, :, at : at + width]
    return rows.reshape(ROW_BLOCKS * 16, width)


def columns(chunk, width):
    return slice(chunk * width, (chunk + 1) * width)


def dot_nt(a, b):
    return lax.dot_general(a, b, (((1,), (1,)), ((), ())), preferred_element_type=jnp.float32)


def turn(x, cosines, sines):
    return x * cosines + pltpu.roll(x, HEAD_SIZE // 2, 1) * sines


def kv_kernel(plan_ref, hidden_ref, key_ref, value_ref, cos_ref, sin_ref, piece_ref, out_ref):
    d = hidden_ref.shape[1] // CHUNKS
    rank = ROW_BLOCKS * 16
    low = jnp.zeros((hidden_ref.shape[0], 2 * rank), jnp.float32)
    for chunk in range(CHUNKS):
        down = jnp.concatenate(
            [factor(piece_ref, chunk, 0, d), factor(piece_ref, chunk, d, d)], axis=0
        )
        low += dot_nt(hidden_ref[:, columns(chunk, d)], down)
    low = low.astype(jnp.bfloat16)
    width = 2 * key_ref.shape[1] // CHUNKS
    own = plan_ref[COUNT] - 1
    cosines, sines = cos_ref[own], sin_ref[own]
    for chunk in range(CHUNKS):
        is_key = chunk < CHUNKS // 2
        up = factor(piece_ref, chunk, 2 * d, width)
        part = low[:, :rank] if is_key else low[:, rank:]
        update = jnp.dot(part, up, preferred_element_type=jnp.float32)
        frozen = (key_ref if is_key else value_ref)[:, columns(chunk % (CHUNKS // 2), width)]
        result = frozen.astype(jnp.float32) + adapter_scale * update
        if is_key:
            result = turn(result, cosines, sines)
        out_ref[:, columns(chunk, width)] = result.astype(jnp.bfloat16)


def make_keys_values(plan, hidden, key, value, tables, pieces):
    return pl.pallas_call(
        kv_kernel,
        out_shape=jax.ShapeDtypeStruct((key.shape[0], 2 * key.shape[1]), jnp.bfloat16),
        in_specs=smem() + vmem(6),
        out_specs=vmem()[0],
        compiler_params=PARAMS,
        cost_estimate=pl.CostEstimate(
            flops=150_000_000, bytes_accessed=3 << 20, transcendentals=0
        ),
        name="keys_values",
    )(plan, hidden, key, value, *tables, pieces)


def query_kernel(at, plan_ref, hidden_ref, query_ref, cos_ref, sin_ref, piece_ref, out_ref):
    tokens = query_ref.shape[0]
    d = hidden_ref.shape[1] // CHUNKS
    width = query_ref.shape[1] // CHUNKS
    low = jnp.zeros((tokens, ROW_BLOCKS * 16), jnp.float32)
    for chunk in range(CHUNKS):
        low += dot_nt(hidden_ref[:, columns(chunk, d)], factor(piece_ref, chunk, at, d))
    low = low.astype(jnp.bfloat16)
    own = plan_ref[COUNT] - 1
    cosines, sines = cos_ref[own], sin_ref[own]
    for chunk in range(CHUNKS):
        up = factor(piece_ref, chunk, at + d, width)
        update = jnp.dot(low, up, preferred_element_type=jnp.float32)
        result = query_ref[:, columns(chunk, width)].astype(jnp.float32) + adapter_scale * update
        for part in range(width // HEAD_SIZE):
            head = chunk * (width // HEAD_SIZE) + part
            turned = turn(result[:, columns(part, HEAD_SIZE)], cosines, sines)
            out_ref[head // GROUP_SPLIT, pl.ds((head % GROUP_SPLIT) * tokens, tokens)] = (
                turned.astype(jnp.bfloat16)
            )


def make_queries(plan, hidden, query, tables, pieces, at):
    tokens = hidden.shape[0]
    return pl.pallas_call(
        functools.partial(query_kernel, at),
        out_shape=jax.ShapeDtypeStruct(
            (KEY_VALUE_HEADS, GROUP_SPLIT * tokens, HEAD_SIZE), jnp.bfloat16
        ),
        in_specs=smem() + vmem(5),
        out_specs=vmem()[0],
        compiler_params=PARAMS,
        cost_estimate=pl.CostEstimate(
            flops=100_000_000, bytes_accessed=3 << 20, transcendentals=0
        ),
        name="queries",
    )(plan, hidden, query, *tables, pieces)


REGION = 4


def attend_kernel(plan_ref, queries, *refs):
    blocks, (out_ref, high, acc) = refs[:-3], refs[-3:]
    count = plan_ref[COUNT]
    tokens = out_ref.shape[0]
    rows = GROUP_SPLIT * tokens
    bf16 = jnp.bfloat16
    base2 = 1.4426950408889634 / (HEAD_SIZE**0.5)
    ones = jnp.ones((tokens, HEAD_SIZE), bf16)

    def region(first, number):
        shards = blocks[first : first + number]
        for g in range(KEY_VALUE_HEADS):
            keys = [b[:, columns(g, HEAD_SIZE)] for b in shards]
            values = [
                jnp.concatenate([b[:, columns(KEY_VALUE_HEADS + g, HEAD_SIZE)], ones], axis=1)
                for b in shards
            ]
            score = dot_nt(queries[g], jnp.concatenate(keys, axis=0))
            tiles = [score[:, columns(i, tokens)] for i in range(number)]
            if first == 0:
                row = lax.broadcasted_iota(jnp.int32, (rows, tokens), 0) % tokens
                column = lax.broadcasted_iota(jnp.int32, (rows, tokens), 1)
                tiles = [jnp.where(column <= row, tiles[0], score_masked)]
            else:
                tiles = tiles[:1] + [
                    jnp.where(count > first + i, tiles[i], score_masked)
                    for i in range(1, number)
                ]
            top = functools.reduce(jnp.maximum, tiles)
            top = jnp.max(top, axis=1, keepdims=True) * base2
            top = jnp.broadcast_to(top, (rows, HEAD_SIZE))
            if first:
                old = high[g]
                top = jnp.maximum(old, top)
            weight = [jnp.exp2(t * base2 - top).astype(bf16) for t in tiles]
            blend = jnp.dot(
                jnp.concatenate(weight, axis=1),
                jnp.concatenate(values, axis=0),
                preferred_element_type=jnp.float32,
            )
            if first:
                shrink = jnp.exp2(old - top)
                blend += acc[g] * jnp.concatenate([shrink, shrink], axis=1)
            high[g] = top
            acc[g] = blend

    region(0, 1)
    for first in range(1, len(blocks), REGION):
        number = min(REGION, len(blocks) - first)
        pl.when(count > first)(functools.partial(region, first, number))

    for g in range(KEY_VALUE_HEADS):
        result = (acc[g, :, :HEAD_SIZE] / acc[g, :, HEAD_SIZE:]).astype(bf16)
        for j in range(GROUP_SPLIT):
            out_ref[:, columns(g * GROUP_SPLIT + j, HEAD_SIZE)] = result[columns(j, tokens)]


def attend(plan, queries, blocks):
    tokens = blocks[0].shape[0]
    rows = GROUP_SPLIT * tokens
    limit = VMEM_LIMIT if len(blocks) < 16 else 2 * VMEM_LIMIT
    return pl.pallas_call(
        attend_kernel,
        out_shape=jax.ShapeDtypeStruct((tokens, QUERY_HEADS * HEAD_SIZE), jnp.bfloat16),
        in_specs=smem() + vmem(1 + len(blocks)),
        out_specs=vmem()[0],
        scratch_shapes=[
            pltpu.VMEM((KEY_VALUE_HEADS, rows, HEAD_SIZE), jnp.float32),
            pltpu.VMEM((KEY_VALUE_HEADS, rows, 2 * HEAD_SIZE), jnp.float32),
        ],
        compiler_params=pltpu.CompilerParams(vmem_limit_bytes=limit),
        cost_estimate=pl.CostEstimate(
            flops=2_000_000_000, bytes_accessed=8 << 20, transcendentals=4 << 20
        ),
        name="attend",
    )(plan, queries, *blocks)


def output_kernel(at, attended_ref, piece_ref, out_ref):
    q_head = attended_ref.shape[1] // CHUNKS
    d = out_ref.shape[1] // CHUNKS
    low = jnp.zeros((attended_ref.shape[0], ROW_BLOCKS * 16), jnp.float32)
    for chunk in range(CHUNKS):
        down = factor(piece_ref, chunk, at, q_head)
        low += dot_nt(attended_ref[:, columns(chunk, q_head)], down)
    low = low.astype(jnp.bfloat16)
    for chunk in range(CHUNKS):
        result = adapter_scale * jnp.dot(
            low, factor(piece_ref, chunk, at + q_head, d), preferred_element_type=jnp.float32
        )
        out_ref[:, columns(chunk, d)] = result.astype(jnp.bfloat16)


def output_adapter(attended, pieces, model_width, at):
    return pl.pallas_call(
        functools.partial(output_kernel, at),
        out_shape=jax.ShapeDtypeStruct((attended.shape[0], model_width), jnp.bfloat16),
        in_specs=vmem(2),
        out_specs=vmem()[0],
        compiler_params=PARAMS,
        cost_estimate=pl.CostEstimate(
            flops=100_000_000, bytes_accessed=3 << 20, transcendentals=0
        ),
        name="output",
    )(attended, pieces)


def reach_pairs(shards, shift):
    longest = shards // 2 + 1
    low = -(longest // 2)
    runs = (
        [i % shards for i in range(low, low + longest)],
        [i % shards for i in range(low + longest, low + shards)],
    )
    limits = (longest, shards - longest - 1)
    return [
        (run[i], run[i + shift])
        for run, limit in zip(runs, limits)
        if shift < limit
        for i in range(len(run) - shift)
    ]


def body(
    hidden,
    frozen_query,
    frozen_key,
    frozen_value,
    adapter_bank,
    request_shards,
    request_adapter,
    adapter_owner,
):
    shards = lax.axis_size("ctx")
    groups = lax.axis_size("groups")
    tokens, model_width = hidden.shape
    halves = 2 if groups == 2 and 2 * shards == ROW_BLOCKS * CHUNKS else 1
    own_half = lax.axis_index("groups") if halves == 2 else 0
    me = jnp.stack([lax.axis_index("ctx"), own_half]).astype(jnp.int32)
    parts = Parts(model_width, frozen_query.shape[1], frozen_key.shape[1])
    reach = shards // 2

    packed = pack(parts, halves, shards, me, adapter_bank)
    spread = lax.all_to_all(packed, "ctx", split_axis=0, concat_axis=0, tiled=True)

    tables = rope_tables(jnp.arange((reach + 1) * tokens, dtype=jnp.int32).reshape(-1, tokens))
    requests = jnp.stack([request_shards, request_adapter])[:, None]
    if halves == 2:
        theirs = lax.ppermute(requests, "groups", [(0, 1), (1, 0)])
        requests = jnp.concatenate([requests, theirs], axis=1)
    plan = make_plan(shards, reach, me, requests[0], requests[1], adapter_owner)
    spread, tables = lax.optimization_barrier((spread, tables))

    def collect(pieces):
        axes = ("groups", "ctx") if halves == 2 else "ctx"
        pieces = lax.all_to_all(pieces, axes, split_axis=0, concat_axis=0, tiled=True)
        return pieces.reshape((halves, shards) + pieces.shape[1:])[:, : ROW_BLOCKS * CHUNKS]

    kv_width, q_width, _ = parts.widths
    pieces = collect(route(plan, spread))
    kv = make_keys_values(plan, hidden, frozen_key, frozen_value, tables, pieces)
    blocks = [kv] + [
        lax.ppermute(kv, "ctx", reach_pairs(shards, shift)) for shift in range(1, reach + 1)
    ]
    queries = make_queries(plan, hidden, frozen_query, tables, pieces, kv_width)
    attended = attend(plan, queries, blocks)
    return attended, output_adapter(attended, pieces, model_width, kv_width + q_width)


def solution(mesh):
    return jax.shard_map(
        body,
        mesh=mesh,
        in_specs=(
            P(("groups", "ctx"), None),
            P(("groups", "ctx"), None),
            P(("groups", "ctx"), None),
            P(("groups", "ctx"), None),
            P("ctx", None, None),
            P("groups"),
            P("groups"),
            P(),
        ),
        out_specs=(P(("groups", "ctx"), None), P(("groups", "ctx"), None)),
        check_vma=False,
    )
```

```python
import functools

import jax
import jax.numpy as jnp
from jax import lax
from jax.experimental import pallas as pl
from jax.experimental.pallas import tpu as pltpu
from jax.sharding import PartitionSpec as P

HEAD_SIZE = 128
QUERY_HEADS = 16
KEY_VALUE_HEADS = 4
GROUP_SPLIT = QUERY_HEADS // KEY_VALUE_HEADS

adapter_scale = 0.5
rope_theta = 500000.0
score_masked = -1e30

VMEM_LIMIT = 24 * 1024 * 1024

ROW_BLOCKS = 4
CHUNKS = 8


def rope_tables(positions):
    half_dim = HEAD_SIZE // 2
    frequency = rope_theta ** (-(jnp.arange(half_dim, dtype=jnp.float32) * 2.0) / HEAD_SIZE)
    angles = positions.astype(jnp.float32)[..., None] * frequency
    cosines = jnp.cos(angles)
    sines = jnp.sin(angles)
    return (jnp.concatenate([cosines, cosines], -1), jnp.concatenate([-sines, sines], -1))


class Parts:
    def __init__(self, model_width, query_width, key_width):
        d, q, k = model_width, query_width, key_width
        up = 3 * d
        self.kv = ((d, d // CHUNKS), (2 * d, d // CHUNKS), (up + q, 2 * k // CHUNKS))
        self.q = ((0, d // CHUNKS), (up, q // CHUNKS))
        self.o = ((up + q + 2 * k, q // CHUNKS), (up + 2 * q + 2 * k, d // CHUNKS))
        self.all = self.kv + self.q + self.o
        self.widths = tuple(sum(w for _, w in part) for part in (self.kv, self.q, self.o))


def vmem(count=1):
    return [pl.BlockSpec(memory_space=pltpu.VMEM)] * count


def smem(count=1):
    return [pl.BlockSpec(memory_space=pltpu.SMEM)] * count


PARAMS = pltpu.CompilerParams(vmem_limit_bytes=VMEM_LIMIT)


OWN_INDEX, OWN_HALF, COUNT, ENTRY = 0, 1, 2, 8


def layout(lengths_ref, which, shards):
    starts, start, length = [jnp.int32(0)], jnp.int32(0), lengths_ref[which, 0]
    for r in range(1, lengths_ref.shape[1]):
        starts.append(starts[-1] + lengths_ref[which, r - 1])
        longer = lengths_ref[which, r] > length
        start = jnp.where(longer, starts[-1], start)
        length = jnp.where(longer, lengths_ref[which, r], length)
    return starts, start + lax.div(length, 2)


def plan_kernel(shards, reach, me_ref, lengths_ref, adapters_ref, owner_ref, out_ref):
    own_index, own_half = me_ref[0], me_ref[1]
    starts, offset = layout(lengths_ref, 0, shards)
    own_packed = lax.rem(own_index + offset, shards)
    first = jnp.int32(0)
    for start in starts[1:]:
        first = jnp.where(start <= own_packed, start, first)
    out_ref[OWN_INDEX] = own_index
    out_ref[OWN_HALF] = own_half
    out_ref[COUNT] = jnp.minimum(own_packed - first, reach) + 1
    for which in range(lengths_ref.shape[0]):
        starts, offset = layout(lengths_ref, which, shards)
        entries = [owner_ref[adapters_ref[which, r]] for r in range(len(starts))]
        at = ENTRY + shards * (own_half if which == 0 else 1 - own_half)
        for shard in range(shards):
            packed = lax.rem(shard + offset, shards)
            entry = entries[0]
            for start, later in zip(starts[1:], entries[1:]):
                entry = jnp.where(start <= packed, later, entry)
            out_ref[at + shard] = entry


def make_plan(shards, reach, me, lengths, adapters, owner):
    return pl.pallas_call(
        functools.partial(plan_kernel, shards, reach),
        out_shape=jax.ShapeDtypeStruct((ENTRY + lengths.shape[0] * shards,), jnp.int32),
        in_specs=smem(4),
        out_specs=smem()[0],
        name="plan",
    )(me, lengths, adapters, owner)


def pack_kernel(parts, halves, x_ref, bank_ref, out):
    own_half = x_ref[1]
    for block in range(out.shape[0]):
        piece = block % (ROW_BLOCKS * CHUNKS // halves)
        rows = pl.ds((piece % ROW_BLOCKS) * 16, 16)
        chunk = (piece // ROW_BLOCKS) * halves + own_half
        at = 0
        for first, width in parts.all:
            start = pl.multiple_of(first + chunk * width, 128)
            out[block, :, at : at + width] = bank_ref[0, rows, pl.ds(start, width)]
            at += width


def pack(parts, halves, shards, me, bank):
    width = sum(parts.widths)
    return pl.pallas_call(
        functools.partial(pack_kernel, parts, halves),
        out_shape=jax.ShapeDtypeStruct((shards, 16, width), bank.dtype),
        in_specs=smem() + vmem(),
        out_specs=vmem()[0],
        compiler_params=PARAMS,
        name="pack",
    )(me, bank)


ROUTE_STEPS = 4


def route_kernel(plan_ref, spread_ref, *outs):
    number = outs[0].shape[0]
    for i in range(number):
        entry = plan_ref[ENTRY + pl.program_id(0) * number + i]
        at = 0
        for out in outs:
            out[i] = spread_ref[entry, :, at : at + out.shape[2]]
            at += out.shape[2]


def route(plan, spread, first_width):
    dests = plan.shape[0] - ENTRY
    widths = (first_width, spread.shape[2] - first_width)
    return pl.pallas_call(
        route_kernel,
        out_shape=[jax.ShapeDtypeStruct((dests, 16, w), spread.dtype) for w in widths],
        grid=(ROUTE_STEPS,),
        in_specs=smem() + vmem(),
        out_specs=[
            pl.BlockSpec((dests // ROUTE_STEPS, 16, w), lambda i: (i, 0, 0)) for w in widths
        ],
        compiler_params=PARAMS,
        name="route",
    )(plan, spread)


def factor(piece_ref, chunk, at, width):
    halves = piece_ref.shape[0]
    place = chunk // halves * ROW_BLOCKS
    rows = piece_ref[chunk % halves, place : place + ROW_BLOCKS, :, at : at + width]
    return rows.reshape(ROW_BLOCKS * 16, width)


def columns(chunk, width):
    return slice(chunk * width, (chunk + 1) * width)


def dot_nt(a, b):
    return lax.dot_general(a, b, (((1,), (1,)), ((), ())), preferred_element_type=jnp.float32)


def turn(x, cosines, sines):
    return x * cosines + pltpu.roll(x, HEAD_SIZE // 2, 1) * sines


def kv_kernel(plan_ref, hidden_ref, key_ref, value_ref, cos_ref, sin_ref, piece_ref, out_ref):
    d = hidden_ref.shape[1] // CHUNKS
    rank = ROW_BLOCKS * 16
    low = jnp.zeros((hidden_ref.shape[0], 2 * rank), jnp.float32)
    for chunk in range(CHUNKS):
        down = jnp.concatenate(
            [factor(piece_ref, chunk, 0, d), factor(piece_ref, chunk, d, d)], axis=0
        )
        low += dot_nt(hidden_ref[:, columns(chunk, d)], down)
    low = low.astype(jnp.bfloat16)
    width = 2 * key_ref.shape[1] // CHUNKS
    own = plan_ref[COUNT] - 1
    cosines, sines = cos_ref[own], sin_ref[own]
    for chunk in range(CHUNKS):
        is_key = chunk < CHUNKS // 2
        up = factor(piece_ref, chunk, 2 * d, width)
        part = low[:, :rank] if is_key else low[:, rank:]
        update = jnp.dot(part, up, preferred_element_type=jnp.float32)
        frozen = (key_ref if is_key else value_ref)[:, columns(chunk % (CHUNKS // 2), width)]
        result = frozen.astype(jnp.float32) + adapter_scale * update
        if is_key:
            result = turn(result, cosines, sines)
        out_ref[:, columns(chunk, width)] = result.astype(jnp.bfloat16)


def make_keys_values(plan, hidden, key, value, tables, pieces):
    return pl.pallas_call(
        kv_kernel,
        out_shape=jax.ShapeDtypeStruct((key.shape[0], 2 * key.shape[1]), jnp.bfloat16),
        in_specs=smem() + vmem(6),
        out_specs=vmem()[0],
        compiler_params=PARAMS,
        cost_estimate=pl.CostEstimate(
            flops=150_000_000, bytes_accessed=3 << 20, transcendentals=0
        ),
        name="keys_values",
    )(plan, hidden, key, value, *tables, pieces)


def query_kernel(at, plan_ref, hidden_ref, query_ref, cos_ref, sin_ref, piece_ref, out_ref):
    tokens = query_ref.shape[0]
    d = hidden_ref.shape[1] // CHUNKS
    width = query_ref.shape[1] // CHUNKS
    low = jnp.zeros((tokens, ROW_BLOCKS * 16), jnp.float32)
    for chunk in range(CHUNKS):
        low += dot_nt(hidden_ref[:, columns(chunk, d)], factor(piece_ref, chunk, at, d))
    low = low.astype(jnp.bfloat16)
    own = plan_ref[COUNT] - 1
    cosines, sines = cos_ref[own], sin_ref[own]
    for chunk in range(CHUNKS):
        up = factor(piece_ref, chunk, at + d, width)
        update = jnp.dot(low, up, preferred_element_type=jnp.float32)
        result = query_ref[:, columns(chunk, width)].astype(jnp.float32) + adapter_scale * update
        for part in range(width // HEAD_SIZE):
            head = chunk * (width // HEAD_SIZE) + part
            turned = turn(result[:, columns(part, HEAD_SIZE)], cosines, sines)
            out_ref[head // GROUP_SPLIT, pl.ds((head % GROUP_SPLIT) * tokens, tokens)] = (
                turned.astype(jnp.bfloat16)
            )


def make_queries(plan, hidden, query, tables, pieces, at):
    tokens = hidden.shape[0]
    return pl.pallas_call(
        functools.partial(query_kernel, at),
        out_shape=jax.ShapeDtypeStruct(
            (KEY_VALUE_HEADS, GROUP_SPLIT * tokens, HEAD_SIZE), jnp.bfloat16
        ),
        in_specs=smem() + vmem(5),
        out_specs=vmem()[0],
        compiler_params=PARAMS,
        cost_estimate=pl.CostEstimate(
            flops=100_000_000, bytes_accessed=3 << 20, transcendentals=0
        ),
        name="queries",
    )(plan, hidden, query, *tables, pieces)


REGION = 5


def attend_kernel(steps, plan_ref, queries, *refs):
    blocks, (out_ref, copy_ref, high, acc) = refs[:-4], refs[-4:]
    count = plan_ref[COUNT]
    odd = lax.rem(plan_ref[OWN_INDEX], 2)
    aside = 2 * odd - 1
    steps = [s if even else s + aside for s, even in steps]
    tokens = out_ref.shape[0]
    rows = GROUP_SPLIT * tokens
    bf16 = jnp.bfloat16
    base2 = 1.4426950408889634 / (HEAD_SIZE**0.5)
    ones = jnp.ones((tokens, HEAD_SIZE), bf16)

    def region(first, number):
        shards = blocks[first : first + number]
        for g in range(KEY_VALUE_HEADS):
            keys = [b[:, columns(g, HEAD_SIZE)] for b in shards]
            values = [
                jnp.concatenate([b[:, columns(KEY_VALUE_HEADS + g, HEAD_SIZE)], ones], axis=1)
                for b in shards
            ]
            score = dot_nt(queries[g], jnp.concatenate(keys, axis=0))
            tiles = [score[:, columns(i, tokens)] for i in range(number)]
            if first == 0:
                row = lax.broadcasted_iota(jnp.int32, (rows, tokens), 0) % tokens
                column = lax.broadcasted_iota(jnp.int32, (rows, tokens), 1)
                tiles = [jnp.where(column <= row, tiles[0], score_masked)]
            else:
                tiles = [
                    jnp.where((step > 0) & (step < count), tile, score_masked)
                    for step, tile in zip(steps[first : first + number], tiles)
                ]
            top = functools.reduce(jnp.maximum, tiles)
            top = jnp.max(top, axis=1, keepdims=True) * base2
            top = jnp.broadcast_to(top, (rows, HEAD_SIZE))
            if first:
                old = high[g]
                top = jnp.maximum(old, top)
            weight = [jnp.exp2(t * base2 - top).astype(bf16) for t in tiles]
            blend = jnp.dot(
                jnp.concatenate(weight, axis=1),
                jnp.concatenate(values, axis=0),
                preferred_element_type=jnp.float32,
            )
            if first:
                shrink = jnp.exp2(old - top)
                blend += acc[g] * jnp.concatenate([shrink, shrink], axis=1)
            high[g] = top
            acc[g] = blend

    region(0, 1)
    for first in range(1, len(blocks), REGION):
        number = min(REGION, len(blocks) - first)
        nearest = functools.reduce(jnp.minimum, steps[first : first + number])
        pl.when(count > nearest)(functools.partial(region, first, number))

    for g in range(KEY_VALUE_HEADS):
        result = (acc[g, :, :HEAD_SIZE] / acc[g, :, HEAD_SIZE:]).astype(bf16)
        for j in range(GROUP_SPLIT):
            for ref in (out_ref, copy_ref):
                ref[:, columns(g * GROUP_SPLIT + j, HEAD_SIZE)] = result[columns(j, tokens)]


def attend(plan, queries, blocks, steps):
    tokens = blocks[0].shape[0]
    rows = GROUP_SPLIT * tokens
    limit = VMEM_LIMIT if len(blocks) < 16 else 2 * VMEM_LIMIT
    return pl.pallas_call(
        functools.partial(attend_kernel, steps),
        out_shape=[jax.ShapeDtypeStruct((tokens, QUERY_HEADS * HEAD_SIZE), jnp.bfloat16)] * 2,
        in_specs=smem() + vmem(1 + len(blocks)),
        out_specs=vmem(2),
        scratch_shapes=[
            pltpu.VMEM((KEY_VALUE_HEADS, rows, HEAD_SIZE), jnp.float32),
            pltpu.VMEM((KEY_VALUE_HEADS, rows, 2 * HEAD_SIZE), jnp.float32),
        ],
        compiler_params=pltpu.CompilerParams(vmem_limit_bytes=limit),
        cost_estimate=pl.CostEstimate(
            flops=2_000_000_000, bytes_accessed=8 << 20, transcendentals=4 << 20
        ),
        name="attend",
    )(plan, queries, *blocks)


def output_kernel(at, attended_ref, piece_ref, out_ref):
    q_head = attended_ref.shape[1] // CHUNKS
    d = out_ref.shape[1] // CHUNKS
    low = jnp.zeros((attended_ref.shape[0], ROW_BLOCKS * 16), jnp.float32)
    for chunk in range(CHUNKS):
        down = factor(piece_ref, chunk, at, q_head)
        low += dot_nt(attended_ref[:, columns(chunk, q_head)], down)
    low = low.astype(jnp.bfloat16)
    for chunk in range(CHUNKS):
        result = adapter_scale * jnp.dot(
            low, factor(piece_ref, chunk, at + q_head, d), preferred_element_type=jnp.float32
        )
        out_ref[:, columns(chunk, d)] = result.astype(jnp.bfloat16)


def output_adapter(attended, pieces, model_width, at):
    return pl.pallas_call(
        functools.partial(output_kernel, at),
        out_shape=jax.ShapeDtypeStruct((attended.shape[0], model_width), jnp.bfloat16),
        in_specs=vmem(2),
        out_specs=vmem()[0],
        compiler_params=PARAMS,
        cost_estimate=pl.CostEstimate(
            flops=100_000_000, bytes_accessed=3 << 20, transcendentals=0
        ),
        name="output",
    )(attended, pieces)


def earlier_shards(shards):
    longest = shards // 2 + 1
    low = -(longest // 2)
    runs = (
        [i % shards for i in range(low, low + longest)],
        [i % shards for i in range(low + longest, low + shards)],
    )
    limits = (longest, shards - longest - 1)
    earlier = {}
    for run, limit in zip(runs, limits):
        for i, shard in enumerate(run):
            earlier[shard] = set(run[max(0, i - limit + 1) : i])
    return earlier


def shift_pairs(shards, shift):
    earlier = earlier_shards(shards)
    pairs = [((d - shift) % shards, d) for d in range(shards)]
    return [(s, d) for s, d in pairs if s in earlier[d] or s in earlier[d ^ 1]]


def swap_pairs(shards, shift):
    earlier = earlier_shards(shards)
    return [(d, d ^ 1) for d in range(shards) if (d - shift) % shards in earlier[d ^ 1]]


def exchange(kv, shards, reach):
    shifts = range(0, reach + 1, 2)
    got = [kv] + [lax.ppermute(kv, "ctx", shift_pairs(shards, s)) for s in shifts[1:]]
    swapped = [lax.ppermute(b, "ctx", swap_pairs(shards, s)) for s, b in zip(shifts, got)]
    blocks, steps = [kv], [(0, True)]
    for s, even, odd in zip(shifts, got, swapped):
        if s:
            blocks.append(even)
            steps.append((s, True))
        blocks.append(odd)
        steps.append((s, False))
    return blocks, steps


def body(
    hidden,
    frozen_query,
    frozen_key,
    frozen_value,
    adapter_bank,
    request_shards,
    request_adapter,
    adapter_owner,
):
    shards = lax.axis_size("ctx")
    groups = lax.axis_size("groups")
    tokens, model_width = hidden.shape
    halves = 2 if groups == 2 and 2 * shards == ROW_BLOCKS * CHUNKS else 1
    own_half = lax.axis_index("groups") if halves == 2 else 0
    me = jnp.stack([lax.axis_index("ctx"), own_half]).astype(jnp.int32)
    parts = Parts(model_width, frozen_query.shape[1], frozen_key.shape[1])
    reach = shards // 2

    packed = pack(parts, halves, shards, me, adapter_bank)
    spread = lax.all_to_all(packed, "ctx", split_axis=0, concat_axis=0, tiled=True)

    tables = rope_tables(jnp.arange((reach + 1) * tokens, dtype=jnp.int32).reshape(-1, tokens))
    requests = jnp.stack([request_shards, request_adapter])[:, None]
    if halves == 2:
        theirs = lax.ppermute(requests, "groups", [(0, 1), (1, 0)])
        requests = jnp.concatenate([requests, theirs], axis=1)
    plan = make_plan(shards, reach, me, requests[0], requests[1], adapter_owner)
    spread, tables = lax.optimization_barrier((spread, tables))

    def collect(pieces):
        axes = ("groups", "ctx") if halves == 2 else "ctx"
        pieces = lax.all_to_all(pieces, axes, split_axis=0, concat_axis=0, tiled=True)
        return pieces.reshape((halves, shards) + pieces.shape[1:])[:, : ROW_BLOCKS * CHUNKS]

    kv_width, q_width, _ = parts.widths
    first, later = route(plan, spread, kv_width + q_width)
    pieces = collect(first)
    kv = make_keys_values(plan, hidden, frozen_key, frozen_value, tables, pieces)
    blocks, steps = exchange(kv, shards, reach)
    blocks[1], later = lax.optimization_barrier((blocks[1], later))
    later = collect(later)
    queries = make_queries(plan, hidden, frozen_query, tables, pieces, kv_width)
    attended, copy = attend(plan, queries, blocks, steps)
    return attended, output_adapter(copy, later, model_width, 0)


def solution(mesh):
    return jax.shard_map(
        body,
        mesh=mesh,
        in_specs=(
            P(("groups", "ctx"), None),
            P(("groups", "ctx"), None),
            P(("groups", "ctx"), None),
            P(("groups", "ctx"), None),
            P("ctx", None, None),
            P("groups"),
            P("groups"),
            P(),
        ),
        out_specs=(P(("groups", "ctx"), None), P(("groups", "ctx"), None)),
        check_vma=False,
    )
```

```python
import functools

import jax
import jax.numpy as jnp
from jax import lax
from jax.experimental import pallas as pl
from jax.experimental.pallas import tpu as pltpu
from jax.sharding import PartitionSpec as P

HEAD_SIZE = 128
QUERY_HEADS = 16
KEY_VALUE_HEADS = 4
GROUP_SPLIT = QUERY_HEADS // KEY_VALUE_HEADS

adapter_scale = 0.5
rope_theta = 500000.0
score_masked = -1e30

VMEM_LIMIT = 24 * 1024 * 1024

ROW_BLOCKS = 4
CHUNKS = 8


def rope_tables(positions):
    half_dim = HEAD_SIZE // 2
    frequency = rope_theta ** (-(jnp.arange(half_dim, dtype=jnp.float32) * 2.0) / HEAD_SIZE)
    angles = positions.astype(jnp.float32)[..., None] * frequency
    cosines = jnp.cos(angles)
    sines = jnp.sin(angles)
    return (jnp.concatenate([cosines, cosines], -1), jnp.concatenate([-sines, sines], -1))


class Parts:
    def __init__(self, model_width, query_width, key_width):
        d, q, k = model_width, query_width, key_width
        up = 3 * d
        self.kv = ((d, d // CHUNKS), (2 * d, d // CHUNKS), (up + q, 2 * k // CHUNKS))
        self.q = ((0, d // CHUNKS), (up, q // CHUNKS))
        self.o = ((up + q + 2 * k, q // CHUNKS), (up + 2 * q + 2 * k, d // CHUNKS))
        self.all = self.kv + self.q + self.o
        self.widths = tuple(sum(w for _, w in part) for part in (self.kv, self.q, self.o))


def vmem(count=1):
    return [pl.BlockSpec(memory_space=pltpu.VMEM)] * count


def smem(count=1):
    return [pl.BlockSpec(memory_space=pltpu.SMEM)] * count


PARAMS = pltpu.CompilerParams(vmem_limit_bytes=VMEM_LIMIT)


OWN_INDEX, OWN_HALF, COUNT, ENTRY = 0, 1, 2, 8


def layout(lengths_ref, which, shards):
    starts, start, length = [jnp.int32(0)], jnp.int32(0), lengths_ref[which, 0]
    for r in range(1, lengths_ref.shape[1]):
        starts.append(starts[-1] + lengths_ref[which, r - 1])
        longer = lengths_ref[which, r] > length
        start = jnp.where(longer, starts[-1], start)
        length = jnp.where(longer, lengths_ref[which, r], length)
    return starts, start + lax.div(length, 2)


def plan_kernel(shards, reach, me_ref, lengths_ref, adapters_ref, owner_ref, out_ref):
    own_index, own_half = me_ref[0], me_ref[1]
    starts, offset = layout(lengths_ref, 0, shards)
    own_packed = lax.rem(own_index + offset, shards)
    first = jnp.int32(0)
    for start in starts[1:]:
        first = jnp.where(start <= own_packed, start, first)
    out_ref[OWN_INDEX] = own_index
    out_ref[OWN_HALF] = own_half
    out_ref[COUNT] = jnp.minimum(own_packed - first, reach) + 1
    for which in range(lengths_ref.shape[0]):
        starts, offset = layout(lengths_ref, which, shards)
        entries = [owner_ref[adapters_ref[which, r]] for r in range(len(starts))]
        at = ENTRY + shards * (own_half if which == 0 else 1 - own_half)
        for shard in range(shards):
            packed = lax.rem(shard + offset, shards)
            entry = entries[0]
            for start, later in zip(starts[1:], entries[1:]):
                entry = jnp.where(start <= packed, later, entry)
            out_ref[at + shard] = entry


def make_plan(shards, reach, me, lengths, adapters, owner):
    return pl.pallas_call(
        functools.partial(plan_kernel, shards, reach),
        out_shape=jax.ShapeDtypeStruct((ENTRY + lengths.shape[0] * shards,), jnp.int32),
        in_specs=smem(4),
        out_specs=smem()[0],
        name="plan",
    )(me, lengths, adapters, owner)


def pack_kernel(parts, halves, x_ref, bank_ref, out):
    own_half = x_ref[1]
    for block in range(out.shape[0]):
        piece = block % (ROW_BLOCKS * CHUNKS // halves)
        rows = pl.ds((piece % ROW_BLOCKS) * 16, 16)
        chunk = (piece // ROW_BLOCKS) * halves + own_half
        at = 0
        for first, width in parts.all:
            start = pl.multiple_of(first + chunk * width, 128)
            out[block, :, at : at + width] = bank_ref[0, rows, pl.ds(start, width)]
            at += width


def pack(parts, halves, shards, me, bank):
    width = sum(parts.widths)
    return pl.pallas_call(
        functools.partial(pack_kernel, parts, halves),
        out_shape=jax.ShapeDtypeStruct((shards, 16, width), bank.dtype),
        in_specs=smem() + vmem(),
        out_specs=vmem()[0],
        compiler_params=PARAMS,
        name="pack",
    )(me, bank)


ROUTE_STEPS = 4


def route_kernel(plan_ref, spread_ref, *outs):
    number = outs[0].shape[0]
    for i in range(number):
        entry = plan_ref[ENTRY + pl.program_id(0) * number + i]
        at = 0
        for out in outs:
            out[i] = spread_ref[entry, :, at : at + out.shape[2]]
            at += out.shape[2]


def route(plan, spread, first_width):
    dests = plan.shape[0] - ENTRY
    widths = (first_width, spread.shape[2] - first_width)
    return pl.pallas_call(
        route_kernel,
        out_shape=[jax.ShapeDtypeStruct((dests, 16, w), spread.dtype) for w in widths],
        grid=(ROUTE_STEPS,),
        in_specs=smem() + vmem(),
        out_specs=[
            pl.BlockSpec((dests // ROUTE_STEPS, 16, w), lambda i: (i, 0, 0)) for w in widths
        ],
        compiler_params=PARAMS,
        name="route",
    )(plan, spread)


def factor(piece_ref, chunk, at, width):
    halves = piece_ref.shape[0]
    place = chunk // halves * ROW_BLOCKS
    rows = piece_ref[chunk % halves, place : place + ROW_BLOCKS, :, at : at + width]
    return rows.reshape(ROW_BLOCKS * 16, width)


def columns(chunk, width):
    return slice(chunk * width, (chunk + 1) * width)


def dot_nt(a, b):
    return lax.dot_general(a, b, (((1,), (1,)), ((), ())), preferred_element_type=jnp.float32)


def turn(x, cosines, sines):
    return x * cosines + pltpu.roll(x, HEAD_SIZE // 2, 1) * sines


def kv_kernel(plan_ref, hidden_ref, key_ref, value_ref, cos_ref, sin_ref, piece_ref, out_ref):
    d = hidden_ref.shape[1] // CHUNKS
    rank = ROW_BLOCKS * 16
    low = jnp.zeros((hidden_ref.shape[0], 2 * rank), jnp.float32)
    for chunk in range(CHUNKS):
        down = jnp.concatenate(
            [factor(piece_ref, chunk, 0, d), factor(piece_ref, chunk, d, d)], axis=0
        )
        low += dot_nt(hidden_ref[:, columns(chunk, d)], down)
    low = low.astype(jnp.bfloat16)
    width = 2 * key_ref.shape[1] // CHUNKS
    own = plan_ref[COUNT] - 1
    cosines, sines = cos_ref[own], sin_ref[own]
    for chunk in range(CHUNKS):
        is_key = chunk < CHUNKS // 2
        up = factor(piece_ref, chunk, 2 * d, width)
        part = low[:, :rank] if is_key else low[:, rank:]
        update = jnp.dot(part, up, preferred_element_type=jnp.float32)
        frozen = (key_ref if is_key else value_ref)[:, columns(chunk % (CHUNKS // 2), width)]
        result = frozen.astype(jnp.float32) + adapter_scale * update
        if is_key:
            result = turn(result, cosines, sines)
        out_ref[:, columns(chunk, width)] = result.astype(jnp.bfloat16)


def make_keys_values(plan, hidden, key, value, tables, pieces):
    return pl.pallas_call(
        kv_kernel,
        out_shape=jax.ShapeDtypeStruct((key.shape[0], 2 * key.shape[1]), jnp.bfloat16),
        in_specs=smem() + vmem(6),
        out_specs=vmem()[0],
        compiler_params=PARAMS,
        cost_estimate=pl.CostEstimate(
            flops=150_000_000, bytes_accessed=3 << 20, transcendentals=0
        ),
        name="keys_values",
    )(plan, hidden, key, value, *tables, pieces)


def query_kernel(at, plan_ref, hidden_ref, query_ref, cos_ref, sin_ref, piece_ref, out_ref):
    tokens = query_ref.shape[0]
    d = hidden_ref.shape[1] // CHUNKS
    width = query_ref.shape[1] // CHUNKS
    low = jnp.zeros((tokens, ROW_BLOCKS * 16), jnp.float32)
    for chunk in range(CHUNKS):
        low += dot_nt(hidden_ref[:, columns(chunk, d)], factor(piece_ref, chunk, at, d))
    low = low.astype(jnp.bfloat16)
    own = plan_ref[COUNT] - 1
    cosines, sines = cos_ref[own], sin_ref[own]
    for chunk in range(CHUNKS):
        up = factor(piece_ref, chunk, at + d, width)
        update = jnp.dot(low, up, preferred_element_type=jnp.float32)
        result = query_ref[:, columns(chunk, width)].astype(jnp.float32) + adapter_scale * update
        for part in range(width // HEAD_SIZE):
            head = chunk * (width // HEAD_SIZE) + part
            turned = turn(result[:, columns(part, HEAD_SIZE)], cosines, sines)
            out_ref[head // GROUP_SPLIT, pl.ds((head % GROUP_SPLIT) * tokens, tokens)] = (
                turned.astype(jnp.bfloat16)
            )


def make_queries(plan, hidden, query, tables, pieces, at):
    tokens = hidden.shape[0]
    return pl.pallas_call(
        functools.partial(query_kernel, at),
        out_shape=jax.ShapeDtypeStruct(
            (KEY_VALUE_HEADS, GROUP_SPLIT * tokens, HEAD_SIZE), jnp.bfloat16
        ),
        in_specs=smem() + vmem(5),
        out_specs=vmem()[0],
        compiler_params=PARAMS,
        cost_estimate=pl.CostEstimate(
            flops=100_000_000, bytes_accessed=3 << 20, transcendentals=0
        ),
        name="queries",
    )(plan, hidden, query, *tables, pieces)


REGION = 5


def attend_kernel(steps, plan_ref, queries, *refs):
    blocks, (out_ref, copy_ref, high, acc) = refs[:-4], refs[-4:]
    count = plan_ref[COUNT]
    odd = lax.rem(plan_ref[OWN_INDEX], 2)
    aside = 2 * odd - 1
    steps = [s if even else s + aside for s, even in steps]
    tokens = out_ref.shape[0]
    rows = GROUP_SPLIT * tokens
    bf16 = jnp.bfloat16
    base2 = 1.4426950408889634 / (HEAD_SIZE**0.5)
    ones = jnp.ones((tokens, HEAD_SIZE), bf16)

    def region(first, number):
        shards = blocks[first : first + number]
        for g in range(KEY_VALUE_HEADS):
            keys = [b[:, columns(g, HEAD_SIZE)] for b in shards]
            values = [
                jnp.concatenate([b[:, columns(KEY_VALUE_HEADS + g, HEAD_SIZE)], ones], axis=1)
                for b in shards
            ]
            score = dot_nt(queries[g], jnp.concatenate(keys, axis=0))
            tiles = [score[:, columns(i, tokens)] for i in range(number)]
            if first == 0:
                row = lax.broadcasted_iota(jnp.int32, (rows, tokens), 0) % tokens
                column = lax.broadcasted_iota(jnp.int32, (rows, tokens), 1)
                tiles = [jnp.where(column <= row, tiles[0], score_masked)]
            else:
                tiles = [
                    jnp.where((step > 0) & (step < count), tile, score_masked)
                    for step, tile in zip(steps[first : first + number], tiles)
                ]
            top = functools.reduce(jnp.maximum, tiles)
            top = jnp.max(top, axis=1, keepdims=True) * base2
            top = jnp.broadcast_to(top, (rows, HEAD_SIZE))
            if first:
                old = high[g]
                top = jnp.maximum(old, top)
            weight = [jnp.exp2(t * base2 - top).astype(bf16) for t in tiles]
            blend = jnp.dot(
                jnp.concatenate(weight, axis=1),
                jnp.concatenate(values, axis=0),
                preferred_element_type=jnp.float32,
            )
            if first:
                shrink = jnp.exp2(old - top)
                blend += acc[g] * jnp.concatenate([shrink, shrink], axis=1)
            high[g] = top
            acc[g] = blend

    region(0, 1)
    for first in range(1, len(blocks), REGION):
        number = min(REGION, len(blocks) - first)
        nearest = functools.reduce(jnp.minimum, steps[first : first + number])
        pl.when(count > nearest)(functools.partial(region, first, number))

    for g in range(KEY_VALUE_HEADS):
        result = (acc[g, :, :HEAD_SIZE] / acc[g, :, HEAD_SIZE:]).astype(bf16)
        for j in range(GROUP_SPLIT):
            for ref in (out_ref, copy_ref):
                ref[:, columns(g * GROUP_SPLIT + j, HEAD_SIZE)] = result[columns(j, tokens)]


def attend(plan, queries, blocks, steps):
    tokens = blocks[0].shape[0]
    rows = GROUP_SPLIT * tokens
    limit = VMEM_LIMIT if len(blocks) < 16 else 2 * VMEM_LIMIT
    return pl.pallas_call(
        functools.partial(attend_kernel, steps),
        out_shape=[jax.ShapeDtypeStruct((tokens, QUERY_HEADS * HEAD_SIZE), jnp.bfloat16)] * 2,
        in_specs=smem() + vmem(1 + len(blocks)),
        out_specs=vmem(2),
        scratch_shapes=[
            pltpu.VMEM((KEY_VALUE_HEADS, rows, HEAD_SIZE), jnp.float32),
            pltpu.VMEM((KEY_VALUE_HEADS, rows, 2 * HEAD_SIZE), jnp.float32),
        ],
        compiler_params=pltpu.CompilerParams(vmem_limit_bytes=limit),
        cost_estimate=pl.CostEstimate(
            flops=200_000_000_000, bytes_accessed=8 << 20, transcendentals=4 << 20
        ),
        name="attend",
    )(plan, queries, *blocks)


def output_kernel(at, attended_ref, piece_ref, out_ref):
    q_head = attended_ref.shape[1] // CHUNKS
    d = out_ref.shape[1] // CHUNKS
    low = jnp.zeros((attended_ref.shape[0], ROW_BLOCKS * 16), jnp.float32)
    for chunk in range(CHUNKS):
        down = factor(piece_ref, chunk, at, q_head)
        low += dot_nt(attended_ref[:, columns(chunk, q_head)], down)
    low = low.astype(jnp.bfloat16)
    for chunk in range(CHUNKS):
        result = adapter_scale * jnp.dot(
            low, factor(piece_ref, chunk, at + q_head, d), preferred_element_type=jnp.float32
        )
        out_ref[:, columns(chunk, d)] = result.astype(jnp.bfloat16)


def output_adapter(attended, pieces, model_width, at):
    return pl.pallas_call(
        functools.partial(output_kernel, at),
        out_shape=jax.ShapeDtypeStruct((attended.shape[0], model_width), jnp.bfloat16),
        in_specs=vmem(2),
        out_specs=vmem()[0],
        compiler_params=PARAMS,
        cost_estimate=pl.CostEstimate(
            flops=100_000_000, bytes_accessed=3 << 20, transcendentals=0
        ),
        name="output",
    )(attended, pieces)


def earlier_shards(shards):
    longest = shards // 2 + 1
    low = -(longest // 2)
    runs = (
        [i % shards for i in range(low, low + longest)],
        [i % shards for i in range(low + longest, low + shards)],
    )
    limits = (longest, shards - longest - 1)
    earlier = {}
    for run, limit in zip(runs, limits):
        for i, shard in enumerate(run):
            earlier[shard] = set(run[max(0, i - limit + 1) : i])
    return earlier


def shift_pairs(shards, shift):
    earlier = earlier_shards(shards)
    pairs = [((d - shift) % shards, d) for d in range(shards)]
    return [(s, d) for s, d in pairs if s in earlier[d] or s in earlier[d ^ 1]]


def swap_pairs(shards, shift):
    earlier = earlier_shards(shards)
    return [(d, d ^ 1) for d in range(shards) if (d - shift) % shards in earlier[d ^ 1]]


def exchange(kv, queries, shards, reach):
    shifts = range(0, reach + 1, 2)
    got = [kv] + [lax.ppermute(kv, "ctx", shift_pairs(shards, s)) for s in shifts[1:]]
    got[1:], queries = lax.optimization_barrier((got[1:], queries))
    swapped = [lax.ppermute(b, "ctx", swap_pairs(shards, s)) for s, b in zip(shifts, got)]
    blocks, steps = [kv], [(0, True)]
    for s, even, odd in zip(shifts, got, swapped):
        if s:
            blocks.append(even)
            steps.append((s, True))
        blocks.append(odd)
        steps.append((s, False))
    return blocks, steps, queries


def body(
    hidden,
    frozen_query,
    frozen_key,
    frozen_value,
    adapter_bank,
    request_shards,
    request_adapter,
    adapter_owner,
):
    shards = lax.axis_size("ctx")
    groups = lax.axis_size("groups")
    tokens, model_width = hidden.shape
    halves = 2 if groups == 2 and 2 * shards == ROW_BLOCKS * CHUNKS else 1
    own_half = lax.axis_index("groups") if halves == 2 else 0
    me = jnp.stack([lax.axis_index("ctx"), own_half]).astype(jnp.int32)
    parts = Parts(model_width, frozen_query.shape[1], frozen_key.shape[1])
    reach = shards // 2

    packed = pack(parts, halves, shards, me, adapter_bank)
    spread = lax.all_to_all(packed, "ctx", split_axis=0, concat_axis=0, tiled=True)

    tables = rope_tables(jnp.arange((reach + 1) * tokens, dtype=jnp.int32).reshape(-1, tokens))
    requests = jnp.stack([request_shards, request_adapter])[:, None]
    if halves == 2:
        theirs = lax.ppermute(requests, "groups", [(0, 1), (1, 0)])
        requests = jnp.concatenate([requests, theirs], axis=1)
    plan = make_plan(shards, reach, me, requests[0], requests[1], adapter_owner)
    spread, tables = lax.optimization_barrier((spread, tables))

    def collect(pieces):
        axes = ("groups", "ctx") if halves == 2 else "ctx"
        pieces = lax.all_to_all(pieces, axes, split_axis=0, concat_axis=0, tiled=True)
        return pieces.reshape((halves, shards) + pieces.shape[1:])[:, : ROW_BLOCKS * CHUNKS]

    kv_width, q_width, _ = parts.widths
    first, later = route(plan, spread, kv_width + q_width)
    pieces = collect(first)
    kv = make_keys_values(plan, hidden, frozen_key, frozen_value, tables, pieces)
    queries = make_queries(plan, hidden, frozen_query, tables, pieces, kv_width)
    blocks, steps, queries = exchange(kv, queries, shards, reach)
    blocks[1], later = lax.optimization_barrier((blocks[1], later))
    later = collect(later)
    attended, copy = attend(plan, queries, blocks, steps)
    return attended, output_adapter(copy, later, model_width, 0)


def solution(mesh):
    return jax.shard_map(
        body,
        mesh=mesh,
        in_specs=(
            P(("groups", "ctx"), None),
            P(("groups", "ctx"), None),
            P(("groups", "ctx"), None),
            P(("groups", "ctx"), None),
            P("ctx", None, None),
            P("groups"),
            P("groups"),
            P(),
        ),
        out_specs=(P(("groups", "ctx"), None), P(("groups", "ctx"), None)),
        check_vma=False,
    )
```

```python
import functools

import jax
import jax.numpy as jnp
from jax import lax
from jax.experimental import pallas as pl
from jax.experimental.pallas import tpu as pltpu
from jax.sharding import PartitionSpec as P

HEAD_SIZE = 128
QUERY_HEADS = 16
KEY_VALUE_HEADS = 4
GROUP_SPLIT = QUERY_HEADS // KEY_VALUE_HEADS

adapter_scale = 0.5
rope_theta = 500000.0
score_masked = -1e30

VMEM_LIMIT = 24 * 1024 * 1024

ROW_BLOCKS = 4
CHUNKS = 8


def rope_tables(positions):
    half_dim = HEAD_SIZE // 2
    frequency = rope_theta ** (-(jnp.arange(half_dim, dtype=jnp.float32) * 2.0) / HEAD_SIZE)
    angles = positions.astype(jnp.float32)[..., None] * frequency
    cosines = jnp.cos(angles)
    sines = jnp.sin(angles)
    return (jnp.concatenate([cosines, cosines], -1), jnp.concatenate([-sines, sines], -1))


class Parts:
    def __init__(self, model_width, query_width, key_width):
        d, q, k = model_width, query_width, key_width
        up = 3 * d
        self.kv = ((d, d // CHUNKS), (2 * d, d // CHUNKS), (up + q, 2 * k // CHUNKS))
        self.q = ((0, d // CHUNKS), (up, q // CHUNKS))
        self.o = ((up + q + 2 * k, q // CHUNKS), (up + 2 * q + 2 * k, d // CHUNKS))
        self.all = self.kv + self.q + self.o
        self.widths = tuple(sum(w for _, w in part) for part in (self.kv, self.q, self.o))


def vmem(count=1):
    return [pl.BlockSpec(memory_space=pltpu.VMEM)] * count


def smem(count=1):
    return [pl.BlockSpec(memory_space=pltpu.SMEM)] * count


PARAMS = pltpu.CompilerParams(vmem_limit_bytes=VMEM_LIMIT)


OWN_INDEX, OWN_HALF, COUNT, ENTRY = 0, 1, 2, 8


def layout(lengths_ref, which, shards):
    starts, start, length = [jnp.int32(0)], jnp.int32(0), lengths_ref[which, 0]
    for r in range(1, lengths_ref.shape[1]):
        starts.append(starts[-1] + lengths_ref[which, r - 1])
        longer = lengths_ref[which, r] > length
        start = jnp.where(longer, starts[-1], start)
        length = jnp.where(longer, lengths_ref[which, r], length)
    return starts, start + lax.div(length, 2)


def plan_kernel(shards, reach, me_ref, lengths_ref, adapters_ref, owner_ref, out_ref):
    own_index, own_half = me_ref[0], me_ref[1]
    starts, offset = layout(lengths_ref, 0, shards)
    own_packed = lax.rem(own_index + offset, shards)
    first = jnp.int32(0)
    for start in starts[1:]:
        first = jnp.where(start <= own_packed, start, first)
    out_ref[OWN_INDEX] = own_index
    out_ref[OWN_HALF] = own_half
    out_ref[COUNT] = jnp.minimum(own_packed - first, reach) + 1
    for which in range(lengths_ref.shape[0]):
        starts, offset = layout(lengths_ref, which, shards)
        entries = [owner_ref[adapters_ref[which, r]] for r in range(len(starts))]
        at = ENTRY + shards * (own_half if which == 0 else 1 - own_half)
        for shard in range(shards):
            packed = lax.rem(shard + offset, shards)
            entry = entries[0]
            for start, later in zip(starts[1:], entries[1:]):
                entry = jnp.where(start <= packed, later, entry)
            out_ref[at + shard] = entry


def make_plan(shards, reach, me, lengths, adapters, owner):
    return pl.pallas_call(
        functools.partial(plan_kernel, shards, reach),
        out_shape=jax.ShapeDtypeStruct((ENTRY + lengths.shape[0] * shards,), jnp.int32),
        in_specs=smem(4),
        out_specs=smem()[0],
        name="plan",
    )(me, lengths, adapters, owner)


def pack_kernel(parts, halves, x_ref, bank_ref, out):
    own_half = x_ref[1]
    for block in range(out.shape[0]):
        piece = block % (ROW_BLOCKS * CHUNKS // halves)
        rows = pl.ds((piece % ROW_BLOCKS) * 16, 16)
        chunk = (piece // ROW_BLOCKS) * halves + own_half
        at = 0
        for first, width in parts.all:
            start = pl.multiple_of(first + chunk * width, 128)
            out[block, :, at : at + width] = bank_ref[0, rows, pl.ds(start, width)]
            at += width


def pack(parts, halves, shards, me, bank):
    width = sum(parts.widths)
    return pl.pallas_call(
        functools.partial(pack_kernel, parts, halves),
        out_shape=jax.ShapeDtypeStruct((shards, 16, width), bank.dtype),
        in_specs=smem() + vmem(),
        out_specs=vmem()[0],
        compiler_params=PARAMS,
        name="pack",
    )(me, bank)


ROUTE_STEPS = 4


def route_kernel(plan_ref, spread_ref, *outs):
    number = outs[0].shape[0]
    for i in range(number):
        entry = plan_ref[ENTRY + pl.program_id(0) * number + i]
        at = 0
        for out in outs:
            out[i] = spread_ref[entry, :, at : at + out.shape[2]]
            at += out.shape[2]


def route(plan, spread, first_width):
    dests = plan.shape[0] - ENTRY
    widths = (first_width, spread.shape[2] - first_width)
    return pl.pallas_call(
        route_kernel,
        out_shape=[jax.ShapeDtypeStruct((dests, 16, w), spread.dtype) for w in widths],
        grid=(ROUTE_STEPS,),
        in_specs=smem() + vmem(),
        out_specs=[
            pl.BlockSpec((dests // ROUTE_STEPS, 16, w), lambda i: (i, 0, 0)) for w in widths
        ],
        compiler_params=PARAMS,
        name="route",
    )(plan, spread)


def factor(piece_ref, chunk, at, width):
    halves = piece_ref.shape[0]
    place = chunk // halves * ROW_BLOCKS
    rows = piece_ref[chunk % halves, place : place + ROW_BLOCKS, :, at : at + width]
    return rows.reshape(ROW_BLOCKS * 16, width)


def columns(chunk, width):
    return slice(chunk * width, (chunk + 1) * width)


def dot_nt(a, b):
    return lax.dot_general(a, b, (((1,), (1,)), ((), ())), preferred_element_type=jnp.float32)


def turn(x, cosines, sines):
    return x * cosines + pltpu.roll(x, HEAD_SIZE // 2, 1) * sines


def kv_kernel(plan_ref, hidden_ref, key_ref, value_ref, cos_ref, sin_ref, piece_ref, out_ref):
    d = hidden_ref.shape[1] // CHUNKS
    rank = ROW_BLOCKS * 16
    low = jnp.zeros((hidden_ref.shape[0], 2 * rank), jnp.float32)
    for chunk in range(CHUNKS):
        down = jnp.concatenate(
            [factor(piece_ref, chunk, 0, d), factor(piece_ref, chunk, d, d)], axis=0
        )
        low += dot_nt(hidden_ref[:, columns(chunk, d)], down)
    low = low.astype(jnp.bfloat16)
    width = 2 * key_ref.shape[1] // CHUNKS
    own = plan_ref[COUNT] - 1
    cosines, sines = cos_ref[own], sin_ref[own]
    for chunk in range(CHUNKS):
        is_key = chunk < CHUNKS // 2
        up = factor(piece_ref, chunk, 2 * d, width)
        part = low[:, :rank] if is_key else low[:, rank:]
        update = jnp.dot(part, up, preferred_element_type=jnp.float32)
        frozen = (key_ref if is_key else value_ref)[:, columns(chunk % (CHUNKS // 2), width)]
        result = frozen.astype(jnp.float32) + adapter_scale * update
        if is_key:
            result = turn(result, cosines, sines)
        out_ref[:, columns(chunk, width)] = result.astype(jnp.bfloat16)


def make_keys_values(plan, hidden, key, value, tables, pieces):
    return pl.pallas_call(
        kv_kernel,
        out_shape=jax.ShapeDtypeStruct((key.shape[0], 2 * key.shape[1]), jnp.bfloat16),
        in_specs=smem() + vmem(6),
        out_specs=vmem()[0],
        compiler_params=PARAMS,
        cost_estimate=pl.CostEstimate(
            flops=150_000_000, bytes_accessed=3 << 20, transcendentals=0
        ),
        name="keys_values",
    )(plan, hidden, key, value, *tables, pieces)


def query_kernel(at, plan_ref, hidden_ref, query_ref, cos_ref, sin_ref, piece_ref, out_ref):
    tokens = query_ref.shape[0]
    d = hidden_ref.shape[1] // CHUNKS
    width = query_ref.shape[1] // CHUNKS
    low = jnp.zeros((tokens, ROW_BLOCKS * 16), jnp.float32)
    for chunk in range(CHUNKS):
        low += dot_nt(hidden_ref[:, columns(chunk, d)], factor(piece_ref, chunk, at, d))
    low = low.astype(jnp.bfloat16)
    own = plan_ref[COUNT] - 1
    cosines, sines = cos_ref[own], sin_ref[own]
    for chunk in range(CHUNKS):
        up = factor(piece_ref, chunk, at + d, width)
        update = jnp.dot(low, up, preferred_element_type=jnp.float32)
        result = query_ref[:, columns(chunk, width)].astype(jnp.float32) + adapter_scale * update
        for part in range(width // HEAD_SIZE):
            head = chunk * (width // HEAD_SIZE) + part
            turned = turn(result[:, columns(part, HEAD_SIZE)], cosines, sines)
            out_ref[head // GROUP_SPLIT, pl.ds((head % GROUP_SPLIT) * tokens, tokens)] = (
                turned.astype(jnp.bfloat16)
            )


def make_queries(plan, hidden, query, tables, pieces, at):
    tokens = hidden.shape[0]
    return pl.pallas_call(
        functools.partial(query_kernel, at),
        out_shape=jax.ShapeDtypeStruct(
            (KEY_VALUE_HEADS, GROUP_SPLIT * tokens, HEAD_SIZE), jnp.bfloat16
        ),
        in_specs=smem() + vmem(5),
        out_specs=vmem()[0],
        compiler_params=PARAMS,
        cost_estimate=pl.CostEstimate(
            flops=100_000_000, bytes_accessed=3 << 20, transcendentals=0
        ),
        name="queries",
    )(plan, hidden, query, *tables, pieces)


REGION = 5


def attend_kernel(steps, plan_ref, queries, *refs):
    blocks, (out_ref, copy_ref, high, acc) = refs[:-4], refs[-4:]
    count = plan_ref[COUNT]
    odd = lax.rem(plan_ref[OWN_INDEX], 2)
    aside = 2 * odd - 1
    steps = [s if even else s + aside for s, even in steps]
    tokens = out_ref.shape[0]
    rows = GROUP_SPLIT * tokens
    bf16 = jnp.bfloat16
    base2 = 1.4426950408889634 / (HEAD_SIZE**0.5)
    ones = jnp.ones((tokens, HEAD_SIZE), bf16)

    def region(first, number):
        shards = blocks[first : first + number]
        for g in range(KEY_VALUE_HEADS):
            keys = [b[:, columns(g, HEAD_SIZE)] for b in shards]
            values = [
                jnp.concatenate([b[:, columns(KEY_VALUE_HEADS + g, HEAD_SIZE)], ones], axis=1)
                for b in shards
            ]
            score = dot_nt(queries[g], jnp.concatenate(keys, axis=0))
            tiles = [score[:, columns(i, tokens)] for i in range(number)]
            if first == 0:
                row = lax.broadcasted_iota(jnp.int32, (rows, tokens), 0) % tokens
                column = lax.broadcasted_iota(jnp.int32, (rows, tokens), 1)
                tiles = [jnp.where(column <= row, tiles[0], score_masked)]
            else:
                tiles = [
                    jnp.where((step > 0) & (step < count), tile, score_masked)
                    for step, tile in zip(steps[first : first + number], tiles)
                ]
            top = functools.reduce(jnp.maximum, tiles)
            top = jnp.max(top, axis=1, keepdims=True) * base2
            top = jnp.broadcast_to(top, (rows, HEAD_SIZE))
            if first:
                old = high[g]
                top = jnp.maximum(old, top)
            weight = [jnp.exp2(t * base2 - top).astype(bf16) for t in tiles]
            blend = jnp.dot(
                jnp.concatenate(weight, axis=1),
                jnp.concatenate(values, axis=0),
                preferred_element_type=jnp.float32,
            )
            if first:
                shrink = jnp.exp2(old - top)
                blend += acc[g] * jnp.concatenate([shrink, shrink], axis=1)
            high[g] = top
            acc[g] = blend

    region(0, 1)
    for first in range(1, len(blocks), REGION):
        number = min(REGION, len(blocks) - first)
        nearest = functools.reduce(jnp.minimum, steps[first : first + number])
        pl.when(count > nearest)(functools.partial(region, first, number))

    for g in range(KEY_VALUE_HEADS):
        result = (acc[g, :, :HEAD_SIZE] / acc[g, :, HEAD_SIZE:]).astype(bf16)
        for j in range(GROUP_SPLIT):
            for ref in (out_ref, copy_ref):
                ref[:, columns(g * GROUP_SPLIT + j, HEAD_SIZE)] = result[columns(j, tokens)]


def attend(plan, queries, blocks, steps):
    tokens = blocks[0].shape[0]
    rows = GROUP_SPLIT * tokens
    limit = VMEM_LIMIT if len(blocks) < 16 else 2 * VMEM_LIMIT
    return pl.pallas_call(
        functools.partial(attend_kernel, steps),
        out_shape=[jax.ShapeDtypeStruct((tokens, QUERY_HEADS * HEAD_SIZE), jnp.bfloat16)] * 2,
        in_specs=smem() + vmem(1 + len(blocks)),
        out_specs=vmem(2),
        scratch_shapes=[
            pltpu.VMEM((KEY_VALUE_HEADS, rows, HEAD_SIZE), jnp.float32),
            pltpu.VMEM((KEY_VALUE_HEADS, rows, 2 * HEAD_SIZE), jnp.float32),
        ],
        compiler_params=pltpu.CompilerParams(vmem_limit_bytes=limit),
        cost_estimate=pl.CostEstimate(
            flops=9_000_000_000, bytes_accessed=8 << 20, transcendentals=4 << 20
        ),
        name="attend",
    )(plan, queries, *blocks)


def output_kernel(at, attended_ref, piece_ref, out_ref):
    q_head = attended_ref.shape[1] // CHUNKS
    d = out_ref.shape[1] // CHUNKS
    low = jnp.zeros((attended_ref.shape[0], ROW_BLOCKS * 16), jnp.float32)
    for chunk in range(CHUNKS):
        down = factor(piece_ref, chunk, at, q_head)
        low += dot_nt(attended_ref[:, columns(chunk, q_head)], down)
    low = low.astype(jnp.bfloat16)
    for chunk in range(CHUNKS):
        result = adapter_scale * jnp.dot(
            low, factor(piece_ref, chunk, at + q_head, d), preferred_element_type=jnp.float32
        )
        out_ref[:, columns(chunk, d)] = result.astype(jnp.bfloat16)


def output_adapter(attended, pieces, model_width, at):
    return pl.pallas_call(
        functools.partial(output_kernel, at),
        out_shape=jax.ShapeDtypeStruct((attended.shape[0], model_width), jnp.bfloat16),
        in_specs=vmem(2),
        out_specs=vmem()[0],
        compiler_params=PARAMS,
        cost_estimate=pl.CostEstimate(
            flops=100_000_000, bytes_accessed=3 << 20, transcendentals=0
        ),
        name="output",
    )(attended, pieces)


def earlier_shards(shards):
    longest = shards // 2 + 1
    low = -(longest // 2)
    runs = (
        [i % shards for i in range(low, low + longest)],
        [i % shards for i in range(low + longest, low + shards)],
    )
    limits = (longest, shards - longest - 1)
    earlier = {}
    for run, limit in zip(runs, limits):
        for i, shard in enumerate(run):
            earlier[shard] = set(run[max(0, i - limit + 1) : i])
    return earlier


def shift_pairs(shards, shift):
    earlier = earlier_shards(shards)
    pairs = [((d - shift) % shards, d) for d in range(shards)]
    return [(s, d) for s, d in pairs if s in earlier[d] or s in earlier[d ^ 1]]


def swap_pairs(shards, shift):
    earlier = earlier_shards(shards)
    return [(d, d ^ 1) for d in range(shards) if (d - shift) % shards in earlier[d ^ 1]]


def exchange(kv, queries, shards, reach):
    shifts = range(0, reach + 1, 2)
    got = [kv] + [lax.ppermute(kv, "ctx", shift_pairs(shards, s)) for s in shifts[1:]]
    got[1:], queries = lax.optimization_barrier((got[1:], queries))
    swapped = [lax.ppermute(b, "ctx", swap_pairs(shards, s)) for s, b in zip(shifts, got)]
    blocks, steps = [kv], [(0, True)]
    for s, even, odd in zip(shifts, got, swapped):
        if s:
            blocks.append(even)
            steps.append((s, True))
        blocks.append(odd)
        steps.append((s, False))
    return blocks, steps, queries


def body(
    hidden,
    frozen_query,
    frozen_key,
    frozen_value,
    adapter_bank,
    request_shards,
    request_adapter,
    adapter_owner,
):
    shards = lax.axis_size("ctx")
    groups = lax.axis_size("groups")
    tokens, model_width = hidden.shape
    halves = 2 if groups == 2 and 2 * shards == ROW_BLOCKS * CHUNKS else 1
    own_half = lax.axis_index("groups") if halves == 2 else 0
    me = jnp.stack([lax.axis_index("ctx"), own_half]).astype(jnp.int32)
    parts = Parts(model_width, frozen_query.shape[1], frozen_key.shape[1])
    reach = shards // 2

    packed = pack(parts, halves, shards, me, adapter_bank)
    spread = lax.all_to_all(packed, "ctx", split_axis=0, concat_axis=0, tiled=True)

    tables = rope_tables(jnp.arange((reach + 1) * tokens, dtype=jnp.int32).reshape(-1, tokens))
    requests = jnp.stack([request_shards, request_adapter])[:, None]
    if halves == 2:
        theirs = lax.ppermute(requests, "groups", [(0, 1), (1, 0)])
        requests = jnp.concatenate([requests, theirs], axis=1)
    plan = make_plan(shards, reach, me, requests[0], requests[1], adapter_owner)
    spread, tables = lax.optimization_barrier((spread, tables))

    def collect(pieces):
        axes = ("groups", "ctx") if halves == 2 else "ctx"
        pieces = lax.all_to_all(pieces, axes, split_axis=0, concat_axis=0, tiled=True)
        return pieces.reshape((halves, shards) + pieces.shape[1:])[:, : ROW_BLOCKS * CHUNKS]

    kv_width, q_width, _ = parts.widths
    first, later = route(plan, spread, kv_width + q_width)
    pieces = collect(first)
    kv = make_keys_values(plan, hidden, frozen_key, frozen_value, tables, pieces)
    queries = make_queries(plan, hidden, frozen_query, tables, pieces, kv_width)
    blocks, steps, queries = exchange(kv, queries, shards, reach)
    blocks[1], later = lax.optimization_barrier((blocks[1], later))
    later = collect(later)
    attended, copy = attend(plan, queries, blocks, steps)
    return attended, output_adapter(copy, later, model_width, 0)


def solution(mesh):
    return jax.shard_map(
        body,
        mesh=mesh,
        in_specs=(
            P(("groups", "ctx"), None),
            P(("groups", "ctx"), None),
            P(("groups", "ctx"), None),
            P(("groups", "ctx"), None),
            P("ctx", None, None),
            P("groups"),
            P("groups"),
            P(),
        ),
        out_specs=(P(("groups", "ctx"), None), P(("groups", "ctx"), None)),
        check_vma=False,
    )
```

```python
import functools

import jax
import jax.numpy as jnp
from jax import lax
from jax.experimental import pallas as pl
from jax.experimental.pallas import tpu as pltpu
from jax.sharding import PartitionSpec as P

HEAD_SIZE = 128
QUERY_HEADS = 16
KEY_VALUE_HEADS = 4
GROUP_SPLIT = QUERY_HEADS // KEY_VALUE_HEADS

adapter_scale = 0.5
rope_theta = 500000.0
score_masked = -1e30

VMEM_LIMIT = 24 * 1024 * 1024

ROW_BLOCKS = 4
CHUNKS = 8


def rope_tables(positions):
    half_dim = HEAD_SIZE // 2
    frequency = rope_theta ** (-(jnp.arange(half_dim, dtype=jnp.float32) * 2.0) / HEAD_SIZE)
    angles = positions.astype(jnp.float32)[..., None] * frequency
    cosines = jnp.cos(angles)
    sines = jnp.sin(angles)
    return (jnp.concatenate([cosines, cosines], -1), jnp.concatenate([-sines, sines], -1))


class Parts:
    def __init__(self, model_width, query_width, key_width):
        d, q, k = model_width, query_width, key_width
        up = 3 * d
        self.kv = ((d, d // CHUNKS), (2 * d, d // CHUNKS), (up + q, 2 * k // CHUNKS))
        self.q = ((0, d // CHUNKS), (up, q // CHUNKS))
        self.o = ((up + q + 2 * k, q // CHUNKS), (up + 2 * q + 2 * k, d // CHUNKS))
        self.all = self.kv + self.q + self.o
        self.widths = tuple(sum(w for _, w in part) for part in (self.kv, self.q, self.o))


def vmem(count=1):
    return [pl.BlockSpec(memory_space=pltpu.VMEM)] * count


def smem(count=1):
    return [pl.BlockSpec(memory_space=pltpu.SMEM)] * count


PARAMS = pltpu.CompilerParams(vmem_limit_bytes=VMEM_LIMIT)


OWN_INDEX, OWN_HALF, COUNT, ENTRY = 0, 1, 2, 8


def layout(lengths_ref, which, shards):
    starts, start, length = [jnp.int32(0)], jnp.int32(0), lengths_ref[which, 0]
    for r in range(1, lengths_ref.shape[1]):
        starts.append(starts[-1] + lengths_ref[which, r - 1])
        longer = lengths_ref[which, r] > length
        start = jnp.where(longer, starts[-1], start)
        length = jnp.where(longer, lengths_ref[which, r], length)
    return starts, start + lax.div(length, 2)


def plan_kernel(shards, reach, me_ref, lengths_ref, adapters_ref, owner_ref, out_ref):
    own_index, own_half = me_ref[0], me_ref[1]
    starts, offset = layout(lengths_ref, 0, shards)
    own_packed = lax.rem(own_index + offset, shards)
    first = jnp.int32(0)
    for start in starts[1:]:
        first = jnp.where(start <= own_packed, start, first)
    out_ref[OWN_INDEX] = own_index
    out_ref[OWN_HALF] = own_half
    out_ref[COUNT] = jnp.minimum(own_packed - first, reach) + 1
    for which in range(lengths_ref.shape[0]):
        starts, offset = layout(lengths_ref, which, shards)
        entries = [owner_ref[adapters_ref[which, r]] for r in range(len(starts))]
        at = ENTRY + shards * (own_half if which == 0 else 1 - own_half)
        for shard in range(shards):
            packed = lax.rem(shard + offset, shards)
            entry = entries[0]
            for start, later in zip(starts[1:], entries[1:]):
                entry = jnp.where(start <= packed, later, entry)
            out_ref[at + shard] = entry


def make_plan(shards, reach, me, lengths, adapters, owner):
    return pl.pallas_call(
        functools.partial(plan_kernel, shards, reach),
        out_shape=jax.ShapeDtypeStruct((ENTRY + lengths.shape[0] * shards,), jnp.int32),
        in_specs=smem(4),
        out_specs=smem()[0],
        name="plan",
    )(me, lengths, adapters, owner)


def pack_kernel(parts, halves, x_ref, bank_ref, out):
    own_half = x_ref[1]
    for block in range(out.shape[0]):
        piece = block % (ROW_BLOCKS * CHUNKS // halves)
        rows = pl.ds((piece % ROW_BLOCKS) * 16, 16)
        chunk = (piece // ROW_BLOCKS) * halves + own_half
        at = 0
        for first, width in parts.all:
            start = pl.multiple_of(first + chunk * width, 128)
            out[block, :, at : at + width] = bank_ref[0, rows, pl.ds(start, width)]
            at += width


def pack(parts, halves, shards, me, bank):
    width = sum(parts.widths)
    return pl.pallas_call(
        functools.partial(pack_kernel, parts, halves),
        out_shape=jax.ShapeDtypeStruct((shards, 16, width), bank.dtype),
        in_specs=smem() + vmem(),
        out_specs=vmem()[0],
        compiler_params=PARAMS,
        name="pack",
    )(me, bank)


ROUTE_STEPS = 4


def route_kernel(plan_ref, spread_ref, *outs):
    number = outs[0].shape[0]
    for i in range(number):
        entry = plan_ref[ENTRY + pl.program_id(0) * number + i]
        at = 0
        for out in outs:
            out[i] = spread_ref[entry, :, at : at + out.shape[2]]
            at += out.shape[2]


def route(plan, spread, first_width):
    dests = plan.shape[0] - ENTRY
    widths = (first_width, spread.shape[2] - first_width)
    return pl.pallas_call(
        route_kernel,
        out_shape=[jax.ShapeDtypeStruct((dests, 16, w), spread.dtype) for w in widths],
        grid=(ROUTE_STEPS,),
        in_specs=smem() + vmem(),
        out_specs=[
            pl.BlockSpec((dests // ROUTE_STEPS, 16, w), lambda i: (i, 0, 0)) for w in widths
        ],
        compiler_params=PARAMS,
        name="route",
    )(plan, spread)


def factor(piece_ref, chunk, at, width):
    halves = piece_ref.shape[0]
    place = chunk // halves * ROW_BLOCKS
    rows = piece_ref[chunk % halves, place : place + ROW_BLOCKS, :, at : at + width]
    return rows.reshape(ROW_BLOCKS * 16, width)


def columns(chunk, width):
    return slice(chunk * width, (chunk + 1) * width)


def dot_nt(a, b):
    return lax.dot_general(a, b, (((1,), (1,)), ((), ())), preferred_element_type=jnp.float32)


def turn(x, cosines, sines):
    return x * cosines + pltpu.roll(x, HEAD_SIZE // 2, 1) * sines


def kv_kernel(plan_ref, hidden_ref, key_ref, value_ref, cos_ref, sin_ref, piece_ref, out_ref):
    d = hidden_ref.shape[1] // CHUNKS
    rank = ROW_BLOCKS * 16
    low = jnp.zeros((hidden_ref.shape[0], 2 * rank), jnp.float32)
    for chunk in range(CHUNKS):
        down = jnp.concatenate(
            [factor(piece_ref, chunk, 0, d), factor(piece_ref, chunk, d, d)], axis=0
        )
        low += dot_nt(hidden_ref[:, columns(chunk, d)], down)
    low = low.astype(jnp.bfloat16)
    width = 2 * key_ref.shape[1] // CHUNKS
    own = plan_ref[COUNT] - 1
    cosines, sines = cos_ref[own], sin_ref[own]
    for chunk in range(CHUNKS):
        is_key = chunk < CHUNKS // 2
        up = factor(piece_ref, chunk, 2 * d, width)
        part = low[:, :rank] if is_key else low[:, rank:]
        update = jnp.dot(part, up, preferred_element_type=jnp.float32)
        frozen = (key_ref if is_key else value_ref)[:, columns(chunk % (CHUNKS // 2), width)]
        result = frozen.astype(jnp.float32) + adapter_scale * update
        if is_key:
            result = turn(result, cosines, sines)
        out_ref[:, columns(chunk, width)] = result.astype(jnp.bfloat16)


def make_keys_values(plan, hidden, key, value, tables, pieces):
    return pl.pallas_call(
        kv_kernel,
        out_shape=jax.ShapeDtypeStruct((key.shape[0], 2 * key.shape[1]), jnp.bfloat16),
        in_specs=smem() + vmem(6),
        out_specs=vmem()[0],
        compiler_params=PARAMS,
        cost_estimate=pl.CostEstimate(
            flops=150_000_000, bytes_accessed=3 << 20, transcendentals=0
        ),
        name="keys_values",
    )(plan, hidden, key, value, *tables, pieces)


def query_kernel(at, plan_ref, hidden_ref, query_ref, cos_ref, sin_ref, piece_ref, out_ref):
    tokens = query_ref.shape[0]
    d = hidden_ref.shape[1] // CHUNKS
    width = query_ref.shape[1] // CHUNKS
    low = jnp.zeros((tokens, ROW_BLOCKS * 16), jnp.float32)
    for chunk in range(CHUNKS):
        low += dot_nt(hidden_ref[:, columns(chunk, d)], factor(piece_ref, chunk, at, d))
    low = low.astype(jnp.bfloat16)
    own = plan_ref[COUNT] - 1
    cosines, sines = cos_ref[own], sin_ref[own]
    for chunk in range(CHUNKS):
        up = factor(piece_ref, chunk, at + d, width)
        update = jnp.dot(low, up, preferred_element_type=jnp.float32)
        result = query_ref[:, columns(chunk, width)].astype(jnp.float32) + adapter_scale * update
        for part in range(width // HEAD_SIZE):
            head = chunk * (width // HEAD_SIZE) + part
            turned = turn(result[:, columns(part, HEAD_SIZE)], cosines, sines)
            out_ref[head // GROUP_SPLIT, pl.ds((head % GROUP_SPLIT) * tokens, tokens)] = (
                turned.astype(jnp.bfloat16)
            )


def make_queries(plan, hidden, query, tables, pieces, at):
    tokens = hidden.shape[0]
    return pl.pallas_call(
        functools.partial(query_kernel, at),
        out_shape=jax.ShapeDtypeStruct(
            (KEY_VALUE_HEADS, GROUP_SPLIT * tokens, HEAD_SIZE), jnp.bfloat16
        ),
        in_specs=smem() + vmem(5),
        out_specs=vmem()[0],
        compiler_params=PARAMS,
        cost_estimate=pl.CostEstimate(
            flops=100_000_000, bytes_accessed=3 << 20, transcendentals=0
        ),
        name="queries",
    )(plan, hidden, query, *tables, pieces)


REGION = 5


def attend_kernel(steps, plan_ref, queries, *refs):
    blocks, (out_ref, copy_ref, high, acc) = refs[:-4], refs[-4:]
    count = plan_ref[COUNT]
    odd = lax.rem(plan_ref[OWN_INDEX], 2)
    aside = 2 * odd - 1
    steps = [s if even else s + aside for s, even in steps]
    tokens = out_ref.shape[0]
    rows = GROUP_SPLIT * tokens
    bf16 = jnp.bfloat16
    base2 = 1.4426950408889634 / (HEAD_SIZE**0.5)
    ones = jnp.ones((tokens, HEAD_SIZE), bf16)

    def region(first, number):
        shards = blocks[first : first + number]
        for g in range(KEY_VALUE_HEADS):
            keys = [b[:, columns(g, HEAD_SIZE)] for b in shards]
            values = [
                jnp.concatenate([b[:, columns(KEY_VALUE_HEADS + g, HEAD_SIZE)], ones], axis=1)
                for b in shards
            ]
            score = dot_nt(queries[g], jnp.concatenate(keys, axis=0))
            tiles = [score[:, columns(i, tokens)] for i in range(number)]
            if first == 0:
                row = lax.broadcasted_iota(jnp.int32, (rows, tokens), 0) % tokens
                column = lax.broadcasted_iota(jnp.int32, (rows, tokens), 1)
                tiles = [jnp.where(column <= row, tiles[0], score_masked)]
            else:
                tiles = [
                    jnp.where((step > 0) & (step < count), tile, score_masked)
                    for step, tile in zip(steps[first : first + number], tiles)
                ]
            top = functools.reduce(jnp.maximum, tiles)
            top = jnp.max(top, axis=1, keepdims=True) * base2
            top = jnp.broadcast_to(top, (rows, HEAD_SIZE))
            if first:
                old = high[g]
                top = jnp.maximum(old, top)
            weight = [jnp.exp2(t * base2 - top).astype(bf16) for t in tiles]
            blend = jnp.dot(
                jnp.concatenate(weight, axis=1),
                jnp.concatenate(values, axis=0),
                preferred_element_type=jnp.float32,
            )
            if first:
                shrink = jnp.exp2(old - top)
                blend += acc[g] * jnp.concatenate([shrink, shrink], axis=1)
            high[g] = top
            acc[g] = blend

    region(0, 1)
    for first in range(1, len(blocks), REGION):
        number = min(REGION, len(blocks) - first)
        nearest = functools.reduce(jnp.minimum, steps[first : first + number])
        pl.when(count > nearest)(functools.partial(region, first, number))

    for g in range(KEY_VALUE_HEADS):
        result = (acc[g, :, :HEAD_SIZE] / acc[g, :, HEAD_SIZE:]).astype(bf16)
        for j in range(GROUP_SPLIT):
            for ref in (out_ref, copy_ref):
                ref[:, columns(g * GROUP_SPLIT + j, HEAD_SIZE)] = result[columns(j, tokens)]


def attend(plan, queries, blocks, steps):
    tokens = blocks[0].shape[0]
    rows = GROUP_SPLIT * tokens
    limit = VMEM_LIMIT if len(blocks) < 16 else 2 * VMEM_LIMIT
    return pl.pallas_call(
        functools.partial(attend_kernel, steps),
        out_shape=[jax.ShapeDtypeStruct((tokens, QUERY_HEADS * HEAD_SIZE), jnp.bfloat16)] * 2,
        in_specs=smem() + vmem(1 + len(blocks)),
        out_specs=vmem(2),
        scratch_shapes=[
            pltpu.VMEM((KEY_VALUE_HEADS, rows, HEAD_SIZE), jnp.float32),
            pltpu.VMEM((KEY_VALUE_HEADS, rows, 2 * HEAD_SIZE), jnp.float32),
        ],
        compiler_params=pltpu.CompilerParams(vmem_limit_bytes=limit),
        cost_estimate=pl.CostEstimate(
            flops=12_000_000_000, bytes_accessed=8 << 20, transcendentals=4 << 20
        ),
        name="attend",
    )(plan, queries, *blocks)


def output_kernel(at, attended_ref, piece_ref, out_ref):
    q_head = attended_ref.shape[1] // CHUNKS
    d = out_ref.shape[1] // CHUNKS
    low = jnp.zeros((attended_ref.shape[0], ROW_BLOCKS * 16), jnp.float32)
    for chunk in range(CHUNKS):
        down = factor(piece_ref, chunk, at, q_head)
        low += dot_nt(attended_ref[:, columns(chunk, q_head)], down)
    low = low.astype(jnp.bfloat16)
    for chunk in range(CHUNKS):
        result = adapter_scale * jnp.dot(
            low, factor(piece_ref, chunk, at + q_head, d), preferred_element_type=jnp.float32
        )
        out_ref[:, columns(chunk, d)] = result.astype(jnp.bfloat16)


def output_adapter(attended, pieces, model_width, at):
    return pl.pallas_call(
        functools.partial(output_kernel, at),
        out_shape=jax.ShapeDtypeStruct((attended.shape[0], model_width), jnp.bfloat16),
        in_specs=vmem(2),
        out_specs=vmem()[0],
        compiler_params=PARAMS,
        cost_estimate=pl.CostEstimate(
            flops=100_000_000, bytes_accessed=3 << 20, transcendentals=0
        ),
        name="output",
    )(attended, pieces)


def earlier_shards(shards):
    longest = shards // 2 + 1
    low = -(longest // 2)
    runs = (
        [i % shards for i in range(low, low + longest)],
        [i % shards for i in range(low + longest, low + shards)],
    )
    limits = (longest, shards - longest - 1)
    earlier = {}
    for run, limit in zip(runs, limits):
        for i, shard in enumerate(run):
            earlier[shard] = set(run[max(0, i - limit + 1) : i])
    return earlier


def shift_pairs(shards, shift):
    earlier = earlier_shards(shards)
    pairs = [((d - shift) % shards, d) for d in range(shards)]
    return [(s, d) for s, d in pairs if s in earlier[d] or s in earlier[d ^ 1]]


def swap_pairs(shards, shift):
    earlier = earlier_shards(shards)
    return [(d, d ^ 1) for d in range(shards) if (d - shift) % shards in earlier[d ^ 1]]


def exchange(kv, queries, shards, reach):
    shifts = range(0, reach + 1, 2)
    got = [kv] + [lax.ppermute(kv, "ctx", shift_pairs(shards, s)) for s in shifts[1:]]
    got[1:], queries = lax.optimization_barrier((got[1:], queries))
    swapped = [lax.ppermute(b, "ctx", swap_pairs(shards, s)) for s, b in zip(shifts, got)]
    blocks, steps = [kv], [(0, True)]
    for s, even, odd in zip(shifts, got, swapped):
        if s:
            blocks.append(even)
            steps.append((s, True))
        blocks.append(odd)
        steps.append((s, False))
    return blocks, steps, queries


def body(
    hidden,
    frozen_query,
    frozen_key,
    frozen_value,
    adapter_bank,
    request_shards,
    request_adapter,
    adapter_owner,
):
    shards = lax.axis_size("ctx")
    groups = lax.axis_size("groups")
    tokens, model_width = hidden.shape
    halves = 2 if groups == 2 and 2 * shards == ROW_BLOCKS * CHUNKS else 1
    own_half = lax.axis_index("groups") if halves == 2 else 0
    me = jnp.stack([lax.axis_index("ctx"), own_half]).astype(jnp.int32)
    parts = Parts(model_width, frozen_query.shape[1], frozen_key.shape[1])
    reach = shards // 2

    packed = pack(parts, halves, shards, me, adapter_bank)
    spread = lax.all_to_all(packed, "ctx", split_axis=0, concat_axis=0, tiled=True)

    tables = rope_tables(jnp.arange((reach + 1) * tokens, dtype=jnp.int32).reshape(-1, tokens))
    requests = jnp.stack([request_shards, request_adapter])[:, None]
    if halves == 2:
        theirs = lax.ppermute(requests, "groups", [(0, 1), (1, 0)])
        requests = jnp.concatenate([requests, theirs], axis=1)
    plan = make_plan(shards, reach, me, requests[0], requests[1], adapter_owner)
    spread, tables = lax.optimization_barrier((spread, tables))

    def collect(pieces):
        axes = ("groups", "ctx") if halves == 2 else "ctx"
        pieces = lax.all_to_all(pieces, axes, split_axis=0, concat_axis=0, tiled=True)
        return pieces.reshape((halves, shards) + pieces.shape[1:])[:, : ROW_BLOCKS * CHUNKS]

    kv_width, q_width, _ = parts.widths
    first, later = route(plan, spread, kv_width + q_width)
    pieces = collect(first)
    kv = make_keys_values(plan, hidden, frozen_key, frozen_value, tables, pieces)
    queries = make_queries(plan, hidden, frozen_query, tables, pieces, kv_width)
    blocks, steps, queries = exchange(kv, queries, shards, reach)
    blocks[1], later = lax.optimization_barrier((blocks[1], later))
    later = collect(later)
    attended, copy = attend(plan, queries, blocks, steps)
    return attended, output_adapter(copy, later, model_width, 0)


def solution(mesh):
    return jax.shard_map(
        body,
        mesh=mesh,
        in_specs=(
            P(("groups", "ctx"), None),
            P(("groups", "ctx"), None),
            P(("groups", "ctx"), None),
            P(("groups", "ctx"), None),
            P("ctx", None, None),
            P("groups"),
            P("groups"),
            P(),
        ),
        out_specs=(P(("groups", "ctx"), None), P(("groups", "ctx"), None)),
        check_vma=False,
    )
```

```python
import functools

import jax
import jax.numpy as jnp
from jax import lax
from jax.experimental import pallas as pl
from jax.experimental.pallas import tpu as pltpu
from jax.sharding import PartitionSpec as P

HEAD_SIZE = 128
QUERY_HEADS = 16
KEY_VALUE_HEADS = 4
GROUP_SPLIT = QUERY_HEADS // KEY_VALUE_HEADS

adapter_scale = 0.5
rope_theta = 500000.0
score_masked = -1e30

VMEM_LIMIT = 24 * 1024 * 1024

ROW_BLOCKS = 4
CHUNKS = 8


def rope_tables(positions):
    half_dim = HEAD_SIZE // 2
    frequency = rope_theta ** (-(jnp.arange(half_dim, dtype=jnp.float32) * 2.0) / HEAD_SIZE)
    angles = positions.astype(jnp.float32)[..., None] * frequency
    cosines = jnp.cos(angles)
    sines = jnp.sin(angles)
    return (jnp.concatenate([cosines, cosines], -1), jnp.concatenate([-sines, sines], -1))


class Parts:
    def __init__(self, model_width, query_width, key_width):
        d, q, k = model_width, query_width, key_width
        up = 3 * d
        self.kv = ((d, d // CHUNKS), (2 * d, d // CHUNKS), (up + q, 2 * k // CHUNKS))
        self.q = ((0, d // CHUNKS), (up, q // CHUNKS))
        self.o = ((up + q + 2 * k, q // CHUNKS), (up + 2 * q + 2 * k, d // CHUNKS))
        self.all = self.kv + self.q + self.o
        self.widths = tuple(sum(w for _, w in part) for part in (self.kv, self.q, self.o))


def vmem(count=1):
    return [pl.BlockSpec(memory_space=pltpu.VMEM)] * count


def smem(count=1):
    return [pl.BlockSpec(memory_space=pltpu.SMEM)] * count


PARAMS = pltpu.CompilerParams(vmem_limit_bytes=VMEM_LIMIT)


OWN_INDEX, COUNT, ENTRY = 0, 1, 8


def layout(lengths_ref, which, shards):
    starts, start, length = [jnp.int32(0)], jnp.int32(0), lengths_ref[which, 0]
    for r in range(1, lengths_ref.shape[1]):
        starts.append(starts[-1] + lengths_ref[which, r - 1])
        longer = lengths_ref[which, r] > length
        start = jnp.where(longer, starts[-1], start)
        length = jnp.where(longer, lengths_ref[which, r], length)
    return starts, start + lax.div(length, 2)


def plan_kernel(shards, reach, me_ref, lengths_ref, adapters_ref, owner_ref, out_ref):
    own_index, own_half = me_ref[0], me_ref[1]
    starts, offset = layout(lengths_ref, 0, shards)
    own_packed = lax.rem(own_index + offset, shards)
    first = jnp.int32(0)
    for start in starts[1:]:
        first = jnp.where(start <= own_packed, start, first)
    lanes = lax.broadcasted_iota(jnp.int32, out_ref.shape, 1)
    plan = jnp.where(lanes == COUNT, jnp.minimum(own_packed - first, reach) + 1, own_index)
    for which in range(lengths_ref.shape[0]):
        starts, offset = layout(lengths_ref, which, shards)
        entries = [owner_ref[adapters_ref[which, r]] for r in range(len(starts))]
        at = ENTRY + shards * (own_half if which == 0 else 1 - own_half)
        for shard in range(shards):
            packed = lax.rem(shard + offset, shards)
            entry = entries[0]
            for start, later in zip(starts[1:], entries[1:]):
                entry = jnp.where(start <= packed, later, entry)
            plan = jnp.where(lanes == at + shard, entry, plan)
    out_ref[...] = plan


def make_plan(shards, reach, me, lengths, adapters, owner):
    return pl.pallas_call(
        functools.partial(plan_kernel, shards, reach),
        out_shape=jax.ShapeDtypeStruct((1, 128), jnp.int32),
        in_specs=smem(4),
        out_specs=vmem()[0],
        name="plan",
    )(me, lengths, adapters, owner)


def pack_kernel(parts, halves, me_ref, bank_ref, out_ref, sem):
    own_half = me_ref[1]
    copies = []
    for again in range(out_ref.shape[0]):
        for place in range(out_ref.shape[1]):
            at = 0
            for first, width in parts.all:
                start = pl.multiple_of(first + (place * halves + own_half) * width, 128)
                copies.append(
                    pltpu.make_async_copy(
                        bank_ref.at[:, :, pl.ds(start, width)],
                        out_ref.at[again, place, :, :, pl.ds(at, width)],
                        sem.at[len(copies)],
                    )
                )
                at += width
    for copy in copies:
        copy.start()
    for copy in copies:
        copy.wait()


def pack(parts, halves, shards, me, bank):
    width, places = sum(parts.widths), CHUNKS // halves
    again = shards // (places * ROW_BLOCKS)
    packed = pl.pallas_call(
        functools.partial(pack_kernel, parts, halves),
        out_shape=jax.ShapeDtypeStruct((again, places, ROW_BLOCKS, 16, width), bank.dtype),
        in_specs=smem() + [pl.BlockSpec(memory_space=pl.ANY)],
        out_specs=vmem()[0],
        scratch_shapes=[pltpu.SemaphoreType.DMA((again * places * len(parts.all),))],
        compiler_params=pltpu.CompilerParams(vmem_limit_bytes=62 * 1024 * 1024),
        name="pack",
    )(me, bank.reshape(ROW_BLOCKS, 16, bank.shape[2]))
    return packed.reshape(shards, 16, width)


ROUTE_STEPS = 4


def route_kernel(at, plan_ref, spread_ref, out_ref):
    number = out_ref.shape[0]
    for i in range(number):
        entry = plan_ref[0, ENTRY + pl.program_id(0) * number + i]
        out_ref[i] = spread_ref[entry, :, at : at + out_ref.shape[2]]


def route(plan, spread, dests, at, width):
    return pl.pallas_call(
        functools.partial(route_kernel, at),
        out_shape=jax.ShapeDtypeStruct((dests, 16, width), spread.dtype),
        grid=(ROUTE_STEPS,),
        in_specs=smem() + vmem(),
        out_specs=pl.BlockSpec((dests // ROUTE_STEPS, 16, width), lambda i: (i, 0, 0)),
        compiler_params=PARAMS,
        name="route",
    )(plan, spread)


def factor(piece_ref, chunk, at, width):
    halves = piece_ref.shape[0]
    place = chunk // halves * ROW_BLOCKS
    rows = piece_ref[chunk % halves, place : place + ROW_BLOCKS, :, at : at + width]
    return rows.reshape(ROW_BLOCKS * 16, width)


def columns(chunk, width):
    return slice(chunk * width, (chunk + 1) * width)


def dot_nt(a, b):
    return lax.dot_general(a, b, (((1,), (1,)), ((), ())), preferred_element_type=jnp.float32)


def turn(x, cosines, sines):
    return x * cosines + pltpu.roll(x, HEAD_SIZE // 2, 1) * sines


def kv_kernel(plan_ref, hidden_ref, key_ref, value_ref, cos_ref, sin_ref, piece_ref, out_ref):
    d = hidden_ref.shape[1] // CHUNKS
    rank = ROW_BLOCKS * 16
    low = jnp.zeros((hidden_ref.shape[0], 2 * rank), jnp.float32)
    for chunk in range(CHUNKS):
        down = jnp.concatenate(
            [factor(piece_ref, chunk, 0, d), factor(piece_ref, chunk, d, d)], axis=0
        )
        low += dot_nt(hidden_ref[:, columns(chunk, d)], down)
    low = low.astype(jnp.bfloat16)
    width = 2 * key_ref.shape[1] // CHUNKS
    own = plan_ref[0, COUNT] - 1
    cosines, sines = cos_ref[own], sin_ref[own]
    for chunk in range(CHUNKS):
        is_key = chunk < CHUNKS // 2
        up = factor(piece_ref, chunk, 2 * d, width)
        part = low[:, :rank] if is_key else low[:, rank:]
        update = jnp.dot(part, up, preferred_element_type=jnp.float32)
        frozen = (key_ref if is_key else value_ref)[:, columns(chunk % (CHUNKS // 2), width)]
        result = frozen.astype(jnp.float32) + adapter_scale * update
        if is_key:
            result = turn(result, cosines, sines)
        out_ref[:, columns(chunk, width)] = result.astype(jnp.bfloat16)


def make_keys_values(plan, hidden, key, value, tables, pieces):
    return pl.pallas_call(
        kv_kernel,
        out_shape=jax.ShapeDtypeStruct((key.shape[0], 2 * key.shape[1]), jnp.bfloat16),
        in_specs=smem() + vmem(6),
        out_specs=vmem()[0],
        compiler_params=PARAMS,
        cost_estimate=pl.CostEstimate(
            flops=150_000_000, bytes_accessed=3 << 20, transcendentals=0
        ),
        name="keys_values",
    )(plan, hidden, key, value, *tables, pieces)


def query_kernel(at, plan_ref, hidden_ref, query_ref, cos_ref, sin_ref, piece_ref, out_ref):
    tokens = query_ref.shape[0]
    d = hidden_ref.shape[1] // CHUNKS
    width = query_ref.shape[1] // CHUNKS
    low = jnp.zeros((tokens, ROW_BLOCKS * 16), jnp.float32)
    for chunk in range(CHUNKS):
        low += dot_nt(hidden_ref[:, columns(chunk, d)], factor(piece_ref, chunk, at, d))
    low = low.astype(jnp.bfloat16)
    own = plan_ref[0, COUNT] - 1
    cosines, sines = cos_ref[own], sin_ref[own]
    for chunk in range(CHUNKS):
        up = factor(piece_ref, chunk, at + d, width)
        update = jnp.dot(low, up, preferred_element_type=jnp.float32)
        result = query_ref[:, columns(chunk, width)].astype(jnp.float32) + adapter_scale * update
        for part in range(width // HEAD_SIZE):
            head = chunk * (width // HEAD_SIZE) + part
            turned = turn(result[:, columns(part, HEAD_SIZE)], cosines, sines)
            out_ref[head // GROUP_SPLIT, pl.ds((head % GROUP_SPLIT) * tokens, tokens)] = (
                turned.astype(jnp.bfloat16)
            )


def make_queries(plan, hidden, query, tables, pieces, at):
    tokens = hidden.shape[0]
    return pl.pallas_call(
        functools.partial(query_kernel, at),
        out_shape=jax.ShapeDtypeStruct(
            (KEY_VALUE_HEADS, GROUP_SPLIT * tokens, HEAD_SIZE), jnp.bfloat16
        ),
        in_specs=smem() + vmem(5),
        out_specs=vmem()[0],
        compiler_params=PARAMS,
        cost_estimate=pl.CostEstimate(
            flops=100_000_000, bytes_accessed=3 << 20, transcendentals=0
        ),
        name="queries",
    )(plan, hidden, query, *tables, pieces)


REGION = 5


def attend_kernel(steps, plan_ref, queries, *refs):
    blocks, (out_ref, copy_ref, high, acc) = refs[:-4], refs[-4:]
    count = plan_ref[0, COUNT]
    odd = lax.rem(plan_ref[0, OWN_INDEX], 2)
    aside = 2 * odd - 1
    steps = [s if even else s + aside for s, even in steps]
    tokens = out_ref.shape[0]
    rows = GROUP_SPLIT * tokens
    bf16 = jnp.bfloat16
    base2 = 1.4426950408889634 / (HEAD_SIZE**0.5)
    ones = jnp.ones((tokens, HEAD_SIZE), bf16)

    def region(first, number):
        shards = blocks[first : first + number]
        for g in range(KEY_VALUE_HEADS):
            keys = [b[:, columns(g, HEAD_SIZE)] for b in shards]
            values = [
                jnp.concatenate([b[:, columns(KEY_VALUE_HEADS + g, HEAD_SIZE)], ones], axis=1)
                for b in shards
            ]
            score = dot_nt(queries[g], jnp.concatenate(keys, axis=0))
            tiles = [score[:, columns(i, tokens)] for i in range(number)]
            if first == 0:
                row = lax.broadcasted_iota(jnp.int32, (rows, tokens), 0) % tokens
                column = lax.broadcasted_iota(jnp.int32, (rows, tokens), 1)
                tiles = [jnp.where(column <= row, tiles[0], score_masked)]
            else:
                tiles = [
                    jnp.where((step > 0) & (step < count), tile, score_masked)
                    for step, tile in zip(steps[first : first + number], tiles)
                ]
            top = functools.reduce(jnp.maximum, tiles)
            top = jnp.max(top, axis=1, keepdims=True) * base2
            top = jnp.broadcast_to(top, (rows, HEAD_SIZE))
            if first:
                old = high[g]
                top = jnp.maximum(old, top)
            weight = [jnp.exp2(t * base2 - top).astype(bf16) for t in tiles]
            blend = jnp.dot(
                jnp.concatenate(weight, axis=1),
                jnp.concatenate(values, axis=0),
                preferred_element_type=jnp.float32,
            )
            if first:
                shrink = jnp.exp2(old - top)
                blend += acc[g] * jnp.concatenate([shrink, shrink], axis=1)
            high[g] = top
            acc[g] = blend

    region(0, 1)
    for first in range(1, len(blocks), REGION):
        number = min(REGION, len(blocks) - first)
        nearest = functools.reduce(jnp.minimum, steps[first : first + number])
        pl.when(count > nearest)(functools.partial(region, first, number))

    for g in range(KEY_VALUE_HEADS):
        result = (acc[g, :, :HEAD_SIZE] / acc[g, :, HEAD_SIZE:]).astype(bf16)
        for j in range(GROUP_SPLIT):
            for ref in (out_ref, copy_ref):
                ref[:, columns(g * GROUP_SPLIT + j, HEAD_SIZE)] = result[columns(j, tokens)]


def attend(plan, queries, blocks, steps):
    tokens = blocks[0].shape[0]
    rows = GROUP_SPLIT * tokens
    limit = VMEM_LIMIT if len(blocks) < 16 else 2 * VMEM_LIMIT
    return pl.pallas_call(
        functools.partial(attend_kernel, steps),
        out_shape=[jax.ShapeDtypeStruct((tokens, QUERY_HEADS * HEAD_SIZE), jnp.bfloat16)] * 2,
        in_specs=smem() + vmem(1 + len(blocks)),
        out_specs=vmem(2),
        scratch_shapes=[
            pltpu.VMEM((KEY_VALUE_HEADS, rows, HEAD_SIZE), jnp.float32),
            pltpu.VMEM((KEY_VALUE_HEADS, rows, 2 * HEAD_SIZE), jnp.float32),
        ],
        compiler_params=pltpu.CompilerParams(vmem_limit_bytes=limit),
        cost_estimate=pl.CostEstimate(
            flops=12_000_000_000, bytes_accessed=8 << 20, transcendentals=4 << 20
        ),
        name="attend",
    )(plan, queries, *blocks)


def output_kernel(at, attended_ref, piece_ref, out_ref):
    q_head = attended_ref.shape[1] // CHUNKS
    d = out_ref.shape[1] // CHUNKS
    low = jnp.zeros((attended_ref.shape[0], ROW_BLOCKS * 16), jnp.float32)
    for chunk in range(CHUNKS):
        down = factor(piece_ref, chunk, at, q_head)
        low += dot_nt(attended_ref[:, columns(chunk, q_head)], down)
    low = low.astype(jnp.bfloat16)
    for chunk in range(CHUNKS):
        result = adapter_scale * jnp.dot(
            low, factor(piece_ref, chunk, at + q_head, d), preferred_element_type=jnp.float32
        )
        out_ref[:, columns(chunk, d)] = result.astype(jnp.bfloat16)


def output_adapter(attended, pieces, model_width, at):
    return pl.pallas_call(
        functools.partial(output_kernel, at),
        out_shape=jax.ShapeDtypeStruct((attended.shape[0], model_width), jnp.bfloat16),
        in_specs=vmem(2),
        out_specs=vmem()[0],
        compiler_params=PARAMS,
        cost_estimate=pl.CostEstimate(
            flops=100_000_000, bytes_accessed=3 << 20, transcendentals=0
        ),
        name="output",
    )(attended, pieces)


def earlier_shards(shards):
    longest = shards // 2 + 1
    low = -(longest // 2)
    runs = (
        [i % shards for i in range(low, low + longest)],
        [i % shards for i in range(low + longest, low + shards)],
    )
    limits = (longest, shards - longest - 1)
    earlier = {}
    for run, limit in zip(runs, limits):
        for i, shard in enumerate(run):
            earlier[shard] = set(run[max(0, i - limit + 1) : i])
    return earlier


def shift_pairs(shards, shift):
    earlier = earlier_shards(shards)
    pairs = [((d - shift) % shards, d) for d in range(shards)]
    return [(s, d) for s, d in pairs if s in earlier[d] or s in earlier[d ^ 1]]


def swap_pairs(shards, shift):
    earlier = earlier_shards(shards)
    return [(d, d ^ 1) for d in range(shards) if (d - shift) % shards in earlier[d ^ 1]]


def exchange(kv, queries, shards, reach):
    shifts = range(0, reach + 1, 2)
    got = [kv] + [lax.ppermute(kv, "ctx", shift_pairs(shards, s)) for s in shifts[1:]]
    got[1:], queries = lax.optimization_barrier((got[1:], queries))
    swapped = [lax.ppermute(b, "ctx", swap_pairs(shards, s)) for s, b in zip(shifts, got)]
    blocks, steps = [kv], [(0, True)]
    for s, even, odd in zip(shifts, got, swapped):
        if s:
            blocks.append(even)
            steps.append((s, True))
        blocks.append(odd)
        steps.append((s, False))
    return blocks, steps, queries


def body(
    hidden,
    frozen_query,
    frozen_key,
    frozen_value,
    adapter_bank,
    request_shards,
    request_adapter,
    adapter_owner,
):
    shards = lax.axis_size("ctx")
    groups = lax.axis_size("groups")
    tokens, model_width = hidden.shape
    halves = 2 if groups == 2 and 2 * shards == ROW_BLOCKS * CHUNKS else 1
    own_half = lax.axis_index("groups") if halves == 2 else 0
    me = jnp.stack([lax.axis_index("ctx"), own_half]).astype(jnp.int32)
    parts = Parts(model_width, frozen_query.shape[1], frozen_key.shape[1])
    reach = shards // 2

    packed = pack(parts, halves, shards, me, adapter_bank)
    spread = lax.all_to_all(packed, "ctx", split_axis=0, concat_axis=0, tiled=True)

    tables = rope_tables(jnp.arange((reach + 1) * tokens, dtype=jnp.int32).reshape(-1, tokens))
    requests = jnp.stack([request_shards, request_adapter])[:, None]
    if halves == 2:
        theirs = lax.ppermute(requests, "groups", [(0, 1), (1, 0)])
        requests = jnp.concatenate([requests, theirs], axis=1)
    plan = make_plan(shards, reach, me, requests[0], requests[1], adapter_owner)
    spread, tables = lax.optimization_barrier((spread, tables))

    def collect(pieces):
        axes = ("groups", "ctx") if halves == 2 else "ctx"
        pieces = lax.all_to_all(pieces, axes, split_axis=0, concat_axis=0, tiled=True)
        return pieces.reshape((halves, shards) + pieces.shape[1:])[:, : ROW_BLOCKS * CHUNKS]

    kv_width, q_width, o_width = parts.widths
    dests = shards * halves
    pieces = collect(route(plan, spread, dests, 0, kv_width + q_width))
    kv = make_keys_values(plan, hidden, frozen_key, frozen_value, tables, pieces)
    queries = make_queries(plan, hidden, frozen_query, tables, pieces, kv_width)
    blocks, steps, queries = exchange(kv, queries, shards, reach)
    later = route(plan, spread, dests, kv_width + q_width, o_width)
    kv, later = lax.optimization_barrier((kv, later))
    later = collect(later)
    attended, copy = attend(plan, queries, blocks, steps)
    return attended, output_adapter(copy, later, model_width, 0)


def solution(mesh):
    return jax.shard_map(
        body,
        mesh=mesh,
        in_specs=(
            P(("groups", "ctx"), None),
            P(("groups", "ctx"), None),
            P(("groups", "ctx"), None),
            P(("groups", "ctx"), None),
            P("ctx", None, None),
            P("groups"),
            P("groups"),
            P(),
        ),
        out_specs=(P(("groups", "ctx"), None), P(("groups", "ctx"), None)),
        check_vma=False,
    )
```

```python
import functools

import jax
import jax.numpy as jnp
from jax import lax
from jax.experimental import pallas as pl
from jax.experimental.pallas import tpu as pltpu
from jax.sharding import PartitionSpec as P

HEAD_SIZE = 128
QUERY_HEADS = 16
KEY_VALUE_HEADS = 4
GROUP_SPLIT = QUERY_HEADS // KEY_VALUE_HEADS

adapter_scale = 0.5
rope_theta = 500000.0
score_masked = -1e30

VMEM_LIMIT = 24 * 1024 * 1024

ROW_BLOCKS = 4
CHUNKS = 8


def rope_tables(positions):
    half_dim = HEAD_SIZE // 2
    frequency = rope_theta ** (-(jnp.arange(half_dim, dtype=jnp.float32) * 2.0) / HEAD_SIZE)
    angles = positions.astype(jnp.float32)[..., None] * frequency
    cosines = jnp.cos(angles)
    sines = jnp.sin(angles)
    return (jnp.concatenate([cosines, cosines], -1), jnp.concatenate([-sines, sines], -1))


class Parts:
    def __init__(self, model_width, query_width, key_width):
        d, q, k = model_width, query_width, key_width
        up = 3 * d
        self.kv = ((d, d // CHUNKS), (2 * d, d // CHUNKS), (up + q, 2 * k // CHUNKS))
        self.q = ((0, d // CHUNKS), (up, q // CHUNKS))
        self.o = ((up + q + 2 * k, q // CHUNKS), (up + 2 * q + 2 * k, d // CHUNKS))
        self.all = self.kv + self.q + self.o
        self.widths = tuple(sum(w for _, w in part) for part in (self.kv, self.q, self.o))


def vmem(count=1):
    return [pl.BlockSpec(memory_space=pltpu.VMEM)] * count


def smem(count=1):
    return [pl.BlockSpec(memory_space=pltpu.SMEM)] * count


PARAMS = pltpu.CompilerParams(vmem_limit_bytes=VMEM_LIMIT)


OWN_INDEX, COUNT, ENTRY = 0, 1, 8


def layout(lengths_ref, which, shards):
    starts, start, length = [jnp.int32(0)], jnp.int32(0), lengths_ref[which, 0]
    for r in range(1, lengths_ref.shape[1]):
        starts.append(starts[-1] + lengths_ref[which, r - 1])
        longer = lengths_ref[which, r] > length
        start = jnp.where(longer, starts[-1], start)
        length = jnp.where(longer, lengths_ref[which, r], length)
    return starts, start + lax.div(length, 2)


def plan_kernel(shards, reach, me_ref, lengths_ref, adapters_ref, owner_ref, out_ref):
    own_index, own_half = me_ref[0], me_ref[1]
    starts, offset = layout(lengths_ref, 0, shards)
    own_packed = lax.rem(own_index + offset, shards)
    first = jnp.int32(0)
    for start in starts[1:]:
        first = jnp.where(start <= own_packed, start, first)
    lanes = lax.broadcasted_iota(jnp.int32, out_ref.shape, 1)
    plan = jnp.where(lanes == COUNT, jnp.minimum(own_packed - first, reach) + 1, own_index)
    for which in range(lengths_ref.shape[0]):
        starts, offset = layout(lengths_ref, which, shards)
        entries = [owner_ref[adapters_ref[which, r]] for r in range(len(starts))]
        at = ENTRY + shards * (own_half if which == 0 else 1 - own_half)
        for shard in range(shards):
            packed = lax.rem(shard + offset, shards)
            entry = entries[0]
            for start, later in zip(starts[1:], entries[1:]):
                entry = jnp.where(start <= packed, later, entry)
            plan = jnp.where(lanes == at + shard, entry, plan)
    out_ref[...] = plan


def make_plan(shards, reach, me, lengths, adapters, owner):
    return pl.pallas_call(
        functools.partial(plan_kernel, shards, reach),
        out_shape=jax.ShapeDtypeStruct((1, 128), jnp.int32),
        in_specs=smem(4),
        out_specs=vmem()[0],
        name="plan",
    )(me, lengths, adapters, owner)


def pack_kernel(parts, halves, bank_ref, out_ref, held, in_sem, out_sem):
    own_half = lax.axis_index("groups") if halves == 2 else 0
    takes, gives = [], []
    for place in range(held.shape[0]):
        at = 0
        for index, (first, width) in enumerate(parts.all):
            start = pl.multiple_of(first + (place * halves + own_half) * width, 128)
            takes.append(
                pltpu.make_async_copy(
                    bank_ref.at[:, :, pl.ds(start, width)],
                    held.at[place, :, :, pl.ds(at, width)],
                    in_sem.at[place, index],
                )
            )
            at += width
        gives += [
            pltpu.make_async_copy(
                held.at[place], out_ref.at[again, place], out_sem.at[again, place]
            )
            for again in range(out_ref.shape[0])
        ]
    for copy in takes:
        copy.start()
    each, again = len(parts.all), out_ref.shape[0]
    for place in range(held.shape[0]):
        for copy in takes[place * each : (place + 1) * each]:
            copy.wait()
        for copy in gives[place * again : (place + 1) * again]:
            copy.start()
    for copy in gives:
        copy.wait()


def pack(parts, halves, shards, bank):
    width, places = sum(parts.widths), CHUNKS // halves
    again = shards // (places * ROW_BLOCKS)
    packed = pl.pallas_call(
        functools.partial(pack_kernel, parts, halves),
        out_shape=jax.ShapeDtypeStruct((again, places, ROW_BLOCKS, 16, width), bank.dtype),
        in_specs=[pl.BlockSpec(memory_space=pl.ANY)],
        out_specs=pl.BlockSpec(memory_space=pl.ANY),
        scratch_shapes=[
            pltpu.VMEM((places, ROW_BLOCKS, 16, width), bank.dtype),
            pltpu.SemaphoreType.DMA((places, len(parts.all))),
            pltpu.SemaphoreType.DMA((again, places)),
        ],
        compiler_params=pltpu.CompilerParams(vmem_limit_bytes=62 * 1024 * 1024),
        name="pack",
    )(bank.reshape(ROW_BLOCKS, 16, bank.shape[2]))
    return packed.reshape(shards, 16, width)


ROUTE_STEPS = 4


def route_kernel(at, plan_ref, spread_ref, out_ref):
    number = out_ref.shape[0]
    for i in range(number):
        entry = plan_ref[0, ENTRY + pl.program_id(0) * number + i]
        out_ref[i] = spread_ref[entry, :, at : at + out_ref.shape[2]]


def route(plan, spread, dests, at, width):
    return pl.pallas_call(
        functools.partial(route_kernel, at),
        out_shape=jax.ShapeDtypeStruct((dests, 16, width), spread.dtype),
        grid=(ROUTE_STEPS,),
        in_specs=smem() + vmem(),
        out_specs=pl.BlockSpec((dests // ROUTE_STEPS, 16, width), lambda i: (i, 0, 0)),
        compiler_params=PARAMS,
        name="route",
    )(plan, spread)


def factor(piece_ref, chunk, at, width):
    halves = piece_ref.shape[0]
    place = chunk // halves * ROW_BLOCKS
    rows = piece_ref[chunk % halves, place : place + ROW_BLOCKS, :, at : at + width]
    return rows.reshape(ROW_BLOCKS * 16, width)


def columns(chunk, width):
    return slice(chunk * width, (chunk + 1) * width)


def dot_nt(a, b):
    return lax.dot_general(a, b, (((1,), (1,)), ((), ())), preferred_element_type=jnp.float32)


def turn(x, cosines, sines):
    return x * cosines + pltpu.roll(x, HEAD_SIZE // 2, 1) * sines


def kv_kernel(hidden_ref, key_ref, value_ref, cos_ref, sin_ref, piece_ref, out_ref):
    d = hidden_ref.shape[1] // CHUNKS
    rank = ROW_BLOCKS * 16
    low = jnp.zeros((hidden_ref.shape[0], 2 * rank), jnp.float32)
    for chunk in range(CHUNKS):
        down = jnp.concatenate(
            [factor(piece_ref, chunk, 0, d), factor(piece_ref, chunk, d, d)], axis=0
        )
        low += dot_nt(hidden_ref[:, columns(chunk, d)], down)
    low = low.astype(jnp.bfloat16)
    width = 2 * key_ref.shape[1] // CHUNKS
    cosines, sines = cos_ref[...], sin_ref[...]
    for chunk in range(CHUNKS):
        is_key = chunk < CHUNKS // 2
        up = factor(piece_ref, chunk, 2 * d, width)
        part = low[:, :rank] if is_key else low[:, rank:]
        update = jnp.dot(part, up, preferred_element_type=jnp.float32)
        frozen = (key_ref if is_key else value_ref)[:, columns(chunk % (CHUNKS // 2), width)]
        result = frozen.astype(jnp.float32) + adapter_scale * update
        if is_key:
            result = turn(result, cosines, sines)
        out_ref[:, columns(chunk, width)] = result.astype(jnp.bfloat16)


def make_keys_values(hidden, key, value, tables, pieces):
    return pl.pallas_call(
        kv_kernel,
        out_shape=jax.ShapeDtypeStruct((key.shape[0], 2 * key.shape[1]), jnp.bfloat16),
        in_specs=vmem(6),
        out_specs=vmem()[0],
        compiler_params=PARAMS,
        cost_estimate=pl.CostEstimate(
            flops=150_000_000, bytes_accessed=3 << 20, transcendentals=0
        ),
        name="keys_values",
    )(hidden, key, value, *tables, pieces)


def query_kernel(at, hidden_ref, query_ref, cos_ref, sin_ref, piece_ref, out_ref):
    tokens = query_ref.shape[0]
    d = hidden_ref.shape[1] // CHUNKS
    width = query_ref.shape[1] // CHUNKS
    low = jnp.zeros((tokens, ROW_BLOCKS * 16), jnp.float32)
    for chunk in range(CHUNKS):
        low += dot_nt(hidden_ref[:, columns(chunk, d)], factor(piece_ref, chunk, at, d))
    low = low.astype(jnp.bfloat16)
    cosines, sines = cos_ref[...], sin_ref[...]
    for chunk in range(CHUNKS):
        up = factor(piece_ref, chunk, at + d, width)
        update = jnp.dot(low, up, preferred_element_type=jnp.float32)
        result = query_ref[:, columns(chunk, width)].astype(jnp.float32) + adapter_scale * update
        for part in range(width // HEAD_SIZE):
            head = chunk * (width // HEAD_SIZE) + part
            turned = turn(result[:, columns(part, HEAD_SIZE)], cosines, sines)
            out_ref[head // GROUP_SPLIT, pl.ds((head % GROUP_SPLIT) * tokens, tokens)] = (
                turned.astype(jnp.bfloat16)
            )


def make_queries(hidden, query, tables, pieces, at):
    tokens = hidden.shape[0]
    return pl.pallas_call(
        functools.partial(query_kernel, at),
        out_shape=jax.ShapeDtypeStruct(
            (KEY_VALUE_HEADS, GROUP_SPLIT * tokens, HEAD_SIZE), jnp.bfloat16
        ),
        in_specs=vmem(5),
        out_specs=vmem()[0],
        compiler_params=PARAMS,
        cost_estimate=pl.CostEstimate(
            flops=100_000_000, bytes_accessed=3 << 20, transcendentals=0
        ),
        name="queries",
    )(hidden, query, *tables, pieces)


REGION = 5


def attend_kernel(steps, plan_ref, queries, *refs):
    blocks, (out_ref, copy_ref, high, acc) = refs[:-4], refs[-4:]
    count = plan_ref[0, COUNT]
    odd = lax.rem(plan_ref[0, OWN_INDEX], 2)
    aside = 2 * odd - 1
    steps = [s if even else s + aside for s, even in steps]
    tokens = out_ref.shape[0]
    rows = GROUP_SPLIT * tokens
    bf16 = jnp.bfloat16
    base2 = 1.4426950408889634 / (HEAD_SIZE**0.5)
    ones = jnp.ones((tokens, HEAD_SIZE), bf16)

    def region(first, number):
        shards = blocks[first : first + number]
        for g in range(KEY_VALUE_HEADS):
            keys = [b[:, columns(g, HEAD_SIZE)] for b in shards]
            values = [
                jnp.concatenate([b[:, columns(KEY_VALUE_HEADS + g, HEAD_SIZE)], ones], axis=1)
                for b in shards
            ]
            score = dot_nt(queries[g], jnp.concatenate(keys, axis=0))
            tiles = [score[:, columns(i, tokens)] for i in range(number)]
            if first == 0:
                row = lax.broadcasted_iota(jnp.int32, (rows, tokens), 0) % tokens
                column = lax.broadcasted_iota(jnp.int32, (rows, tokens), 1)
                tiles = [jnp.where(column <= row, tiles[0], score_masked)]
            else:
                tiles = [
                    jnp.where((step > 0) & (step < count), tile, score_masked)
                    for step, tile in zip(steps[first : first + number], tiles)
                ]
            top = functools.reduce(jnp.maximum, tiles)
            top = jnp.max(top, axis=1, keepdims=True) * base2
            top = jnp.broadcast_to(top, (rows, HEAD_SIZE))
            if first:
                old = high[g]
                top = jnp.maximum(old, top)
            weight = [jnp.exp2(t * base2 - top).astype(bf16) for t in tiles]
            blend = jnp.dot(
                jnp.concatenate(weight, axis=1),
                jnp.concatenate(values, axis=0),
                preferred_element_type=jnp.float32,
            )
            if first:
                shrink = jnp.exp2(old - top)
                blend += acc[g] * jnp.concatenate([shrink, shrink], axis=1)
            high[g] = top
            acc[g] = blend

    region(0, 1)
    for first in range(1, len(blocks), REGION):
        number = min(REGION, len(blocks) - first)
        nearest = functools.reduce(jnp.minimum, steps[first : first + number])
        pl.when(count > nearest)(functools.partial(region, first, number))

    for g in range(KEY_VALUE_HEADS):
        result = (acc[g, :, :HEAD_SIZE] / acc[g, :, HEAD_SIZE:]).astype(bf16)
        for j in range(GROUP_SPLIT):
            for ref in (out_ref, copy_ref):
                ref[:, columns(g * GROUP_SPLIT + j, HEAD_SIZE)] = result[columns(j, tokens)]


def attend(plan, queries, blocks, steps):
    tokens = blocks[0].shape[0]
    rows = GROUP_SPLIT * tokens
    limit = VMEM_LIMIT if len(blocks) < 16 else 2 * VMEM_LIMIT
    return pl.pallas_call(
        functools.partial(attend_kernel, steps),
        out_shape=[jax.ShapeDtypeStruct((tokens, QUERY_HEADS * HEAD_SIZE), jnp.bfloat16)] * 2,
        in_specs=smem() + vmem(1 + len(blocks)),
        out_specs=vmem(2),
        scratch_shapes=[
            pltpu.VMEM((KEY_VALUE_HEADS, rows, HEAD_SIZE), jnp.float32),
            pltpu.VMEM((KEY_VALUE_HEADS, rows, 2 * HEAD_SIZE), jnp.float32),
        ],
        compiler_params=pltpu.CompilerParams(vmem_limit_bytes=limit),
        cost_estimate=pl.CostEstimate(
            flops=12_000_000_000, bytes_accessed=8 << 20, transcendentals=4 << 20
        ),
        name="attend",
    )(plan, queries, *blocks)


def output_kernel(attended_ref, piece_ref, out_ref, down, up, held, in_sem, out_sem):
    q_head, d = down.shape[3], up.shape[3]
    places = down.shape[1]
    halves = down.shape[0]

    def take(copy, at, half, index):
        source = piece_ref.at[half, pl.ds(0, places), :, pl.ds(at, copy.shape[3])]
        return pltpu.make_async_copy(source, copy.at[half], in_sem.at[index, half])

    takes = [take(down, 0, h, 0) for h in range(halves)]
    takes_up = [take(up, q_head, h, 1) for h in range(halves)]
    for copy in takes + takes_up:
        copy.start()
    for copy in takes:
        copy.wait()
    low = jnp.zeros((attended_ref.shape[0], ROW_BLOCKS * 16), jnp.float32)
    for chunk in range(CHUNKS):
        low += dot_nt(attended_ref[:, columns(chunk, q_head)], factor(down, chunk, 0, q_head))
    low = low.astype(jnp.bfloat16)
    for copy in takes_up:
        copy.wait()
    gives = []
    for chunk in range(CHUNKS):
        result = adapter_scale * jnp.dot(
            low, factor(up, chunk, 0, d), preferred_element_type=jnp.float32
        )
        at = pl.ds(chunk * d, d)
        held[:, at] = result.astype(jnp.bfloat16)
        gives.append(
            pltpu.make_async_copy(held.at[:, at], out_ref.at[:, at], out_sem.at[chunk])
        )
        gives[-1].start()
    for copy in gives:
        copy.wait()


def output_adapter(attended, pieces, model_width):
    tokens, query_width = attended.shape
    halves, places = pieces.shape[0], pieces.shape[1]
    any_space = pl.BlockSpec(memory_space=pl.ANY)
    return pl.pallas_call(
        output_kernel,
        out_shape=jax.ShapeDtypeStruct((tokens, model_width), jnp.bfloat16),
        in_specs=vmem() + [any_space],
        out_specs=any_space,
        scratch_shapes=[
            pltpu.VMEM((halves, places, 16, query_width // CHUNKS), jnp.bfloat16),
            pltpu.VMEM((halves, places, 16, model_width // CHUNKS), jnp.bfloat16),
            pltpu.VMEM((tokens, model_width), jnp.bfloat16),
            pltpu.SemaphoreType.DMA((2, halves)),
            pltpu.SemaphoreType.DMA((CHUNKS,)),
        ],
        compiler_params=PARAMS,
        cost_estimate=pl.CostEstimate(
            flops=100_000_000, bytes_accessed=3 << 20, transcendentals=0
        ),
        name="output",
    )(attended, pieces)


def earlier_shards(shards):
    longest = shards // 2 + 1
    low = -(longest // 2)
    runs = (
        [i % shards for i in range(low, low + longest)],
        [i % shards for i in range(low + longest, low + shards)],
    )
    limits = (longest, shards - longest - 1)
    earlier = {}
    for run, limit in zip(runs, limits):
        for i, shard in enumerate(run):
            earlier[shard] = set(run[max(0, i - limit + 1) : i])
    return earlier


def shift_pairs(shards, shift):
    earlier = earlier_shards(shards)
    pairs = [((d - shift) % shards, d) for d in range(shards)]
    return [(s, d) for s, d in pairs if s in earlier[d] or s in earlier[d ^ 1]]


def swap_pairs(shards, shift):
    earlier = earlier_shards(shards)
    return [(d, d ^ 1) for d in range(shards) if (d - shift) % shards in earlier[d ^ 1]]


def exchange(kv, queries, shards, reach):
    shifts = range(0, reach + 1, 2)
    got = [kv] + [lax.ppermute(kv, "ctx", shift_pairs(shards, s)) for s in shifts[1:]]
    got[1:], queries = lax.optimization_barrier((got[1:], queries))
    swapped = [lax.ppermute(b, "ctx", swap_pairs(shards, s)) for s, b in zip(shifts, got)]
    blocks, steps = [kv], [(0, True)]
    for s, even, odd in zip(shifts, got, swapped):
        if s:
            blocks.append(even)
            steps.append((s, True))
        blocks.append(odd)
        steps.append((s, False))
    return blocks, steps, queries


def body(
    hidden,
    frozen_query,
    frozen_key,
    frozen_value,
    adapter_bank,
    request_shards,
    request_adapter,
    adapter_owner,
):
    shards = lax.axis_size("ctx")
    groups = lax.axis_size("groups")
    tokens, model_width = hidden.shape
    halves = 2 if groups == 2 and 2 * shards == ROW_BLOCKS * CHUNKS else 1
    own_half = lax.axis_index("groups") if halves == 2 else 0
    me = jnp.stack([lax.axis_index("ctx"), own_half]).astype(jnp.int32)
    parts = Parts(model_width, frozen_query.shape[1], frozen_key.shape[1])
    reach = shards // 2

    packed = pack(parts, halves, shards, adapter_bank)
    spread = lax.all_to_all(packed, "ctx", split_axis=0, concat_axis=0, tiled=True)

    requests = jnp.stack([request_shards, request_adapter])[:, None]
    if halves == 2:
        theirs = lax.ppermute(requests, "groups", [(0, 1), (1, 0)])
        requests = jnp.concatenate([requests, theirs], axis=1)
    plan = make_plan(shards, reach, me, requests[0], requests[1], adapter_owner)
    positions = (plan[0, COUNT] - 1) * tokens + jnp.arange(tokens, dtype=jnp.int32)
    tables = rope_tables(positions)
    spread, tables = lax.optimization_barrier((spread, tables))

    def collect(pieces):
        axes = ("groups", "ctx") if halves == 2 else "ctx"
        pieces = lax.all_to_all(pieces, axes, split_axis=0, concat_axis=0, tiled=True)
        return pieces.reshape((halves, shards) + pieces.shape[1:])[:, : ROW_BLOCKS * CHUNKS]

    kv_width, q_width, o_width = parts.widths
    dests = shards * halves
    pieces = collect(route(plan, spread, dests, 0, kv_width + q_width))
    kv = make_keys_values(hidden, frozen_key, frozen_value, tables, pieces)
    queries = make_queries(hidden, frozen_query, tables, pieces, kv_width)
    blocks, steps, queries = exchange(kv, queries, shards, reach)
    later = route(plan, spread, dests, kv_width + q_width, o_width)
    kv, later = lax.optimization_barrier((kv, later))
    later = collect(later)
    attended, copy = attend(plan, queries, blocks, steps)
    return attended, output_adapter(copy, later, model_width)


def solution(mesh):
    return jax.shard_map(
        body,
        mesh=mesh,
        in_specs=(
            P(("groups", "ctx"), None),
            P(("groups", "ctx"), None),
            P(("groups", "ctx"), None),
            P(("groups", "ctx"), None),
            P("ctx", None, None),
            P("groups"),
            P("groups"),
            P(),
        ),
        out_specs=(P(("groups", "ctx"), None), P(("groups", "ctx"), None)),
        check_vma=False,
    )
```

```python
import functools

import jax
import jax.numpy as jnp
from jax import lax
from jax.experimental import pallas as pl
from jax.experimental.pallas import tpu as pltpu
from jax.sharding import PartitionSpec as P

HEAD_SIZE = 128
QUERY_HEADS = 16
KEY_VALUE_HEADS = 4
GROUP_SPLIT = QUERY_HEADS // KEY_VALUE_HEADS

adapter_scale = 0.5
rope_theta = 500000.0
score_masked = -1e30

VMEM_LIMIT = 24 * 1024 * 1024

ROW_BLOCKS = 4
CHUNKS = 8


def rope_tables(positions):
    half_dim = HEAD_SIZE // 2
    frequency = rope_theta ** (-(jnp.arange(half_dim, dtype=jnp.float32) * 2.0) / HEAD_SIZE)
    angles = positions.astype(jnp.float32)[..., None] * frequency
    cosines = jnp.cos(angles)
    sines = jnp.sin(angles)
    return (jnp.concatenate([cosines, cosines], -1), jnp.concatenate([-sines, sines], -1))


class Parts:
    def __init__(self, model_width, query_width, key_width):
        d, q, k = model_width, query_width, key_width
        up = 3 * d
        self.kv = ((d, d // CHUNKS), (2 * d, d // CHUNKS), (up + q, 2 * k // CHUNKS))
        self.q = ((0, d // CHUNKS), (up, q // CHUNKS))
        self.o = ((up + q + 2 * k, q // CHUNKS), (up + 2 * q + 2 * k, d // CHUNKS))
        self.all = self.kv + self.q + self.o
        self.widths = tuple(sum(w for _, w in part) for part in (self.kv, self.q, self.o))


def vmem(count=1):
    return [pl.BlockSpec(memory_space=pltpu.VMEM)] * count


def smem(count=1):
    return [pl.BlockSpec(memory_space=pltpu.SMEM)] * count


PARAMS = pltpu.CompilerParams(vmem_limit_bytes=VMEM_LIMIT)


OWN_INDEX, COUNT, ENTRY = 0, 1, 8


def layout(lengths_ref, which, shards):
    starts, start, length = [jnp.int32(0)], jnp.int32(0), lengths_ref[which, 0]
    for r in range(1, lengths_ref.shape[1]):
        starts.append(starts[-1] + lengths_ref[which, r - 1])
        longer = lengths_ref[which, r] > length
        start = jnp.where(longer, starts[-1], start)
        length = jnp.where(longer, lengths_ref[which, r], length)
    return starts, start + lax.div(length, 2)


def plan_kernel(shards, reach, me_ref, lengths_ref, adapters_ref, owner_ref, out_ref):
    own_index, own_half = me_ref[0], me_ref[1]
    starts, offset = layout(lengths_ref, 0, shards)
    own_packed = lax.rem(own_index + offset, shards)
    first = jnp.int32(0)
    for start in starts[1:]:
        first = jnp.where(start <= own_packed, start, first)
    lanes = lax.broadcasted_iota(jnp.int32, out_ref.shape, 1)
    plan = jnp.where(lanes == COUNT, jnp.minimum(own_packed - first, reach) + 1, own_index)
    for which in range(lengths_ref.shape[0]):
        starts, offset = layout(lengths_ref, which, shards)
        entries = [owner_ref[adapters_ref[which, r]] for r in range(len(starts))]
        at = ENTRY + shards * (own_half if which == 0 else 1 - own_half)
        for shard in range(shards):
            packed = lax.rem(shard + offset, shards)
            entry = entries[0]
            for start, later in zip(starts[1:], entries[1:]):
                entry = jnp.where(start <= packed, later, entry)
            plan = jnp.where(lanes == at + shard, entry, plan)
    out_ref[...] = plan


def make_plan(shards, reach, me, lengths, adapters, owner):
    return pl.pallas_call(
        functools.partial(plan_kernel, shards, reach),
        out_shape=jax.ShapeDtypeStruct((1, 128), jnp.int32),
        in_specs=smem(4),
        out_specs=vmem()[0],
        name="plan",
    )(me, lengths, adapters, owner)


def pack_kernel(parts, halves, bank_ref, out_ref, held, in_sem, out_sem):
    own_half = lax.axis_index("groups") if halves == 2 else 0
    takes, gives = [], []
    for place in range(held.shape[0]):
        at = 0
        for index, (first, width) in enumerate(parts.all):
            start = pl.multiple_of(first + (place * halves + own_half) * width, 128)
            takes.append(
                pltpu.make_async_copy(
                    bank_ref.at[:, :, pl.ds(start, width)],
                    held.at[place, :, :, pl.ds(at, width)],
                    in_sem.at[place, index],
                )
            )
            at += width
        gives += [
            pltpu.make_async_copy(
                held.at[place], out_ref.at[again, place], out_sem.at[again, place]
            )
            for again in range(out_ref.shape[0])
        ]
    for copy in takes:
        copy.start()
    each, again = len(parts.all), out_ref.shape[0]
    for place in range(held.shape[0]):
        for copy in takes[place * each : (place + 1) * each]:
            copy.wait()
        for copy in gives[place * again : (place + 1) * again]:
            copy.start()
    for copy in gives:
        copy.wait()


def pack(parts, halves, shards, bank):
    width, places = sum(parts.widths), CHUNKS // halves
    again = shards // (places * ROW_BLOCKS)
    packed = pl.pallas_call(
        functools.partial(pack_kernel, parts, halves),
        out_shape=jax.ShapeDtypeStruct((again, places, ROW_BLOCKS, 16, width), bank.dtype),
        in_specs=[pl.BlockSpec(memory_space=pl.ANY)],
        out_specs=pl.BlockSpec(memory_space=pl.ANY),
        scratch_shapes=[
            pltpu.VMEM((places, ROW_BLOCKS, 16, width), bank.dtype),
            pltpu.SemaphoreType.DMA((places, len(parts.all))),
            pltpu.SemaphoreType.DMA((again, places)),
        ],
        compiler_params=pltpu.CompilerParams(vmem_limit_bytes=62 * 1024 * 1024),
        name="pack",
    )(bank.reshape(ROW_BLOCKS, 16, bank.shape[2]))
    return packed.reshape(shards, 16, width)


ROUTE_STEPS = 4


def route_kernel(at, plan_ref, spread_ref, out_ref):
    number = out_ref.shape[0]
    for i in range(number):
        entry = plan_ref[0, ENTRY + pl.program_id(0) * number + i]
        out_ref[i] = spread_ref[entry, :, at : at + out_ref.shape[2]]


def route(plan, spread, dests, at, width):
    return pl.pallas_call(
        functools.partial(route_kernel, at),
        out_shape=jax.ShapeDtypeStruct((dests, 16, width), spread.dtype),
        grid=(ROUTE_STEPS,),
        in_specs=smem() + vmem(),
        out_specs=pl.BlockSpec((dests // ROUTE_STEPS, 16, width), lambda i: (i, 0, 0)),
        compiler_params=PARAMS,
        name="route",
    )(plan, spread)


def factor(piece_ref, chunk, at, width):
    halves = piece_ref.shape[0]
    place = chunk // halves * ROW_BLOCKS
    rows = piece_ref[chunk % halves, place : place + ROW_BLOCKS, :, at : at + width]
    return rows.reshape(ROW_BLOCKS * 16, width)


def columns(chunk, width):
    return slice(chunk * width, (chunk + 1) * width)


def dot_nt(a, b):
    return lax.dot_general(a, b, (((1,), (1,)), ((), ())), preferred_element_type=jnp.float32)


def turn(x, cosines, sines):
    return x * cosines + pltpu.roll(x, HEAD_SIZE // 2, 1) * sines


def kv_kernel(hidden_ref, key_ref, value_ref, cos_ref, sin_ref, piece_ref, out_ref):
    d = hidden_ref.shape[1] // CHUNKS
    rank = ROW_BLOCKS * 16
    low = jnp.zeros((hidden_ref.shape[0], 2 * rank), jnp.float32)
    for chunk in range(CHUNKS):
        down = jnp.concatenate(
            [factor(piece_ref, chunk, 0, d), factor(piece_ref, chunk, d, d)], axis=0
        )
        low += dot_nt(hidden_ref[:, columns(chunk, d)], down)
    low = low.astype(jnp.bfloat16)
    width = 2 * key_ref.shape[1] // CHUNKS
    cosines, sines = cos_ref[...], sin_ref[...]
    for chunk in range(CHUNKS):
        is_key = chunk < CHUNKS // 2
        up = factor(piece_ref, chunk, 2 * d, width)
        part = low[:, :rank] if is_key else low[:, rank:]
        update = jnp.dot(part, up, preferred_element_type=jnp.float32)
        frozen = (key_ref if is_key else value_ref)[:, columns(chunk % (CHUNKS // 2), width)]
        result = frozen.astype(jnp.float32) + adapter_scale * update
        if is_key:
            result = turn(result, cosines, sines)
        out_ref[:, columns(chunk, width)] = result.astype(jnp.bfloat16)


def make_keys_values(hidden, key, value, tables, pieces):
    return pl.pallas_call(
        kv_kernel,
        out_shape=jax.ShapeDtypeStruct((key.shape[0], 2 * key.shape[1]), jnp.bfloat16),
        in_specs=vmem(6),
        out_specs=vmem()[0],
        compiler_params=PARAMS,
        cost_estimate=pl.CostEstimate(
            flops=150_000_000, bytes_accessed=3 << 20, transcendentals=0
        ),
        name="keys_values",
    )(hidden, key, value, *tables, pieces)


def query_kernel(at, hidden_ref, query_ref, cos_ref, sin_ref, piece_ref, out_ref):
    tokens = query_ref.shape[0]
    d = hidden_ref.shape[1] // CHUNKS
    width = query_ref.shape[1] // CHUNKS
    low = jnp.zeros((tokens, ROW_BLOCKS * 16), jnp.float32)
    for chunk in range(CHUNKS):
        low += dot_nt(hidden_ref[:, columns(chunk, d)], factor(piece_ref, chunk, at, d))
    low = low.astype(jnp.bfloat16)
    cosines, sines = cos_ref[...], sin_ref[...]
    for chunk in range(CHUNKS):
        up = factor(piece_ref, chunk, at + d, width)
        update = jnp.dot(low, up, preferred_element_type=jnp.float32)
        result = query_ref[:, columns(chunk, width)].astype(jnp.float32) + adapter_scale * update
        for part in range(width // HEAD_SIZE):
            head = chunk * (width // HEAD_SIZE) + part
            turned = turn(result[:, columns(part, HEAD_SIZE)], cosines, sines)
            out_ref[head // GROUP_SPLIT, pl.ds((head % GROUP_SPLIT) * tokens, tokens)] = (
                turned.astype(jnp.bfloat16)
            )


def make_queries(hidden, query, tables, pieces, at):
    tokens = hidden.shape[0]
    return pl.pallas_call(
        functools.partial(query_kernel, at),
        out_shape=jax.ShapeDtypeStruct(
            (KEY_VALUE_HEADS, GROUP_SPLIT * tokens, HEAD_SIZE), jnp.bfloat16
        ),
        in_specs=vmem(5),
        out_specs=vmem()[0],
        compiler_params=PARAMS,
        cost_estimate=pl.CostEstimate(
            flops=100_000_000, bytes_accessed=3 << 20, transcendentals=0
        ),
        name="queries",
    )(hidden, query, *tables, pieces)


REGION = 5


def attend_kernel(steps, plan_ref, queries, *refs):
    blocks, (out_ref, copy_ref, high, acc) = refs[:-4], refs[-4:]
    count = plan_ref[0, COUNT]
    odd = lax.rem(plan_ref[0, OWN_INDEX], 2)
    aside = 2 * odd - 1
    steps = [s if even else s + aside for s, even in steps]
    tokens = out_ref.shape[0]
    rows = GROUP_SPLIT * tokens
    bf16 = jnp.bfloat16
    base2 = 1.4426950408889634 / (HEAD_SIZE**0.5)
    ones = jnp.ones((tokens, HEAD_SIZE), bf16)

    def region(first, number):
        shards = blocks[first : first + number]
        for g in range(KEY_VALUE_HEADS):
            keys = [b[:, columns(g, HEAD_SIZE)] for b in shards]
            values = [
                jnp.concatenate([b[:, columns(KEY_VALUE_HEADS + g, HEAD_SIZE)], ones], axis=1)
                for b in shards
            ]
            score = dot_nt(queries[g], jnp.concatenate(keys, axis=0))
            tiles = [score[:, columns(i, tokens)] for i in range(number)]
            if first == 0:
                row = lax.broadcasted_iota(jnp.int32, (rows, tokens), 0) % tokens
                column = lax.broadcasted_iota(jnp.int32, (rows, tokens), 1)
                tiles = [jnp.where(column <= row, tiles[0], score_masked)]
            else:
                tiles = [
                    jnp.where((step > 0) & (step < count), tile, score_masked)
                    for step, tile in zip(steps[first : first + number], tiles)
                ]
            top = functools.reduce(jnp.maximum, tiles)
            top = jnp.max(top, axis=1, keepdims=True) * base2
            top = jnp.broadcast_to(top, (rows, HEAD_SIZE))
            if first:
                old = high[g]
                top = jnp.maximum(old, top)
            weight = [jnp.exp2(t * base2 - top).astype(bf16) for t in tiles]
            blend = jnp.dot(
                jnp.concatenate(weight, axis=1),
                jnp.concatenate(values, axis=0),
                preferred_element_type=jnp.float32,
            )
            if first:
                shrink = jnp.exp2(old - top)
                blend += acc[g] * jnp.concatenate([shrink, shrink], axis=1)
            high[g] = top
            acc[g] = blend

    region(0, 1)
    for first in range(1, len(blocks), REGION):
        number = min(REGION, len(blocks) - first)
        nearest = functools.reduce(jnp.minimum, steps[first : first + number])
        pl.when(count > nearest)(functools.partial(region, first, number))

    for g in range(KEY_VALUE_HEADS):
        result = (acc[g, :, :HEAD_SIZE] / acc[g, :, HEAD_SIZE:]).astype(bf16)
        for j in range(GROUP_SPLIT):
            for ref in (out_ref, copy_ref):
                ref[:, columns(g * GROUP_SPLIT + j, HEAD_SIZE)] = result[columns(j, tokens)]


def attend(plan, queries, blocks, steps):
    tokens = blocks[0].shape[0]
    rows = GROUP_SPLIT * tokens
    limit = VMEM_LIMIT if len(blocks) < 16 else 2 * VMEM_LIMIT
    return pl.pallas_call(
        functools.partial(attend_kernel, steps),
        out_shape=[jax.ShapeDtypeStruct((tokens, QUERY_HEADS * HEAD_SIZE), jnp.bfloat16)] * 2,
        in_specs=smem() + vmem(1 + len(blocks)),
        out_specs=vmem(2),
        scratch_shapes=[
            pltpu.VMEM((KEY_VALUE_HEADS, rows, HEAD_SIZE), jnp.float32),
            pltpu.VMEM((KEY_VALUE_HEADS, rows, 2 * HEAD_SIZE), jnp.float32),
        ],
        compiler_params=pltpu.CompilerParams(vmem_limit_bytes=limit),
        cost_estimate=pl.CostEstimate(
            flops=12_000_000_000, bytes_accessed=8 << 20, transcendentals=4 << 20
        ),
        name="attend",
    )(plan, queries, *blocks)


def output_kernel(attended_ref, piece_ref, out_ref, down, up, held, in_sem, out_sem):
    q_head, d = down.shape[3], up.shape[3]
    places = down.shape[1]
    halves = down.shape[0]

    def take(copy, at, half, index):
        source = piece_ref.at[half, pl.ds(0, places), :, pl.ds(at, copy.shape[3])]
        return pltpu.make_async_copy(source, copy.at[half], in_sem.at[index, half])

    takes = [take(down, 0, h, 0) for h in range(halves)]
    takes_up = [take(up, q_head, h, 1) for h in range(halves)]
    for copy in takes + takes_up:
        copy.start()
    for copy in takes:
        copy.wait()
    low = jnp.zeros((attended_ref.shape[0], ROW_BLOCKS * 16), jnp.float32)
    for chunk in range(CHUNKS):
        low += dot_nt(attended_ref[:, columns(chunk, q_head)], factor(down, chunk, 0, q_head))
    low = low.astype(jnp.bfloat16)
    for copy in takes_up:
        copy.wait()
    gives = []
    for chunk in range(CHUNKS):
        result = adapter_scale * jnp.dot(
            low, factor(up, chunk, 0, d), preferred_element_type=jnp.float32
        )
        at = pl.ds(chunk * d, d)
        held[:, at] = result.astype(jnp.bfloat16)
        gives.append(
            pltpu.make_async_copy(held.at[:, at], out_ref.at[:, at], out_sem.at[chunk])
        )
        gives[-1].start()
    for copy in gives:
        copy.wait()


def output_adapter(attended, pieces, model_width):
    tokens, query_width = attended.shape
    halves, places = pieces.shape[0], pieces.shape[1]
    any_space = pl.BlockSpec(memory_space=pl.ANY)
    return pl.pallas_call(
        output_kernel,
        out_shape=jax.ShapeDtypeStruct((tokens, model_width), jnp.bfloat16),
        in_specs=vmem() + [any_space],
        out_specs=any_space,
        scratch_shapes=[
            pltpu.VMEM((halves, places, 16, query_width // CHUNKS), jnp.bfloat16),
            pltpu.VMEM((halves, places, 16, model_width // CHUNKS), jnp.bfloat16),
            pltpu.VMEM((tokens, model_width), jnp.bfloat16),
            pltpu.SemaphoreType.DMA((2, halves)),
            pltpu.SemaphoreType.DMA((CHUNKS,)),
        ],
        compiler_params=PARAMS,
        cost_estimate=pl.CostEstimate(
            flops=100_000_000, bytes_accessed=3 << 20, transcendentals=0
        ),
        name="output",
    )(attended, pieces)


def earlier_shards(shards):
    longest = shards // 2 + 1
    low = -(longest // 2)
    runs = (
        [i % shards for i in range(low, low + longest)],
        [i % shards for i in range(low + longest, low + shards)],
    )
    limits = (longest, shards - longest - 1)
    earlier = {}
    for run, limit in zip(runs, limits):
        for i, shard in enumerate(run):
            earlier[shard] = set(run[max(0, i - limit + 1) : i])
    return earlier


def shift_pairs(shards, shift):
    earlier = earlier_shards(shards)
    pairs = [((d - shift) % shards, d) for d in range(shards)]
    return [(s, d) for s, d in pairs if s in earlier[d] or s in earlier[d ^ 1]]


def swap_pairs(shards, shift):
    earlier = earlier_shards(shards)
    return [(d, d ^ 1) for d in range(shards) if (d - shift) % shards in earlier[d ^ 1]]


DETOUR_SHIFT, DETOUR_FIRST, DETOUR_VIA = 6, (4, 5), 2


def exchange(kv, queries, shards, reach, detour):
    shifts = range(0, reach + 1, 2)
    routes = [shift_pairs(shards, s) for s in shifts]
    if detour:
        direct, later = DETOUR_SHIFT // 2, (DETOUR_SHIFT + DETOUR_VIA) // 2
        turned = [(s, d) for s, d in routes[direct] if d in DETOUR_FIRST]
        routes[direct] = [pair for pair in routes[direct] if pair not in turned]
        routes[later] = routes[later] + [(s, d + DETOUR_VIA) for s, d in turned]
    got = [kv] + [lax.ppermute(kv, "ctx", route) for route in routes[1:]]
    if detour:
        hop = lax.ppermute(got[later], "ctx", [(d + DETOUR_VIA, d) for _, d in turned])
        got[direct] = got[direct] + hop
    got[1:], queries = lax.optimization_barrier((got[1:], queries))
    swapped = [lax.ppermute(b, "ctx", swap_pairs(shards, s)) for s, b in zip(shifts, got)]
    blocks, steps = [kv], [(0, True)]
    for s, even, odd in zip(shifts, got, swapped):
        if s:
            blocks.append(even)
            steps.append((s, True))
        blocks.append(odd)
        steps.append((s, False))
    return blocks, steps, queries


def body(
    hidden,
    frozen_query,
    frozen_key,
    frozen_value,
    adapter_bank,
    request_shards,
    request_adapter,
    adapter_owner,
):
    shards = lax.axis_size("ctx")
    groups = lax.axis_size("groups")
    tokens, model_width = hidden.shape
    halves = 2 if groups == 2 and 2 * shards == ROW_BLOCKS * CHUNKS else 1
    own_half = lax.axis_index("groups") if halves == 2 else 0
    me = jnp.stack([lax.axis_index("ctx"), own_half]).astype(jnp.int32)
    parts = Parts(model_width, frozen_query.shape[1], frozen_key.shape[1])
    reach = shards // 2

    packed = pack(parts, halves, shards, adapter_bank)
    spread = lax.all_to_all(packed, "ctx", split_axis=0, concat_axis=0, tiled=True)

    requests = jnp.stack([request_shards, request_adapter])[:, None]
    if halves == 2:
        theirs = lax.ppermute(requests, "groups", [(0, 1), (1, 0)])
        requests = jnp.concatenate([requests, theirs], axis=1)
    plan = make_plan(shards, reach, me, requests[0], requests[1], adapter_owner)
    plan = jnp.maximum(plan, 0)
    positions = (plan[0, COUNT] - 1) * tokens + jnp.arange(tokens, dtype=jnp.int32)
    tables = rope_tables(positions)
    spread, tables, plan = lax.optimization_barrier((spread, tables, plan))

    def collect(pieces):
        axes = ("groups", "ctx") if halves == 2 else "ctx"
        pieces = lax.all_to_all(pieces, axes, split_axis=0, concat_axis=0, tiled=True)
        return pieces.reshape((halves, shards) + pieces.shape[1:])[:, : ROW_BLOCKS * CHUNKS]

    kv_width, q_width, o_width = parts.widths
    dests = shards * halves
    pieces = collect(route(plan, spread, dests, 0, kv_width + q_width))
    kv = make_keys_values(hidden, frozen_key, frozen_value, tables, pieces)
    queries = make_queries(hidden, frozen_query, tables, pieces, kv_width)
    blocks, steps, queries = exchange(kv, queries, shards, reach, halves == 2)
    later = route(plan, spread, dests, kv_width + q_width, o_width)
    kv, later = lax.optimization_barrier((kv, later))
    later = collect(later)
    attended, copy = attend(plan, queries, blocks, steps)
    return attended, output_adapter(copy, later, model_width)


def solution(mesh):
    return jax.shard_map(
        body,
        mesh=mesh,
        in_specs=(
            P(("groups", "ctx"), None),
            P(("groups", "ctx"), None),
            P(("groups", "ctx"), None),
            P(("groups", "ctx"), None),
            P("ctx", None, None),
            P("groups"),
            P("groups"),
            P(),
        ),
        out_specs=(P(("groups", "ctx"), None), P(("groups", "ctx"), None)),
        check_vma=False,
    )
```

```python
import functools

import jax
import jax.numpy as jnp
from jax import lax
from jax.experimental import pallas as pl
from jax.experimental.pallas import tpu as pltpu
from jax.sharding import PartitionSpec as P

HEAD_SIZE = 128
QUERY_HEADS = 16
KEY_VALUE_HEADS = 4
GROUP_SPLIT = QUERY_HEADS // KEY_VALUE_HEADS

adapter_scale = 0.5
rope_theta = 500000.0
score_masked = -1e30

VMEM_LIMIT = 24 * 1024 * 1024

ROW_BLOCKS = 4
CHUNKS = 8


def rope_tables(positions):
    half_dim = HEAD_SIZE // 2
    frequency = rope_theta ** (-(jnp.arange(half_dim, dtype=jnp.float32) * 2.0) / HEAD_SIZE)
    angles = positions.astype(jnp.float32)[..., None] * frequency
    cosines = jnp.cos(angles)
    sines = jnp.sin(angles)
    return (jnp.concatenate([cosines, cosines], -1), jnp.concatenate([-sines, sines], -1))


class Parts:
    def __init__(self, model_width, query_width, key_width):
        d, q, k = model_width, query_width, key_width
        up = 3 * d
        self.kv = ((d, d // CHUNKS), (2 * d, d // CHUNKS), (up + q, 2 * k // CHUNKS))
        self.q = ((0, d // CHUNKS), (up, q // CHUNKS))
        self.o = ((up + q + 2 * k, q // CHUNKS), (up + 2 * q + 2 * k, d // CHUNKS))
        self.all = self.kv + self.q + self.o
        self.widths = tuple(sum(w for _, w in part) for part in (self.kv, self.q, self.o))


def vmem(count=1):
    return [pl.BlockSpec(memory_space=pltpu.VMEM)] * count


def smem(count=1):
    return [pl.BlockSpec(memory_space=pltpu.SMEM)] * count


PARAMS = pltpu.CompilerParams(vmem_limit_bytes=VMEM_LIMIT)


OWN_INDEX, COUNT, ENTRY = 0, 1, 8


def layout(lengths_ref, which, shards):
    starts, start, length = [jnp.int32(0)], jnp.int32(0), lengths_ref[which, 0]
    for r in range(1, lengths_ref.shape[1]):
        starts.append(starts[-1] + lengths_ref[which, r - 1])
        longer = lengths_ref[which, r] > length
        start = jnp.where(longer, starts[-1], start)
        length = jnp.where(longer, lengths_ref[which, r], length)
    return starts, start + lax.div(length, 2)


def plan_kernel(shards, reach, me_ref, lengths_ref, adapters_ref, owner_ref, out_ref):
    own_index, own_half = me_ref[0], me_ref[1]
    starts, offset = layout(lengths_ref, 0, shards)
    own_packed = lax.rem(own_index + offset, shards)
    first = jnp.int32(0)
    for start in starts[1:]:
        first = jnp.where(start <= own_packed, start, first)
    lanes = lax.broadcasted_iota(jnp.int32, out_ref.shape, 1)
    plan = jnp.where(lanes == COUNT, jnp.minimum(own_packed - first, reach) + 1, own_index)
    for which in range(lengths_ref.shape[0]):
        starts, offset = layout(lengths_ref, which, shards)
        entries = [owner_ref[adapters_ref[which, r]] for r in range(len(starts))]
        at = ENTRY + shards * (own_half if which == 0 else 1 - own_half)
        for shard in range(shards):
            packed = lax.rem(shard + offset, shards)
            entry = entries[0]
            for start, later in zip(starts[1:], entries[1:]):
                entry = jnp.where(start <= packed, later, entry)
            plan = jnp.where(lanes == at + shard, entry, plan)
    out_ref[...] = plan


def make_plan(shards, reach, me, lengths, adapters, owner):
    return pl.pallas_call(
        functools.partial(plan_kernel, shards, reach),
        out_shape=jax.ShapeDtypeStruct((1, 128), jnp.int32),
        in_specs=smem(4),
        out_specs=vmem()[0],
        name="plan",
    )(me, lengths, adapters, owner)


def pack_kernel(parts, halves, bank_ref, out_ref, held, in_sem, out_sem):
    own_half = lax.axis_index("groups") if halves == 2 else 0
    takes, gives = [], []
    for place in range(held.shape[0]):
        at = 0
        for index, (first, width) in enumerate(parts.all):
            start = pl.multiple_of(first + (place * halves + own_half) * width, 128)
            takes.append(
                pltpu.make_async_copy(
                    bank_ref.at[:, :, pl.ds(start, width)],
                    held.at[place, :, :, pl.ds(at, width)],
                    in_sem.at[place, index],
                )
            )
            at += width
        gives += [
            pltpu.make_async_copy(
                held.at[place], out_ref.at[again, place], out_sem.at[again, place]
            )
            for again in range(out_ref.shape[0])
        ]
    for copy in takes:
        copy.start()
    each, again = len(parts.all), out_ref.shape[0]
    for place in range(held.shape[0]):
        for copy in takes[place * each : (place + 1) * each]:
            copy.wait()
        for copy in gives[place * again : (place + 1) * again]:
            copy.start()
    for copy in gives:
        copy.wait()


def pack(parts, halves, shards, bank):
    width, places = sum(parts.widths), CHUNKS // halves
    again = shards // (places * ROW_BLOCKS)
    packed = pl.pallas_call(
        functools.partial(pack_kernel, parts, halves),
        out_shape=jax.ShapeDtypeStruct((again, places, ROW_BLOCKS, 16, width), bank.dtype),
        in_specs=[pl.BlockSpec(memory_space=pl.ANY)],
        out_specs=pl.BlockSpec(memory_space=pl.ANY),
        scratch_shapes=[
            pltpu.VMEM((places, ROW_BLOCKS, 16, width), bank.dtype),
            pltpu.SemaphoreType.DMA((places, len(parts.all))),
            pltpu.SemaphoreType.DMA((again, places)),
        ],
        compiler_params=pltpu.CompilerParams(vmem_limit_bytes=62 * 1024 * 1024),
        name="pack",
    )(bank.reshape(ROW_BLOCKS, 16, bank.shape[2]))
    return packed.reshape(shards, 16, width)


ROUTE_STEPS = 4


def route_kernel(at, plan_ref, spread_ref, out_ref):
    number = out_ref.shape[0]
    for i in range(number):
        entry = plan_ref[0, ENTRY + pl.program_id(0) * number + i]
        out_ref[i] = spread_ref[entry, :, at : at + out_ref.shape[2]]


def route(plan, spread, dests, at, width):
    return pl.pallas_call(
        functools.partial(route_kernel, at),
        out_shape=jax.ShapeDtypeStruct((dests, 16, width), spread.dtype),
        grid=(ROUTE_STEPS,),
        in_specs=smem() + vmem(),
        out_specs=pl.BlockSpec((dests // ROUTE_STEPS, 16, width), lambda i: (i, 0, 0)),
        compiler_params=PARAMS,
        name="route",
    )(plan, spread)


def factor(piece_ref, chunk, at, width):
    halves = piece_ref.shape[0]
    place = chunk // halves * ROW_BLOCKS
    rows = piece_ref[chunk % halves, place : place + ROW_BLOCKS, :, at : at + width]
    return rows.reshape(ROW_BLOCKS * 16, width)


def columns(chunk, width):
    return slice(chunk * width, (chunk + 1) * width)


def dot_nt(a, b):
    return lax.dot_general(a, b, (((1,), (1,)), ((), ())), preferred_element_type=jnp.float32)


def turn(x, cosines, sines):
    return x * cosines + pltpu.roll(x, HEAD_SIZE // 2, 1) * sines


def kv_kernel(hidden_ref, key_ref, value_ref, cos_ref, sin_ref, piece_ref, out_ref):
    d = hidden_ref.shape[1] // CHUNKS
    rank = ROW_BLOCKS * 16
    low = jnp.zeros((hidden_ref.shape[0], 2 * rank), jnp.float32)
    for chunk in range(CHUNKS):
        down = jnp.concatenate(
            [factor(piece_ref, chunk, 0, d), factor(piece_ref, chunk, d, d)], axis=0
        )
        low += dot_nt(hidden_ref[:, columns(chunk, d)], down)
    low = low.astype(jnp.bfloat16)
    width = 2 * key_ref.shape[1] // CHUNKS
    cosines, sines = cos_ref[...], sin_ref[...]
    for chunk in range(CHUNKS):
        is_key = chunk < CHUNKS // 2
        up = factor(piece_ref, chunk, 2 * d, width)
        part = low[:, :rank] if is_key else low[:, rank:]
        update = jnp.dot(part, up, preferred_element_type=jnp.float32)
        frozen = (key_ref if is_key else value_ref)[:, columns(chunk % (CHUNKS // 2), width)]
        result = frozen.astype(jnp.float32) + adapter_scale * update
        if is_key:
            result = turn(result, cosines, sines)
        out_ref[:, columns(chunk, width)] = result.astype(jnp.bfloat16)


def make_keys_values(hidden, key, value, tables, pieces):
    return pl.pallas_call(
        kv_kernel,
        out_shape=jax.ShapeDtypeStruct((key.shape[0], 2 * key.shape[1]), jnp.bfloat16),
        in_specs=vmem(6),
        out_specs=vmem()[0],
        compiler_params=PARAMS,
        cost_estimate=pl.CostEstimate(
            flops=150_000_000, bytes_accessed=3 << 20, transcendentals=0
        ),
        name="keys_values",
    )(hidden, key, value, *tables, pieces)


def query_kernel(at, hidden_ref, query_ref, cos_ref, sin_ref, piece_ref, out_ref):
    tokens = query_ref.shape[0]
    d = hidden_ref.shape[1] // CHUNKS
    width = query_ref.shape[1] // CHUNKS
    low = jnp.zeros((tokens, ROW_BLOCKS * 16), jnp.float32)
    for chunk in range(CHUNKS):
        low += dot_nt(hidden_ref[:, columns(chunk, d)], factor(piece_ref, chunk, at, d))
    low = low.astype(jnp.bfloat16)
    cosines, sines = cos_ref[...], sin_ref[...]
    for chunk in range(CHUNKS):
        up = factor(piece_ref, chunk, at + d, width)
        update = jnp.dot(low, up, preferred_element_type=jnp.float32)
        result = query_ref[:, columns(chunk, width)].astype(jnp.float32) + adapter_scale * update
        for part in range(width // HEAD_SIZE):
            head = chunk * (width // HEAD_SIZE) + part
            turned = turn(result[:, columns(part, HEAD_SIZE)], cosines, sines)
            out_ref[head // GROUP_SPLIT, pl.ds((head % GROUP_SPLIT) * tokens, tokens)] = (
                turned.astype(jnp.bfloat16)
            )


def make_queries(hidden, query, tables, pieces, at):
    tokens = hidden.shape[0]
    return pl.pallas_call(
        functools.partial(query_kernel, at),
        out_shape=jax.ShapeDtypeStruct(
            (KEY_VALUE_HEADS, GROUP_SPLIT * tokens, HEAD_SIZE), jnp.bfloat16
        ),
        in_specs=vmem(5),
        out_specs=vmem()[0],
        compiler_params=PARAMS,
        cost_estimate=pl.CostEstimate(
            flops=100_000_000, bytes_accessed=3 << 20, transcendentals=0
        ),
        name="queries",
    )(hidden, query, *tables, pieces)


REGION = 5


def attend_kernel(steps, plan_ref, queries, *refs):
    blocks, (out_ref, copy_ref, high, acc) = refs[:-4], refs[-4:]
    count = plan_ref[0, COUNT]
    odd = lax.rem(plan_ref[0, OWN_INDEX], 2)
    aside = 2 * odd - 1
    steps = [s if even else s + aside for s, even in steps]
    tokens = out_ref.shape[0]
    rows = GROUP_SPLIT * tokens
    bf16 = jnp.bfloat16
    base2 = 1.4426950408889634 / (HEAD_SIZE**0.5)
    ones = jnp.ones((tokens, HEAD_SIZE), bf16)

    def region(first, number):
        shards = blocks[first : first + number]
        for g in range(KEY_VALUE_HEADS):
            keys = [b[:, columns(g, HEAD_SIZE)] for b in shards]
            values = [
                jnp.concatenate([b[:, columns(KEY_VALUE_HEADS + g, HEAD_SIZE)], ones], axis=1)
                for b in shards
            ]
            score = dot_nt(queries[g], jnp.concatenate(keys, axis=0))
            tiles = [score[:, columns(i, tokens)] for i in range(number)]
            if first == 0:
                row = lax.broadcasted_iota(jnp.int32, (rows, tokens), 0) % tokens
                column = lax.broadcasted_iota(jnp.int32, (rows, tokens), 1)
                tiles = [jnp.where(column <= row, tiles[0], score_masked)]
            else:
                tiles = [
                    jnp.where((step > 0) & (step < count), tile, score_masked)
                    for step, tile in zip(steps[first : first + number], tiles)
                ]
            top = functools.reduce(jnp.maximum, tiles)
            top = jnp.max(top, axis=1, keepdims=True) * base2
            top = jnp.broadcast_to(top, (rows, HEAD_SIZE))
            if first:
                old = high[g]
                top = jnp.maximum(old, top)
            weight = [jnp.exp2(t * base2 - top).astype(bf16) for t in tiles]
            blend = jnp.dot(
                jnp.concatenate(weight, axis=1),
                jnp.concatenate(values, axis=0),
                preferred_element_type=jnp.float32,
            )
            if first:
                shrink = jnp.exp2(old - top)
                blend += acc[g] * jnp.concatenate([shrink, shrink], axis=1)
            high[g] = top
            acc[g] = blend

    region(0, 1)
    for first in range(1, len(blocks), REGION):
        number = min(REGION, len(blocks) - first)
        nearest = functools.reduce(jnp.minimum, steps[first : first + number])
        pl.when(count > nearest)(functools.partial(region, first, number))

    for g in range(KEY_VALUE_HEADS):
        result = (acc[g, :, :HEAD_SIZE] / acc[g, :, HEAD_SIZE:]).astype(bf16)
        for j in range(GROUP_SPLIT):
            for ref in (out_ref, copy_ref):
                ref[:, columns(g * GROUP_SPLIT + j, HEAD_SIZE)] = result[columns(j, tokens)]


def attend(plan, queries, blocks, steps):
    tokens = blocks[0].shape[0]
    rows = GROUP_SPLIT * tokens
    limit = VMEM_LIMIT if len(blocks) < 16 else 2 * VMEM_LIMIT
    return pl.pallas_call(
        functools.partial(attend_kernel, steps),
        out_shape=[jax.ShapeDtypeStruct((tokens, QUERY_HEADS * HEAD_SIZE), jnp.bfloat16)] * 2,
        in_specs=smem() + vmem(1 + len(blocks)),
        out_specs=vmem(2),
        scratch_shapes=[
            pltpu.VMEM((KEY_VALUE_HEADS, rows, HEAD_SIZE), jnp.float32),
            pltpu.VMEM((KEY_VALUE_HEADS, rows, 2 * HEAD_SIZE), jnp.float32),
        ],
        compiler_params=pltpu.CompilerParams(vmem_limit_bytes=limit),
        cost_estimate=pl.CostEstimate(
            flops=12_000_000_000, bytes_accessed=8 << 20, transcendentals=4 << 20
        ),
        name="attend",
    )(plan, queries, *blocks)


def output_kernel(attended_ref, piece_ref, out_ref, down, up, held, in_sem, out_sem):
    q_head, d = down.shape[3], up.shape[3]
    places = down.shape[1]
    halves = down.shape[0]

    def take(copy, at, half, index):
        source = piece_ref.at[half, pl.ds(0, places), :, pl.ds(at, copy.shape[3])]
        return pltpu.make_async_copy(source, copy.at[half], in_sem.at[index, half])

    takes = [take(down, 0, h, 0) for h in range(halves)]
    takes_up = [take(up, q_head, h, 1) for h in range(halves)]
    for copy in takes + takes_up:
        copy.start()
    for copy in takes:
        copy.wait()
    low = jnp.zeros((attended_ref.shape[0], ROW_BLOCKS * 16), jnp.float32)
    for chunk in range(CHUNKS):
        low += dot_nt(attended_ref[:, columns(chunk, q_head)], factor(down, chunk, 0, q_head))
    low = low.astype(jnp.bfloat16)
    for copy in takes_up:
        copy.wait()
    gives = []
    for chunk in range(CHUNKS):
        result = adapter_scale * jnp.dot(
            low, factor(up, chunk, 0, d), preferred_element_type=jnp.float32
        )
        at = pl.ds(chunk * d, d)
        held[:, at] = result.astype(jnp.bfloat16)
        gives.append(
            pltpu.make_async_copy(held.at[:, at], out_ref.at[:, at], out_sem.at[chunk])
        )
        gives[-1].start()
    for copy in gives:
        copy.wait()


def output_adapter(attended, pieces, model_width):
    tokens, query_width = attended.shape
    halves, places = pieces.shape[0], pieces.shape[1]
    any_space = pl.BlockSpec(memory_space=pl.ANY)
    return pl.pallas_call(
        output_kernel,
        out_shape=jax.ShapeDtypeStruct((tokens, model_width), jnp.bfloat16),
        in_specs=vmem() + [any_space],
        out_specs=any_space,
        scratch_shapes=[
            pltpu.VMEM((halves, places, 16, query_width // CHUNKS), jnp.bfloat16),
            pltpu.VMEM((halves, places, 16, model_width // CHUNKS), jnp.bfloat16),
            pltpu.VMEM((tokens, model_width), jnp.bfloat16),
            pltpu.SemaphoreType.DMA((2, halves)),
            pltpu.SemaphoreType.DMA((CHUNKS,)),
        ],
        compiler_params=PARAMS,
        cost_estimate=pl.CostEstimate(
            flops=100_000_000, bytes_accessed=3 << 20, transcendentals=0
        ),
        name="output",
    )(attended, pieces)


def earlier_shards(shards):
    longest = shards // 2 + 1
    low = -(longest // 2)
    runs = (
        [i % shards for i in range(low, low + longest)],
        [i % shards for i in range(low + longest, low + shards)],
    )
    limits = (longest, shards - longest - 1)
    earlier = {}
    for run, limit in zip(runs, limits):
        for i, shard in enumerate(run):
            earlier[shard] = set(run[max(0, i - limit + 1) : i])
    return earlier


def shift_pairs(shards, shift):
    earlier = earlier_shards(shards)
    pairs = [((d - shift) % shards, d) for d in range(shards)]
    return [(s, d) for s, d in pairs if s in earlier[d] or s in earlier[d ^ 1]]


def swap_pairs(shards, shift):
    earlier = earlier_shards(shards)
    return [(d, d ^ 1) for d in range(shards) if (d - shift) % shards in earlier[d ^ 1]]


def exchange(kv, queries, shards, reach):
    shifts = range(0, reach + 1, 2)
    got = [kv] + [lax.ppermute(kv, "ctx", shift_pairs(shards, s)) for s in shifts[1:]]
    got[1:], queries = lax.optimization_barrier((got[1:], queries))
    swapped = [lax.ppermute(b, "ctx", swap_pairs(shards, s)) for s, b in zip(shifts, got)]
    blocks, steps = [kv], [(0, True)]
    for s, even, odd in zip(shifts, got, swapped):
        if s:
            blocks.append(even)
            steps.append((s, True))
        blocks.append(odd)
        steps.append((s, False))
    return blocks, steps, queries


def body(
    hidden,
    frozen_query,
    frozen_key,
    frozen_value,
    adapter_bank,
    request_shards,
    request_adapter,
    adapter_owner,
):
    shards = lax.axis_size("ctx")
    groups = lax.axis_size("groups")
    tokens, model_width = hidden.shape
    halves = 2 if groups == 2 and 2 * shards == ROW_BLOCKS * CHUNKS else 1
    own_half = lax.axis_index("groups") if halves == 2 else 0
    me = jnp.stack([lax.axis_index("ctx"), own_half]).astype(jnp.int32)
    parts = Parts(model_width, frozen_query.shape[1], frozen_key.shape[1])
    reach = shards // 2

    packed = pack(parts, halves, shards, adapter_bank)
    spread = lax.all_to_all(packed, "ctx", split_axis=0, concat_axis=0, tiled=True)

    requests = jnp.stack([request_shards, request_adapter])[:, None]
    if halves == 2:
        theirs = lax.ppermute(requests, "groups", [(0, 1), (1, 0)])
        requests = jnp.concatenate([requests, theirs], axis=1)
    plan = make_plan(shards, reach, me, requests[0], requests[1], adapter_owner)
    plan = jnp.maximum(plan, 0)
    positions = (plan[0, COUNT] - 1) * tokens + jnp.arange(tokens, dtype=jnp.int32)
    tables = rope_tables(positions)
    spread, tables, plan = lax.optimization_barrier((spread, tables, plan))

    def collect(pieces):
        axes = ("groups", "ctx") if halves == 2 else "ctx"
        pieces = lax.all_to_all(pieces, axes, split_axis=0, concat_axis=0, tiled=True)
        return pieces.reshape((halves, shards) + pieces.shape[1:])[:, : ROW_BLOCKS * CHUNKS]

    kv_width, q_width, o_width = parts.widths
    dests = shards * halves
    pieces = collect(route(plan, spread, dests, 0, kv_width + q_width))
    kv = make_keys_values(hidden, frozen_key, frozen_value, tables, pieces)
    queries = make_queries(hidden, frozen_query, tables, pieces, kv_width)
    blocks, steps, queries = exchange(kv, queries, shards, reach)
    later = route(plan, spread, dests, kv_width + q_width, o_width)
    kv, later = lax.optimization_barrier((kv, later))
    later = collect(later)
    attended, copy = attend(plan, queries, blocks, steps)
    return attended, output_adapter(copy, later, model_width)


def solution(mesh):
    return jax.shard_map(
        body,
        mesh=mesh,
        in_specs=(
            P(("groups", "ctx"), None),
            P(("groups", "ctx"), None),
            P(("groups", "ctx"), None),
            P(("groups", "ctx"), None),
            P("ctx", None, None),
            P("groups"),
            P("groups"),
            P(),
        ),
        out_specs=(P(("groups", "ctx"), None), P(("groups", "ctx"), None)),
        check_vma=False,
    )
```

```python
import functools

import jax
import jax.numpy as jnp
from jax import lax
from jax.experimental import pallas as pl
from jax.experimental.pallas import tpu as pltpu
from jax.sharding import PartitionSpec as P

HEAD_SIZE = 128
QUERY_HEADS = 16
KEY_VALUE_HEADS = 4
GROUP_SPLIT = QUERY_HEADS // KEY_VALUE_HEADS

adapter_scale = 0.5
rope_theta = 500000.0
score_masked = -1e30

VMEM_LIMIT = 24 * 1024 * 1024

ROW_BLOCKS = 4
CHUNKS = 8


def rope_tables(positions):
    half_dim = HEAD_SIZE // 2
    frequency = rope_theta ** (-(jnp.arange(half_dim, dtype=jnp.float32) * 2.0) / HEAD_SIZE)
    angles = positions.astype(jnp.float32)[..., None] * frequency
    cosines = jnp.cos(angles)
    sines = jnp.sin(angles)
    return (jnp.concatenate([cosines, cosines], -1), jnp.concatenate([-sines, sines], -1))


class Parts:
    def __init__(self, model_width, query_width, key_width):
        d, q, k = model_width, query_width, key_width
        up = 3 * d
        self.kv = ((d, d // CHUNKS), (2 * d, d // CHUNKS), (up + q, 2 * k // CHUNKS))
        self.q = ((0, d // CHUNKS), (up, q // CHUNKS))
        self.o = ((up + q + 2 * k, q // CHUNKS), (up + 2 * q + 2 * k, d // CHUNKS))
        self.all = self.kv + self.q + self.o
        self.widths = tuple(sum(w for _, w in part) for part in (self.kv, self.q, self.o))


def vmem(count=1):
    return [pl.BlockSpec(memory_space=pltpu.VMEM)] * count


def smem(count=1):
    return [pl.BlockSpec(memory_space=pltpu.SMEM)] * count


PARAMS = pltpu.CompilerParams(vmem_limit_bytes=VMEM_LIMIT)


OWN_INDEX, COUNT, ENTRY = 0, 1, 8


def layout(lengths_ref, which, shards):
    starts, start, length = [jnp.int32(0)], jnp.int32(0), lengths_ref[which, 0]
    for r in range(1, lengths_ref.shape[1]):
        starts.append(starts[-1] + lengths_ref[which, r - 1])
        longer = lengths_ref[which, r] > length
        start = jnp.where(longer, starts[-1], start)
        length = jnp.where(longer, lengths_ref[which, r], length)
    return starts, start + lax.div(length, 2)


def plan_kernel(shards, reach, me_ref, lengths_ref, adapters_ref, owner_ref, out_ref):
    own_index, own_half = me_ref[0], me_ref[1]
    starts, offset = layout(lengths_ref, 0, shards)
    own_packed = lax.rem(own_index + offset, shards)
    first = jnp.int32(0)
    for start in starts[1:]:
        first = jnp.where(start <= own_packed, start, first)
    lanes = lax.broadcasted_iota(jnp.int32, out_ref.shape, 1)
    plan = jnp.where(lanes == COUNT, jnp.minimum(own_packed - first, reach) + 1, own_index)
    for which in range(lengths_ref.shape[0]):
        starts, offset = layout(lengths_ref, which, shards)
        entries = [owner_ref[adapters_ref[which, r]] for r in range(len(starts))]
        halves = lengths_ref.shape[0]
        half = own_half if which == 0 else 1 - own_half
        for shard in range(shards):
            packed = lax.rem(shard + offset, shards)
            entry = entries[0]
            for start, later in zip(starts[1:], entries[1:]):
                entry = jnp.where(start <= packed, later, entry)
            plan = jnp.where(lanes == ENTRY + shard * halves + half, entry, plan)
    out_ref[...] = plan


def make_plan(shards, reach, me, lengths, adapters, owner):
    return pl.pallas_call(
        functools.partial(plan_kernel, shards, reach),
        out_shape=jax.ShapeDtypeStruct((1, 128), jnp.int32),
        in_specs=smem(4),
        out_specs=vmem()[0],
        name="plan",
    )(me, lengths, adapters, owner)


def pack_kernel(parts, halves, bank_ref, out_ref, held, in_sem, out_sem):
    own_half = lax.axis_index("groups") if halves == 2 else 0
    takes, gives = [], []
    for place in range(held.shape[0]):
        at = 0
        for index, (first, width) in enumerate(parts.all):
            start = pl.multiple_of(first + (place * halves + own_half) * width, 128)
            takes.append(
                pltpu.make_async_copy(
                    bank_ref.at[:, :, pl.ds(start, width)],
                    held.at[place, :, :, pl.ds(at, width)],
                    in_sem.at[place, index],
                )
            )
            at += width
        gives += [
            pltpu.make_async_copy(
                held.at[place], out_ref.at[again, place], out_sem.at[again, place]
            )
            for again in range(out_ref.shape[0])
        ]
    for copy in takes:
        copy.start()
    each, again = len(parts.all), out_ref.shape[0]
    for place in range(held.shape[0]):
        for copy in takes[place * each : (place + 1) * each]:
            copy.wait()
        for copy in gives[place * again : (place + 1) * again]:
            copy.start()
    for copy in gives:
        copy.wait()


def pack(parts, halves, shards, bank):
    width, places = sum(parts.widths), CHUNKS // halves
    again = shards // (places * ROW_BLOCKS)
    packed = pl.pallas_call(
        functools.partial(pack_kernel, parts, halves),
        out_shape=jax.ShapeDtypeStruct((again, places, ROW_BLOCKS, 16, width), bank.dtype),
        in_specs=[pl.BlockSpec(memory_space=pl.ANY)],
        out_specs=pl.BlockSpec(memory_space=pl.ANY),
        scratch_shapes=[
            pltpu.VMEM((places, ROW_BLOCKS, 16, width), bank.dtype),
            pltpu.SemaphoreType.DMA((places, len(parts.all))),
            pltpu.SemaphoreType.DMA((again, places)),
        ],
        compiler_params=pltpu.CompilerParams(vmem_limit_bytes=62 * 1024 * 1024),
        name="pack",
    )(bank.reshape(ROW_BLOCKS, 16, bank.shape[2]))
    return packed.reshape(shards, 16, width)


ROUTE_STEPS = 4


def route_kernel(at, plan_ref, spread_ref, out_ref):
    number = out_ref.shape[0]
    for i in range(number):
        entry = plan_ref[0, ENTRY + pl.program_id(0) * number + i]
        out_ref[i] = spread_ref[entry, :, at : at + out_ref.shape[2]]


def route(plan, spread, dests, at, width):
    return pl.pallas_call(
        functools.partial(route_kernel, at),
        out_shape=jax.ShapeDtypeStruct((dests, 16, width), spread.dtype),
        grid=(ROUTE_STEPS,),
        in_specs=smem() + vmem(),
        out_specs=pl.BlockSpec((dests // ROUTE_STEPS, 16, width), lambda i: (i, 0, 0)),
        compiler_params=PARAMS,
        name="route",
    )(plan, spread)


def factor(piece_ref, chunk, at, width):
    halves = piece_ref.shape[1]
    place = chunk // halves * ROW_BLOCKS
    rows = piece_ref[place : place + ROW_BLOCKS, chunk % halves, :, at : at + width]
    return rows.reshape(ROW_BLOCKS * 16, width)


def columns(chunk, width):
    return slice(chunk * width, (chunk + 1) * width)


def dot_nt(a, b):
    return lax.dot_general(a, b, (((1,), (1,)), ((), ())), preferred_element_type=jnp.float32)


def turn(x, cosines, sines):
    return x * cosines + pltpu.roll(x, HEAD_SIZE // 2, 1) * sines


def kv_kernel(hidden_ref, key_ref, value_ref, cos_ref, sin_ref, piece_ref, out_ref):
    d = hidden_ref.shape[1] // CHUNKS
    rank = ROW_BLOCKS * 16
    low = jnp.zeros((hidden_ref.shape[0], 2 * rank), jnp.float32)
    for chunk in range(CHUNKS):
        down = jnp.concatenate(
            [factor(piece_ref, chunk, 0, d), factor(piece_ref, chunk, d, d)], axis=0
        )
        low += dot_nt(hidden_ref[:, columns(chunk, d)], down)
    low = low.astype(jnp.bfloat16)
    width = 2 * key_ref.shape[1] // CHUNKS
    cosines, sines = cos_ref[...], sin_ref[...]
    for chunk in range(CHUNKS):
        is_key = chunk < CHUNKS // 2
        up = factor(piece_ref, chunk, 2 * d, width)
        part = low[:, :rank] if is_key else low[:, rank:]
        update = jnp.dot(part, up, preferred_element_type=jnp.float32)
        frozen = (key_ref if is_key else value_ref)[:, columns(chunk % (CHUNKS // 2), width)]
        result = frozen.astype(jnp.float32) + adapter_scale * update
        if is_key:
            result = turn(result, cosines, sines)
        out_ref[:, columns(chunk, width)] = result.astype(jnp.bfloat16)


def make_keys_values(hidden, key, value, tables, pieces):
    return pl.pallas_call(
        kv_kernel,
        out_shape=jax.ShapeDtypeStruct((key.shape[0], 2 * key.shape[1]), jnp.bfloat16),
        in_specs=vmem(6),
        out_specs=vmem()[0],
        compiler_params=PARAMS,
        cost_estimate=pl.CostEstimate(
            flops=150_000_000, bytes_accessed=3 << 20, transcendentals=0
        ),
        name="keys_values",
    )(hidden, key, value, *tables, pieces)


def query_kernel(at, hidden_ref, query_ref, cos_ref, sin_ref, piece_ref, out_ref):
    tokens = query_ref.shape[0]
    d = hidden_ref.shape[1] // CHUNKS
    width = query_ref.shape[1] // CHUNKS
    low = jnp.zeros((tokens, ROW_BLOCKS * 16), jnp.float32)
    for chunk in range(CHUNKS):
        low += dot_nt(hidden_ref[:, columns(chunk, d)], factor(piece_ref, chunk, at, d))
    low = low.astype(jnp.bfloat16)
    cosines, sines = cos_ref[...], sin_ref[...]
    for chunk in range(CHUNKS):
        up = factor(piece_ref, chunk, at + d, width)
        update = jnp.dot(low, up, preferred_element_type=jnp.float32)
        result = query_ref[:, columns(chunk, width)].astype(jnp.float32) + adapter_scale * update
        for part in range(width // HEAD_SIZE):
            head = chunk * (width // HEAD_SIZE) + part
            turned = turn(result[:, columns(part, HEAD_SIZE)], cosines, sines)
            out_ref[head // GROUP_SPLIT, pl.ds((head % GROUP_SPLIT) * tokens, tokens)] = (
                turned.astype(jnp.bfloat16)
            )


def make_queries(hidden, query, tables, pieces, at):
    tokens = hidden.shape[0]
    return pl.pallas_call(
        functools.partial(query_kernel, at),
        out_shape=jax.ShapeDtypeStruct(
            (KEY_VALUE_HEADS, GROUP_SPLIT * tokens, HEAD_SIZE), jnp.bfloat16
        ),
        in_specs=vmem(5),
        out_specs=vmem()[0],
        compiler_params=PARAMS,
        cost_estimate=pl.CostEstimate(
            flops=100_000_000, bytes_accessed=3 << 20, transcendentals=0
        ),
        name="queries",
    )(hidden, query, *tables, pieces)


REGION = 5


def attend_kernel(steps, plan_ref, queries, *refs):
    blocks, (out_ref, copy_ref, high, acc) = refs[:-4], refs[-4:]
    count = plan_ref[0, COUNT]
    odd = lax.rem(plan_ref[0, OWN_INDEX], 2)
    aside = 2 * odd - 1
    steps = [s if even else s + aside for s, even in steps]
    tokens = out_ref.shape[0]
    rows = GROUP_SPLIT * tokens
    bf16 = jnp.bfloat16
    base2 = 1.4426950408889634 / (HEAD_SIZE**0.5)
    ones = jnp.ones((tokens, HEAD_SIZE), bf16)

    def region(first, number):
        shards = blocks[first : first + number]
        for g in range(KEY_VALUE_HEADS):
            keys = [b[:, columns(g, HEAD_SIZE)] for b in shards]
            values = [
                jnp.concatenate([b[:, columns(KEY_VALUE_HEADS + g, HEAD_SIZE)], ones], axis=1)
                for b in shards
            ]
            score = dot_nt(queries[g], jnp.concatenate(keys, axis=0))
            tiles = [score[:, columns(i, tokens)] for i in range(number)]
            if first == 0:
                row = lax.broadcasted_iota(jnp.int32, (rows, tokens), 0) % tokens
                column = lax.broadcasted_iota(jnp.int32, (rows, tokens), 1)
                tiles = [jnp.where(column <= row, tiles[0], score_masked)]
            else:
                tiles = [
                    jnp.where((step > 0) & (step < count), tile, score_masked)
                    for step, tile in zip(steps[first : first + number], tiles)
                ]
            top = functools.reduce(jnp.maximum, tiles)
            top = jnp.max(top, axis=1, keepdims=True) * base2
            top = jnp.broadcast_to(top, (rows, HEAD_SIZE))
            if first:
                old = high[g]
                top = jnp.maximum(old, top)
            weight = [jnp.exp2(t * base2 - top).astype(bf16) for t in tiles]
            blend = jnp.dot(
                jnp.concatenate(weight, axis=1),
                jnp.concatenate(values, axis=0),
                preferred_element_type=jnp.float32,
            )
            if first:
                shrink = jnp.exp2(old - top)
                blend += acc[g] * jnp.concatenate([shrink, shrink], axis=1)
            high[g] = top
            acc[g] = blend

    region(0, 1)
    for first in range(1, len(blocks), REGION):
        number = min(REGION, len(blocks) - first)
        nearest = functools.reduce(jnp.minimum, steps[first : first + number])
        pl.when(count > nearest)(functools.partial(region, first, number))

    for g in range(KEY_VALUE_HEADS):
        result = (acc[g, :, :HEAD_SIZE] / acc[g, :, HEAD_SIZE:]).astype(bf16)
        for j in range(GROUP_SPLIT):
            for ref in (out_ref, copy_ref):
                ref[:, columns(g * GROUP_SPLIT + j, HEAD_SIZE)] = result[columns(j, tokens)]


def attend(plan, queries, blocks, steps):
    tokens = blocks[0].shape[0]
    rows = GROUP_SPLIT * tokens
    limit = VMEM_LIMIT if len(blocks) < 16 else 2 * VMEM_LIMIT
    return pl.pallas_call(
        functools.partial(attend_kernel, steps),
        out_shape=[jax.ShapeDtypeStruct((tokens, QUERY_HEADS * HEAD_SIZE), jnp.bfloat16)] * 2,
        in_specs=smem() + vmem(1 + len(blocks)),
        out_specs=vmem(2),
        scratch_shapes=[
            pltpu.VMEM((KEY_VALUE_HEADS, rows, HEAD_SIZE), jnp.float32),
            pltpu.VMEM((KEY_VALUE_HEADS, rows, 2 * HEAD_SIZE), jnp.float32),
        ],
        compiler_params=pltpu.CompilerParams(vmem_limit_bytes=limit),
        cost_estimate=pl.CostEstimate(
            flops=12_000_000_000, bytes_accessed=8 << 20, transcendentals=4 << 20
        ),
        name="attend",
    )(plan, queries, *blocks)


def output_kernel(attended_ref, piece_ref, out_ref, down, up, held, in_sem, out_sem):
    q_head, d = down.shape[3], up.shape[3]
    halves = down.shape[1]

    def take(copy, at, half, index):
        source = piece_ref.at[pl.ds(0, copy.shape[0]), half, :, pl.ds(at, copy.shape[3])]
        return pltpu.make_async_copy(source, copy.at[:, half], in_sem.at[index, half])

    takes = [take(down, 0, h, 0) for h in range(halves)]
    takes_up = [take(up, q_head, h, 1) for h in range(halves)]
    for copy in takes + takes_up:
        copy.start()
    for copy in takes:
        copy.wait()
    low = jnp.zeros((attended_ref.shape[0], ROW_BLOCKS * 16), jnp.float32)
    for chunk in range(CHUNKS):
        low += dot_nt(attended_ref[:, columns(chunk, q_head)], factor(down, chunk, 0, q_head))
    low = low.astype(jnp.bfloat16)
    for copy in takes_up:
        copy.wait()
    gives = []
    for chunk in range(CHUNKS):
        result = adapter_scale * jnp.dot(
            low, factor(up, chunk, 0, d), preferred_element_type=jnp.float32
        )
        at = pl.ds(chunk * d, d)
        held[:, at] = result.astype(jnp.bfloat16)
        gives.append(
            pltpu.make_async_copy(held.at[:, at], out_ref.at[:, at], out_sem.at[chunk])
        )
        gives[-1].start()
    for copy in gives:
        copy.wait()


def output_adapter(attended, pieces, model_width):
    tokens, query_width = attended.shape
    places, halves = pieces.shape[0], pieces.shape[1]
    any_space = pl.BlockSpec(memory_space=pl.ANY)
    return pl.pallas_call(
        output_kernel,
        out_shape=jax.ShapeDtypeStruct((tokens, model_width), jnp.bfloat16),
        in_specs=vmem() + [any_space],
        out_specs=any_space,
        scratch_shapes=[
            pltpu.VMEM((places, halves, 16, query_width // CHUNKS), jnp.bfloat16),
            pltpu.VMEM((places, halves, 16, model_width // CHUNKS), jnp.bfloat16),
            pltpu.VMEM((tokens, model_width), jnp.bfloat16),
            pltpu.SemaphoreType.DMA((2, halves)),
            pltpu.SemaphoreType.DMA((CHUNKS,)),
        ],
        compiler_params=PARAMS,
        cost_estimate=pl.CostEstimate(
            flops=100_000_000, bytes_accessed=3 << 20, transcendentals=0
        ),
        name="output",
    )(attended, pieces)


def earlier_shards(shards):
    longest = shards // 2 + 1
    low = -(longest // 2)
    runs = (
        [i % shards for i in range(low, low + longest)],
        [i % shards for i in range(low + longest, low + shards)],
    )
    limits = (longest, shards - longest - 1)
    earlier = {}
    for run, limit in zip(runs, limits):
        for i, shard in enumerate(run):
            earlier[shard] = set(run[max(0, i - limit + 1) : i])
    return earlier


def shift_pairs(shards, shift):
    earlier = earlier_shards(shards)
    pairs = [((d - shift) % shards, d) for d in range(shards)]
    return [(s, d) for s, d in pairs if s in earlier[d] or s in earlier[d ^ 1]]


def swap_pairs(shards, shift):
    earlier = earlier_shards(shards)
    return [(d, d ^ 1) for d in range(shards) if (d - shift) % shards in earlier[d ^ 1]]


def exchange(kv, queries, shards, reach):
    shifts = range(0, reach + 1, 2)
    got = [kv] + [lax.ppermute(kv, "ctx", shift_pairs(shards, s)) for s in shifts[1:]]
    got[1:], queries = lax.optimization_barrier((got[1:], queries))
    swapped = [lax.ppermute(b, "ctx", swap_pairs(shards, s)) for s, b in zip(shifts, got)]
    blocks, steps = [kv], [(0, True)]
    for s, even, odd in zip(shifts, got, swapped):
        if s:
            blocks.append(even)
            steps.append((s, True))
        blocks.append(odd)
        steps.append((s, False))
    return blocks, steps, queries


def body(
    hidden,
    frozen_query,
    frozen_key,
    frozen_value,
    adapter_bank,
    request_shards,
    request_adapter,
    adapter_owner,
):
    shards = lax.axis_size("ctx")
    groups = lax.axis_size("groups")
    tokens, model_width = hidden.shape
    halves = 2 if groups == 2 and 2 * shards == ROW_BLOCKS * CHUNKS else 1
    own_half = lax.axis_index("groups") if halves == 2 else 0
    me = jnp.stack([lax.axis_index("ctx"), own_half]).astype(jnp.int32)
    parts = Parts(model_width, frozen_query.shape[1], frozen_key.shape[1])
    reach = shards // 2

    packed = pack(parts, halves, shards, adapter_bank)
    spread = lax.all_to_all(packed, "ctx", split_axis=0, concat_axis=0, tiled=True)

    requests = jnp.stack([request_shards, request_adapter])[:, None]
    if halves == 2:
        theirs = lax.ppermute(requests, "groups", [(0, 1), (1, 0)])
        requests = jnp.concatenate([requests, theirs], axis=1)
    plan = make_plan(shards, reach, me, requests[0], requests[1], adapter_owner)
    plan = jnp.maximum(plan, 0)
    positions = (plan[0, COUNT] - 1) * tokens + jnp.arange(tokens, dtype=jnp.int32)
    tables = rope_tables(positions)
    spread, tables, plan = lax.optimization_barrier((spread, tables, plan))

    def collect(pieces):
        axes = ("ctx", "groups") if halves == 2 else "ctx"
        pieces = lax.all_to_all(pieces, axes, split_axis=0, concat_axis=0, tiled=True)
        pieces = pieces.reshape((shards, halves) + pieces.shape[1:])
        return pieces[: ROW_BLOCKS * CHUNKS // halves]

    kv_width, q_width, o_width = parts.widths
    dests = shards * halves
    pieces = collect(route(plan, spread, dests, 0, kv_width + q_width))
    kv = make_keys_values(hidden, frozen_key, frozen_value, tables, pieces)
    queries = make_queries(hidden, frozen_query, tables, pieces, kv_width)
    blocks, steps, queries = exchange(kv, queries, shards, reach)
    later = route(plan, spread, dests, kv_width + q_width, o_width)
    kv, later = lax.optimization_barrier((kv, later))
    later = collect(later)
    attended, copy = attend(plan, queries, blocks, steps)
    return attended, output_adapter(copy, later, model_width)


def solution(mesh):
    return jax.shard_map(
        body,
        mesh=mesh,
        in_specs=(
            P(("groups", "ctx"), None),
            P(("groups", "ctx"), None),
            P(("groups", "ctx"), None),
            P(("groups", "ctx"), None),
            P("ctx", None, None),
            P("groups"),
            P("groups"),
            P(),
        ),
        out_specs=(P(("groups", "ctx"), None), P(("groups", "ctx"), None)),
        check_vma=False,
    )
```

```python
import functools

import jax
import jax.numpy as jnp
from jax import lax
from jax.experimental import pallas as pl
from jax.experimental.pallas import tpu as pltpu
from jax.sharding import PartitionSpec as P

HEAD_SIZE = 128
QUERY_HEADS = 16
KEY_VALUE_HEADS = 4
GROUP_SPLIT = QUERY_HEADS // KEY_VALUE_HEADS

adapter_scale = 0.5
rope_theta = 500000.0
score_masked = -1e30

VMEM_LIMIT = 24 * 1024 * 1024

ROW_BLOCKS = 4
CHUNKS = 8


def rope_tables(positions):
    half_dim = HEAD_SIZE // 2
    frequency = rope_theta ** (-(jnp.arange(half_dim, dtype=jnp.float32) * 2.0) / HEAD_SIZE)
    angles = positions.astype(jnp.float32)[..., None] * frequency
    cosines = jnp.cos(angles)
    sines = jnp.sin(angles)
    return (jnp.concatenate([cosines, cosines], -1), jnp.concatenate([-sines, sines], -1))


class Parts:
    def __init__(self, model_width, query_width, key_width):
        d, q, k = model_width, query_width, key_width
        up = 3 * d
        self.kv = ((d, d // CHUNKS), (2 * d, d // CHUNKS), (up + q, 2 * k // CHUNKS))
        self.q = ((0, d // CHUNKS), (up, q // CHUNKS))
        self.o = ((up + q + 2 * k, q // CHUNKS), (up + 2 * q + 2 * k, d // CHUNKS))
        self.all = self.kv + self.q + self.o
        self.widths = tuple(sum(w for _, w in part) for part in (self.kv, self.q, self.o))


def vmem(count=1):
    return [pl.BlockSpec(memory_space=pltpu.VMEM)] * count


def smem(count=1):
    return [pl.BlockSpec(memory_space=pltpu.SMEM)] * count


PARAMS = pltpu.CompilerParams(vmem_limit_bytes=VMEM_LIMIT)


OWN_INDEX, COUNT, ENTRY = 0, 1, 8


def layout(lengths_ref, which, shards):
    starts, start, length = [jnp.int32(0)], jnp.int32(0), lengths_ref[which, 0]
    for r in range(1, lengths_ref.shape[1]):
        starts.append(starts[-1] + lengths_ref[which, r - 1])
        longer = lengths_ref[which, r] > length
        start = jnp.where(longer, starts[-1], start)
        length = jnp.where(longer, lengths_ref[which, r], length)
    return starts, start + lax.div(length, 2)


def plan_kernel(shards, reach, me_ref, lengths_ref, adapters_ref, owner_ref, out_ref):
    own_index, own_half = me_ref[0], me_ref[1]
    starts, offset = layout(lengths_ref, 0, shards)
    own_packed = lax.rem(own_index + offset, shards)
    first = jnp.int32(0)
    for start in starts[1:]:
        first = jnp.where(start <= own_packed, start, first)
    lanes = lax.broadcasted_iota(jnp.int32, out_ref.shape, 1)
    plan = jnp.where(lanes == COUNT, jnp.minimum(own_packed - first, reach) + 1, own_index)
    for which in range(lengths_ref.shape[0]):
        starts, offset = layout(lengths_ref, which, shards)
        entries = [owner_ref[adapters_ref[which, r]] for r in range(len(starts))]
        halves = lengths_ref.shape[0]
        half = own_half if which == 0 else 1 - own_half
        for shard in range(shards):
            packed = lax.rem(shard + offset, shards)
            entry = entries[0]
            for start, later in zip(starts[1:], entries[1:]):
                entry = jnp.where(start <= packed, later, entry)
            plan = jnp.where(lanes == ENTRY + shard * halves + half, entry, plan)
    out_ref[...] = plan


def make_plan(shards, reach, me, lengths, adapters, owner):
    return pl.pallas_call(
        functools.partial(plan_kernel, shards, reach),
        out_shape=jax.ShapeDtypeStruct((1, 128), jnp.int32),
        in_specs=smem(4),
        out_specs=vmem()[0],
        name="plan",
    )(me, lengths, adapters, owner)


def pack_kernel(parts, halves, bank_ref, out_ref, held, in_sem, out_sem):
    own_half = lax.axis_index("groups") if halves == 2 else 0
    takes, gives = [], []
    for place in range(held.shape[0]):
        at = 0
        for index, (first, width) in enumerate(parts.all):
            start = pl.multiple_of(first + (place * halves + own_half) * width, 128)
            takes.append(
                pltpu.make_async_copy(
                    bank_ref.at[:, :, pl.ds(start, width)],
                    held.at[place, :, :, pl.ds(at, width)],
                    in_sem.at[place, index],
                )
            )
            at += width
        gives += [
            pltpu.make_async_copy(
                held.at[place], out_ref.at[again, place], out_sem.at[again, place]
            )
            for again in range(out_ref.shape[0])
        ]
    for copy in takes:
        copy.start()
    each, again = len(parts.all), out_ref.shape[0]
    for place in range(held.shape[0]):
        for copy in takes[place * each : (place + 1) * each]:
            copy.wait()
        for copy in gives[place * again : (place + 1) * again]:
            copy.start()
    for copy in gives:
        copy.wait()


def pack(parts, halves, shards, bank):
    width, places = sum(parts.widths), CHUNKS // halves
    again = shards // (places * ROW_BLOCKS)
    packed = pl.pallas_call(
        functools.partial(pack_kernel, parts, halves),
        out_shape=jax.ShapeDtypeStruct((again, places, ROW_BLOCKS, 16, width), bank.dtype),
        in_specs=[pl.BlockSpec(memory_space=pl.ANY)],
        out_specs=pl.BlockSpec(memory_space=pl.ANY),
        scratch_shapes=[
            pltpu.VMEM((places, ROW_BLOCKS, 16, width), bank.dtype),
            pltpu.SemaphoreType.DMA((places, len(parts.all))),
            pltpu.SemaphoreType.DMA((again, places)),
        ],
        compiler_params=pltpu.CompilerParams(vmem_limit_bytes=62 * 1024 * 1024),
        name="pack",
    )(bank.reshape(ROW_BLOCKS, 16, bank.shape[2]))
    return packed.reshape(shards, 16, width)


ROUTE_STEPS = 4


def route_kernel(at, halves, plan_ref, spread_ref, out_ref):
    number = out_ref.shape[0]
    for i in range(number):
        dest = pl.program_id(0) * number + i
        if halves > 1:
            shards = number * ROUTE_STEPS // halves
            dest = lax.rem(dest, shards) * halves + lax.div(dest, shards)
        entry = plan_ref[0, ENTRY + dest]
        out_ref[i] = spread_ref[entry, :, at : at + out_ref.shape[2]]


def route(plan, spread, dests, at, width, halves=1):
    return pl.pallas_call(
        functools.partial(route_kernel, at, halves),
        out_shape=jax.ShapeDtypeStruct((dests, 16, width), spread.dtype),
        grid=(ROUTE_STEPS,),
        in_specs=smem() + vmem(),
        out_specs=pl.BlockSpec((dests // ROUTE_STEPS, 16, width), lambda i: (i, 0, 0)),
        compiler_params=PARAMS,
        name="route",
    )(plan, spread)


def factor(piece_ref, chunk, at, width):
    halves = piece_ref.shape[1]
    place = chunk // halves * ROW_BLOCKS
    rows = piece_ref[place : place + ROW_BLOCKS, chunk % halves, :, at : at + width]
    return rows.reshape(ROW_BLOCKS * 16, width)


def columns(chunk, width):
    return slice(chunk * width, (chunk + 1) * width)


def dot_nt(a, b):
    return lax.dot_general(a, b, (((1,), (1,)), ((), ())), preferred_element_type=jnp.float32)


def turn(x, cosines, sines):
    return x * cosines + pltpu.roll(x, HEAD_SIZE // 2, 1) * sines


def kv_kernel(hidden_ref, key_ref, value_ref, cos_ref, sin_ref, piece_ref, out_ref):
    d = hidden_ref.shape[1] // CHUNKS
    rank = ROW_BLOCKS * 16
    low = jnp.zeros((hidden_ref.shape[0], 2 * rank), jnp.float32)
    for chunk in range(CHUNKS):
        down = jnp.concatenate(
            [factor(piece_ref, chunk, 0, d), factor(piece_ref, chunk, d, d)], axis=0
        )
        low += dot_nt(hidden_ref[:, columns(chunk, d)], down)
    low = low.astype(jnp.bfloat16)
    width = 2 * key_ref.shape[1] // CHUNKS
    cosines, sines = cos_ref[...], sin_ref[...]
    for chunk in range(CHUNKS):
        is_key = chunk < CHUNKS // 2
        up = factor(piece_ref, chunk, 2 * d, width)
        part = low[:, :rank] if is_key else low[:, rank:]
        update = jnp.dot(part, up, preferred_element_type=jnp.float32)
        frozen = (key_ref if is_key else value_ref)[:, columns(chunk % (CHUNKS // 2), width)]
        result = frozen.astype(jnp.float32) + adapter_scale * update
        if is_key:
            result = turn(result, cosines, sines)
        out_ref[:, columns(chunk, width)] = result.astype(jnp.bfloat16)


def make_keys_values(hidden, key, value, tables, pieces):
    return pl.pallas_call(
        kv_kernel,
        out_shape=jax.ShapeDtypeStruct((key.shape[0], 2 * key.shape[1]), jnp.bfloat16),
        in_specs=vmem(6),
        out_specs=vmem()[0],
        compiler_params=PARAMS,
        cost_estimate=pl.CostEstimate(
            flops=150_000_000, bytes_accessed=3 << 20, transcendentals=0
        ),
        name="keys_values",
    )(hidden, key, value, *tables, pieces)


def query_kernel(at, hidden_ref, query_ref, cos_ref, sin_ref, piece_ref, out_ref):
    tokens = query_ref.shape[0]
    d = hidden_ref.shape[1] // CHUNKS
    width = query_ref.shape[1] // CHUNKS
    low = jnp.zeros((tokens, ROW_BLOCKS * 16), jnp.float32)
    for chunk in range(CHUNKS):
        low += dot_nt(hidden_ref[:, columns(chunk, d)], factor(piece_ref, chunk, at, d))
    low = low.astype(jnp.bfloat16)
    cosines, sines = cos_ref[...], sin_ref[...]
    for chunk in range(CHUNKS):
        up = factor(piece_ref, chunk, at + d, width)
        update = jnp.dot(low, up, preferred_element_type=jnp.float32)
        result = query_ref[:, columns(chunk, width)].astype(jnp.float32) + adapter_scale * update
        for part in range(width // HEAD_SIZE):
            head = chunk * (width // HEAD_SIZE) + part
            turned = turn(result[:, columns(part, HEAD_SIZE)], cosines, sines)
            out_ref[head // GROUP_SPLIT, pl.ds((head % GROUP_SPLIT) * tokens, tokens)] = (
                turned.astype(jnp.bfloat16)
            )


def make_queries(hidden, query, tables, pieces, at):
    tokens = hidden.shape[0]
    return pl.pallas_call(
        functools.partial(query_kernel, at),
        out_shape=jax.ShapeDtypeStruct(
            (KEY_VALUE_HEADS, GROUP_SPLIT * tokens, HEAD_SIZE), jnp.bfloat16
        ),
        in_specs=vmem(5),
        out_specs=vmem()[0],
        compiler_params=PARAMS,
        cost_estimate=pl.CostEstimate(
            flops=100_000_000, bytes_accessed=3 << 20, transcendentals=0
        ),
        name="queries",
    )(hidden, query, *tables, pieces)


REGION = 5


def attend_kernel(steps, plan_ref, queries, *refs):
    blocks, (out_ref, copy_ref, high, acc) = refs[:-4], refs[-4:]
    count = plan_ref[0, COUNT]
    odd = lax.rem(plan_ref[0, OWN_INDEX], 2)
    aside = 2 * odd - 1
    steps = [s if even else s + aside for s, even in steps]
    tokens = out_ref.shape[0]
    rows = GROUP_SPLIT * tokens
    bf16 = jnp.bfloat16
    base2 = 1.4426950408889634 / (HEAD_SIZE**0.5)
    ones = jnp.ones((tokens, HEAD_SIZE), bf16)

    def region(first, number):
        shards = blocks[first : first + number]
        for g in range(KEY_VALUE_HEADS):
            keys = [b[:, columns(g, HEAD_SIZE)] for b in shards]
            values = [
                jnp.concatenate([b[:, columns(KEY_VALUE_HEADS + g, HEAD_SIZE)], ones], axis=1)
                for b in shards
            ]
            score = dot_nt(queries[g], jnp.concatenate(keys, axis=0))
            tiles = [score[:, columns(i, tokens)] for i in range(number)]
            if first == 0:
                row = lax.broadcasted_iota(jnp.int32, (rows, tokens), 0) % tokens
                column = lax.broadcasted_iota(jnp.int32, (rows, tokens), 1)
                tiles = [jnp.where(column <= row, tiles[0], score_masked)]
            else:
                tiles = [
                    jnp.where((step > 0) & (step < count), tile, score_masked)
                    for step, tile in zip(steps[first : first + number], tiles)
                ]
            top = functools.reduce(jnp.maximum, tiles)
            top = jnp.max(top, axis=1, keepdims=True) * base2
            top = jnp.broadcast_to(top, (rows, HEAD_SIZE))
            if first:
                old = high[g]
                top = jnp.maximum(old, top)
            weight = [jnp.exp2(t * base2 - top).astype(bf16) for t in tiles]
            blend = jnp.dot(
                jnp.concatenate(weight, axis=1),
                jnp.concatenate(values, axis=0),
                preferred_element_type=jnp.float32,
            )
            if first:
                shrink = jnp.exp2(old - top)
                blend += acc[g] * jnp.concatenate([shrink, shrink], axis=1)
            high[g] = top
            acc[g] = blend

    region(0, 1)
    for first in range(1, len(blocks), REGION):
        number = min(REGION, len(blocks) - first)
        nearest = functools.reduce(jnp.minimum, steps[first : first + number])
        pl.when(count > nearest)(functools.partial(region, first, number))

    for g in range(KEY_VALUE_HEADS):
        result = (acc[g, :, :HEAD_SIZE] / acc[g, :, HEAD_SIZE:]).astype(bf16)
        for j in range(GROUP_SPLIT):
            for ref in (out_ref, copy_ref):
                ref[:, columns(g * GROUP_SPLIT + j, HEAD_SIZE)] = result[columns(j, tokens)]


def attend(plan, queries, blocks, steps):
    tokens = blocks[0].shape[0]
    rows = GROUP_SPLIT * tokens
    limit = VMEM_LIMIT if len(blocks) < 16 else 2 * VMEM_LIMIT
    return pl.pallas_call(
        functools.partial(attend_kernel, steps),
        out_shape=[jax.ShapeDtypeStruct((tokens, QUERY_HEADS * HEAD_SIZE), jnp.bfloat16)] * 2,
        in_specs=smem() + vmem(1 + len(blocks)),
        out_specs=vmem(2),
        scratch_shapes=[
            pltpu.VMEM((KEY_VALUE_HEADS, rows, HEAD_SIZE), jnp.float32),
            pltpu.VMEM((KEY_VALUE_HEADS, rows, 2 * HEAD_SIZE), jnp.float32),
        ],
        compiler_params=pltpu.CompilerParams(vmem_limit_bytes=limit),
        cost_estimate=pl.CostEstimate(
            flops=12_000_000_000, bytes_accessed=8 << 20, transcendentals=4 << 20
        ),
        name="attend",
    )(plan, queries, *blocks)


def output_kernel(attended_ref, piece_ref, out_ref, down, up, held, in_sem, out_sem):
    q_head, d = down.shape[3], up.shape[3]
    halves = down.shape[1]

    def take(copy, at, half, index):
        source = piece_ref.at[half, pl.ds(0, copy.shape[0]), :, pl.ds(at, copy.shape[3])]
        return pltpu.make_async_copy(source, copy.at[:, half], in_sem.at[index, half])

    takes = [take(down, 0, h, 0) for h in range(halves)]
    takes_up = [take(up, q_head, h, 1) for h in range(halves)]
    for copy in takes + takes_up:
        copy.start()
    for copy in takes:
        copy.wait()
    low = jnp.zeros((attended_ref.shape[0], ROW_BLOCKS * 16), jnp.float32)
    for chunk in range(CHUNKS):
        low += dot_nt(attended_ref[:, columns(chunk, q_head)], factor(down, chunk, 0, q_head))
    low = low.astype(jnp.bfloat16)
    for copy in takes_up:
        copy.wait()
    gives = []
    for chunk in range(CHUNKS):
        result = adapter_scale * jnp.dot(
            low, factor(up, chunk, 0, d), preferred_element_type=jnp.float32
        )
        at = pl.ds(chunk * d, d)
        held[:, at] = result.astype(jnp.bfloat16)
        gives.append(
            pltpu.make_async_copy(held.at[:, at], out_ref.at[:, at], out_sem.at[chunk])
        )
        gives[-1].start()
    for copy in gives:
        copy.wait()


def output_adapter(attended, pieces, model_width):
    tokens, query_width = attended.shape
    halves, places = pieces.shape[0], pieces.shape[1]
    any_space = pl.BlockSpec(memory_space=pl.ANY)
    return pl.pallas_call(
        output_kernel,
        out_shape=jax.ShapeDtypeStruct((tokens, model_width), jnp.bfloat16),
        in_specs=vmem() + [any_space],
        out_specs=any_space,
        scratch_shapes=[
            pltpu.VMEM((places, halves, 16, query_width // CHUNKS), jnp.bfloat16),
            pltpu.VMEM((places, halves, 16, model_width // CHUNKS), jnp.bfloat16),
            pltpu.VMEM((tokens, model_width), jnp.bfloat16),
            pltpu.SemaphoreType.DMA((2, halves)),
            pltpu.SemaphoreType.DMA((CHUNKS,)),
        ],
        compiler_params=PARAMS,
        cost_estimate=pl.CostEstimate(
            flops=100_000_000, bytes_accessed=3 << 20, transcendentals=0
        ),
        name="output",
    )(attended, pieces)


def earlier_shards(shards):
    longest = shards // 2 + 1
    low = -(longest // 2)
    runs = (
        [i % shards for i in range(low, low + longest)],
        [i % shards for i in range(low + longest, low + shards)],
    )
    limits = (longest, shards - longest - 1)
    earlier = {}
    for run, limit in zip(runs, limits):
        for i, shard in enumerate(run):
            earlier[shard] = set(run[max(0, i - limit + 1) : i])
    return earlier


def shift_pairs(shards, shift):
    earlier = earlier_shards(shards)
    pairs = [((d - shift) % shards, d) for d in range(shards)]
    return [(s, d) for s, d in pairs if s in earlier[d] or s in earlier[d ^ 1]]


def swap_pairs(shards, shift):
    earlier = earlier_shards(shards)
    return [(d, d ^ 1) for d in range(shards) if (d - shift) % shards in earlier[d ^ 1]]


def exchange(kv, queries, shards, reach):
    shifts = range(0, reach + 1, 2)
    got = [kv] + [lax.ppermute(kv, "ctx", shift_pairs(shards, s)) for s in shifts[1:]]
    got[1:], queries = lax.optimization_barrier((got[1:], queries))
    swapped = [lax.ppermute(b, "ctx", swap_pairs(shards, s)) for s, b in zip(shifts, got)]
    blocks, steps = [kv], [(0, True)]
    for s, even, odd in zip(shifts, got, swapped):
        if s:
            blocks.append(even)
            steps.append((s, True))
        blocks.append(odd)
        steps.append((s, False))
    return blocks, steps, queries


def body(
    hidden,
    frozen_query,
    frozen_key,
    frozen_value,
    adapter_bank,
    request_shards,
    request_adapter,
    adapter_owner,
):
    shards = lax.axis_size("ctx")
    groups = lax.axis_size("groups")
    tokens, model_width = hidden.shape
    halves = 2 if groups == 2 and 2 * shards == ROW_BLOCKS * CHUNKS else 1
    own_half = lax.axis_index("groups") if halves == 2 else 0
    me = jnp.stack([lax.axis_index("ctx"), own_half]).astype(jnp.int32)
    parts = Parts(model_width, frozen_query.shape[1], frozen_key.shape[1])
    reach = shards // 2

    packed = pack(parts, halves, shards, adapter_bank)
    spread = lax.all_to_all(packed, "ctx", split_axis=0, concat_axis=0, tiled=True)

    requests = jnp.stack([request_shards, request_adapter])[:, None]
    if halves == 2:
        theirs = lax.ppermute(requests, "groups", [(0, 1), (1, 0)])
        requests = jnp.concatenate([requests, theirs], axis=1)
    plan = make_plan(shards, reach, me, requests[0], requests[1], adapter_owner)
    plan = jnp.maximum(plan, 0)
    positions = (plan[0, COUNT] - 1) * tokens + jnp.arange(tokens, dtype=jnp.int32)
    tables = rope_tables(positions)
    spread, tables, plan = lax.optimization_barrier((spread, tables, plan))

    def collect(pieces, axes, sizes):
        axes = axes if halves == 2 else "ctx"
        pieces = lax.all_to_all(pieces, axes, split_axis=0, concat_axis=0, tiled=True)
        return pieces.reshape(sizes + pieces.shape[1:])

    places = ROW_BLOCKS * CHUNKS // halves
    kv_width, q_width, o_width = parts.widths
    dests = shards * halves
    pieces = route(plan, spread, dests, 0, kv_width + q_width)
    pieces = collect(pieces, ("ctx", "groups"), (shards, halves))[:places]
    kv = make_keys_values(hidden, frozen_key, frozen_value, tables, pieces)
    queries = make_queries(hidden, frozen_query, tables, pieces, kv_width)
    blocks, steps, queries = exchange(kv, queries, shards, reach)
    later = route(plan, spread, dests, kv_width + q_width, o_width, halves)
    kv, later = lax.optimization_barrier((kv, later))
    later = collect(later, ("groups", "ctx"), (halves, shards))[:, :places]
    attended, copy = attend(plan, queries, blocks, steps)
    return attended, output_adapter(copy, later, model_width)


def solution(mesh):
    return jax.shard_map(
        body,
        mesh=mesh,
        in_specs=(
            P(("groups", "ctx"), None),
            P(("groups", "ctx"), None),
            P(("groups", "ctx"), None),
            P(("groups", "ctx"), None),
            P("ctx", None, None),
            P("groups"),
            P("groups"),
            P(),
        ),
        out_specs=(P(("groups", "ctx"), None), P(("groups", "ctx"), None)),
        check_vma=False,
    )
```

```python
import functools

import jax
import jax.numpy as jnp
from jax import lax
from jax.experimental import pallas as pl
from jax.experimental.pallas import tpu as pltpu
from jax.sharding import PartitionSpec as P

HEAD_SIZE = 128
QUERY_HEADS = 16
KEY_VALUE_HEADS = 4
GROUP_SPLIT = QUERY_HEADS // KEY_VALUE_HEADS

adapter_scale = 0.5
rope_theta = 500000.0
score_masked = -1e30

VMEM_LIMIT = 24 * 1024 * 1024

ROW_BLOCKS = 4
CHUNKS = 8


def rope_tables(positions):
    half_dim = HEAD_SIZE // 2
    frequency = rope_theta ** (-(jnp.arange(half_dim, dtype=jnp.float32) * 2.0) / HEAD_SIZE)
    angles = positions.astype(jnp.float32)[..., None] * frequency
    cosines = jnp.cos(angles)
    sines = jnp.sin(angles)
    return (jnp.concatenate([cosines, cosines], -1), jnp.concatenate([-sines, sines], -1))


class Parts:
    def __init__(self, model_width, query_width, key_width):
        d, q, k = model_width, query_width, key_width
        up = 3 * d
        self.kv = ((d, d // CHUNKS), (2 * d, d // CHUNKS), (up + q, 2 * k // CHUNKS))
        self.q = ((0, d // CHUNKS), (up, q // CHUNKS))
        self.o = ((up + q + 2 * k, q // CHUNKS), (up + 2 * q + 2 * k, d // CHUNKS))
        self.all = self.kv + self.q + self.o
        self.widths = tuple(sum(w for _, w in part) for part in (self.kv, self.q, self.o))


def vmem(count=1):
    return [pl.BlockSpec(memory_space=pltpu.VMEM)] * count


def smem(count=1):
    return [pl.BlockSpec(memory_space=pltpu.SMEM)] * count


PARAMS = pltpu.CompilerParams(vmem_limit_bytes=VMEM_LIMIT)


OWN_INDEX, COUNT, ENTRY = 0, 1, 8


def layout(lengths_ref, which, shards):
    starts, start, length = [jnp.int32(0)], jnp.int32(0), lengths_ref[which, 0]
    for r in range(1, lengths_ref.shape[1]):
        starts.append(starts[-1] + lengths_ref[which, r - 1])
        longer = lengths_ref[which, r] > length
        start = jnp.where(longer, starts[-1], start)
        length = jnp.where(longer, lengths_ref[which, r], length)
    return starts, start + lax.div(length, 2)


def plan_kernel(shards, reach, me_ref, lengths_ref, adapters_ref, owner_ref, out_ref):
    own_index, own_half = me_ref[0], me_ref[1]
    starts, offset = layout(lengths_ref, 0, shards)
    own_packed = lax.rem(own_index + offset, shards)
    first = jnp.int32(0)
    for start in starts[1:]:
        first = jnp.where(start <= own_packed, start, first)
    lanes = lax.broadcasted_iota(jnp.int32, out_ref.shape, 1)
    plan = jnp.where(lanes == COUNT, jnp.minimum(own_packed - first, reach) + 1, own_index)
    for which in range(lengths_ref.shape[0]):
        starts, offset = layout(lengths_ref, which, shards)
        entries = [owner_ref[adapters_ref[which, r]] for r in range(len(starts))]
        at = ENTRY + shards * (own_half if which == 0 else 1 - own_half)
        for shard in range(shards):
            packed = lax.rem(shard + offset, shards)
            entry = entries[0]
            for start, later in zip(starts[1:], entries[1:]):
                entry = jnp.where(start <= packed, later, entry)
            plan = jnp.where(lanes == at + shard, entry, plan)
    out_ref[...] = plan


def make_plan(shards, reach, me, lengths, adapters, owner):
    return pl.pallas_call(
        functools.partial(plan_kernel, shards, reach),
        out_shape=jax.ShapeDtypeStruct((1, 128), jnp.int32),
        in_specs=smem(4),
        out_specs=vmem()[0],
        name="plan",
    )(me, lengths, adapters, owner)


def pack_kernel(parts, halves, bank_ref, out_ref, held, in_sem, out_sem):
    own_half = lax.axis_index("groups") if halves == 2 else 0
    takes, gives = [], []
    for place in range(held.shape[0]):
        at = 0
        for index, (first, width) in enumerate(parts.all):
            start = pl.multiple_of(first + (place * halves + own_half) * width, 128)
            takes.append(
                pltpu.make_async_copy(
                    bank_ref.at[:, :, pl.ds(start, width)],
                    held.at[place, :, :, pl.ds(at, width)],
                    in_sem.at[place, index],
                )
            )
            at += width
        gives += [
            pltpu.make_async_copy(
                held.at[place], out_ref.at[again, place], out_sem.at[again, place]
            )
            for again in range(out_ref.shape[0])
        ]
    for copy in takes:
        copy.start()
    each, again = len(parts.all), out_ref.shape[0]
    for place in range(held.shape[0]):
        for copy in takes[place * each : (place + 1) * each]:
            copy.wait()
        for copy in gives[place * again : (place + 1) * again]:
            copy.start()
    for copy in gives:
        copy.wait()


def pack(parts, halves, shards, bank):
    width, places = sum(parts.widths), CHUNKS // halves
    again = shards // (places * ROW_BLOCKS)
    packed = pl.pallas_call(
        functools.partial(pack_kernel, parts, halves),
        out_shape=jax.ShapeDtypeStruct((again, places, ROW_BLOCKS, 16, width), bank.dtype),
        in_specs=[pl.BlockSpec(memory_space=pl.ANY)],
        out_specs=pl.BlockSpec(memory_space=pl.ANY),
        scratch_shapes=[
            pltpu.VMEM((places, ROW_BLOCKS, 16, width), bank.dtype),
            pltpu.SemaphoreType.DMA((places, len(parts.all))),
            pltpu.SemaphoreType.DMA((again, places)),
        ],
        compiler_params=pltpu.CompilerParams(vmem_limit_bytes=62 * 1024 * 1024),
        name="pack",
    )(bank.reshape(ROW_BLOCKS, 16, bank.shape[2]))
    return packed.reshape(shards, 16, width)


ROUTE_STEPS = 4


def route_kernel(at, plan_ref, spread_ref, out_ref):
    number = out_ref.shape[0]
    for i in range(number):
        entry = plan_ref[0, ENTRY + pl.program_id(0) * number + i]
        out_ref[i] = spread_ref[entry, :, at : at + out_ref.shape[2]]


def route(plan, spread, dests, at, width):
    return pl.pallas_call(
        functools.partial(route_kernel, at),
        out_shape=jax.ShapeDtypeStruct((dests, 16, width), spread.dtype),
        grid=(ROUTE_STEPS,),
        in_specs=smem() + vmem(),
        out_specs=pl.BlockSpec((dests // ROUTE_STEPS, 16, width), lambda i: (i, 0, 0)),
        compiler_params=PARAMS,
        name="route",
    )(plan, spread)


def factor(piece_ref, chunk, at, width):
    halves = piece_ref.shape[0]
    place = chunk // halves * ROW_BLOCKS
    rows = piece_ref[chunk % halves, place : place + ROW_BLOCKS, :, at : at + width]
    return rows.reshape(ROW_BLOCKS * 16, width)


def columns(chunk, width):
    return slice(chunk * width, (chunk + 1) * width)


def dot_nt(a, b):
    return lax.dot_general(a, b, (((1,), (1,)), ((), ())), preferred_element_type=jnp.float32)


def turn(x, cosines, sines):
    return x * cosines + pltpu.roll(x, HEAD_SIZE // 2, 1) * sines


def kv_kernel(hidden_ref, key_ref, value_ref, cos_ref, sin_ref, piece_ref, out_ref):
    d = hidden_ref.shape[1] // CHUNKS
    rank = ROW_BLOCKS * 16
    low = jnp.zeros((hidden_ref.shape[0], 2 * rank), jnp.float32)
    for chunk in range(CHUNKS):
        down = jnp.concatenate(
            [factor(piece_ref, chunk, 0, d), factor(piece_ref, chunk, d, d)], axis=0
        )
        low += dot_nt(hidden_ref[:, columns(chunk, d)], down)
    low = low.astype(jnp.bfloat16)
    width = 2 * key_ref.shape[1] // CHUNKS
    cosines, sines = cos_ref[...], sin_ref[...]
    for chunk in range(CHUNKS):
        is_key = chunk < CHUNKS // 2
        up = factor(piece_ref, chunk, 2 * d, width)
        part = low[:, :rank] if is_key else low[:, rank:]
        update = jnp.dot(part, up, preferred_element_type=jnp.float32)
        frozen = (key_ref if is_key else value_ref)[:, columns(chunk % (CHUNKS // 2), width)]
        result = frozen.astype(jnp.float32) + adapter_scale * update
        if is_key:
            result = turn(result, cosines, sines)
        out_ref[:, columns(chunk, width)] = result.astype(jnp.bfloat16)


def make_keys_values(hidden, key, value, tables, pieces):
    return pl.pallas_call(
        kv_kernel,
        out_shape=jax.ShapeDtypeStruct((key.shape[0], 2 * key.shape[1]), jnp.bfloat16),
        in_specs=vmem(6),
        out_specs=vmem()[0],
        compiler_params=PARAMS,
        cost_estimate=pl.CostEstimate(
            flops=150_000_000, bytes_accessed=3 << 20, transcendentals=0
        ),
        name="keys_values",
    )(hidden, key, value, *tables, pieces)


def query_kernel(at, hidden_ref, query_ref, cos_ref, sin_ref, piece_ref, out_ref):
    tokens = query_ref.shape[0]
    d = hidden_ref.shape[1] // CHUNKS
    width = query_ref.shape[1] // CHUNKS
    low = jnp.zeros((tokens, ROW_BLOCKS * 16), jnp.float32)
    for chunk in range(CHUNKS):
        low += dot_nt(hidden_ref[:, columns(chunk, d)], factor(piece_ref, chunk, at, d))
    low = low.astype(jnp.bfloat16)
    cosines, sines = cos_ref[...], sin_ref[...]
    for chunk in range(CHUNKS):
        up = factor(piece_ref, chunk, at + d, width)
        update = jnp.dot(low, up, preferred_element_type=jnp.float32)
        result = query_ref[:, columns(chunk, width)].astype(jnp.float32) + adapter_scale * update
        for part in range(width // HEAD_SIZE):
            head = chunk * (width // HEAD_SIZE) + part
            turned = turn(result[:, columns(part, HEAD_SIZE)], cosines, sines)
            out_ref[head // GROUP_SPLIT, pl.ds((head % GROUP_SPLIT) * tokens, tokens)] = (
                turned.astype(jnp.bfloat16)
            )


def make_queries(hidden, query, tables, pieces, at):
    tokens = hidden.shape[0]
    return pl.pallas_call(
        functools.partial(query_kernel, at),
        out_shape=jax.ShapeDtypeStruct(
            (KEY_VALUE_HEADS, GROUP_SPLIT * tokens, HEAD_SIZE), jnp.bfloat16
        ),
        in_specs=vmem(5),
        out_specs=vmem()[0],
        compiler_params=PARAMS,
        cost_estimate=pl.CostEstimate(
            flops=100_000_000, bytes_accessed=3 << 20, transcendentals=0
        ),
        name="queries",
    )(hidden, query, *tables, pieces)


REGION = 5


def attend_kernel(steps, plan_ref, queries, *refs):
    blocks, (out_ref, copy_ref, high, acc) = refs[:-4], refs[-4:]
    count = plan_ref[0, COUNT]
    odd = lax.rem(plan_ref[0, OWN_INDEX], 2)
    aside = 2 * odd - 1
    steps = [s if even else s + aside for s, even in steps]
    tokens = out_ref.shape[0]
    rows = GROUP_SPLIT * tokens
    bf16 = jnp.bfloat16
    base2 = 1.4426950408889634 / (HEAD_SIZE**0.5)
    ones = jnp.ones((tokens, HEAD_SIZE), bf16)

    def region(first, number):
        shards = blocks[first : first + number]
        for g in range(KEY_VALUE_HEADS):
            keys = [b[:, columns(g, HEAD_SIZE)] for b in shards]
            values = [
                jnp.concatenate([b[:, columns(KEY_VALUE_HEADS + g, HEAD_SIZE)], ones], axis=1)
                for b in shards
            ]
            score = dot_nt(queries[g], jnp.concatenate(keys, axis=0))
            tiles = [score[:, columns(i, tokens)] for i in range(number)]
            if first == 0:
                row = lax.broadcasted_iota(jnp.int32, (rows, tokens), 0) % tokens
                column = lax.broadcasted_iota(jnp.int32, (rows, tokens), 1)
                tiles = [jnp.where(column <= row, tiles[0], score_masked)]
            else:
                tiles = [
                    jnp.where((step > 0) & (step < count), tile, score_masked)
                    for step, tile in zip(steps[first : first + number], tiles)
                ]
            top = functools.reduce(jnp.maximum, tiles)
            top = jnp.max(top, axis=1, keepdims=True) * base2
            top = jnp.broadcast_to(top, (rows, HEAD_SIZE))
            if first:
                old = high[g]
                top = jnp.maximum(old, top)
            weight = [jnp.exp2(t * base2 - top).astype(bf16) for t in tiles]
            blend = jnp.dot(
                jnp.concatenate(weight, axis=1),
                jnp.concatenate(values, axis=0),
                preferred_element_type=jnp.float32,
            )
            if first:
                shrink = jnp.exp2(old - top)
                blend += acc[g] * jnp.concatenate([shrink, shrink], axis=1)
            high[g] = top
            acc[g] = blend

    region(0, 1)
    for first in range(1, len(blocks), REGION):
        number = min(REGION, len(blocks) - first)
        nearest = functools.reduce(jnp.minimum, steps[first : first + number])
        pl.when(count > nearest)(functools.partial(region, first, number))

    for g in range(KEY_VALUE_HEADS):
        result = (acc[g, :, :HEAD_SIZE] / acc[g, :, HEAD_SIZE:]).astype(bf16)
        for j in range(GROUP_SPLIT):
            for ref in (out_ref, copy_ref):
                ref[:, columns(g * GROUP_SPLIT + j, HEAD_SIZE)] = result[columns(j, tokens)]


def attend(plan, queries, blocks, steps):
    tokens = blocks[0].shape[0]
    rows = GROUP_SPLIT * tokens
    limit = VMEM_LIMIT if len(blocks) < 16 else 2 * VMEM_LIMIT
    return pl.pallas_call(
        functools.partial(attend_kernel, steps),
        out_shape=[jax.ShapeDtypeStruct((tokens, QUERY_HEADS * HEAD_SIZE), jnp.bfloat16)] * 2,
        in_specs=smem() + vmem(1 + len(blocks)),
        out_specs=vmem(2),
        scratch_shapes=[
            pltpu.VMEM((KEY_VALUE_HEADS, rows, HEAD_SIZE), jnp.float32),
            pltpu.VMEM((KEY_VALUE_HEADS, rows, 2 * HEAD_SIZE), jnp.float32),
        ],
        compiler_params=pltpu.CompilerParams(vmem_limit_bytes=limit),
        cost_estimate=pl.CostEstimate(
            flops=12_000_000_000, bytes_accessed=8 << 20, transcendentals=4 << 20
        ),
        name="attend",
    )(plan, queries, *blocks)


def output_kernel(attended_ref, piece_ref, out_ref, down, up, held, in_sem, out_sem):
    q_head, d = down.shape[3], up.shape[3]
    places = down.shape[1]
    halves = down.shape[0]

    def take(copy, at, half, index):
        source = piece_ref.at[half, pl.ds(0, places), :, pl.ds(at, copy.shape[3])]
        return pltpu.make_async_copy(source, copy.at[half], in_sem.at[index, half])

    takes = [take(down, 0, h, 0) for h in range(halves)]
    takes_up = [take(up, q_head, h, 1) for h in range(halves)]
    for copy in takes + takes_up:
        copy.start()
    for copy in takes:
        copy.wait()
    low = jnp.zeros((attended_ref.shape[0], ROW_BLOCKS * 16), jnp.float32)
    for chunk in range(CHUNKS):
        low += dot_nt(attended_ref[:, columns(chunk, q_head)], factor(down, chunk, 0, q_head))
    low = low.astype(jnp.bfloat16)
    for copy in takes_up:
        copy.wait()
    gives = []
    for chunk in range(CHUNKS):
        result = adapter_scale * jnp.dot(
            low, factor(up, chunk, 0, d), preferred_element_type=jnp.float32
        )
        at = pl.ds(chunk * d, d)
        held[:, at] = result.astype(jnp.bfloat16)
        gives.append(
            pltpu.make_async_copy(held.at[:, at], out_ref.at[:, at], out_sem.at[chunk])
        )
        gives[-1].start()
    for copy in gives:
        copy.wait()


def output_adapter(attended, pieces, model_width):
    tokens, query_width = attended.shape
    halves, places = pieces.shape[0], pieces.shape[1]
    any_space = pl.BlockSpec(memory_space=pl.ANY)
    return pl.pallas_call(
        output_kernel,
        out_shape=jax.ShapeDtypeStruct((tokens, model_width), jnp.bfloat16),
        in_specs=vmem() + [any_space],
        out_specs=any_space,
        scratch_shapes=[
            pltpu.VMEM((halves, places, 16, query_width // CHUNKS), jnp.bfloat16),
            pltpu.VMEM((halves, places, 16, model_width // CHUNKS), jnp.bfloat16),
            pltpu.VMEM((tokens, model_width), jnp.bfloat16),
            pltpu.SemaphoreType.DMA((2, halves)),
            pltpu.SemaphoreType.DMA((CHUNKS,)),
        ],
        compiler_params=PARAMS,
        cost_estimate=pl.CostEstimate(
            flops=100_000_000, bytes_accessed=3 << 20, transcendentals=0
        ),
        name="output",
    )(attended, pieces)


def earlier_shards(shards):
    longest = shards // 2 + 1
    low = -(longest // 2)
    runs = (
        [i % shards for i in range(low, low + longest)],
        [i % shards for i in range(low + longest, low + shards)],
    )
    limits = (longest, shards - longest - 1)
    earlier = {}
    for run, limit in zip(runs, limits):
        for i, shard in enumerate(run):
            earlier[shard] = set(run[max(0, i - limit + 1) : i])
    return earlier


def shift_pairs(shards, shift):
    earlier = earlier_shards(shards)
    pairs = [((d - shift) % shards, d) for d in range(shards)]
    return [(s, d) for s, d in pairs if s in earlier[d] or s in earlier[d ^ 1]]


def swap_pairs(shards, shift):
    earlier = earlier_shards(shards)
    return [(d, d ^ 1) for d in range(shards) if (d - shift) % shards in earlier[d ^ 1]]


def exchange(kv, queries, shards, reach):
    shifts = range(0, reach + 1, 2)
    far = [lax.ppermute(kv, "ctx", shift_pairs(shards, s)) for s in reversed(shifts[1:])]
    got = [kv] + far[::-1]
    got[1:], queries = lax.optimization_barrier((got[1:], queries))
    swapped = [lax.ppermute(b, "ctx", swap_pairs(shards, s)) for s, b in zip(shifts, got)]
    blocks, steps = [kv], [(0, True)]
    for s, even, odd in zip(shifts, got, swapped):
        if s:
            blocks.append(even)
            steps.append((s, True))
        blocks.append(odd)
        steps.append((s, False))
    return blocks, steps, queries


def body(
    hidden,
    frozen_query,
    frozen_key,
    frozen_value,
    adapter_bank,
    request_shards,
    request_adapter,
    adapter_owner,
):
    shards = lax.axis_size("ctx")
    groups = lax.axis_size("groups")
    tokens, model_width = hidden.shape
    halves = 2 if groups == 2 and 2 * shards == ROW_BLOCKS * CHUNKS else 1
    own_half = lax.axis_index("groups") if halves == 2 else 0
    me = jnp.stack([lax.axis_index("ctx"), own_half]).astype(jnp.int32)
    parts = Parts(model_width, frozen_query.shape[1], frozen_key.shape[1])
    reach = shards // 2

    packed = pack(parts, halves, shards, adapter_bank)
    spread = lax.all_to_all(packed, "ctx", split_axis=0, concat_axis=0, tiled=True)

    requests = jnp.stack([request_shards, request_adapter])[:, None]
    if halves == 2:
        theirs = lax.ppermute(requests, "groups", [(0, 1), (1, 0)])
        requests = jnp.concatenate([requests, theirs], axis=1)
    plan = make_plan(shards, reach, me, requests[0], requests[1], adapter_owner)
    plan = jnp.maximum(plan, 0)
    positions = (plan[0, COUNT] - 1) * tokens + jnp.arange(tokens, dtype=jnp.int32)
    tables = rope_tables(positions)
    spread, tables, plan = lax.optimization_barrier((spread, tables, plan))

    def collect(pieces):
        axes = ("groups", "ctx") if halves == 2 else "ctx"
        pieces = lax.all_to_all(pieces, axes, split_axis=0, concat_axis=0, tiled=True)
        return pieces.reshape((halves, shards) + pieces.shape[1:])[:, : ROW_BLOCKS * CHUNKS]

    kv_width, q_width, o_width = parts.widths
    dests = shards * halves
    pieces = collect(route(plan, spread, dests, 0, kv_width + q_width))
    kv = make_keys_values(hidden, frozen_key, frozen_value, tables, pieces)
    queries = make_queries(hidden, frozen_query, tables, pieces, kv_width)
    blocks, steps, queries = exchange(kv, queries, shards, reach)
    later = route(plan, spread, dests, kv_width + q_width, o_width)
    kv, later = lax.optimization_barrier((kv, later))
    later = collect(later)
    attended, copy = attend(plan, queries, blocks, steps)
    return attended, output_adapter(copy, later, model_width)


def solution(mesh):
    return jax.shard_map(
        body,
        mesh=mesh,
        in_specs=(
            P(("groups", "ctx"), None),
            P(("groups", "ctx"), None),
            P(("groups", "ctx"), None),
            P(("groups", "ctx"), None),
            P("ctx", None, None),
            P("groups"),
            P("groups"),
            P(),
        ),
        out_specs=(P(("groups", "ctx"), None), P(("groups", "ctx"), None)),
        check_vma=False,
    )
```
